32 devices in a mesh: fsdp: 8 (over z, x), dp: 4 (over y, core).
Axes of the slice: x: 2, y: 2, z: 4, core: 2. Of those that a mesh axis runs over, the one named last changes fastest.
Arguments:
- patches: bfloat16 [128, 256, 588], P(('fsdp', 'dp')), may hold values from -6 to 6
- patch_mask: int32 [128, 256], P(('fsdp', 'dp')), may hold values 0 or 1
- image_valid: int32 [128], replicated, may hold values from 0 to 1, as said below
- centre: float32 [65536], replicated, may hold values from -0.6 to 0.6
- w_patch: float32 [384, 588], P('fsdp'), may hold values from -0.25 to 0.25
- first_patch: float32 [384, 588], P('fsdp'), may hold values from -1.1920929e-06 to 1.1920929e-06
- second_patch: float32 [384, 588], P('fsdp'), may hold values from 9.598043e-16 to 3.839217e-15
- teacher_patch: float32 [384, 588], P('fsdp'), may hold values from -0.25 to 0.25
- w_layer: float32 [2, 384, 4608], P(None, 'fsdp'), may hold values from -0.3125 to 0.3125
- first_layer: float32 [2, 384, 4608], P(None, 'fsdp'), may hold values from -1.1920929e-06 to 1.1920929e-06
- second_layer: float32 [2, 384, 4608], P(None, 'fsdp'), may hold values from 3.839217e-15 to 1.5356868e-14
- teacher_layer: float32 [2, 384, 4608], P(None, 'fsdp'), may hold values from -0.3125 to 0.3125
- w_head: float32 [2688, 2048], P('fsdp'), may hold values from -0.125 to 0.125
- first_head: float32 [2688, 2048], P('fsdp'), may hold values from -1.1920929e-06 to 1.1920929e-06
- second_head: float32 [2688, 2048], P('fsdp'), may hold values from 3.839217e-15 to 1.5356868e-14
- teacher_head: float32 [2688, 2048], P('fsdp'), may hold values from -0.125 to 0.125
- w_proto: float32 [65536, 256], P('fsdp'), may hold values from -1.25 to 1.25
- first_proto: float32 [65536, 256], P('fsdp'), may hold values from -1.1920929e-06 to 1.1920929e-06
- second_proto: float32 [65536, 256], P('fsdp'), may hold values from 3.839217e-15 to 1.5356868e-14
- teacher_proto: float32 [65536, 256], P('fsdp'), may hold values from -1.25 to 1.25
- vectors: float32 [274, 384], replicated, as said below
- first_vectors: float32 [274, 384], replicated, may hold values from -1.1920929e-06 to 1.1920929e-06
- second_vectors: float32 [274, 384], replicated, may hold values from 1.1517652e-14 to 4.6070607e-14
- teacher_vectors: float32 [274, 384], replicated, as said below
Outputs:
- loss_sum: float32 [], replicated
- valid_count: float32 [], replicated
- grad_norm: float32 [], replicated
- new_centre: float32 [65536], replicated
- new_patch: float32 [384, 588], P('fsdp')
- new_first_patch: float32 [384, 588], P('fsdp')
- new_second_patch: float32 [384, 588], P('fsdp')
- new_teacher_patch: float32 [384, 588], P('fsdp')
- new_layer: float32 [2, 384, 4608], P(None, 'fsdp')
- new_first_layer: float32 [2, 384, 4608], P(None, 'fsdp')
- new_second_layer: float32 [2, 384, 4608], P(None, 'fsdp')
- new_teacher_layer: float32 [2, 384, 4608], P(None, 'fsdp')
- new_head: float32 [2688, 2048], P('fsdp')
- new_first_head: float32 [2688, 2048], P('fsdp')
- new_second_head: float32 [2688, 2048], P('fsdp')
- new_teacher_head: float32 [2688, 2048], P('fsdp')
- new_proto: float32 [65536, 256], P('fsdp')
- new_first_proto: float32 [65536, 256], P('fsdp')
- new_second_proto: float32 [65536, 256], P('fsdp')
- new_teacher_proto: float32 [65536, 256], P('fsdp')
- new_vectors: float32 [274, 384], replicated
- new_first_vectors: float32 [274, 384], replicated
- new_second_vectors: float32 [274, 384], replicated
- new_teacher_vectors: float32 [274, 384], replicated
The draws below stay inside these ranges and needn't reach their ends.
Inputs may be any that keep to these rules, and one draw needn't show every extreme that they name: `image_valid`: the last image always counts. `vectors`: rows follow the layout of the vector table; gains are positive. `teacher_vectors`: same layout as vectors.
All inputs are finite; a program needn't handle non-finite values. No bound on the sum of `patch_mask` on one device may be relied on, other than what follows from the above.
Results may differ from the reference program's by a relative error of at most 0.02.
Values may be sent and summed in bfloat16 or wider, within the bound.
A program may use at most 448 MiB of HBM per device.

```python
import math
import jax
import jax.numpy as jnp
from jax import lax

D = 384
HEADS = 6
FF = 1536
PATCHES = 256
PDIM = 588
HH = 2048
BOT = 256
K = 65536
L = 2
STEP = 10
SEQ = 257
IMAGES = 128
NV = 274
PARAMS = 26046976


def vector_table(key):
    rows_index = jax.lax.broadcasted_iota(jnp.int32, (NV, D), 0)
    cols_index = jax.lax.broadcasted_iota(jnp.int32, (NV, D), 1)
    normal_key, uniform_key = jax.random.split(key)
    normals = jax.random.normal(normal_key, (NV, D), jnp.float32)
    uniforms = jax.random.uniform(uniform_key, (NV, D), jnp.float32)
    rising = 0.5 + cols_index.astype(jnp.float32) / D
    layer_kind = jnp.mod(rows_index - SEQ - 3, 6)
    kind_code = jnp.where(rows_index < SEQ + 3, 6, layer_kind)
    kind_code = jnp.where(rows_index == NV - 2, 0, kind_code)
    kind_code = jnp.where(rows_index == NV - 1, 1, kind_code)
    gains = rising * (0.8 + 0.4 * uniforms)
    shifts = 0.1 * normals
    scales = 0.3 + 0.7 * uniforms
    embeds = 0.5 * normals
    gain_like = (kind_code == 0) | (kind_code == 3)
    shift_like = (kind_code == 1) | (kind_code == 4)
    scale_like = (kind_code == 2) | (kind_code == 5)
    table = jnp.where(gain_like, gains, jnp.where(shift_like, shifts, jnp.where(scale_like, scales, embeds)))
    return table.astype(jnp.float32)


def draw_vectors(key, part):
    key = jax.random.fold_in(key, 1)
    return vector_table(key)


def draw_teacher_vectors(key, part):
    key = jax.random.fold_in(key, 2)
    return vector_table(key)


def draw_image_valid(key, part):
    key = jax.random.fold_in(key, 3)
    positions = jnp.arange(IMAGES, dtype=jnp.int32)
    limits = 300 + 700 * positions // IMAGES
    picks = jax.random.randint(key, (IMAGES,), 0, 1000, dtype=jnp.int32)
    chosen = jnp.where(picks < limits, 1, 0)
    return jnp.where(positions == IMAGES - 1, 1, chosen).astype(jnp.int32)


def set_ends(array, own_key, low, high):
    place = [jax.random.randint(jax.random.fold_in(own_key, axis), (), 0, length) for axis, length in enumerate(array.shape)]
    longest = array.shape.index(max(array.shape))
    next_to = place[:longest] + [(place[longest] + 1) % array.shape[longest]] + place[longest + 1:]
    return array.at[tuple(place)].set(low).at[tuple(next_to)].set(high)


def shard_levels(stream_key, extent, cuts, low, top_value):
    level, own = 1.0, jax.random.fold_in(stream_key, 6)
    for position, shards_of in cuts:
        draws = jnp.exp(jax.random.uniform(jax.random.fold_in(own, position), (shards_of,), jnp.float32, low / len(cuts), top_value / len(cuts)))
        level = level * jnp.repeat(draws, extent[position] // shards_of).reshape([-1 if axis == position else 1 for axis in range(len(extent))])
    return level


def scatter_about(own_key, dims, scale, reach, cuts=(), kind=jnp.bfloat16):
    result = scale * jax.random.normal(own_key, dims, jnp.float32)
    if cuts:
        result = result * shard_levels(own_key, dims, cuts, -0.22, 0.18)
    return jnp.clip(result, -reach, reach).astype(kind)


def setup_inputs(seed: int = 0) -> dict:
    keys = jax.random.split(jax.random.key(seed), 25)
    return {
        "patches": scatter_about(keys[0], (IMAGES, PATCHES, PDIM), 1.0, 6.0, ((0, 32),)),
        "patch_mask": set_ends((jax.random.randint(keys[1], (IMAGES, PATCHES), 0, 10) < 3).astype(jnp.int32), jax.random.fold_in(keys[1], 1), 0, 1),
        "image_valid": draw_image_valid(jax.random.fold_in(keys[24], 71), 0),
        "centre": scatter_about(keys[3], (K,), 0.1, 0.6, (), jnp.float32),
        "w_patch": scatter_about(keys[4], (D, PDIM), PDIM ** -0.5, 0.25, ((0, 8),), jnp.float32),
        "first_patch": scatter_about(keys[5], (D, PDIM), (0.0011 * PARAMS ** -0.5), 1.1920928955078125e-06, ((0, 8),), jnp.float32),
        "second_patch": jnp.clip(jnp.exp(math.log(3.839217067495111e-15) - 1.3862944 * jax.random.uniform(keys[6], (D, PDIM), jnp.float32) ** shard_levels(keys[6], (D, PDIM), ((0, 8),), -0.2, 0.2)), 9.598042668737777e-16, 3.839217067495111e-15),
        "teacher_patch": scatter_about(keys[7], (D, PDIM), PDIM ** -0.5, 0.25, ((0, 8),), jnp.float32),
        "w_layer": scatter_about(keys[8], (L, D, 4 * D + 2 * FF), D ** -0.5, 0.3125, ((1, 8),), jnp.float32),
        "first_layer": scatter_about(keys[9], (L, D, 4 * D + 2 * FF), (0.0011 * PARAMS ** -0.5), 1.1920928955078125e-06, ((1, 8),), jnp.float32),
        "second_layer": jnp.clip(jnp.exp(math.log(1.5356868269980443e-14) - 1.3862944 * jax.random.uniform(keys[10], (L, D, 4 * D + 2 * FF), jnp.float32) ** shard_levels(keys[10], (L, D, 4 * D + 2 * FF), ((1, 8),), -0.2, 0.2)), 3.839217067495111e-15, 1.5356868269980443e-14),
        "teacher_layer": scatter_about(keys[11], (L, D, 4 * D + 2 * FF), D ** -0.5, 0.3125, ((1, 8),), jnp.float32),
        "w_head": scatter_about(keys[12], (D + HH + BOT, HH), HH ** -0.5, 0.125, ((0, 8),), jnp.float32),
        "first_head": scatter_about(keys[13], (D + HH + BOT, HH), (0.0011 * PARAMS ** -0.5), 1.1920928955078125e-06, ((0, 8),), jnp.float32),
        "second_head": jnp.clip(jnp.exp(math.log(1.5356868269980443e-14) - 1.3862944 * jax.random.uniform(keys[14], (D + HH + BOT, HH), jnp.float32) ** shard_levels(keys[14], (D + HH + BOT, HH), ((0, 8),), -0.2, 0.2)), 3.839217067495111e-15, 1.5356868269980443e-14),
        "teacher_head": scatter_about(keys[15], (D + HH + BOT, HH), HH ** -0.5, 0.125, ((0, 8),), jnp.float32),
        "w_proto": scatter_about(keys[16], (K, BOT), 25 ** -0.5, 1.25, ((0, 8),), jnp.float32),
        "first_proto": scatter_about(keys[17], (K, BOT), (0.0011 * PARAMS ** -0.5), 1.1920928955078125e-06, ((0, 8),), jnp.float32),
        "second_proto": jnp.clip(jnp.exp(math.log(1.5356868269980443e-14) - 1.3862944 * jax.random.uniform(keys[18], (K, BOT), jnp.float32) ** shard_levels(keys[18], (K, BOT), ((0, 8),), -0.2, 0.2)), 3.839217067495111e-15, 1.5356868269980443e-14),
        "teacher_proto": scatter_about(keys[19], (K, BOT), 25 ** -0.5, 1.25, ((0, 8),), jnp.float32),
        "vectors": draw_vectors(jax.random.fold_in(keys[24], 71), 0),
        "first_vectors": scatter_about(keys[21], (NV, D), (0.0011 * PARAMS ** -0.5), 1.1920928955078125e-06, (), jnp.float32),
        "second_vectors": jnp.clip(jnp.exp(jax.random.uniform(keys[22], (NV, D), jnp.float32, math.log(1.1517651626001806e-14), math.log(4.6070606504007225e-14))), 1.1517651626001806e-14, 4.6070606504007225e-14),
        "teacher_vectors": draw_teacher_vectors(jax.random.fold_in(keys[24], 71), 0),
    }


PRECISION_MODE = lax.Precision.HIGHEST
STUDENT_TEMP = 0.1
TEACHER_TEMP = 0.07
CENTRE_KEEP = 0.9
TEACHER_KEEP = 0.8
BETA_ONE = 0.9
BETA_TWO = 0.999
CLIP_NORM = 0.01
RATES = (0.1, 0.15, 0.07, 0.5, 0.5)
DECAYS = (0.04, 0.04, 0.04, 0.04, 0.0)

@jax.custom_vjp
def low(v):
    return lax.optimization_barrier(v.astype(jnp.bfloat16)).astype(jnp.float32)

@jax.custom_vjp
def low_back(v):
    return v

def low_keep(v):
    return (low(v), None)

def low_pass(kept, grad):
    return (grad,)

def back_keep(v):
    return (v, None)

def back_low(kept, grad):
    return (low(grad),)
low.defvjp(low_keep, low_pass)
low_back.defvjp(back_keep, back_low)

def matmul(left, right):
    return low_back(jnp.dot(low(left), low(right), precision=PRECISION_MODE))

def layer_norm(x, gain, shift):
    centred = x - lax.optimization_barrier(jnp.mean(x, -1, keepdims=True))
    spread = lax.optimization_barrier(jnp.mean(centred * centred, -1, keepdims=True))
    return centred * lax.rsqrt(spread + 1e-06) * gain + shift

def embed(pixels, covered, patch_weight, vecs):
    length = pixels.shape[1] + 1
    tokens = matmul(pixels, patch_weight.T) + vecs[length + 2]
    covered_col = covered[..., None]
    tokens = tokens * (1.0 - covered_col) + vecs[length + 1] * covered_col
    leading = jnp.broadcast_to(vecs[length], (pixels.shape[0], 1, vecs.shape[1]))
    return jnp.concatenate([leading, tokens], 1) + vecs[:length]

def block(x, layer_weight, vecs, depth_index):
    images, length, model_width = x.shape
    layer_rows = vecs[length + 3 + 6 * depth_index:length + 9 + 6 * depth_index]
    head_width = model_width // HEADS
    normed = layer_norm(x, layer_rows[0], layer_rows[1])
    triple = matmul(normed, layer_weight[:, :3 * model_width]).reshape(images, length, 3, HEADS, head_width)
    queries = low(triple[:, :, 0])
    key_rows = low(triple[:, :, 1])
    value_rows = low(triple[:, :, 2])
    scores = low_back(jnp.einsum('nqhe,nkhe->nhqk', queries, key_rows, precision=PRECISION_MODE)) * head_width ** (-0.5)
    scores = scores - lax.optimization_barrier(jnp.max(scores, -1, keepdims=True))
    attention = jnp.exp(scores)
    attention = attention / lax.optimization_barrier(jnp.sum(attention, -1, keepdims=True))
    mixture = low_back(jnp.einsum('nhqk,nkhe->nqhe', low(attention), value_rows, precision=PRECISION_MODE))
    mixture = mixture.reshape(images, length, model_width)
    x = x + layer_rows[2] * matmul(mixture, layer_weight[:, 3 * model_width:4 * model_width])
    normed = layer_norm(x, layer_rows[3], layer_rows[4])
    hidden = (layer_weight.shape[1] - 4 * model_width) // 2
    activated = jax.nn.gelu(matmul(normed, layer_weight[:, 4 * model_width:4 * model_width + hidden]))
    return x + layer_rows[5] * matmul(activated, layer_weight[:, 4 * model_width + hidden:].T)

def head(cls_rows, head_weight, vecs):
    model_width = cls_rows.shape[-1]
    hidden = head_weight.shape[1]
    normed = layer_norm(cls_rows, vecs[-2], vecs[-1])
    leading = jax.nn.gelu(matmul(normed, head_weight[:model_width]))
    second = jax.nn.gelu(matmul(leading, head_weight[model_width:model_width + hidden]))
    bottleneck = matmul(second, head_weight[model_width + hidden:].T)
    return bottleneck * lax.rsqrt(lax.optimization_barrier(jnp.sum(bottleneck * bottleneck, -1, keepdims=True)) + 1e-06)

def teacher_probs(logits, centre):
    scaled = (logits - centre) / TEACHER_TEMP
    expo = jnp.exp(scaled - lax.optimization_barrier(jnp.max(scaled, -1, keepdims=True)))
    return expo / lax.optimization_barrier(jnp.sum(expo, -1, keepdims=True))

def adamw(weight, moment, second, gradient, factor, step_rate, weight_decay):
    clipped = gradient * factor
    moment = BETA_ONE * moment + (1.0 - BETA_ONE) * clipped
    second = BETA_TWO * second + (1.0 - BETA_TWO) * clipped * clipped
    direction = moment / (1.0 - BETA_ONE ** STEP) / (jnp.sqrt(second / (1.0 - BETA_TWO ** STEP)) + 1e-08)
    return (weight - step_rate * (direction + weight_decay * weight), moment, second)

def cross(logits, target):
    scaled = logits / STUDENT_TEMP
    shifted = scaled - lax.optimization_barrier(jnp.max(scaled, -1, keepdims=True))
    return -lax.optimization_barrier(jnp.sum(target * (shifted - jnp.log(lax.optimization_barrier(jnp.sum(jnp.exp(shifted), -1, keepdims=True)))), -1))

def forward(params, pixels, covered):
    patch_weight, layer_weight, head_weight, proto_weight, vecs = params
    x = embed(pixels, covered, patch_weight, vecs)
    for depth_index in range(layer_weight.shape[0]):
        x = block(x, layer_weight[depth_index], vecs, depth_index)
    return matmul(head(x[:, 0], head_weight, vecs), proto_weight.T)

def reference(patches, patch_mask, image_valid, centre, w_patch, first_patch, second_patch, teacher_patch, w_layer, first_layer, second_layer, teacher_layer, w_head, first_head, second_head, teacher_head, w_proto, first_proto, second_proto, teacher_proto, vectors, first_vectors, second_vectors, teacher_vectors):
    counted = image_valid.astype(jnp.float32)
    counted_total = jnp.maximum(jnp.sum(counted), 1.0)
    params = (w_patch, w_layer, w_head, w_proto, vectors)
    teacher = (teacher_patch, teacher_layer, teacher_head, teacher_proto, teacher_vectors)
    groups = IMAGES // 16
    pixels_all = patches.astype(jnp.float32).reshape(groups, 16, PATCHES, PDIM)
    covered_all = patch_mask.astype(jnp.float32).reshape(groups, 16, PATCHES)
    counted_all = counted.reshape(groups, 16)

    def accumulate(running, sliced):
        gradients, loss_total, teacher_total = running
        pixels, covered, counted_rows = sliced
        teacher_logits = forward(teacher, pixels, jnp.zeros_like(covered))
        target = teacher_probs(teacher_logits, centre)

        def block_loss(weights):
            return jnp.sum(counted_rows * cross(forward(weights, pixels, covered), target))
        loss_value, pullback = jax.vjp(block_loss, params)
        gradient, = pullback(jnp.ones_like(loss_value) / counted_total)
        gradients = jax.tree.map(jnp.add, gradients, gradient)
        teacher_total = teacher_total + lax.optimization_barrier(jnp.sum(counted_rows[:, None] * teacher_logits, 0))
        return ((gradients, loss_total + loss_value, teacher_total), None)
    start_grads = jax.tree.map(jnp.zeros_like, params)
    start_state = (start_grads, jnp.zeros((), jnp.float32), jnp.zeros((K,), jnp.float32))
    (gradients, loss_total, teacher_total), _ = lax.scan(accumulate, start_state, (pixels_all, covered_all, counted_all))
    squares = sum((jnp.sum(gradient * gradient) for gradient in gradients))
    norm_value = jnp.sqrt(squares)
    factor = CLIP_NORM / jnp.maximum(norm_value, CLIP_NORM)
    updated_centre = CENTRE_KEEP * centre + (1.0 - CENTRE_KEEP) * teacher_total / counted_total
    moments = (first_patch, first_layer, first_head, first_proto, first_vectors)
    seconds = (second_patch, second_layer, second_head, second_proto, second_vectors)
    results = []
    for group in range(5):
        updated, moment, second = adamw(params[group], moments[group], seconds[group], gradients[group], factor, RATES[group], DECAYS[group])
        results.append((updated, moment, second, TEACHER_KEEP * teacher[group] + (1.0 - TEACHER_KEEP) * updated))
    return (loss_total, counted_total, norm_value, updated_centre, results[0][0], results[0][1], results[0][2], results[0][3], results[1][0], results[1][1], results[1][2], results[1][3], results[2][0], results[2][1], results[2][2], results[2][3], results[3][0], results[3][1], results[3][2], results[3][3], results[4][0], results[4][1], results[4][2], results[4][3])
```

```python
from functools import partial

import jax
import jax.numpy as jnp
from jax import lax
from jax.sharding import PartitionSpec as P

HEADS = 6
STEP = 10
STUDENT_TEMP = 0.1
TEACHER_TEMP = 0.07
CENTRE_KEEP = 0.9
TEACHER_KEEP = 0.8
BETA_ONE = 0.9
BETA_TWO = 0.999
CLIP_NORM = 0.01
RATES = (0.1, 0.15, 0.07, 0.5, 0.5)
DECAYS = (0.04, 0.04, 0.04, 0.04, 0.0)
F32 = jnp.float32
BF16 = jnp.bfloat16


def dot(left, right, dims):
    return lax.dot_general(left, right, (dims, ((), ())), preferred_element_type=F32)


@jax.custom_vjp
def matmul(left, right):
    return jnp.dot(left.astype(BF16), right.astype(BF16), preferred_element_type=F32)


def matmul_keep(left, right):
    left, right = left.astype(BF16), right.astype(BF16)
    return jnp.dot(left, right, preferred_element_type=F32), (left, right)


def matmul_pull(kept, grad):
    left, right = kept
    grad = grad.astype(BF16)
    width = left.ndim - 1
    lead = tuple(range(width))
    return dot(grad, right, ((width,), (1,))), dot(left, grad, (lead, lead))


matmul.defvjp(matmul_keep, matmul_pull)


@partial(jax.custom_vjp, nondiff_argnums=(2,))
def contract(left, right, spec):
    return jnp.einsum(spec, left.astype(BF16), right.astype(BF16), preferred_element_type=F32)


def contract_keep(left, right, spec):
    left, right = left.astype(BF16), right.astype(BF16)
    return jnp.einsum(spec, left, right, preferred_element_type=F32), (left, right)


def contract_pull(spec, kept, grad):
    left, right = kept
    grad = grad.astype(BF16)
    operands, result = spec.split("->")
    first, second = operands.split(",")
    return (
        jnp.einsum(result + "," + second + "->" + first, grad, right, preferred_element_type=F32),
        jnp.einsum(result + "," + first + "->" + second, grad, left, preferred_element_type=F32),
    )


contract.defvjp(contract_keep, contract_pull)


def layer_norm(x, gain, shift):
    centred = x - jnp.mean(x, -1, keepdims=True)
    spread = jnp.mean(centred * centred, -1, keepdims=True)
    return centred * lax.rsqrt(spread + 1e-06) * gain + shift


def embed(pixels, covered, patch_weight, vecs):
    length = pixels.shape[1] + 1
    tokens = matmul(pixels, patch_weight.T) + vecs[length + 2]
    covered_col = covered[..., None]
    tokens = tokens * (1.0 - covered_col) + vecs[length + 1] * covered_col
    leading = jnp.broadcast_to(vecs[length], (pixels.shape[0], 1, vecs.shape[1]))
    return jnp.concatenate([leading, tokens], 1) + vecs[:length]


def mlp(x, layer_weight, rows):
    model_width = x.shape[-1]
    normed = layer_norm(x, rows[3], rows[4])
    hidden = (layer_weight.shape[1] - 4 * model_width) // 2
    up = layer_weight[:, 4 * model_width : 4 * model_width + hidden]
    down = layer_weight[:, 4 * model_width + hidden :]
    activated = jax.nn.gelu(matmul(normed, up))
    return x + rows[5] * matmul(activated, down.T)


def block(x, layer_weight, vecs, depth_index, last):
    images, length, model_width = x.shape
    rows = vecs[length + 3 + 6 * depth_index : length + 9 + 6 * depth_index]
    head_width = model_width // HEADS
    normed = layer_norm(x, rows[0], rows[1])
    asking = normed[:, :1] if last else normed
    queries = matmul(asking, layer_weight[:, :model_width])
    pair = matmul(normed, layer_weight[:, model_width : 3 * model_width])
    queries = queries.reshape(images, -1, HEADS, head_width)
    pair = pair.reshape(images, length, 2, HEADS, head_width)
    scores = contract(queries, pair[:, :, 0], "nqhe,nkhe->nhqk") * head_width ** (-0.5)
    attention = jax.nn.softmax(scores, -1)
    mixture = contract(attention, pair[:, :, 1], "nhqk,nkhe->nqhe")
    mixture = mixture.reshape(images, -1, model_width)
    kept = x[:, :1] if last else x
    x = kept + rows[2] * matmul(mixture, layer_weight[:, 3 * model_width : 4 * model_width])
    return mlp(x, layer_weight, rows)


def backbone(patch_weight, layers, vecs, pixels, covered):
    x = embed(pixels, covered, patch_weight, vecs)
    count = len(layers)
    for depth_index in range(count):
        x = block(x, layers[depth_index], vecs, depth_index, depth_index == count - 1)
    return x[:, 0]


def gathered(owned, axis):
    return lax.all_gather(owned.astype(BF16), "fsdp", axis=axis, tiled=True)


def gathered_layers(owned):
    return [gathered(owned[index], 0) for index in range(owned.shape[0])]


def gelu_slope(x):
    _, pull = jax.vjp(jax.nn.gelu, x)
    return pull(jnp.ones_like(x))[0]


def head_forward(cls, weight, vecs):
    width, hidden = cls.shape[1], weight.shape[1]
    low_n = layer_norm(cls, vecs[-2], vecs[-1]).astype(BF16)
    pre_a = jnp.dot(low_n, weight[:width], preferred_element_type=F32)
    low_a = jax.nn.gelu(pre_a).astype(BF16)
    pre_b = jnp.dot(low_a, weight[width : width + hidden], preferred_element_type=F32)
    low_b = jax.nn.gelu(pre_b).astype(BF16)
    raw = dot(low_b, weight[width + hidden :], ((1,), (1,)))
    return low_n, pre_a, low_a, pre_b, low_b, raw


def unit(raw):
    return raw * lax.rsqrt(jnp.sum(raw * raw, -1, keepdims=True) + 1e-06)


def adamw(weight, moment, second, gradient, factor, step_rate, weight_decay):
    clipped = gradient * factor
    moment = BETA_ONE * moment + (1.0 - BETA_ONE) * clipped
    second = BETA_TWO * second + (1.0 - BETA_TWO) * clipped * clipped
    direction = (
        moment / (1.0 - BETA_ONE**STEP) / (jnp.sqrt(second / (1.0 - BETA_TWO**STEP)) + 1e-08)
    )
    return (weight - step_rate * (direction + weight_decay * weight), moment, second)


def per_device(
    patches,
    patch_mask,
    image_valid,
    centre,
    w_patch,
    first_patch,
    second_patch,
    teacher_patch,
    w_layer,
    first_layer,
    second_layer,
    teacher_layer,
    w_head,
    first_head,
    second_head,
    teacher_head,
    w_proto,
    first_proto,
    second_proto,
    teacher_proto,
    vectors,
    first_vectors,
    second_vectors,
    teacher_vectors,
):
    everyone = ("fsdp", "dp")
    local = patches.shape[0]
    place = lax.axis_index(everyone) * local
    fsdp_index = lax.axis_index("fsdp")
    counted = image_valid.astype(F32)
    counted_total = jnp.maximum(jnp.sum(counted), 1.0)
    covered = patch_mask.astype(F32)

    teacher_patch_full = gathered(teacher_patch, 0)
    teacher_layers_full = gathered_layers(teacher_layer)
    patch_full = gathered(w_patch, 0)
    layers_full = gathered_layers(w_layer)
    teacher_head_full = gathered(teacher_head, 0)
    head_full = gathered(w_head, 0)

    teacher_cls = backbone(
        teacher_patch_full, teacher_layers_full, teacher_vectors, patches, jnp.zeros_like(covered)
    )
    cls, pull_backbone = jax.vjp(
        lambda pw, lw, vv: backbone(pw, lw, vv, patches, covered),
        patch_full.astype(F32),
        [weight.astype(F32) for weight in layers_full],
        vectors,
    )

    teacher_unit = unit(head_forward(teacher_cls, teacher_head_full, teacher_vectors)[-1])
    low_n, pre_a, low_a, pre_b, low_b, raw = head_forward(cls, head_full, vectors)
    bottleneck, pull_unit = jax.vjp(unit, raw)
    both = jnp.concatenate([teacher_unit.astype(BF16), bottleneck.astype(BF16)], -1)
    both = lax.all_gather(both, everyone, axis=0, tiled=True)
    width = raw.shape[1]
    teacher_rows, student_rows = both[:, :width], both[:, width:]

    owned_k = w_proto.shape[0]
    low_proto = w_proto.astype(BF16)
    teacher_logits = dot(teacher_rows, teacher_proto.astype(BF16), ((1,), (1,)))
    logits = dot(student_rows, low_proto, ((1,), (1,)))
    own_centre = lax.dynamic_slice_in_dim(centre, fsdp_index * owned_k, owned_k)
    scaled_t = (teacher_logits - own_centre) / TEACHER_TEMP
    scaled_s = logits / STUDENT_TEMP
    max_t = jnp.max(scaled_t, -1)
    max_s = jnp.max(scaled_s, -1)
    expo_t = jnp.exp(scaled_t - max_t[:, None])
    expo_s = jnp.exp(scaled_s - max_s[:, None])
    parts = jnp.stack(
        [
            max_t,
            jnp.sum(expo_t, -1),
            max_s,
            jnp.sum(expo_s, -1),
            jnp.sum(expo_t * (scaled_s - max_s[:, None]), -1),
        ]
    )
    parts = lax.all_gather(parts, "fsdp", axis=0)
    top_t = jnp.max(parts[:, 0], 0)
    lift_t = jnp.exp(parts[:, 0] - top_t)
    total_t = jnp.sum(parts[:, 1] * lift_t, 0)
    top_s = jnp.max(parts[:, 2], 0)
    total_s = jnp.sum(parts[:, 3] * jnp.exp(parts[:, 2] - top_s), 0)
    crossed = jnp.sum(lift_t * (parts[:, 4] + (parts[:, 2] - top_s) * parts[:, 1]), 0) / total_t
    losses = jnp.log(total_s) - crossed
    loss_total = jnp.sum(counted * losses)
    weighting = counted / counted_total / STUDENT_TEMP
    share_s = weighting * jnp.exp(max_s - top_s) / total_s
    share_t = weighting * jnp.exp(max_t - top_t) / total_t
    grad_logits = (expo_s * share_s[:, None] - expo_t * share_t[:, None]).astype(BF16)
    teacher_sum = jnp.sum(counted[:, None] * teacher_logits, 0)
    teacher_total = lax.all_gather(teacher_sum, "fsdp", axis=0, tiled=True)
    grad_proto = dot(grad_logits, student_rows, ((0,), (0,)))
    grad_rows = jnp.dot(grad_logits, low_proto, preferred_element_type=F32)
    dp_count = lax.axis_size("dp")
    grad_rows = grad_rows.reshape(-1, dp_count, local, width)
    grad_rows = lax.dynamic_index_in_dim(grad_rows, lax.axis_index("dp"), 1, keepdims=False)
    grad_bottleneck = lax.psum_scatter(grad_rows, "fsdp", scatter_dimension=0, tiled=False)

    model_width, hidden = cls.shape[1], head_full.shape[1]
    low_dz = pull_unit(grad_bottleneck)[0].astype(BF16)
    grad_b = jnp.dot(low_dz, head_full[model_width + hidden :], preferred_element_type=F32)
    low_db = (grad_b * gelu_slope(pre_b)).astype(BF16)
    grad_a = dot(low_db, head_full[model_width : model_width + hidden], ((1,), (1,)))
    low_da = (grad_a * gelu_slope(pre_a)).astype(BF16)
    grad_n = dot(low_da, head_full[:model_width], ((1,), (1,)))
    _, pull_norm = jax.vjp(layer_norm, cls, vectors[-2], vectors[-1])
    grad_cls, grad_gain, grad_shift = pull_norm(grad_n)

    packed = jnp.concatenate([low_n, low_a, low_dz, low_da, low_db, low_b], -1)
    packed = lax.all_gather(packed, everyone, axis=0, tiled=True)
    total_rows = model_width + hidden + width
    lefts, rights = packed[:, :total_rows], packed[:, total_rows:]
    own_rows = w_head.shape[0]
    start = fsdp_index * own_rows
    left = lax.dynamic_slice_in_dim(lefts, start, own_rows, 1)
    row = start + lax.broadcasted_iota(jnp.int32, (1, own_rows), 1)
    kind = jnp.where(row < model_width, 0, jnp.where(row < model_width + hidden, 1, 2))
    left = jnp.concatenate([jnp.where(kind == index, left, 0) for index in range(3)], 0)
    right = jnp.concatenate(
        [rights[:, index * hidden : (index + 1) * hidden] for index in range(3)], 0
    )
    grad_head = dot(left, right, ((0,), (0,)))

    grad_patch, grad_layers, grad_vectors = pull_backbone(grad_cls)
    grad_vectors = grad_vectors.at[-2].add(grad_gain).at[-1].add(grad_shift)
    own_patch = lax.psum_scatter(
        grad_patch.astype(BF16), "fsdp", scatter_dimension=0, tiled=True
    )
    own_layers = [
        lax.psum_scatter(piece.astype(BF16), "fsdp", scatter_dimension=0, tiled=True)
        for piece in grad_layers
    ]
    own_patch, own_layers = lax.psum((own_patch, jnp.stack(own_layers)), "dp")
    own_patch, own_layers = own_patch.astype(F32), own_layers.astype(F32)
    vector_grad = lax.psum(grad_vectors, everyone)
    owned_grads = (own_patch, own_layers, grad_head, grad_proto)
    owned_squares = sum((jnp.sum(gradient * gradient) for gradient in owned_grads))
    squares = lax.psum(owned_squares, "fsdp") + jnp.sum(vector_grad * vector_grad)
    norm_value = jnp.sqrt(squares)
    factor = CLIP_NORM / jnp.maximum(norm_value, CLIP_NORM)
    updated_centre = CENTRE_KEEP * centre + (1.0 - CENTRE_KEEP) * teacher_total / counted_total
    weights_owned = (w_patch, w_layer, w_head, w_proto, vectors)
    moments = (first_patch, first_layer, first_head, first_proto, first_vectors)
    seconds = (second_patch, second_layer, second_head, second_proto, second_vectors)
    teachers = (teacher_patch, teacher_layer, teacher_head, teacher_proto, teacher_vectors)
    gradients = owned_grads + (vector_grad,)
    results = [loss_total, counted_total, norm_value, updated_centre]
    for group in range(5):
        updated, moment, second = adamw(
            weights_owned[group],
            moments[group],
            seconds[group],
            gradients[group],
            factor,
            RATES[group],
            DECAYS[group],
        )
        results.extend(
            [
                updated,
                moment,
                second,
                TEACHER_KEEP * teachers[group] + (1.0 - TEACHER_KEEP) * updated,
            ]
        )
    return tuple(results)


def solution(mesh):
    whole, rows, middle = P(), P("fsdp", None), P(None, "fsdp", None)
    in_specs = (
        (P(("fsdp", "dp"), None, None), P(("fsdp", "dp"), None), whole, whole)
        + (rows,) * 4
        + (middle,) * 4
        + (rows,) * 8
        + (whole,) * 4
    )
    out_specs = (whole,) * 4 + (rows,) * 4 + (middle,) * 4 + (rows,) * 8 + (whole,) * 4
    return jax.shard_map(
        per_device, mesh=mesh, in_specs=in_specs, out_specs=out_specs, check_vma=False
    )
```

```python
import functools

import jax
import jax.numpy as jnp
from jax import lax
from jax.experimental import pallas as pl
from jax.experimental.pallas import tpu as pltpu
from jax.sharding import PartitionSpec as P

HEADS = 6
STEP = 10
STUDENT_TEMP = 0.1
TEACHER_TEMP = 0.07
CENTRE_KEEP = 0.9
TEACHER_KEEP = 0.8
BETA_ONE = 0.9
BETA_TWO = 0.999
CLIP_NORM = 0.01
RATES = (0.1, 0.15, 0.07, 0.5, 0.5)
DECAYS = (0.04, 0.04, 0.04, 0.04, 0.0)
F32 = jnp.float32
BF16 = jnp.bfloat16
MESH = pl.DeviceIdType.MESH


def third_ranges(width, start):
    tiles = width // 128
    sizes = [(tiles + 2 - part) // 3 * 128 for part in range(3)]
    spans, at = [], start
    for size in sizes:
        spans.append((at, size))
        at += size
    return spans


def gather_kernel(items, lines, sources, targets, send, recv, copied):
    fsdp, dp = lax.axis_index("fsdp"), lax.axis_index("dp")
    z, x = fsdp // 2, fsdp % 2
    y, core = dp // 2, dp % 2
    across = z * 2 + 1 - x
    mate = y * 2 + 1 - core
    opposite = (1 - y) * 2 + core

    barrier = pltpu.get_barrier_semaphore()

    def greet(f, d):
        pl.semaphore_signal(barrier, 1, device_id=(f, d), device_id_type=pl.DeviceIdType.MESH)

    def when(condition, body):
        pl.when(condition)(body)

    greet(across, dp)
    greet(fsdp, mate)
    when(z + 1 < lines, lambda: greet(fsdp + 2, dp))
    when(z > 0, lambda: greet(fsdp - 2, dp))
    when(core == 0, lambda: greet(fsdp, opposite))
    ends = (z + 1 < lines).astype(jnp.int32) + (z > 0).astype(jnp.int32)
    pl.semaphore_wait(barrier, 3 - core + ends)

    hops = lines - 1
    UP, DOWN, ACROSS, OPPOSITE, MATE = 0, hops, 2 * hops, 4 * hops + 1, 4 * hops + 2

    def roles(body):
        when((core == 0) & (y == 0), lambda: body(0))
        when(core == 1, lambda: body(1))
        when((core == 0) & (y == 1), lambda: body(2))

    def region(index, part, f):
        number, rows, spans = items[index]
        at, size = spans[part]
        return targets[number].at[pl.ds(pl.multiple_of(f * rows, rows), rows), pl.ds(at, size)]

    def whole(index, part):
        number, rows, spans = items[index]
        at, size = spans[part]
        return targets[number].at[:, pl.ds(at, size)]

    def own(index, part):
        number, rows, spans = items[index]
        at, size = spans[part]
        return sources[number].at[:, pl.ds(at, size)]

    def move(index, slot, source, target, f, d):
        return pltpu.make_async_remote_copy(
            src_ref=source,
            dst_ref=target,
            send_sem=send.at[index, slot],
            recv_sem=recv.at[index, slot],
            device_id=(f, d),
            device_id_type=pl.DeviceIdType.MESH,
        )

    def piece(index, part, slot, f_source, f_target, mine=False):
        target = region(index, part, f_source)
        return move(index, slot, own(index, part) if mine else target, target, f_target, dp)

    def keep(index, part):
        return pltpu.make_async_copy(own(index, part), region(index, part, fsdp), copied.at[index])

    def z_steps(index, part, hop, act):
        mine = hop == 0
        if hop < hops:
            when(
                (z - hop >= 0) & (z + 1 < lines),
                lambda: act(piece(index, part, UP + hop, fsdp - 2 * hop, fsdp + 2, mine)),
            )
            when(
                (z + hop < lines) & (z > 0),
                lambda: act(piece(index, part, DOWN + hop, fsdp + 2 * hop, fsdp - 2, mine)),
            )

    def x_steps(index, part, hop, act):
        if hop == 0:
            act(piece(index, part, ACROSS, fsdp, across, True))
        else:
            when(
                z - hop >= 0,
                lambda: act(piece(index, part, ACROSS + hop, fsdp - 2 * hop, across)),
            )
            when(
                z + hop < lines,
                lambda: act(piece(index, part, ACROSS + hops + hop, fsdp + 2 * hop, across)),
            )

    def z_arrive(index, part, hop):
        when(
            z - hop >= 0,
            lambda: piece(index, part, UP + hop - 1, fsdp - 2 * hop, fsdp).wait_recv(),
        )
        when(
            z + hop < lines,
            lambda: piece(index, part, DOWN + hop - 1, fsdp + 2 * hop, fsdp).wait_recv(),
        )

    def x_arrive(index, part):
        piece(index, part, ACROSS, across, across).wait_recv()
        for hop in range(1, lines):
            when(
                z - hop >= 0,
                lambda hop=hop: piece(
                    index, part, ACROSS + hop, across - 2 * hop, across
                ).wait_recv(),
            )
            when(
                z + hop < lines,
                lambda hop=hop: piece(
                    index, part, ACROSS + hops + hop, across + 2 * hop, across
                ).wait_recv(),
            )

    def to_opposite(index, part):
        return move(index, OPPOSITE, whole(index, part), whole(index, part), fsdp, opposite)

    def to_mate(index, part, second=0):
        return move(index, MATE + second, whole(index, part), whole(index, part), fsdp, mate)

    def stage(index, part, step):
        if step == 0:
            keep(index, part).start()
            z_steps(index, part, 0, lambda copy: copy.start())
            x_steps(index, part, 0, lambda copy: copy.start())
        elif step < lines:
            z_arrive(index, part, step)
            z_steps(index, part, step, lambda copy: copy.start())
            x_steps(index, part, step, lambda copy: copy.start())
        elif step == lines:
            keep(index, part).wait()
            x_arrive(index, part)
            if part != 1:
                to_opposite(index, part).start()
            to_mate(index, part).start()
        elif step == lines + 1:
            if part != 1:
                to_opposite(index, 2 - part).wait_recv()
                to_mate(index, 2 - part, 1).start()
        else:
            if part != 1:
                to_mate(index, 1).wait_recv()
            else:
                when(y == 0, lambda: to_mate(index, 0).wait_recv())
                when(y == 0, lambda: to_mate(index, 2, 1).wait_recv())
                when(y == 1, lambda: to_mate(index, 2).wait_recv())
                when(y == 1, lambda: to_mate(index, 0, 1).wait_recv())

    def run(part):
        steps = lines + 3
        for tick in range(len(items) + steps - 1):
            for step in range(steps):
                if 0 <= tick - step < len(items):
                    stage(tick - step, part, step)
        for index in range(len(items)):
            for hop in range(lines):
                z_steps(index, part, hop, lambda copy: copy.wait_send())
                x_steps(index, part, hop, lambda copy: copy.wait_send())
            if part != 1:
                to_opposite(index, part).wait_send()
                to_mate(index, 2 - part, 1).wait_send()
            to_mate(index, part).wait_send()

    roles(run)


def gather_rows(arrays, fsdp_count, cuts, collective_id):
    lines = fsdp_count // 2
    items = []
    for number, array in enumerate(arrays):
        rows, width = array.shape
        step = width // cuts[number]
        for cut in range(cuts[number]):
            items.append((number, rows, third_ranges(step, cut * step)))
    count = len(arrays)
    slots = 4 * (lines - 1) + 4

    def kernel(*refs):
        gather_kernel(items, lines, refs[:count], refs[count : 2 * count], *refs[2 * count :])

    return pl.pallas_call(
        kernel,
        out_shape=[
            jax.ShapeDtypeStruct((fsdp_count * a.shape[0], a.shape[1]), a.dtype) for a in arrays
        ],
        in_specs=[pl.BlockSpec(memory_space=pl.ANY)] * count,
        out_specs=[pl.BlockSpec(memory_space=pl.ANY)] * count,
        scratch_shapes=[
            pltpu.SemaphoreType.DMA((len(items), slots)),
            pltpu.SemaphoreType.DMA((len(items), slots)),
            pltpu.SemaphoreType.DMA((len(items),)),
        ],
        compiler_params=pltpu.CompilerParams(collective_id=collective_id, has_side_effects=True),
        name="gather_rows",
    )(*arrays)


def reduce_kernel(
    cuts, lines, grads, out, mate_a, mate_b, facing, side, sums, up_out, up_in, down_out, down_in,
    ending, ended, result, send, recv
):
    fsdp, dp = lax.axis_index("fsdp"), lax.axis_index("dp")
    z, x = fsdp // 2, fsdp % 2
    y, core = dp // 2, dp % 2
    across = z * 2 + 1 - x
    mate = y * 2 + 1 - core
    opposite = (1 - y) * 2 + core
    size = mate_a.shape[-1]
    lone = core == 1
    part = jnp.where(lone, 1, 2 * y)
    mate_part = jnp.where(lone, 2 * y, 1)

    barrier = pltpu.get_barrier_semaphore()

    def greet(f, d):
        pl.semaphore_signal(barrier, 1, device_id=(f, d), device_id_type=MESH)

    greet(across, dp)
    greet(fsdp, mate)
    greet(fsdp, opposite)
    pl.when(z + 1 < lines)(lambda: greet(fsdp + 2, dp))
    pl.when(z > 0)(lambda: greet(fsdp - 2, dp))
    ends = (z + 1 < lines).astype(jnp.int32) + (z > 0).astype(jnp.int32)
    pl.semaphore_wait(barrier, 3 + ends)

    MATE_A, MATE_B, FACING, ACROSS, UP, DOWN, ENDING, LAST_MATE, LAST_SECOND, LAST_FACING = range(10)

    def move(cut, slot, source, target, f, d):
        return pltpu.make_async_remote_copy(
            src_ref=source,
            dst_ref=target,
            send_sem=send.at[cut, slot],
            recv_sem=recv.at[cut, slot],
            device_id=(f, d),
            device_id_type=MESH,
        )

    def columns(cut, which):
        return pl.ds(pl.multiple_of((3 * cut + which) * size, 128), size)

    def mine(cut, which):
        return grads[:, :, :, columns(cut, which)].astype(F32)

    def to_mate_a(cut):
        return move(cut, MATE_A, grads.at[:, :, :, columns(cut, mate_part)], mate_a.at[cut], fsdp, mate)

    def to_mate_b(cut):
        return move(
            cut, MATE_B, grads.at[:, :, :, columns(cut, 2 - mate_part)], mate_b.at[cut], fsdp, mate
        )

    def to_facing(cut):
        return move(cut, FACING, mate_b.at[cut], facing.at[cut], fsdp, opposite)

    def to_across(cut):
        return move(cut, ACROSS, mate_a.at[cut, :, 1 - x], side.at[cut], across, dp)

    def going_up(cut, count):
        blocks = pl.ds(0, count)
        return move(cut, UP, up_out.at[cut, blocks], up_in.at[cut, blocks], fsdp + 2, dp)

    def going_down(cut, count):
        blocks = pl.ds(0, count)
        return move(cut, DOWN, down_out.at[cut, blocks], down_in.at[cut, blocks], fsdp - 2, dp)

    def to_ending(cut):
        return move(cut, ENDING, ending.at[cut], ended.at[cut], fsdp, opposite)

    def last(cut, slot, which, d):
        place = result.at[:, columns(cut, which)]
        return move(cut, slot, place, place, fsdp, d)

    def step_0(cut):
        to_mate_a(cut).start()
        pl.when(lone)(lambda: to_mate_b(cut).start())

    def step_1(cut):
        @pl.when(jnp.logical_not(lone))
        def _():
            to_mate_b(cut).wait_recv()
            mate_b[cut] = (mine(cut, 2 - part) + mate_b[cut].astype(F32)).astype(BF16)
            to_facing(cut).start()

    def step_2(cut):
        to_mate_a(cut).wait_recv()

        @pl.when(lone)
        def _():
            mate_a[cut] = (mine(cut, 1) + mate_a[cut].astype(F32)).astype(BF16)

        @pl.when(jnp.logical_not(lone))
        def _():
            to_facing(cut).wait_recv()
            both = mine(cut, part) + mate_a[cut].astype(F32) + facing[cut].astype(F32)
            mate_a[cut] = both.astype(BF16)

        to_across(cut).start()

    def step_3(cut):
        to_across(cut).wait_recv()
        sums[cut] = mate_a[cut, :, x].astype(F32) + side[cut].astype(F32)

    def lift(cut, hop):
        at = hop - 1

        @pl.when(z == at)
        def _():
            count = lines - hop
            if at > 0:
                going_up(cut, count + 1).wait_recv()
            for ahead in range(1, count + 1):
                value = sums[cut, at + ahead]
                if at > 0:
                    value = value + up_in[cut, ahead].astype(F32)
                up_out[cut, ahead - 1] = value.astype(BF16)
            going_up(cut, count).start()

        low = lines - hop

        @pl.when(z == low)
        def _():
            count = lines - hop
            if low < lines - 1:
                going_down(cut, count + 1).wait_recv()
            for ahead in range(1, count + 1):
                value = sums[cut, low - ahead]
                if low < lines - 1:
                    value = value + down_in[cut, ahead].astype(F32)
                down_out[cut, ahead - 1] = value.astype(BF16)
            going_down(cut, count).start()

    def finish(cut):
        for at in range(lines):

            @pl.when(z == at)
            def _(at=at):
                value = sums[cut, at]
                if at == lines - 1:
                    going_up(cut, 1).wait_recv()
                if at == 0:
                    going_down(cut, 1).wait_recv()
                if at > 0:
                    value = value + up_in[cut, 0].astype(F32)
                if at < lines - 1:
                    value = value + down_in[cut, 0].astype(F32)
                ending[cut] = value.astype(BF16)

        pl.when(lone)(lambda: to_ending(cut).start())

        @pl.when(jnp.logical_not(lone))
        def _():
            result[:, columns(cut, part)] = ending[cut]
            last(cut, LAST_FACING, part, opposite).start()
            last(cut, LAST_MATE, part, mate).start()

    def share(cut):
        @pl.when(lone)
        def _():
            to_ending(cut).wait_recv()
            both = ending[cut].astype(F32) + ended[cut].astype(F32)
            result[:, columns(cut, part)] = both.astype(BF16)
            last(cut, LAST_MATE, part, mate).start()

        @pl.when(jnp.logical_not(lone))
        def _():
            last(cut, LAST_FACING, 2 - part, opposite).wait_recv()
            last(cut, LAST_SECOND, 2 - part, mate).start()

    def close(cut):
        last(cut, LAST_MATE, mate_part, mate).wait_recv()
        pl.when(lone)(lambda: last(cut, LAST_SECOND, 2 - mate_part, mate).wait_recv())

    steps = [step_0, step_1, step_2, step_3]
    steps += [functools.partial(lambda hop, cut: lift(cut, hop), hop) for hop in range(1, lines)]
    steps += [finish, share, close]
    for tick in range(cuts + len(steps) - 1):
        for number, step in enumerate(steps):
            if 0 <= tick - number < cuts:
                step(tick - number)

    out[...] = result[...].astype(F32)
    for cut in range(cuts):
        to_mate_a(cut).wait_send()
        to_across(cut).wait_send()
        for hop in range(1, lines):
            pl.when(z == hop - 1)(lambda hop=hop: going_up(cut, lines - hop).wait_send())
            pl.when(z == lines - hop)(lambda hop=hop: going_down(cut, lines - hop).wait_send())
        last(cut, LAST_MATE, part, mate).wait_send()

        @pl.when(lone)
        def _():
            to_mate_b(cut).wait_send()
            to_ending(cut).wait_send()

        @pl.when(jnp.logical_not(lone))
        def _():
            to_facing(cut).wait_send()
            last(cut, LAST_FACING, part, opposite).wait_send()
            last(cut, LAST_SECOND, 2 - part, mate).wait_send()


def reduce_rows(grads, fsdp_count, cuts, collective_id):
    total, width = grads.shape
    lines, rows = fsdp_count // 2, total // fsdp_count
    size = width // (3 * cuts)
    blocks = (cuts, lines, 2, rows, size)
    return pl.pallas_call(
        functools.partial(reduce_kernel, cuts, lines),
        out_shape=jax.ShapeDtypeStruct((rows, width), F32),
        in_specs=[pl.BlockSpec(memory_space=pltpu.VMEM)],
        out_specs=pl.BlockSpec(memory_space=pltpu.VMEM),
        scratch_shapes=[
            pltpu.VMEM(blocks, BF16),
            pltpu.VMEM(blocks, BF16),
            pltpu.VMEM(blocks, BF16),
            pltpu.VMEM((cuts, lines, rows, size), BF16),
            pltpu.VMEM((cuts, lines, rows, size), F32),
        ]
        + [pltpu.VMEM((cuts, lines - 1, rows, size), BF16)] * 4
        + [pltpu.VMEM((cuts, rows, size), BF16)] * 2
        + [
            pltpu.VMEM((rows, width), BF16),
            pltpu.SemaphoreType.DMA((cuts, 10)),
            pltpu.SemaphoreType.DMA((cuts, 10)),
        ],
        compiler_params=pltpu.CompilerParams(
            collective_id=collective_id, has_side_effects=True, vmem_limit_bytes=58 << 20
        ),
        name="reduce_rows",
    )(grads.reshape(lines, 2, rows, width))


GELU_A = 0.7978845608028654
GELU_B = 0.044715
TAIL = 16


def mm(left, right):
    return lax.dot_general(left, right, (((1,), (0,)), ((), ())), preferred_element_type=F32)


def mm_nt(left, right):
    return lax.dot_general(left, right, (((1,), (1,)), ((), ())), preferred_element_type=F32)


def mm_tn(left, right):
    return lax.dot_general(left, right, (((0,), (0,)), ((), ())), preferred_element_type=F32)


def norm_parts(x):
    centred = x - jnp.mean(x, -1, keepdims=True)
    lift = lax.rsqrt(jnp.mean(centred * centred, -1, keepdims=True) + 1e-06)
    return centred * lift, lift


def norm_back(grad, gain, unit_x, lift):
    inner = grad * gain
    return lift * (
        inner
        - jnp.mean(inner, -1, keepdims=True)
        - unit_x * jnp.mean(inner * unit_x, -1, keepdims=True)
    )


def gelu(x):
    return 0.5 * x * (1.0 + jnp.tanh(GELU_A * (x + GELU_B * (x * x * x))))


def gelu_both(x):
    square = x * x
    slope = jnp.tanh(GELU_A * x * (1.0 + GELU_B * square))
    half = 0.5 * (1.0 + slope)
    turn = half + 0.5 * x * (1.0 - slope * slope) * GELU_A * (1.0 + 3.0 * GELU_B * square)
    return x * half, turn


def half_masks(width):
    lane = lax.broadcasted_iota(jnp.int32, (1, 128), 1)
    first = (lane < width).astype(F32)
    return first, 1.0 - first


def column_sum(x):
    return jnp.sum(x, 0, keepdims=True)


def attend(q, keys, values, valid, scale, lse_store):
    rows, total = q.shape[0], keys.shape[0]
    masks = half_masks(64)
    column = lax.broadcasted_iota(jnp.int32, (rows, total), 1)
    lane = lax.broadcasted_iota(jnp.int32, (rows, 128), 1)
    mixed, lse = [], jnp.zeros((rows, 128), F32)
    for pair in range(HEADS // 2):
        span = slice(128 * pair, 128 * pair + 128)
        halves = []
        for side in range(2):
            asked = q[:, span] * (masks[side] * scale).astype(BF16)
            scores = mm_nt(asked, keys[:, span])
            scores = jnp.where(column < valid, scores, -1e30)
            top = jnp.max(scores, -1, keepdims=True)
            expo = jnp.exp(scores - top)
            total_e = jnp.sum(expo, -1, keepdims=True)
            halves.append(mm(expo.astype(BF16), values[:, span]) / total_e)
            if lse_store:
                lse = jnp.where(lane == 2 * pair + side, top + jnp.log(total_e), lse)
        mixed.append(jnp.where(lane < 64, halves[0], halves[1]))
    return jnp.concatenate(mixed, -1).astype(BF16), lse


def forward_kernel(
    images, hidden, keep, patches, covered, weight_p, weight_0, weight_1, places, rows_table, *rest
):
    if keep:
        (cls_out, x0_out, x1_out, x2_out, qkv_out, o0_out, lse0_out, kv_out, q1_out, lse1_out,
         x1c_out, o1_out, cls_x, cls_o) = rest
    else:
        cls_out, cls_x, cls_o = rest
    image = pl.program_id(0)
    model = weight_0.shape[0]
    count = patches.shape[1]
    valid = count + 1
    scale = (model // HEADS) ** -0.5

    def vec(row):
        return rows_table[row : row + 1, :]

    @pl.when(image == 0)
    def _():
        cls_x[...] = jnp.zeros_like(cls_x)
        cls_o[...] = jnp.zeros_like(cls_o)

    tokens = mm_nt(patches[0], weight_p[:, : patches.shape[2]]) + vec(1)
    if keep:
        hide = covered[0]
        tokens = tokens * (1.0 - hide) + vec(0) * hide
    x = jnp.concatenate([tokens + places[:count, :], places[count:, :]], 0)

    def row(layer, index):
        return vec(2 + 6 * layer + index)

    unit_x, _ = norm_parts(x)
    low = (unit_x * row(0, 0) + row(0, 1)).astype(BF16)
    qkv = mm(low, weight_0[:, : 3 * model]).astype(BF16)
    mixture, lse = attend(
        qkv[:, :model], qkv[:, model : 2 * model], qkv[:, 2 * model :], valid, scale, keep
    )
    x1 = x + row(0, 2) * mm(mixture, weight_0[:, 3 * model : 4 * model])
    unit_x, _ = norm_parts(x1)
    low = (unit_x * row(0, 3) + row(0, 4)).astype(BF16)
    wide = gelu(mm(low, weight_0[:, 4 * model : 4 * model + hidden])).astype(BF16)
    x2 = x1 + row(0, 5) * mm_nt(wide, weight_0[:, 4 * model + hidden :])

    unit_x, _ = norm_parts(x2)
    low = (unit_x * row(1, 0) + row(1, 1)).astype(BF16)
    kv = mm(low, weight_1[:, model : 3 * model]).astype(BF16)
    q1 = mm(low[count:, :], weight_1[:, :model]).astype(BF16)
    mixture1, lse1 = attend(q1, kv[:, :model], kv[:, model:], valid, scale, keep)
    cls_x[pl.ds(image, 1), :] = x2[count : count + 1, :]
    cls_o[pl.ds(image, 1), :] = mixture1[:1, :].astype(F32)
    if keep:
        x0_out[0] = x
        x1_out[0] = x1
        x2_out[0] = x2
        qkv_out[0] = qkv
        o0_out[0] = mixture
        lse0_out[0] = lse
        kv_out[0] = kv
        q1_out[0] = q1
        lse1_out[0] = lse1

    @pl.when(image == images - 1)
    def _():
        mixed = cls_o[...].astype(BF16)
        x1c = cls_x[...] + row(1, 2) * mm(mixed, weight_1[:, 3 * model : 4 * model])
        unit_c, _ = norm_parts(x1c)
        low_c = (unit_c * row(1, 3) + row(1, 4)).astype(BF16)
        wide_c = gelu(mm(low_c, weight_1[:, 4 * model : 4 * model + hidden])).astype(BF16)
        cls_out[...] = x1c + row(1, 5) * mm_nt(wide_c, weight_1[:, 4 * model + hidden :])
        if keep:
            x1c_out[...] = x1c
            o1_out[...] = mixed


def fixed(shape):
    zeros = (0,) * len(shape)
    return pl.BlockSpec(shape, lambda i: zeros, pipeline_mode=pl.Buffered(1))


def each(shape):
    rest = (0,) * len(shape)
    return pl.BlockSpec((1,) + shape, lambda i: (i,) + rest)


def whole_out(shape):
    zeros = (0,) * len(shape)
    return pl.BlockSpec(shape, lambda i: zeros)


def split_table(vecs, count):
    places = jnp.concatenate(
        [
            vecs[1 : count + 1],
            vecs[:1] + vecs[count + 1 : count + 2],
            jnp.zeros((TAIL - 1, vecs.shape[1]), F32),
        ]
    )
    rows = vecs[count + 2 :]
    rows = jnp.concatenate([rows, jnp.zeros(((-rows.shape[0]) % 8, rows.shape[1]), F32)])
    return places, rows


def forward(patches, covered, weight_p, weight_0, weight_1, vecs, keep):
    images, count, pixels = patches.shape
    model, columns = weight_0.shape
    hidden = (columns - 4 * model) // 2
    total = count + TAIL
    places, rows = split_table(vecs, count)
    shape = jax.ShapeDtypeStruct
    outs = [shape((TAIL, model), F32)]
    out_specs = [whole_out((TAIL, model))]
    if keep:
        per_image = [
            ((total, model), F32),
            ((total, model), F32),
            ((total, model), F32),
            ((total, 3 * model), BF16),
            ((total, model), BF16),
            ((total, 128), F32),
            ((total, 2 * model), BF16),
            ((TAIL, model), BF16),
            ((TAIL, 128), F32),
        ]
        outs += [shape((images,) + dims, kind) for dims, kind in per_image]
        out_specs += [each(dims) for dims, kind in per_image]
        outs += [shape((TAIL, model), F32), shape((TAIL, model), BF16)]
        out_specs += [whole_out((TAIL, model))] * 2
    return pl.pallas_call(
        functools.partial(forward_kernel, images, hidden, keep),
        grid=(images,),
        out_shape=outs,
        in_specs=[
            each((count, pixels)),
            each((count, 1)),
            fixed(weight_p.shape),
            fixed(weight_0.shape),
            fixed(weight_1.shape),
            fixed(places.shape),
            fixed(rows.shape),
        ],
        out_specs=out_specs,
        scratch_shapes=[pltpu.VMEM((TAIL, model), F32)] * 2,
        compiler_params=pltpu.CompilerParams(vmem_limit_bytes=56 << 20),
        name="backbone_forward",
    )(patches, covered[..., None], weight_p, weight_0, weight_1, places, rows)


def attend_back(grad_o, q, keys, values, lse, valid, scale):
    rows, total = q.shape[0], keys.shape[0]
    masks = half_masks(64)
    column = lax.broadcasted_iota(jnp.int32, (rows, total), 1)
    lane_row = lax.broadcasted_iota(jnp.int32, (rows, 128), 1)
    grad_q, grad_k, grad_v = [], [], []
    for pair in range(HEADS // 2):
        span = slice(128 * pair, 128 * pair + 128)
        out_q, out_k, out_v = [], None, None
        for side in range(2):
            mask = masks[side].astype(BF16)
            asked = q[:, span] * (masks[side] * scale).astype(BF16)
            given = grad_o[:, span] * mask
            head = 2 * pair + side
            scores = mm_nt(asked, keys[:, span])
            share = jnp.where(column < valid, jnp.exp(scores - lse[:, head : head + 1]), 0.0)
            grad_p = mm_nt(given, values[:, span])
            inner = jnp.sum(share * grad_p, -1, keepdims=True)
            grad_s = (share * (grad_p - inner)).astype(BF16)
            out_q.append(mm(grad_s, keys[:, span]))
            more_k = mm_tn(grad_s, asked)
            more_v = mm_tn(share.astype(BF16), given)
            out_k = more_k if out_k is None else out_k + more_k
            out_v = more_v if out_v is None else out_v + more_v
        grad_q.append(jnp.where(lane_row < 64, out_q[0], out_q[1]) * scale)
        grad_k.append(out_k)
        grad_v.append(out_v)
    return [jnp.concatenate(part, -1).astype(BF16) for part in (grad_q, grad_k, grad_v)]


def backward_kernel(
    images, hidden, count_, patches, covered, weight_p, weight_0, weight_1, rows_table, ends, grad_cls,
    x0_in, x1_in, x2_in, qkv_in, o0_in, lse0_in, kv_in, q1_in, lse1_in, x1c_in, o1_in,
    packed, acc_p, acc_0, acc_kv, acc_q, grad_c, grad_oc, places, rows
):
    image = pl.program_id(0)
    model = weight_0.shape[0]
    count, pixels = patches.shape[1], patches.shape[2]
    valid = count + 1
    scale = (model // HEADS) ** -0.5
    base_0 = packed_width_p(pixels)
    columns = weight_0.shape[1]
    base_1 = base_0 + columns
    base_v = base_1 + columns
    cut_o, cut_u, cut_d = 3 * model, 4 * model, 4 * model + hidden

    def row(layer, index):
        at = 2 + 6 * layer + index
        return rows_table[at : at + 1, :]

    def add_row(layer, index, value):
        at = 2 + 6 * layer + index
        rows[at : at + 1, :] += value

    @pl.when(image == 0)
    def _():
        for ref in (acc_p, acc_0, acc_kv, acc_q, places, rows):
            ref[...] = jnp.zeros_like(ref)
        grad_x = grad_cls[...]
        x1c = x1c_in[...]
        unit_x, lift = norm_parts(x1c)
        low = (unit_x * row(1, 3) + row(1, 4)).astype(BF16)
        wide, slope = gelu_both(mm(low, weight_1[:, cut_u:cut_d]))
        wide = wide.astype(BF16)
        down = mm_nt(wide, weight_1[:, cut_d:])
        add_row(1, 5, column_sum(grad_x * down))
        grad_d = (grad_x * row(1, 5)).astype(BF16)
        grad_u = (mm(grad_d, weight_1[:, cut_d:]) * slope).astype(BF16)
        packed[:, base_1 + cut_d : base_v] = mm_tn(grad_d, wide).astype(BF16)
        packed[:, base_1 + cut_u : base_1 + cut_d] = mm_tn(low, grad_u).astype(BF16)
        grad_n = mm_nt(grad_u, weight_1[:, cut_u:cut_d])
        add_row(1, 3, column_sum(grad_n * unit_x))
        add_row(1, 4, column_sum(grad_n))
        grad_x = grad_x + norm_back(grad_n, row(1, 3), unit_x, lift)
        mixed = o1_in[...]
        add_row(1, 2, column_sum(grad_x * mm(mixed, weight_1[:, cut_o:cut_u])))
        grad_a = (grad_x * row(1, 2)).astype(BF16)
        packed[:, base_1 + cut_o : base_1 + cut_u] = mm_tn(mixed, grad_a).astype(BF16)
        grad_c[...] = grad_x
        grad_oc[...] = mm_nt(grad_a, weight_1[:, cut_o:cut_u])

    first_row = lax.broadcasted_iota(jnp.int32, (TAIL, 1), 0) == 0

    grad_o1 = jnp.where(first_row, grad_oc[pl.ds(image, 1), :], 0.0).astype(BF16)
    kv = kv_in[0]
    grad_q, grad_k, grad_v = attend_back(
        grad_o1, q1_in[0], kv[:, :model], kv[:, model:], lse1_in[0], valid, scale
    )
    unit_x, lift = norm_parts(x2_in[0])
    low = (unit_x * row(1, 0) + row(1, 1)).astype(BF16)
    grad_kv = jnp.concatenate([grad_k, grad_v], -1)
    acc_kv[...] += mm_tn(low, grad_kv)
    acc_q[...] += mm_tn(low[count:, :], grad_q)
    grad_n = mm_nt(grad_kv, weight_1[:, model : 3 * model])
    tail = grad_n[count:, :] + mm_nt(grad_q, weight_1[:, :model])
    grad_n = jnp.concatenate([grad_n[:count, :], tail], 0)
    add_row(1, 0, column_sum(grad_n * unit_x))
    add_row(1, 1, column_sum(grad_n))
    grad_x = norm_back(grad_n, row(1, 0), unit_x, lift)
    tail = grad_x[count:, :] + jnp.where(first_row, grad_c[pl.ds(image, 1), :], 0.0)
    grad_x = jnp.concatenate([grad_x[:count, :], tail], 0)

    unit_x, lift = norm_parts(x1_in[0])
    low = (unit_x * row(0, 3) + row(0, 4)).astype(BF16)
    wide, slope = gelu_both(mm(low, weight_0[:, cut_u:cut_d]))
    wide = wide.astype(BF16)
    down = mm_nt(wide, weight_0[:, cut_d:])
    add_row(0, 5, column_sum(grad_x * down))
    grad_d = (grad_x * row(0, 5)).astype(BF16)
    grad_u = (mm(grad_d, weight_0[:, cut_d:]) * slope).astype(BF16)
    acc_0[:, cut_d:] += mm_tn(grad_d, wide)
    acc_0[:, cut_u:cut_d] += mm_tn(low, grad_u)
    grad_n = mm_nt(grad_u, weight_0[:, cut_u:cut_d])
    add_row(0, 3, column_sum(grad_n * unit_x))
    add_row(0, 4, column_sum(grad_n))
    grad_x = grad_x + norm_back(grad_n, row(0, 3), unit_x, lift)
    mixed = o0_in[0]
    add_row(0, 2, column_sum(grad_x * mm(mixed, weight_0[:, cut_o:cut_u])))
    grad_a = (grad_x * row(0, 2)).astype(BF16)
    acc_0[:, cut_o:cut_u] += mm_tn(mixed, grad_a)
    grad_o = mm_nt(grad_a, weight_0[:, cut_o:cut_u]).astype(BF16)
    qkv = qkv_in[0]
    grad_qkv = jnp.concatenate(
        attend_back(
            grad_o, qkv[:, :model], qkv[:, model : 2 * model], qkv[:, 2 * model :], lse0_in[0],
            valid, scale,
        ),
        -1,
    )
    unit_x, lift = norm_parts(x0_in[0])
    low = (unit_x * row(0, 0) + row(0, 1)).astype(BF16)
    acc_0[:, :cut_o] += mm_tn(low, grad_qkv)
    grad_n = mm_nt(grad_qkv, weight_0[:, :cut_o])
    add_row(0, 0, column_sum(grad_n * unit_x))
    add_row(0, 1, column_sum(grad_n))
    grad_x = grad_x + norm_back(grad_n, row(0, 0), unit_x, lift)

    places[...] += grad_x
    hide = covered[0]
    token = grad_x[:count, :]
    rows[0:1, :] += column_sum(token * hide)
    token = token * (1.0 - hide)
    rows[1:2, :] += column_sum(token)
    acc_p[...] += mm_tn(token.astype(BF16), patches[0])

    @pl.when(image == images - 1)
    def _():
        packed[:, :base_0] = jnp.concatenate(
            [acc_p[...], jnp.zeros((model, base_0 - pixels), F32)], -1
        ).astype(BF16)
        packed[:, base_0:base_1] = acc_0[...].astype(BF16)
        packed[:, base_1 : base_1 + model] = acc_q[...].astype(BF16)
        packed[:, base_1 + model : base_1 + cut_o] = acc_kv[...].astype(BF16)
        used = rows_table.shape[0]
        table = jnp.concatenate(
            [
                places[count : count + 1, :],
                places[:count, :],
                places[count : count + 1, :],
                rows[...] + ends[...],
            ],
            0,
        )
        table = jnp.concatenate(
            [table, jnp.zeros((model - table.shape[0], model), F32)], 0
        )
        packed[:, base_v : base_v + model] = table.astype(BF16)
        spare = packed.shape[1] - base_v - model
        if spare:
            packed[:, base_v + model :] = jnp.zeros((model, spare), BF16)


def packed_width_p(pixels):
    return (pixels + 127) // 128 * 128


def packed_width(pixels, columns, model):
    width = packed_width_p(pixels) + 2 * columns + model
    return (width + 1151) // 1152 * 1152


def backward(patches, covered, weight_p, weight_0, weight_1, vecs, ends, grad_cls, saved):
    images, count, pixels = patches.shape
    model, columns = weight_0.shape
    hidden = (columns - 4 * model) // 2
    total = count + TAIL
    _, rows = split_table(vecs, count)
    ends = jnp.concatenate(
        [jnp.zeros((14, model), F32), ends, jnp.zeros((rows.shape[0] - 16, model), F32)]
    )
    width = packed_width(pixels, columns, model)
    return pl.pallas_call(
        functools.partial(backward_kernel, images, hidden, count),
        grid=(images,),
        out_shape=jax.ShapeDtypeStruct((model, width), BF16),
        in_specs=[
            each((count, pixels)),
            each((count, 1)),
            fixed(weight_p.shape),
            fixed(weight_0.shape),
            fixed(weight_1.shape),
            fixed(rows.shape),
            fixed(ends.shape),
            fixed(grad_cls.shape),
        ]
        + [each(array.shape[1:]) for array in saved[:9]]
        + [fixed(array.shape) for array in saved[9:]],
        out_specs=whole_out((model, width)),
        scratch_shapes=[
            pltpu.VMEM((model, pixels), F32),
            pltpu.VMEM((model, columns), F32),
            pltpu.VMEM((model, 2 * model), F32),
            pltpu.VMEM((model, model), F32),
            pltpu.VMEM((TAIL, model), F32),
            pltpu.VMEM((TAIL, model), F32),
            pltpu.VMEM((total, model), F32),
            pltpu.VMEM(rows.shape, F32),
        ],
        compiler_params=pltpu.CompilerParams(vmem_limit_bytes=58 << 20),
        name="backbone_backward",
    )(patches, covered[..., None], weight_p, weight_0, weight_1, rows, ends, grad_cls, *saved)


def dot(left, right, dims):
    return lax.dot_general(left, right, (dims, ((), ())), preferred_element_type=F32)


def layer_norm(x, gain, shift):
    centred = x - jnp.mean(x, -1, keepdims=True)
    spread = jnp.mean(centred * centred, -1, keepdims=True)
    return centred * lax.rsqrt(spread + 1e-06) * gain + shift


def gelu_slope(x):
    _, pull = jax.vjp(jax.nn.gelu, x)
    return pull(jnp.ones_like(x))[0]


def head_forward(cls, weight, vecs):
    width, hidden = cls.shape[1], weight.shape[1]
    low_n = layer_norm(cls, vecs[-2], vecs[-1]).astype(BF16)
    pre_a = jnp.dot(low_n, weight[:width], preferred_element_type=F32)
    low_a = jax.nn.gelu(pre_a).astype(BF16)
    pre_b = jnp.dot(low_a, weight[width : width + hidden], preferred_element_type=F32)
    low_b = jax.nn.gelu(pre_b).astype(BF16)
    raw = dot(low_b, weight[width + hidden :], ((1,), (1,)))
    return low_n, pre_a, low_a, pre_b, low_b, raw


def unit(raw):
    return raw * lax.rsqrt(jnp.sum(raw * raw, -1, keepdims=True) + 1e-06)


def adamw(weight, moment, second, gradient, factor, step_rate, weight_decay):
    clipped = gradient * factor
    moment = BETA_ONE * moment + (1.0 - BETA_ONE) * clipped
    second = BETA_TWO * second + (1.0 - BETA_TWO) * clipped * clipped
    direction = (
        moment / (1.0 - BETA_ONE**STEP) / (jnp.sqrt(second / (1.0 - BETA_TWO**STEP)) + 1e-08)
    )
    return (weight - step_rate * (direction + weight_decay * weight), moment, second)


def small_mesh():
    return lax.axis_size("dp") == 4 and lax.axis_size("fsdp") in (4, 8)


def gather_all(arrays, cuts):
    if small_mesh():
        return gather_rows(arrays, lax.axis_size("fsdp"), cuts, 1)
    return [lax.all_gather(array, "fsdp", axis=0, tiled=True) for array in arrays]


def reduce_all(grads):
    if small_mesh():
        return reduce_rows(grads, lax.axis_size("fsdp"), 3, 2)
    owned = lax.psum_scatter(grads, "fsdp", scatter_dimension=0, tiled=True)
    return lax.psum(owned, "dp").astype(F32)


def per_device(
    patches,
    patch_mask,
    image_valid,
    centre,
    w_patch,
    first_patch,
    second_patch,
    teacher_patch,
    w_layer,
    first_layer,
    second_layer,
    teacher_layer,
    w_head,
    first_head,
    second_head,
    teacher_head,
    w_proto,
    first_proto,
    second_proto,
    teacher_proto,
    vectors,
    first_vectors,
    second_vectors,
    teacher_vectors,
):
    everyone = ("fsdp", "dp")
    local = patches.shape[0]
    place = lax.axis_index(everyone) * local
    fsdp_index = lax.axis_index("fsdp")
    counted = image_valid.astype(F32)
    counted_total = jnp.maximum(jnp.sum(counted), 1.0)
    covered = patch_mask.astype(F32)
    pixels = w_patch.shape[1]
    model_width, columns = w_layer.shape[1] * lax.axis_size("fsdp"), w_layer.shape[2]
    pad = packed_width_p(pixels) - pixels

    def low_blocks(patch, layers, weight):
        patch = jnp.pad(patch, ((0, 0), (0, pad)))
        return [array.astype(BF16) for array in (patch, layers[0], layers[1], weight)]

    blocks = low_blocks(teacher_patch, teacher_layer, teacher_head)
    blocks += low_blocks(w_patch, w_layer, w_head)
    blocks = [blocks[index] for index in (0, 1, 2, 4, 5, 6, 3, 7)]
    full = gather_all(blocks, (1, 1, 1, 1, 1, 1, 2, 2))
    teacher_patch_full, teacher_0, teacher_1, patch_full, layer_0, layer_1 = full[:6]
    teacher_head_full, head_full = full[6:]

    teacher_cls = forward(
        patches, jnp.zeros_like(covered), teacher_patch_full, teacher_0, teacher_1,
        teacher_vectors, False,
    )[0][:local]
    cls_rows, *saved = forward(patches, covered, patch_full, layer_0, layer_1, vectors, True)
    cls = cls_rows[:local]

    teacher_unit = unit(head_forward(teacher_cls, teacher_head_full, teacher_vectors)[-1])
    low_n, pre_a, low_a, pre_b, low_b, raw = head_forward(cls, head_full, vectors)
    bottleneck, pull_unit = jax.vjp(unit, raw)
    both = jnp.concatenate([teacher_unit.astype(BF16), bottleneck.astype(BF16)], -1)
    both = lax.all_gather(both, everyone, axis=0, tiled=True)
    width = raw.shape[1]
    teacher_rows, student_rows = both[:, :width], both[:, width:]

    owned_k = w_proto.shape[0]
    low_proto = w_proto.astype(BF16)
    teacher_logits = dot(teacher_rows, teacher_proto.astype(BF16), ((1,), (1,)))
    logits = dot(student_rows, low_proto, ((1,), (1,)))
    own_centre = lax.dynamic_slice_in_dim(centre, fsdp_index * owned_k, owned_k)
    scaled_t = (teacher_logits - own_centre) / TEACHER_TEMP
    scaled_s = logits / STUDENT_TEMP
    max_t = jnp.max(scaled_t, -1)
    max_s = jnp.max(scaled_s, -1)
    expo_t = jnp.exp(scaled_t - max_t[:, None])
    expo_s = jnp.exp(scaled_s - max_s[:, None])
    parts = jnp.stack(
        [
            max_t,
            jnp.sum(expo_t, -1),
            max_s,
            jnp.sum(expo_s, -1),
            jnp.sum(expo_t * (scaled_s - max_s[:, None]), -1),
        ]
    )
    parts = lax.all_gather(parts, "fsdp", axis=0)
    top_t = jnp.max(parts[:, 0], 0)
    lift_t = jnp.exp(parts[:, 0] - top_t)
    total_t = jnp.sum(parts[:, 1] * lift_t, 0)
    top_s = jnp.max(parts[:, 2], 0)
    total_s = jnp.sum(parts[:, 3] * jnp.exp(parts[:, 2] - top_s), 0)
    crossed = jnp.sum(lift_t * (parts[:, 4] + (parts[:, 2] - top_s) * parts[:, 1]), 0) / total_t
    losses = jnp.log(total_s) - crossed
    loss_total = jnp.sum(counted * losses)
    weighting = counted / counted_total / STUDENT_TEMP
    share_s = weighting * jnp.exp(max_s - top_s) / total_s
    share_t = weighting * jnp.exp(max_t - top_t) / total_t
    grad_logits = (expo_s * share_s[:, None] - expo_t * share_t[:, None]).astype(BF16)
    teacher_sum = jnp.sum(counted[:, None] * teacher_logits, 0)
    teacher_total = lax.all_gather(teacher_sum, "fsdp", axis=0, tiled=True)
    grad_proto = dot(grad_logits, student_rows, ((0,), (0,)))
    grad_rows = jnp.dot(grad_logits, low_proto, preferred_element_type=F32)
    dp_count = lax.axis_size("dp")
    grad_rows = grad_rows.reshape(-1, dp_count, local, width)
    grad_rows = lax.dynamic_index_in_dim(grad_rows, lax.axis_index("dp"), 1, keepdims=False)
    grad_bottleneck = lax.psum_scatter(grad_rows, "fsdp", scatter_dimension=0, tiled=False)

    hidden = head_full.shape[1]
    low_dz = pull_unit(grad_bottleneck)[0].astype(BF16)
    grad_b = jnp.dot(low_dz, head_full[model_width + hidden :], preferred_element_type=F32)
    low_db = (grad_b * gelu_slope(pre_b)).astype(BF16)
    grad_a = dot(low_db, head_full[model_width : model_width + hidden], ((1,), (1,)))
    low_da = (grad_a * gelu_slope(pre_a)).astype(BF16)
    grad_n = dot(low_da, head_full[:model_width], ((1,), (1,)))
    _, pull_norm = jax.vjp(layer_norm, cls, vectors[-2], vectors[-1])
    grad_cls, grad_gain, grad_shift = pull_norm(grad_n)

    packed = jnp.concatenate([low_n, low_a, low_dz, low_da, low_db, low_b], -1)
    packed = lax.all_gather(packed, everyone, axis=0, tiled=True)
    total_rows = model_width + hidden + width
    lefts, rights = packed[:, :total_rows], packed[:, total_rows:]
    own_rows = w_head.shape[0]
    start = fsdp_index * own_rows
    left = lax.dynamic_slice_in_dim(lefts, start, own_rows, 1)
    row = start + lax.broadcasted_iota(jnp.int32, (1, own_rows), 1)
    kind = jnp.where(row < model_width, 0, jnp.where(row < model_width + hidden, 1, 2))
    left = jnp.concatenate([jnp.where(kind == index, left, 0) for index in range(3)], 0)
    right = jnp.concatenate(
        [rights[:, index * hidden : (index + 1) * hidden] for index in range(3)], 0
    )
    grad_head = dot(left, right, ((0,), (0,)))

    grad_rows = jnp.pad(grad_cls, ((0, TAIL - local), (0, 0)))
    ends = jnp.stack([grad_gain, grad_shift])
    packed_grads = backward(
        patches, covered, patch_full, layer_0, layer_1, vectors, ends, grad_rows, saved
    )
    owned = reduce_all(packed_grads)
    base = packed_width_p(pixels)
    own_patch = owned[:, :pixels]
    own_layers = jnp.stack(
        [owned[:, base : base + columns], owned[:, base + columns : base + 2 * columns]]
    )
    own_rows_grad = owned[:, base + 2 * columns : base + 2 * columns + model_width]
    vector_grad = lax.all_gather(own_rows_grad, "fsdp", axis=0, tiled=True)[: vectors.shape[0]]
    owned_grads = (own_patch, own_layers, grad_head, grad_proto)
    owned_squares = sum((jnp.sum(gradient * gradient) for gradient in owned_grads))
    squares = lax.psum(owned_squares + jnp.sum(own_rows_grad * own_rows_grad), "fsdp")
    norm_value = jnp.sqrt(squares)
    factor = CLIP_NORM / jnp.maximum(norm_value, CLIP_NORM)
    updated_centre = CENTRE_KEEP * centre + (1.0 - CENTRE_KEEP) * teacher_total / counted_total
    weights_owned = (w_patch, w_layer, w_head, w_proto, vectors)
    moments = (first_patch, first_layer, first_head, first_proto, first_vectors)
    seconds = (second_patch, second_layer, second_head, second_proto, second_vectors)
    teachers = (teacher_patch, teacher_layer, teacher_head, teacher_proto, teacher_vectors)
    gradients = owned_grads + (vector_grad,)
    results = [loss_total, counted_total, norm_value, updated_centre]
    for group in range(5):
        updated, moment, second = adamw(
            weights_owned[group],
            moments[group],
            seconds[group],
            gradients[group],
            factor,
            RATES[group],
            DECAYS[group],
        )
        results.extend(
            [
                updated,
                moment,
                second,
                TEACHER_KEEP * teachers[group] + (1.0 - TEACHER_KEEP) * updated,
            ]
        )
    return tuple(results)


def solution(mesh):
    whole, rows, middle = P(), P("fsdp", None), P(None, "fsdp", None)
    in_specs = (
        (P(("fsdp", "dp"), None, None), P(("fsdp", "dp"), None), whole, whole)
        + (rows,) * 4
        + (middle,) * 4
        + (rows,) * 8
        + (whole,) * 4
    )
    out_specs = (whole,) * 4 + (rows,) * 4 + (middle,) * 4 + (rows,) * 8 + (whole,) * 4
    return jax.shard_map(
        per_device, mesh=mesh, in_specs=in_specs, out_specs=out_specs, check_vma=False
    )
```

```python
import functools

import jax
import jax.numpy as jnp
from jax import lax
from jax.experimental import pallas as pl
from jax.experimental.pallas import tpu as pltpu
from jax.sharding import PartitionSpec as P

HEADS = 6
STEP = 10
STUDENT_TEMP = 0.1
TEACHER_TEMP = 0.07
CENTRE_KEEP = 0.9
TEACHER_KEEP = 0.8
BETA_ONE = 0.9
BETA_TWO = 0.999
CLIP_NORM = 0.01
RATES = (0.1, 0.15, 0.07, 0.5, 0.5)
DECAYS = (0.04, 0.04, 0.04, 0.04, 0.0)
F32 = jnp.float32
BF16 = jnp.bfloat16
MESH = pl.DeviceIdType.MESH


def third_ranges(width, start):
    tiles = width // 128
    sizes = [(tiles + 2 - part) // 3 * 128 for part in range(3)]
    spans, at = [], start
    for size in sizes:
        spans.append((at, size))
        at += size
    return spans


def gather_kernel(items, early, lines, sources, heads, targets, send, recv, copied, send_e, recv_e):
    fsdp, dp = lax.axis_index("fsdp"), lax.axis_index("dp")
    z, x = fsdp // 2, fsdp % 2
    y, core = dp // 2, dp % 2
    across = z * 2 + 1 - x
    mate = y * 2 + 1 - core
    opposite = (1 - y) * 2 + core

    barrier = pltpu.get_barrier_semaphore()

    def greet(f, d):
        pl.semaphore_signal(barrier, 1, device_id=(f, d), device_id_type=pl.DeviceIdType.MESH)

    def when(condition, body):
        pl.when(condition)(body)

    for step in range(1, 2 * lines):
        greet(lax.rem(fsdp + step, 2 * lines), dp)
    greet(fsdp, mate)
    when(core == 0, lambda: greet(fsdp, opposite))
    pl.semaphore_wait(barrier, 2 * lines + 1 - core)

    hops = lines - 1
    UP, DOWN, ACROSS, OPPOSITE, MATE = 0, hops, 2 * hops, 4 * hops + 1, 4 * hops + 2

    def roles(body):
        when((core == 0) & (y == 0), lambda: body(0))
        when(core == 1, lambda: body(1))
        when((core == 0) & (y == 1), lambda: body(2))

    def region(index, part, f):
        number, rows, spans = items[index]
        at, size = spans[part]
        return targets[number].at[pl.ds(pl.multiple_of(f * rows, rows), rows), pl.ds(at, size)]

    def whole(index, part):
        number, rows, spans = items[index]
        at, size = spans[part]
        return targets[number].at[:, pl.ds(at, size)]

    def own(index, part):
        number, rows, spans = items[index]
        at, size = spans[part]
        return sources[number].at[:, pl.ds(at, size)]

    def move(index, slot, source, target, f, d):
        return pltpu.make_async_remote_copy(
            src_ref=source,
            dst_ref=target,
            send_sem=send.at[index, slot],
            recv_sem=recv.at[index, slot],
            device_id=(f, d),
            device_id_type=pl.DeviceIdType.MESH,
        )

    def piece(index, part, slot, f_source, f_target, mine=False):
        target = region(index, part, f_source)
        return move(index, slot, own(index, part) if mine else target, target, f_target, dp)

    def keep(index, part):
        return pltpu.make_async_copy(own(index, part), region(index, part, fsdp), copied.at[index])

    def z_steps(index, part, hop, act):
        mine = hop == 0
        if hop < hops:
            when(
                (z - hop >= 0) & (z + 1 < lines),
                lambda: act(piece(index, part, UP + hop, fsdp - 2 * hop, fsdp + 2, mine)),
            )
            when(
                (z + hop < lines) & (z > 0),
                lambda: act(piece(index, part, DOWN + hop, fsdp + 2 * hop, fsdp - 2, mine)),
            )

    def x_steps(index, part, hop, act):
        if hop == 0:
            act(piece(index, part, ACROSS, fsdp, across, True))
        else:
            when(
                z - hop >= 0,
                lambda: act(piece(index, part, ACROSS + hop, fsdp - 2 * hop, across)),
            )
            when(
                z + hop < lines,
                lambda: act(piece(index, part, ACROSS + hops + hop, fsdp + 2 * hop, across)),
            )

    def z_arrive(index, part, hop):
        when(
            z - hop >= 0,
            lambda: piece(index, part, UP + hop - 1, fsdp - 2 * hop, fsdp).wait_recv(),
        )
        when(
            z + hop < lines,
            lambda: piece(index, part, DOWN + hop - 1, fsdp + 2 * hop, fsdp).wait_recv(),
        )

    def x_arrive(index, part):
        piece(index, part, ACROSS, across, across).wait_recv()
        for hop in range(1, lines):
            when(
                z - hop >= 0,
                lambda hop=hop: piece(
                    index, part, ACROSS + hop, across - 2 * hop, across
                ).wait_recv(),
            )
            when(
                z + hop < lines,
                lambda hop=hop: piece(
                    index, part, ACROSS + hops + hop, across + 2 * hop, across
                ).wait_recv(),
            )

    def to_opposite(index, part):
        return move(index, OPPOSITE, whole(index, part), whole(index, part), fsdp, opposite)

    def to_mate(index, part, second=0):
        return move(index, MATE + second, whole(index, part), whole(index, part), fsdp, mate)

    def deal(part, act):
        for index, (number, places) in early.items():
            _, rows, spans = items[index]
            at, size = spans[part]
            target = sources[items[index][0]].at[:, pl.ds(at, size)]
            for f, (owner, start) in enumerate(places):
                source = heads[number].at[pl.ds(start, rows), pl.ds(at, size)]
                act(index, f, owner, source, target)

    def early_copy(index, f, source, target):
        return pltpu.make_async_remote_copy(
            src_ref=source,
            dst_ref=target,
            send_sem=send_e.at[index, f],
            recv_sem=recv_e.at[index],
            device_id=(f, dp),
            device_id_type=pl.DeviceIdType.MESH,
        )

    def deal_start(index, f, owner, source, target):
        if f == owner:
            when(
                fsdp == f,
                lambda: pltpu.make_async_copy(source, target, recv_e.at[index]).start(),
            )
        else:
            when(fsdp == owner, lambda: early_copy(index, f, source, target).start())

    def deal_end(index, f, owner, source, target):
        if f != owner:
            when(fsdp == owner, lambda: early_copy(index, f, source, target).wait_send())

    def dealt(index, part):
        _, rows, spans = items[index]
        at, size = spans[part]
        number, places = early[index]
        target = sources[items[index][0]].at[:, pl.ds(at, size)]
        for f, (owner, start) in enumerate(places):
            source = heads[number].at[pl.ds(start, rows), pl.ds(at, size)]
            if f == owner:
                when(
                    fsdp == f,
                    lambda source=source: pltpu.make_async_copy(
                        source, target, recv_e.at[index]
                    ).wait(),
                )
            else:
                when(
                    fsdp == f,
                    lambda f=f, source=source: early_copy(index, f, source, target).wait_recv(),
                )

    def stage(index, part, step):
        if step == 0:
            if index in early:
                dealt(index, part)
            keep(index, part).start()
            z_steps(index, part, 0, lambda copy: copy.start())
            x_steps(index, part, 0, lambda copy: copy.start())
        elif step < lines:
            z_arrive(index, part, step)
            z_steps(index, part, step, lambda copy: copy.start())
            x_steps(index, part, step, lambda copy: copy.start())
        elif step == lines:
            keep(index, part).wait()
            x_arrive(index, part)
            if part != 1:
                to_opposite(index, part).start()
            to_mate(index, part).start()
        elif step == lines + 1:
            if part != 1:
                to_opposite(index, 2 - part).wait_recv()
                to_mate(index, 2 - part, 1).start()
        else:
            if part != 1:
                to_mate(index, 1).wait_recv()
            else:
                when(y == 0, lambda: to_mate(index, 0).wait_recv())
                when(y == 0, lambda: to_mate(index, 2, 1).wait_recv())
                when(y == 1, lambda: to_mate(index, 2).wait_recv())
                when(y == 1, lambda: to_mate(index, 0, 1).wait_recv())

    def run(part):
        deal(part, deal_start)
        steps = lines + 3
        for tick in range(len(items) + steps - 1):
            for step in range(steps):
                if 0 <= tick - step < len(items):
                    stage(tick - step, part, step)
        for index in range(len(items)):
            for hop in range(lines):
                z_steps(index, part, hop, lambda copy: copy.wait_send())
                x_steps(index, part, hop, lambda copy: copy.wait_send())
            if part != 1:
                to_opposite(index, part).wait_send()
                to_mate(index, 2 - part, 1).wait_send()
            to_mate(index, part).wait_send()
        deal(part, deal_end)

    roles(run)


def gather_rows(arrays, heads, ranges, fsdp_count, collective_id):
    lines = fsdp_count // 2
    head_rows, head_width = heads[0].shape
    shapes = [array.shape for array in arrays]
    items = [(number, shape[0], third_ranges(shape[1], 0)) for number, shape in enumerate(shapes)]
    early = {}
    count = len(arrays)
    for low, high in ranges:
        for number in range(len(heads)):
            rows = (high - low) // fsdp_count
            starts = [low + rows * f for f in range(fsdp_count)]
            early[len(items)] = (
                number,
                [(start // head_rows, start % head_rows) for start in starts],
            )
            shapes.append((rows, head_width))
            items.append((len(shapes) - 1, rows, third_ranges(head_width, 0)))
    slots = 4 * (lines - 1) + 4
    extra = len(shapes) - count
    heads_at = count + len(heads)

    def kernel(*refs):
        targets = refs[heads_at : heads_at + len(shapes)]
        blocks = refs[:count] + refs[heads_at + len(shapes) : heads_at + len(shapes) + extra]
        rest = refs[heads_at + len(shapes) + extra :]
        gather_kernel(items, early, lines, blocks, refs[count:heads_at], targets, *rest)

    anywhere = pl.BlockSpec(memory_space=pl.ANY)
    out = pl.pallas_call(
        kernel,
        out_shape=[jax.ShapeDtypeStruct((fsdp_count * r, c), BF16) for r, c in shapes]
        + [jax.ShapeDtypeStruct(shape, BF16) for shape in shapes[count:]],
        in_specs=[anywhere] * heads_at,
        out_specs=[anywhere] * (len(shapes) + extra),
        scratch_shapes=[
            pltpu.SemaphoreType.DMA((len(items), slots)),
            pltpu.SemaphoreType.DMA((len(items), slots)),
            pltpu.SemaphoreType.DMA((len(items),)),
            pltpu.SemaphoreType.DMA((len(items), fsdp_count)),
            pltpu.SemaphoreType.DMA((len(items),)),
        ],
        compiler_params=pltpu.CompilerParams(collective_id=collective_id, has_side_effects=True),
        name="gather_rows",
    )(*arrays, *heads)
    return out[: len(shapes)]


def reduce_kernel(
    cuts, lines, grads, out, mate_a, mate_b, facing, side, sums, up_out, up_in, down_out, down_in,
    ending, ended, result, send, recv
):
    fsdp, dp = lax.axis_index("fsdp"), lax.axis_index("dp")
    z, x = fsdp // 2, fsdp % 2
    y, core = dp // 2, dp % 2
    across = z * 2 + 1 - x
    mate = y * 2 + 1 - core
    opposite = (1 - y) * 2 + core
    size = mate_a.shape[-1]
    lone = core == 1
    part = jnp.where(lone, 1, 2 * y)
    mate_part = jnp.where(lone, 2 * y, 1)

    barrier = pltpu.get_barrier_semaphore()

    def greet(f, d):
        pl.semaphore_signal(barrier, 1, device_id=(f, d), device_id_type=MESH)

    greet(across, dp)
    greet(fsdp, mate)
    greet(fsdp, opposite)
    pl.when(z + 1 < lines)(lambda: greet(fsdp + 2, dp))
    pl.when(z > 0)(lambda: greet(fsdp - 2, dp))
    ends = (z + 1 < lines).astype(jnp.int32) + (z > 0).astype(jnp.int32)
    pl.semaphore_wait(barrier, 3 + ends)

    MATE_A, MATE_B, FACING, ACROSS, UP, DOWN, ENDING, LAST_MATE, LAST_SECOND, LAST_FACING = range(10)

    def move(cut, slot, source, target, f, d):
        return pltpu.make_async_remote_copy(
            src_ref=source,
            dst_ref=target,
            send_sem=send.at[cut, slot],
            recv_sem=recv.at[cut, slot],
            device_id=(f, d),
            device_id_type=MESH,
        )

    def columns(cut, which):
        return pl.ds(pl.multiple_of((3 * cut + which) * size, 128), size)

    def mine(cut, which):
        return grads[:, :, :, columns(cut, which)].astype(F32)

    def to_mate_a(cut):
        return move(cut, MATE_A, grads.at[:, :, :, columns(cut, mate_part)], mate_a.at[cut], fsdp, mate)

    def to_mate_b(cut):
        return move(
            cut, MATE_B, grads.at[:, :, :, columns(cut, 2 - mate_part)], mate_b.at[cut], fsdp, mate
        )

    def to_facing(cut):
        return move(cut, FACING, mate_b.at[cut], facing.at[cut], fsdp, opposite)

    def to_across(cut):
        return move(cut, ACROSS, mate_a.at[cut, :, 1 - x], side.at[cut], across, dp)

    def going_up(cut, count):
        blocks = pl.ds(0, count)
        return move(cut, UP, up_out.at[cut, blocks], up_in.at[cut, blocks], fsdp + 2, dp)

    def going_down(cut, count):
        blocks = pl.ds(0, count)
        return move(cut, DOWN, down_out.at[cut, blocks], down_in.at[cut, blocks], fsdp - 2, dp)

    def to_ending(cut):
        return move(cut, ENDING, ending.at[cut], ended.at[cut], fsdp, opposite)

    def last(cut, slot, which, d):
        place = result.at[:, columns(cut, which)]
        return move(cut, slot, place, place, fsdp, d)

    def step_0(cut):
        to_mate_a(cut).start()
        pl.when(lone)(lambda: to_mate_b(cut).start())

    def step_1(cut):
        @pl.when(jnp.logical_not(lone))
        def _():
            to_mate_b(cut).wait_recv()
            mate_b[cut] = (mine(cut, 2 - part) + mate_b[cut].astype(F32)).astype(BF16)
            to_facing(cut).start()

    def step_2(cut):
        to_mate_a(cut).wait_recv()

        @pl.when(lone)
        def _():
            mate_a[cut] = (mine(cut, 1) + mate_a[cut].astype(F32)).astype(BF16)

        @pl.when(jnp.logical_not(lone))
        def _():
            to_facing(cut).wait_recv()
            both = mine(cut, part) + mate_a[cut].astype(F32) + facing[cut].astype(F32)
            mate_a[cut] = both.astype(BF16)

        to_across(cut).start()

    def step_3(cut):
        to_across(cut).wait_recv()
        sums[cut] = mate_a[cut, :, x].astype(F32) + side[cut].astype(F32)

    def lift(cut, hop):
        at = hop - 1

        @pl.when(z == at)
        def _():
            count = lines - hop
            if at > 0:
                going_up(cut, count + 1).wait_recv()
            for ahead in range(1, count + 1):
                value = sums[cut, at + ahead]
                if at > 0:
                    value = value + up_in[cut, ahead].astype(F32)
                up_out[cut, ahead - 1] = value.astype(BF16)
            going_up(cut, count).start()

        low = lines - hop

        @pl.when(z == low)
        def _():
            count = lines - hop
            if low < lines - 1:
                going_down(cut, count + 1).wait_recv()
            for ahead in range(1, count + 1):
                value = sums[cut, low - ahead]
                if low < lines - 1:
                    value = value + down_in[cut, ahead].astype(F32)
                down_out[cut, ahead - 1] = value.astype(BF16)
            going_down(cut, count).start()

    def finish(cut):
        for at in range(lines):

            @pl.when(z == at)
            def _(at=at):
                value = sums[cut, at]
                if at == lines - 1:
                    going_up(cut, 1).wait_recv()
                if at == 0:
                    going_down(cut, 1).wait_recv()
                if at > 0:
                    value = value + up_in[cut, 0].astype(F32)
                if at < lines - 1:
                    value = value + down_in[cut, 0].astype(F32)
                ending[cut] = value.astype(BF16)

        pl.when(lone)(lambda: to_ending(cut).start())

        @pl.when(jnp.logical_not(lone))
        def _():
            result[:, columns(cut, part)] = ending[cut]
            last(cut, LAST_FACING, part, opposite).start()
            last(cut, LAST_MATE, part, mate).start()

    def share(cut):
        @pl.when(lone)
        def _():
            to_ending(cut).wait_recv()
            both = ending[cut].astype(F32) + ended[cut].astype(F32)
            result[:, columns(cut, part)] = both.astype(BF16)
            last(cut, LAST_MATE, part, mate).start()

        @pl.when(jnp.logical_not(lone))
        def _():
            last(cut, LAST_FACING, 2 - part, opposite).wait_recv()
            last(cut, LAST_SECOND, 2 - part, mate).start()

    def close(cut):
        last(cut, LAST_MATE, mate_part, mate).wait_recv()
        pl.when(lone)(lambda: last(cut, LAST_SECOND, 2 - mate_part, mate).wait_recv())

    steps = [step_0, step_1, step_2, step_3]
    steps += [functools.partial(lambda hop, cut: lift(cut, hop), hop) for hop in range(1, lines)]
    steps += [finish, share, close]
    for tick in range(cuts + len(steps) - 1):
        for number, step in enumerate(steps):
            if 0 <= tick - number < cuts:
                step(tick - number)

    out[...] = result[...].astype(F32)
    for cut in range(cuts):
        to_mate_a(cut).wait_send()
        to_across(cut).wait_send()
        for hop in range(1, lines):
            pl.when(z == hop - 1)(lambda hop=hop: going_up(cut, lines - hop).wait_send())
            pl.when(z == lines - hop)(lambda hop=hop: going_down(cut, lines - hop).wait_send())
        last(cut, LAST_MATE, part, mate).wait_send()

        @pl.when(lone)
        def _():
            to_mate_b(cut).wait_send()
            to_ending(cut).wait_send()

        @pl.when(jnp.logical_not(lone))
        def _():
            to_facing(cut).wait_send()
            last(cut, LAST_FACING, part, opposite).wait_send()
            last(cut, LAST_SECOND, 2 - part, mate).wait_send()


def reduce_rows(grads, fsdp_count, cuts, collective_id):
    total, width = grads.shape
    lines, rows = fsdp_count // 2, total // fsdp_count
    size = width // (3 * cuts)
    blocks = (cuts, lines, 2, rows, size)
    return pl.pallas_call(
        functools.partial(reduce_kernel, cuts, lines),
        out_shape=jax.ShapeDtypeStruct((rows, width), F32),
        in_specs=[pl.BlockSpec(memory_space=pltpu.VMEM)],
        out_specs=pl.BlockSpec(memory_space=pltpu.VMEM),
        scratch_shapes=[
            pltpu.VMEM(blocks, BF16),
            pltpu.VMEM(blocks, BF16),
            pltpu.VMEM(blocks, BF16),
            pltpu.VMEM((cuts, lines, rows, size), BF16),
            pltpu.VMEM((cuts, lines, rows, size), F32),
        ]
        + [pltpu.VMEM((cuts, lines - 1, rows, size), BF16)] * 4
        + [pltpu.VMEM((cuts, rows, size), BF16)] * 2
        + [
            pltpu.VMEM((rows, width), BF16),
            pltpu.SemaphoreType.DMA((cuts, 10)),
            pltpu.SemaphoreType.DMA((cuts, 10)),
        ],
        compiler_params=pltpu.CompilerParams(
            collective_id=collective_id, has_side_effects=True, vmem_limit_bytes=58 << 20
        ),
        name="reduce_rows",
    )(grads.reshape(lines, 2, rows, width))


GELU_A = 0.7978845608028654
GELU_B = 0.044715
TAIL = 16


def mm(left, right):
    return lax.dot_general(left, right, (((1,), (0,)), ((), ())), preferred_element_type=F32)


def mm_nt(left, right):
    return lax.dot_general(left, right, (((1,), (1,)), ((), ())), preferred_element_type=F32)


def mm_tn(left, right):
    return lax.dot_general(left, right, (((0,), (0,)), ((), ())), preferred_element_type=F32)


def norm_parts(x):
    centred = x - jnp.mean(x, -1, keepdims=True)
    lift = lax.rsqrt(jnp.mean(centred * centred, -1, keepdims=True) + 1e-06)
    return centred * lift, lift


def norm_back(grad, gain, unit_x, lift):
    inner = grad * gain
    return lift * (
        inner
        - jnp.mean(inner, -1, keepdims=True)
        - unit_x * jnp.mean(inner * unit_x, -1, keepdims=True)
    )


def gelu(x):
    return 0.5 * x * (1.0 + jnp.tanh(GELU_A * (x + GELU_B * (x * x * x))))


def gelu_both(x):
    square = x * x
    slope = jnp.tanh(GELU_A * x * (1.0 + GELU_B * square))
    half = 0.5 * (1.0 + slope)
    turn = half + 0.5 * x * (1.0 - slope * slope) * GELU_A * (1.0 + 3.0 * GELU_B * square)
    return x * half, turn


def half_masks(width):
    lane = lax.broadcasted_iota(jnp.int32, (1, 128), 1)
    first = (lane < width).astype(F32)
    return first, 1.0 - first


def column_sum(x):
    return jnp.sum(x, 0, keepdims=True)


def attend(q, keys, values, valid, scale, lse_store):
    rows, total = q.shape[0], keys.shape[0]
    masks = half_masks(64)
    column = lax.broadcasted_iota(jnp.int32, (rows, total), 1)
    lane = lax.broadcasted_iota(jnp.int32, (rows, 128), 1)
    mixed, lse = [], jnp.zeros((rows, 128), F32)
    for pair in range(HEADS // 2):
        span = slice(128 * pair, 128 * pair + 128)
        halves = []
        for side in range(2):
            asked = q[:, span] * (masks[side] * scale).astype(BF16)
            scores = mm_nt(asked, keys[:, span])
            scores = jnp.where(column < valid, scores, -1e30)
            top = jnp.max(scores, -1, keepdims=True)
            expo = jnp.exp(scores - top)
            total_e = jnp.sum(expo, -1, keepdims=True)
            halves.append(mm(expo.astype(BF16), values[:, span]) / total_e)
            if lse_store:
                lse = jnp.where(lane == 2 * pair + side, top + jnp.log(total_e), lse)
        mixed.append(jnp.where(lane < 64, halves[0], halves[1]))
    return jnp.concatenate(mixed, -1).astype(BF16), lse


def forward_kernel(
    images, hidden, keep, patches, covered, weight_p, weight_0, weight_1, places, rows_table, *rest
):
    if keep:
        (cls_out, x0_out, x1_out, x2_out, qkv_out, o0_out, lse0_out, kv_out, q1_out, lse1_out,
         x1c_out, o1_out, cls_x, cls_o) = rest
    else:
        cls_out, cls_x, cls_o = rest
    image = pl.program_id(0)
    model = weight_0.shape[0]
    count = patches.shape[1]
    valid = count + 1
    scale = (model // HEADS) ** -0.5

    def vec(row):
        return rows_table[row : row + 1, :]

    @pl.when(image == 0)
    def _():
        cls_x[...] = jnp.zeros_like(cls_x)
        cls_o[...] = jnp.zeros_like(cls_o)

    tokens = mm_nt(patches[0], weight_p[:, : patches.shape[2]]) + vec(1)
    if keep:
        hide = covered[0]
        tokens = tokens * (1.0 - hide) + vec(0) * hide
    x = jnp.concatenate([tokens + places[:count, :], places[count:, :]], 0)

    def row(layer, index):
        return vec(2 + 6 * layer + index)

    unit_x, _ = norm_parts(x)
    low = (unit_x * row(0, 0) + row(0, 1)).astype(BF16)
    qkv = mm(low, weight_0[:, : 3 * model]).astype(BF16)
    mixture, lse = attend(
        qkv[:, :model], qkv[:, model : 2 * model], qkv[:, 2 * model :], valid, scale, keep
    )
    x1 = x + row(0, 2) * mm(mixture, weight_0[:, 3 * model : 4 * model])
    unit_x, _ = norm_parts(x1)
    low = (unit_x * row(0, 3) + row(0, 4)).astype(BF16)
    wide = gelu(mm(low, weight_0[:, 4 * model : 4 * model + hidden])).astype(BF16)
    x2 = x1 + row(0, 5) * mm_nt(wide, weight_0[:, 4 * model + hidden :])

    unit_x, _ = norm_parts(x2)
    low = (unit_x * row(1, 0) + row(1, 1)).astype(BF16)
    kv = mm(low, weight_1[:, model : 3 * model]).astype(BF16)
    q1 = mm(low[count:, :], weight_1[:, :model]).astype(BF16)
    mixture1, lse1 = attend(q1, kv[:, :model], kv[:, model:], valid, scale, keep)
    cls_x[pl.ds(image, 1), :] = x2[count : count + 1, :]
    cls_o[pl.ds(image, 1), :] = mixture1[:1, :].astype(F32)
    if keep:
        x0_out[0] = x
        x1_out[0] = x1
        x2_out[0] = x2
        qkv_out[0] = qkv
        o0_out[0] = mixture
        lse0_out[0] = lse
        kv_out[0] = kv
        q1_out[0] = q1
        lse1_out[0] = lse1

    @pl.when(image == images - 1)
    def _():
        mixed = cls_o[...].astype(BF16)
        x1c = cls_x[...] + row(1, 2) * mm(mixed, weight_1[:, 3 * model : 4 * model])
        unit_c, _ = norm_parts(x1c)
        low_c = (unit_c * row(1, 3) + row(1, 4)).astype(BF16)
        wide_c = gelu(mm(low_c, weight_1[:, 4 * model : 4 * model + hidden])).astype(BF16)
        cls_out[...] = x1c + row(1, 5) * mm_nt(wide_c, weight_1[:, 4 * model + hidden :])
        if keep:
            x1c_out[...] = x1c
            o1_out[...] = mixed


def fixed(shape):
    zeros = (0,) * len(shape)
    return pl.BlockSpec(shape, lambda i: zeros, pipeline_mode=pl.Buffered(1))


def each(shape):
    rest = (0,) * len(shape)
    return pl.BlockSpec((1,) + shape, lambda i: (i,) + rest)


def whole_out(shape):
    zeros = (0,) * len(shape)
    return pl.BlockSpec(shape, lambda i: zeros)


def split_table(vecs, count):
    places = jnp.concatenate(
        [
            vecs[1 : count + 1],
            vecs[:1] + vecs[count + 1 : count + 2],
            jnp.zeros((TAIL - 1, vecs.shape[1]), F32),
        ]
    )
    rows = vecs[count + 2 :]
    rows = jnp.concatenate([rows, jnp.zeros(((-rows.shape[0]) % 8, rows.shape[1]), F32)])
    return places, rows


def forward(patches, covered, weight_p, weight_0, weight_1, vecs, keep):
    images, count, pixels = patches.shape
    model, columns = weight_0.shape
    hidden = (columns - 4 * model) // 2
    total = count + TAIL
    places, rows = split_table(vecs, count)
    shape = jax.ShapeDtypeStruct
    outs = [shape((TAIL, model), F32)]
    out_specs = [whole_out((TAIL, model))]
    if keep:
        per_image = [
            ((total, model), F32),
            ((total, model), F32),
            ((total, model), F32),
            ((total, 3 * model), BF16),
            ((total, model), BF16),
            ((total, 128), F32),
            ((total, 2 * model), BF16),
            ((TAIL, model), BF16),
            ((TAIL, 128), F32),
        ]
        outs += [shape((images,) + dims, kind) for dims, kind in per_image]
        out_specs += [each(dims) for dims, kind in per_image]
        outs += [shape((TAIL, model), F32), shape((TAIL, model), BF16)]
        out_specs += [whole_out((TAIL, model))] * 2
    return pl.pallas_call(
        functools.partial(forward_kernel, images, hidden, keep),
        grid=(images,),
        out_shape=outs,
        in_specs=[
            each((count, pixels)),
            each((count, 1)),
            fixed(weight_p.shape),
            fixed(weight_0.shape),
            fixed(weight_1.shape),
            fixed(places.shape),
            fixed(rows.shape),
        ],
        out_specs=out_specs,
        scratch_shapes=[pltpu.VMEM((TAIL, model), F32)] * 2,
        compiler_params=pltpu.CompilerParams(vmem_limit_bytes=56 << 20),
        name="backbone_forward",
    )(patches, covered[..., None], weight_p, weight_0, weight_1, places, rows)


def attend_back(grad_o, q, keys, values, lse, valid, scale):
    rows, total = q.shape[0], keys.shape[0]
    masks = half_masks(64)
    column = lax.broadcasted_iota(jnp.int32, (rows, total), 1)
    lane_row = lax.broadcasted_iota(jnp.int32, (rows, 128), 1)
    grad_q, grad_k, grad_v = [], [], []
    for pair in range(HEADS // 2):
        span = slice(128 * pair, 128 * pair + 128)
        out_q, out_k, out_v = [], None, None
        for side in range(2):
            mask = masks[side].astype(BF16)
            asked = q[:, span] * (masks[side] * scale).astype(BF16)
            given = grad_o[:, span] * mask
            head = 2 * pair + side
            scores = mm_nt(asked, keys[:, span])
            share = jnp.where(column < valid, jnp.exp(scores - lse[:, head : head + 1]), 0.0)
            grad_p = mm_nt(given, values[:, span])
            inner = jnp.sum(share * grad_p, -1, keepdims=True)
            grad_s = (share * (grad_p - inner)).astype(BF16)
            out_q.append(mm(grad_s, keys[:, span]))
            more_k = mm_tn(grad_s, asked)
            more_v = mm_tn(share.astype(BF16), given)
            out_k = more_k if out_k is None else out_k + more_k
            out_v = more_v if out_v is None else out_v + more_v
        grad_q.append(jnp.where(lane_row < 64, out_q[0], out_q[1]) * scale)
        grad_k.append(out_k)
        grad_v.append(out_v)
    return [jnp.concatenate(part, -1).astype(BF16) for part in (grad_q, grad_k, grad_v)]


def backward_kernel(
    images, hidden, count_, patches, covered, weight_p, weight_0, weight_1, rows_table, ends, grad_cls,
    x0_in, x1_in, x2_in, qkv_in, o0_in, lse0_in, kv_in, q1_in, lse1_in, x1c_in, o1_in,
    packed, acc_p, acc_0, acc_kv, acc_q, grad_c, grad_oc, places, rows
):
    image = pl.program_id(0)
    model = weight_0.shape[0]
    count, pixels = patches.shape[1], patches.shape[2]
    valid = count + 1
    scale = (model // HEADS) ** -0.5
    base_0 = packed_width_p(pixels)
    columns = weight_0.shape[1]
    base_1 = base_0 + columns
    base_v = base_1 + columns
    cut_o, cut_u, cut_d = 3 * model, 4 * model, 4 * model + hidden

    def row(layer, index):
        at = 2 + 6 * layer + index
        return rows_table[at : at + 1, :]

    def add_row(layer, index, value):
        at = 2 + 6 * layer + index
        rows[at : at + 1, :] += value

    @pl.when(image == 0)
    def _():
        for ref in (acc_p, acc_0, acc_kv, acc_q, places, rows):
            ref[...] = jnp.zeros_like(ref)
        grad_x = grad_cls[...]
        x1c = x1c_in[...]
        unit_x, lift = norm_parts(x1c)
        low = (unit_x * row(1, 3) + row(1, 4)).astype(BF16)
        wide, slope = gelu_both(mm(low, weight_1[:, cut_u:cut_d]))
        wide = wide.astype(BF16)
        down = mm_nt(wide, weight_1[:, cut_d:])
        add_row(1, 5, column_sum(grad_x * down))
        grad_d = (grad_x * row(1, 5)).astype(BF16)
        grad_u = (mm(grad_d, weight_1[:, cut_d:]) * slope).astype(BF16)
        packed[:, base_1 + cut_d : base_v] = mm_tn(grad_d, wide).astype(BF16)
        packed[:, base_1 + cut_u : base_1 + cut_d] = mm_tn(low, grad_u).astype(BF16)
        grad_n = mm_nt(grad_u, weight_1[:, cut_u:cut_d])
        add_row(1, 3, column_sum(grad_n * unit_x))
        add_row(1, 4, column_sum(grad_n))
        grad_x = grad_x + norm_back(grad_n, row(1, 3), unit_x, lift)
        mixed = o1_in[...]
        add_row(1, 2, column_sum(grad_x * mm(mixed, weight_1[:, cut_o:cut_u])))
        grad_a = (grad_x * row(1, 2)).astype(BF16)
        packed[:, base_1 + cut_o : base_1 + cut_u] = mm_tn(mixed, grad_a).astype(BF16)
        grad_c[...] = grad_x
        grad_oc[...] = mm_nt(grad_a, weight_1[:, cut_o:cut_u])

    first_row = lax.broadcasted_iota(jnp.int32, (TAIL, 1), 0) == 0

    grad_o1 = jnp.where(first_row, grad_oc[pl.ds(image, 1), :], 0.0).astype(BF16)
    kv = kv_in[0]
    grad_q, grad_k, grad_v = attend_back(
        grad_o1, q1_in[0], kv[:, :model], kv[:, model:], lse1_in[0], valid, scale
    )
    unit_x, lift = norm_parts(x2_in[0])
    low = (unit_x * row(1, 0) + row(1, 1)).astype(BF16)
    grad_kv = jnp.concatenate([grad_k, grad_v], -1)
    acc_kv[...] += mm_tn(low, grad_kv)
    acc_q[...] += mm_tn(low[count:, :], grad_q)
    grad_n = mm_nt(grad_kv, weight_1[:, model : 3 * model])
    tail = grad_n[count:, :] + mm_nt(grad_q, weight_1[:, :model])
    grad_n = jnp.concatenate([grad_n[:count, :], tail], 0)
    add_row(1, 0, column_sum(grad_n * unit_x))
    add_row(1, 1, column_sum(grad_n))
    grad_x = norm_back(grad_n, row(1, 0), unit_x, lift)
    tail = grad_x[count:, :] + jnp.where(first_row, grad_c[pl.ds(image, 1), :], 0.0)
    grad_x = jnp.concatenate([grad_x[:count, :], tail], 0)

    unit_x, lift = norm_parts(x1_in[0])
    low = (unit_x * row(0, 3) + row(0, 4)).astype(BF16)
    wide, slope = gelu_both(mm(low, weight_0[:, cut_u:cut_d]))
    wide = wide.astype(BF16)
    down = mm_nt(wide, weight_0[:, cut_d:])
    add_row(0, 5, column_sum(grad_x * down))
    grad_d = (grad_x * row(0, 5)).astype(BF16)
    grad_u = (mm(grad_d, weight_0[:, cut_d:]) * slope).astype(BF16)
    acc_0[:, cut_d:] += mm_tn(grad_d, wide)
    acc_0[:, cut_u:cut_d] += mm_tn(low, grad_u)
    grad_n = mm_nt(grad_u, weight_0[:, cut_u:cut_d])
    add_row(0, 3, column_sum(grad_n * unit_x))
    add_row(0, 4, column_sum(grad_n))
    grad_x = grad_x + norm_back(grad_n, row(0, 3), unit_x, lift)
    mixed = o0_in[0]
    add_row(0, 2, column_sum(grad_x * mm(mixed, weight_0[:, cut_o:cut_u])))
    grad_a = (grad_x * row(0, 2)).astype(BF16)
    acc_0[:, cut_o:cut_u] += mm_tn(mixed, grad_a)
    grad_o = mm_nt(grad_a, weight_0[:, cut_o:cut_u]).astype(BF16)
    qkv = qkv_in[0]
    grad_qkv = jnp.concatenate(
        attend_back(
            grad_o, qkv[:, :model], qkv[:, model : 2 * model], qkv[:, 2 * model :], lse0_in[0],
            valid, scale,
        ),
        -1,
    )
    unit_x, lift = norm_parts(x0_in[0])
    low = (unit_x * row(0, 0) + row(0, 1)).astype(BF16)
    acc_0[:, :cut_o] += mm_tn(low, grad_qkv)
    grad_n = mm_nt(grad_qkv, weight_0[:, :cut_o])
    add_row(0, 0, column_sum(grad_n * unit_x))
    add_row(0, 1, column_sum(grad_n))
    grad_x = grad_x + norm_back(grad_n, row(0, 0), unit_x, lift)

    places[...] += grad_x
    hide = covered[0]
    token = grad_x[:count, :]
    rows[0:1, :] += column_sum(token * hide)
    token = token * (1.0 - hide)
    rows[1:2, :] += column_sum(token)
    acc_p[...] += mm_tn(token.astype(BF16), patches[0])

    @pl.when(image == images - 1)
    def _():
        packed[:, :base_0] = jnp.concatenate(
            [acc_p[...], jnp.zeros((model, base_0 - pixels), F32)], -1
        ).astype(BF16)
        packed[:, base_0:base_1] = acc_0[...].astype(BF16)
        packed[:, base_1 : base_1 + model] = acc_q[...].astype(BF16)
        packed[:, base_1 + model : base_1 + cut_o] = acc_kv[...].astype(BF16)
        used = rows_table.shape[0]
        table = jnp.concatenate(
            [
                places[count : count + 1, :],
                places[:count, :],
                places[count : count + 1, :],
                rows[...] + ends[...],
            ],
            0,
        )
        table = jnp.concatenate(
            [table, jnp.zeros((model - table.shape[0], model), F32)], 0
        )
        packed[:, base_v : base_v + model] = table.astype(BF16)
        spare = packed.shape[1] - base_v - model
        if spare:
            packed[:, base_v + model :] = jnp.zeros((model, spare), BF16)


def packed_width_p(pixels):
    return (pixels + 127) // 128 * 128


def packed_width(pixels, columns, model):
    width = packed_width_p(pixels) + 2 * columns + model
    return (width + 1151) // 1152 * 1152


def backward(patches, covered, weight_p, weight_0, weight_1, vecs, ends, grad_cls, saved):
    images, count, pixels = patches.shape
    model, columns = weight_0.shape
    hidden = (columns - 4 * model) // 2
    total = count + TAIL
    _, rows = split_table(vecs, count)
    ends = jnp.concatenate(
        [jnp.zeros((14, model), F32), ends, jnp.zeros((rows.shape[0] - 16, model), F32)]
    )
    width = packed_width(pixels, columns, model)
    return pl.pallas_call(
        functools.partial(backward_kernel, images, hidden, count),
        grid=(images,),
        out_shape=jax.ShapeDtypeStruct((model, width), BF16),
        in_specs=[
            each((count, pixels)),
            each((count, 1)),
            fixed(weight_p.shape),
            fixed(weight_0.shape),
            fixed(weight_1.shape),
            fixed(rows.shape),
            fixed(ends.shape),
            fixed(grad_cls.shape),
        ]
        + [each(array.shape[1:]) for array in saved[:9]]
        + [fixed(array.shape) for array in saved[9:]],
        out_specs=whole_out((model, width)),
        scratch_shapes=[
            pltpu.VMEM((model, pixels), F32),
            pltpu.VMEM((model, columns), F32),
            pltpu.VMEM((model, 2 * model), F32),
            pltpu.VMEM((model, model), F32),
            pltpu.VMEM((TAIL, model), F32),
            pltpu.VMEM((TAIL, model), F32),
            pltpu.VMEM((total, model), F32),
            pltpu.VMEM(rows.shape, F32),
        ],
        compiler_params=pltpu.CompilerParams(vmem_limit_bytes=58 << 20),
        name="backbone_backward",
    )(patches, covered[..., None], weight_p, weight_0, weight_1, rows, ends, grad_cls, *saved)


def owners_of(low, high, rows, count):
    return [f for f in range(count) if f * rows < high and (f + 1) * rows > low]


def two_halves(value):
    half = value.shape[1] // 2
    return jnp.concatenate([value[:, :half], value[:, half:]], 0).astype(BF16)


def from_halves(slots):
    wide = slots.astype(F32)
    half = wide.shape[-1]
    first = wide[:, :8, :].reshape(-1, half)
    second = wide[:, 8:, :].reshape(-1, half)
    return jnp.concatenate([first, second], -1)


def student_rows(value, start=0):
    pieces = [value[at + start : at + start + 4, :] for at in range(0, value.shape[0], 8)]
    return jnp.concatenate(pieces, 0)


def sixteen(value):
    return jnp.concatenate([value, jnp.zeros_like(value)], 0).astype(BF16)


def head_kernel(
    sizes, cls, gains, first_s, first_t, third_s, third_t, shard_s, shard_t, centre, counted_row,
    counted_col, proto_s, proto_t,
    grad_cls, ends, loss_row, totals, grad_logits, unit_rows, grad_head,
    table_s, table_t, loading, wide_s, wide_t, kept, left, acts, parts_out, parts_in, units,
    stats, pulls, pulled, backs, pieces, pieced, extra_1, extra_3, lefts, rights, tall,
    send, recv, send_z, recv_z, send_x, recv_x, send_d, recv_d,
):
    count, dp_count, rows, chunk = sizes
    fsdp, dp = lax.axis_index("fsdp"), lax.axis_index("dp")
    model, hidden = first_s.shape
    width = third_s.shape[0]
    top_2, top_3 = model, model + hidden
    top_4 = top_3 + width
    span = kept.shape[0] // 2
    base = fsdp * rows // 128 * 128
    offset = fsdp * rows - base
    slot_rows = 8 * count
    is_student = lax.broadcasted_iota(jnp.int32, (8, 1), 0) < 4
    owners_1 = owners_of(0, top_2, rows, count)
    owners_2 = owners_of(top_2, top_3, rows, count)
    owners_3 = owners_of(top_3, top_4, rows, count)

    load_s = pltpu.make_async_copy(proto_s, table_s, loading.at[0])
    load_t = pltpu.make_async_copy(proto_t, table_t, loading.at[1])
    load_s.start()
    load_t.start()

    barrier = pltpu.get_barrier_semaphore()
    for f_step in range(count):
        for d_step in range(dp_count):
            if f_step or d_step:
                peer_f = lax.rem(fsdp + f_step, count)
                peer_d = lax.rem(dp + d_step, dp_count)
                pl.semaphore_signal(barrier, 1, device_id=(peer_f, peer_d), device_id_type=MESH)
    pl.semaphore_wait(barrier, count * dp_count - 1)

    ACTS, PARTS, STATS, PULLS, BACKS, PIECES, TOTALS = range(7)

    def swap(kind, step, source_of, target):
        peer = lax.rem(fsdp + step, count)
        return pltpu.make_async_remote_copy(
            src_ref=source_of(peer),
            dst_ref=target.at[fsdp],
            send_sem=send.at[kind, step - 1],
            recv_sem=recv.at[kind, fsdp],
            device_id=(peer, dp),
            device_id_type=MESH,
        )

    def begin(kind, source_of, target):
        for step in range(1, count):
            swap(kind, step, source_of, target).start()

    def arrive(kind, target):
        for step in range(1, count):
            peer = lax.rem(fsdp + step, count)
            pltpu.make_async_remote_copy(
                src_ref=target.at[peer],
                dst_ref=target.at[peer],
                send_sem=send.at[kind, step - 1],
                recv_sem=recv.at[kind, peer],
                device_id=(peer, dp),
                device_id_type=MESH,
            ).wait_recv()

    def end(kind, source_of, target):
        for step in range(1, count):
            swap(kind, step, source_of, target).wait_send()

    def each_net(value, first, second, product):
        low = sixteen(value)
        return jnp.where(is_student, product(low, first)[:8, :], product(low, second)[:8, :])

    unit_c, lift_c = norm_parts(cls[...])
    normed = unit_c * gains[:8, :] + gains[8:, :]
    pre_a = each_net(normed, first_s[...], first_t[...], mm)
    act_a, slope_a = gelu_both(pre_a)
    acts[fsdp] = two_halves(act_a)
    begin(ACTS, lambda peer: acts.at[fsdp], acts)

    row = fsdp * rows + lax.broadcasted_iota(jnp.int32, (rows, 1), 0)
    inside = (row >= top_2) & (row < top_3)
    kept[...] = jnp.zeros_like(kept)
    place = pl.multiple_of(offset, 16)
    kept[pl.ds(place, rows), :] = jnp.where(inside, shard_s[...], 0.0).astype(BF16)
    kept[pl.ds(pl.multiple_of(span + offset, 16), rows), :] = jnp.where(
        inside, shard_t[...], 0.0
    ).astype(BF16)
    left[...] = jnp.zeros_like(left)
    columns = pl.ds(pl.multiple_of(base, 128), span)

    arrive(ACTS, acts)
    left[:, top_2:top_3] = from_halves(acts[...])
    asked = left[:, columns].astype(BF16)
    net = lax.broadcasted_iota(jnp.int32, (slot_rows, 1), 0) % 8 < 4
    product = jnp.where(net, mm(asked, kept[:span, :]), mm(asked, kept[span:, :]))
    for f in range(count):
        parts_out[f] = two_halves(product[8 * f : 8 * f + 8, :])
    parts_in[fsdp] = parts_out[fsdp]
    begin(PARTS, lambda peer: parts_out.at[peer], parts_in)
    arrive(PARTS, parts_in)
    summed = from_halves(parts_in[...])
    pre_b = summed[:8, :]
    for f in range(1, count):
        pre_b = pre_b + summed[8 * f : 8 * f + 8, :]
    act_b, slope_b = gelu_both(pre_b)
    raw = each_net(act_b, third_s[...], third_t[...], mm_nt)
    lift_z = lax.rsqrt(jnp.sum(raw * raw, -1, keepdims=True) + 1e-06)
    unit_z = raw * lift_z

    me = fsdp * dp_count + dp
    everyone = count * dp_count
    units[me] = two_halves(unit_z)

    def unit_copy(step):
        peer = lax.rem(me + step, everyone)
        return pltpu.make_async_remote_copy(
            src_ref=units.at[me],
            dst_ref=units.at[me],
            send_sem=send_z.at[step - 1],
            recv_sem=recv_z.at[me],
            device_id=(peer // dp_count, lax.rem(peer, dp_count)),
            device_id_type=MESH,
        )

    for step in range(1, everyone):
        unit_copy(step).start()

    def owner_copy(kind, owner, source, target):
        return pltpu.make_async_remote_copy(
            src_ref=source,
            dst_ref=target.at[fsdp],
            send_sem=send_x.at[kind, owner],
            recv_sem=recv_x.at[kind, fsdp],
            device_id=(owner, dp),
            device_id_type=MESH,
        )

    def owners_begin(kind, owners, target, value):
        target[fsdp] = value
        for owner in owners:
            pl.when(fsdp != owner)(
                lambda owner=owner: owner_copy(kind, owner, target.at[fsdp], target).start()
            )

    def owners_end(kind, owners, target):
        for owner in owners:
            pl.when(fsdp != owner)(
                lambda owner=owner: owner_copy(kind, owner, target.at[fsdp], target).wait_send()
            )

    def owners_arrive(kind, owners, target):
        for owner in owners:

            @pl.when(fsdp == owner)
            def _(owner=owner):
                for f in range(count):
                    if f != owner:
                        pltpu.make_async_remote_copy(
                            src_ref=target.at[f],
                            dst_ref=target.at[f],
                            send_sem=send_x.at[kind, owner],
                            recv_sem=recv_x.at[kind, f],
                            device_id=(f, dp),
                            device_id_type=MESH,
                        ).wait_recv()

    for step in range(1, everyone):
        peer = lax.rem(me + step, everyone)
        pltpu.make_async_remote_copy(
            src_ref=units.at[peer],
            dst_ref=units.at[peer],
            send_sem=send_z.at[step - 1],
            recv_sem=recv_z.at[peer],
            device_id=(peer // dp_count, lax.rem(peer, dp_count)),
            device_id_type=MESH,
        ).wait_recv()
    all_units = from_halves(units[...])
    rows_s = student_rows(all_units).astype(BF16)
    rows_t = student_rows(all_units, 4).astype(BF16)
    unit_rows[...] = rows_s

    load_s.wait()
    load_t.wait()
    images = rows_s.shape[0]
    chunks = table_s.shape[0] // chunk
    low_start = jnp.full((images, 128), -3.0e38, F32)

    def lanes(op, value):
        out = value[:, :128]
        for at in range(128, value.shape[1], 128):
            out = op(out, value[:, at : at + 128])
        return out

    def logits_pass(index, tops):
        top_t, top_s = tops
        at = pl.ds(pl.multiple_of(index * chunk, chunk), chunk)
        raw_t = mm_nt(rows_t, table_t[at, :].astype(BF16))
        totals[fsdp, pl.ds(index, 1), :] = column_sum(counted_col[...] * raw_t)
        scaled_t = (raw_t - centre[:, at]) * (1.0 / TEACHER_TEMP)
        scaled_s = mm_nt(rows_s, table_s[at, :].astype(BF16)) * (1.0 / STUDENT_TEMP)
        wide_t[:, at] = scaled_t
        wide_s[:, at] = scaled_s
        return (
            jnp.maximum(top_t, lanes(jnp.maximum, scaled_t)),
            jnp.maximum(top_s, lanes(jnp.maximum, scaled_s)),
        )

    top_t, top_s = lax.fori_loop(0, chunks, logits_pass, (low_start, low_start))
    top_t = jnp.max(top_t, -1, keepdims=True)
    top_s = jnp.max(top_s, -1, keepdims=True)
    begin(TOTALS, lambda peer: totals.at[fsdp], totals)

    def expo_pass(index, sums):
        sum_t, sum_s, cross = sums
        at = pl.ds(pl.multiple_of(index * chunk, chunk), chunk)
        shifted_s = wide_s[:, at] - top_s
        expo_t = jnp.exp(wide_t[:, at] - top_t)
        expo_s = jnp.exp(shifted_s)
        wide_t[:, at] = expo_t
        wide_s[:, at] = expo_s
        return (
            sum_t + lanes(jnp.add, expo_t),
            sum_s + lanes(jnp.add, expo_s),
            cross + lanes(jnp.add, expo_t * shifted_s),
        )

    zero = jnp.zeros((images, 128), F32)
    sum_t, sum_s, cross = lax.fori_loop(0, chunks, expo_pass, (zero, zero, zero))
    lane = lax.broadcasted_iota(jnp.int32, (images, 128), 1)
    columns_of = zero
    values = (top_t, jnp.sum(sum_t, -1, keepdims=True), top_s, jnp.sum(sum_s, -1, keepdims=True),
              jnp.sum(cross, -1, keepdims=True))
    for number, value in enumerate(values):
        columns_of = jnp.where(lane == number, value, columns_of)
    stats[fsdp] = columns_of.T[:8, :]
    begin(STATS, lambda peer: stats.at[fsdp], stats)
    arrive(STATS, stats)
    gathered = [stats[f] for f in range(count)]
    high_t, high_s = gathered[0][0:1, :], gathered[0][2:3, :]
    for part in gathered[1:]:
        high_t = jnp.maximum(high_t, part[0:1, :])
        high_s = jnp.maximum(high_s, part[2:3, :])
    total_t = total_s = crossed = jnp.zeros_like(high_t)
    for part in gathered:
        lift_t = jnp.exp(part[0:1, :] - high_t)
        total_t = total_t + part[1:2, :] * lift_t
        total_s = total_s + part[3:4, :] * jnp.exp(part[2:3, :] - high_s)
        crossed = crossed + lift_t * (part[4:5, :] + (part[2:3, :] - high_s) * part[1:2, :])
    counted = counted_row[...]
    loss_row[...] = counted * (jnp.log(total_s) - crossed / total_t)
    weighting = counted / jnp.maximum(jnp.sum(counted, -1, keepdims=True), 1.0) / STUDENT_TEMP
    mine = stats[fsdp]
    share_s = weighting * jnp.exp(mine[2:3, :] - high_s) / total_s
    share_t = weighting * jnp.exp(mine[0:1, :] - high_t) / total_t
    turned = jnp.concatenate([share_s, share_t, jnp.zeros((126, images), F32)], 0).T
    share_s, share_t = turned[:, 0:1], turned[:, 1:2]

    def grad_pass(index, total):
        at = pl.ds(pl.multiple_of(index * chunk, chunk), chunk)
        low = (wide_s[:, at] * share_s - wide_t[:, at] * share_t).astype(BF16)
        grad_logits[:, at] = low
        return total + mm(low, table_s[at, :].astype(BF16))

    partial = lax.fori_loop(0, chunks, grad_pass, jnp.zeros((images, width), F32))
    for slot in range(0, everyone, 2):
        pair = partial[4 * slot : 4 * slot + 8, :]
        pulls[slot] = pair
        pulls[slot + 1] = jnp.concatenate([pair[4:, :], pair[:4, :]], 0)
    pulled[fsdp] = pulls[me]
    begin(PULLS, lambda peer: pulls.at[peer * dp_count + dp], pulled)
    arrive(PULLS, pulled)
    grad_z = pulled[0]
    for f in range(1, count):
        grad_z = grad_z + pulled[f]
    grad_z = jnp.where(is_student, grad_z, 0.0)
    grad_raw = lift_z * (grad_z - unit_z * jnp.sum(unit_z * grad_z, -1, keepdims=True))
    grad_b = mm(sixteen(grad_raw), third_s[...])[:8, :]
    pre_grad_b = jnp.where(is_student, grad_b * slope_b, 0.0)
    backs[fsdp] = two_halves(pre_grad_b)
    begin(BACKS, lambda peer: backs.at[fsdp], backs)
    arrive(BACKS, backs)
    grads_b = from_halves(backs[...])
    piece = mm_nt(grads_b.astype(BF16), kept[:span, :])
    for f in range(count):
        pieces[f] = piece[8 * f : 8 * f + 8, :]
    pieced[fsdp] = pieces[fsdp]
    begin(PIECES, lambda peer: pieces.at[peer], pieced)

    owned = [
        (fsdp >= owners[0]) & (fsdp <= owners[-1]) for owners in (owners_1, owners_2, owners_3)
    ]

    def group_copy(kind, step, place):
        peer = lax.rem(dp + step, dp_count)
        return pltpu.make_async_remote_copy(
            src_ref=place(dp),
            dst_ref=place(dp),
            send_sem=send_d.at[kind, step - 1],
            recv_sem=recv_d.at[kind, dp],
            device_id=(fsdp, peer),
            device_id_type=MESH,
        )

    def group_arrive(kind, place):
        for step in range(1, dp_count):
            peer = lax.rem(dp + step, dp_count)
            pltpu.make_async_remote_copy(
                src_ref=place(peer),
                dst_ref=place(peer),
                send_sem=send_d.at[kind, step - 1],
                recv_sem=recv_d.at[kind, peer],
                device_id=(fsdp, peer),
                device_id_type=MESH,
            ).wait_recv()

    def right_at(number):
        return lambda group: rights.at[group, number]

    def left_at(group):
        return lefts.at[group]

    def group_begin(kind, place):
        for step in range(1, dp_count):
            group_copy(kind, step, place).start()

    def group_end(kind, place):
        for step in range(1, dp_count):
            group_copy(kind, step, place).wait_send()

    @pl.when(owned[1])
    def _():
        rights[dp, 1] = student_rows(grads_b).astype(BF16)
        group_begin(2, right_at(1))

    owners_begin(1, owners_3, extra_3, two_halves(jnp.concatenate([act_b, grad_raw], -1)))
    arrive(PIECES, pieced)
    back_a = jnp.zeros((8, left.shape[1]), F32)
    for f in range(count):
        at = f * rows // 128 * 128
        value = [pieced[f]]
        if at:
            value = [jnp.zeros((8, at), F32)] + value
        if left.shape[1] - at - span:
            value = value + [jnp.zeros((8, left.shape[1] - at - span), F32)]
        back_a = back_a + jnp.concatenate(value, -1)
    pre_grad_a = jnp.where(is_student, back_a[:, top_2:top_3] * slope_a, 0.0)
    spare = jnp.zeros((8, 2 * extra_1.shape[2] - model - hidden), F32)
    owners_begin(
        0, owners_1, extra_1, two_halves(jnp.concatenate([normed, pre_grad_a, spare], -1))
    )
    grad_n = jnp.where(is_student, mm_nt(sixteen(pre_grad_a), first_s[...])[:8, :], 0.0)
    grad_cls[...] = norm_back(grad_n, gains[:8, :], unit_c, lift_c)
    ends[...] = jnp.concatenate(
        [column_sum(grad_n * unit_c), column_sum(grad_n), jnp.zeros((6, model), F32)], 0
    )

    owners_arrive(1, owners_3, extra_3)

    @pl.when(owned[2])
    def _():
        extra = from_halves(extra_3[...])
        left[:, top_3:top_4] = extra[:, hidden:]
        rights[dp, 2] = student_rows(extra[:, :hidden]).astype(BF16)
        group_begin(3, right_at(2))

    owners_arrive(0, owners_1, extra_1)

    @pl.when(owned[0])
    def _():
        extra = from_halves(extra_1[...])
        left[:, :top_2] = extra[:, :model]
        rights[dp, 0] = student_rows(extra[:, model : model + hidden]).astype(BF16)
        group_begin(1, right_at(0))

    lefts[dp] = student_rows(left[:, columns]).astype(BF16)
    group_begin(0, left_at)
    group_arrive(0, left_at)
    tall[...] = jnp.zeros_like(tall)
    column = base + lax.broadcasted_iota(jnp.int32, (1, span), 1)
    for number, (low, high) in enumerate(((0, top_2), (top_2, top_3), (top_3, top_4))):

        @pl.when(owned[number])
        def _(number=number, low=low, high=high):
            group_arrive(1 + number, right_at(number))
            own_side = jnp.concatenate([lefts[group] for group in range(dp_count)], 0)
            keep_columns = ((column >= low) & (column < high)).astype(F32)
            own_side = (own_side.astype(F32) * keep_columns).astype(BF16)
            other = jnp.concatenate([rights[group, number] for group in range(dp_count)], 0)
            tall[...] += mm_tn(own_side, other)
            group_end(1 + number, right_at(number))

    grad_head[...] = tall[pl.ds(place, rows), :]
    group_end(0, left_at)
    arrive(TOTALS, totals)
    end(ACTS, lambda peer: acts.at[fsdp], acts)
    end(PARTS, lambda peer: parts_out.at[peer], parts_in)
    end(STATS, lambda peer: stats.at[fsdp], stats)
    end(PULLS, lambda peer: pulls.at[peer * dp_count + dp], pulled)
    end(BACKS, lambda peer: backs.at[fsdp], backs)
    end(PIECES, lambda peer: pieces.at[peer], pieced)
    end(TOTALS, lambda peer: totals.at[fsdp], totals)
    for step in range(1, everyone):
        unit_copy(step).wait_send()
    owners_end(0, owners_1, extra_1)
    owners_end(1, owners_3, extra_3)


def head_step(
    cls_s, cls_t, vecs_s, vecs_t, weights, shards, centre, counted, protos, counts, collective_id
):
    count, dp_count = counts
    model, hidden = weights[0].shape
    width = weights[2].shape[0]
    rows = shards[0].shape[0]
    owned_k = protos[0].shape[0]
    images = counted.shape[0]
    everyone = count * dp_count
    span = max(f * rows % 128 + rows for f in range(count))
    span = (span + 127) // 128 * 128
    extent = max(f * rows // 128 * 128 + span for f in range(count))
    chunk = 1024
    cls = jnp.concatenate([cls_s[:4], cls_t[:4]])
    gains = jnp.concatenate(
        [
            jnp.broadcast_to(vecs[vecs.shape[0] + row][None], (4, model))
            for row in (-2, -1)
            for vecs in (vecs_s, vecs_t)
        ]
    )
    shape = jax.ShapeDtypeStruct
    vmem = pl.BlockSpec(memory_space=pltpu.VMEM)
    anywhere = pl.BlockSpec(memory_space=pl.ANY)
    extra_width = (model + hidden + 255) // 256 * 128
    sems = pltpu.SemaphoreType.DMA
    return pl.pallas_call(
        functools.partial(head_kernel, (count, dp_count, rows, chunk)),
        out_shape=[
            shape((8, model), F32),
            shape((8, model), F32),
            shape((1, images), F32),
            shape((count, owned_k // chunk, chunk), F32),
            shape((images, owned_k), BF16),
            shape((images, width), BF16),
            shape((rows, hidden), F32),
        ],
        in_specs=[vmem] * 11 + [anywhere] * 2,
        out_specs=[vmem] * 7,
        scratch_shapes=[
            pltpu.VMEM((owned_k, width), F32),
            pltpu.VMEM((owned_k, width), F32),
            sems((2,)),
            pltpu.VMEM((images, owned_k), F32),
            pltpu.VMEM((images, owned_k), F32),
            pltpu.VMEM((2 * span, hidden), BF16),
            pltpu.VMEM((8 * count, extent), F32),
            pltpu.VMEM((count, 16, hidden // 2), BF16),
            pltpu.VMEM((count, 16, hidden // 2), BF16),
            pltpu.VMEM((count, 16, hidden // 2), BF16),
            pltpu.VMEM((everyone, 16, width // 2), BF16),
            pltpu.VMEM((count, 8, 128), F32),
            pltpu.VMEM((everyone, 8, width), F32),
            pltpu.VMEM((count, 8, width), F32),
            pltpu.VMEM((count, 16, hidden // 2), BF16),
            pltpu.VMEM((count, 8, span), F32),
            pltpu.VMEM((count, 8, span), F32),
            pltpu.VMEM((count, 16, extra_width), BF16),
            pltpu.VMEM((count, 16, (hidden + width) // 2), BF16),
            pltpu.VMEM((dp_count, 4 * count, span), BF16),
            pltpu.VMEM((dp_count, 3, 4 * count, hidden), BF16),
            pltpu.VMEM((span, hidden), F32),
            sems((7, count - 1)),
            sems((7, count)),
            sems((everyone - 1,)),
            sems((everyone,)),
            sems((2, count)),
            sems((2, count)),
            sems((4, dp_count - 1)),
            sems((4, dp_count)),
        ],
        compiler_params=pltpu.CompilerParams(
            collective_id=collective_id, has_side_effects=True, vmem_limit_bytes=60 << 20
        ),
        name="head_step",
    )(
        cls, gains, *weights, *shards, centre[None], counted[None], counted[:, None], *protos
    )


def dot(left, right, dims):
    return lax.dot_general(left, right, (dims, ((), ())), preferred_element_type=F32)


def layer_norm(x, gain, shift):
    centred = x - jnp.mean(x, -1, keepdims=True)
    spread = jnp.mean(centred * centred, -1, keepdims=True)
    return centred * lax.rsqrt(spread + 1e-06) * gain + shift


def gelu_slope(x):
    _, pull = jax.vjp(jax.nn.gelu, x)
    return pull(jnp.ones_like(x))[0]


def head_forward(cls, weight, vecs):
    width, hidden = cls.shape[1], weight.shape[1]
    low_n = layer_norm(cls, vecs[-2], vecs[-1]).astype(BF16)
    pre_a = jnp.dot(low_n, weight[:width], preferred_element_type=F32)
    low_a = jax.nn.gelu(pre_a).astype(BF16)
    pre_b = jnp.dot(low_a, weight[width : width + hidden], preferred_element_type=F32)
    low_b = jax.nn.gelu(pre_b).astype(BF16)
    raw = dot(low_b, weight[width + hidden :], ((1,), (1,)))
    return low_n, pre_a, low_a, pre_b, low_b, raw


def unit(raw):
    return raw * lax.rsqrt(jnp.sum(raw * raw, -1, keepdims=True) + 1e-06)


def adamw(weight, moment, second, gradient, factor, step_rate, weight_decay):
    clipped = gradient * factor
    moment = BETA_ONE * moment + (1.0 - BETA_ONE) * clipped
    second = BETA_TWO * second + (1.0 - BETA_TWO) * clipped * clipped
    direction = (
        moment / (1.0 - BETA_ONE**STEP) / (jnp.sqrt(second / (1.0 - BETA_TWO**STEP)) + 1e-08)
    )
    return (weight - step_rate * (direction + weight_decay * weight), moment, second)


def own_kernels(local, head_rows, model, hidden, total):
    count = lax.axis_size("fsdp")
    if lax.axis_size("dp") != 4 or count not in (4, 8) or local != 4 or head_rows % 16:
        return False
    for low, high in ((0, model), (hidden + model, total)):
        rows = (high - low) // count
        if rows % 16 or any((low + rows * f) % head_rows + rows > head_rows for f in range(count)):
            return False
    return True


def reduce_all(grads, own):
    if own:
        return reduce_rows(grads, lax.axis_size("fsdp"), 3, 2)
    owned = lax.psum_scatter(grads, "fsdp", scatter_dimension=0, tiled=True)
    return lax.psum(owned, "dp").astype(F32)


def head_plain(
    cls, teacher_cls, vectors, teacher_vectors, head_full, teacher_head_full, own_centre, counted,
    counted_total, w_proto, teacher_proto, own_rows,
):
    teacher_unit = unit(head_forward(teacher_cls, teacher_head_full, teacher_vectors)[-1])
    low_n, pre_a, low_a, pre_b, low_b, raw = head_forward(cls, head_full, vectors)
    bottleneck, pull_unit = jax.vjp(unit, raw)
    both = jnp.concatenate([teacher_unit.astype(BF16), bottleneck.astype(BF16)], -1)
    both = lax.all_gather(both, ("fsdp", "dp"), axis=0, tiled=True)
    width = raw.shape[1]
    teacher_rows, student_rows = both[:, :width], both[:, width:]

    low_proto = w_proto.astype(BF16)
    teacher_logits = dot(teacher_rows, teacher_proto.astype(BF16), ((1,), (1,)))
    logits = dot(student_rows, low_proto, ((1,), (1,)))
    scaled_t = (teacher_logits - own_centre) / TEACHER_TEMP
    scaled_s = logits / STUDENT_TEMP
    max_t = jnp.max(scaled_t, -1)
    max_s = jnp.max(scaled_s, -1)
    expo_t = jnp.exp(scaled_t - max_t[:, None])
    expo_s = jnp.exp(scaled_s - max_s[:, None])
    parts = jnp.stack(
        [
            max_t,
            jnp.sum(expo_t, -1),
            max_s,
            jnp.sum(expo_s, -1),
            jnp.sum(expo_t * (scaled_s - max_s[:, None]), -1),
        ]
    )
    parts = lax.all_gather(parts, "fsdp", axis=0)
    top_t = jnp.max(parts[:, 0], 0)
    lift_t = jnp.exp(parts[:, 0] - top_t)
    total_t = jnp.sum(parts[:, 1] * lift_t, 0)
    top_s = jnp.max(parts[:, 2], 0)
    total_s = jnp.sum(parts[:, 3] * jnp.exp(parts[:, 2] - top_s), 0)
    crossed = jnp.sum(lift_t * (parts[:, 4] + (parts[:, 2] - top_s) * parts[:, 1]), 0) / total_t
    losses = jnp.log(total_s) - crossed
    loss_total = jnp.sum(counted * losses)
    weighting = counted / counted_total / STUDENT_TEMP
    share_s = weighting * jnp.exp(max_s - top_s) / total_s
    share_t = weighting * jnp.exp(max_t - top_t) / total_t
    grad_logits = (expo_s * share_s[:, None] - expo_t * share_t[:, None]).astype(BF16)
    teacher_sum = jnp.sum(counted[:, None] * teacher_logits, 0)
    teacher_total = lax.all_gather(teacher_sum, "fsdp", axis=0, tiled=True)
    grad_proto = dot(grad_logits, student_rows, ((0,), (0,)))
    grad_rows = jnp.dot(grad_logits, low_proto, preferred_element_type=F32)
    dp_count = lax.axis_size("dp")
    grad_rows = grad_rows.reshape(-1, dp_count, cls.shape[0], width)
    grad_rows = lax.dynamic_index_in_dim(grad_rows, lax.axis_index("dp"), 1, keepdims=False)
    grad_bottleneck = lax.psum_scatter(grad_rows, "fsdp", scatter_dimension=0, tiled=False)

    model_width, hidden = cls.shape[1], head_full.shape[1]
    local = cls.shape[0]
    low_dz = pull_unit(grad_bottleneck)[0].astype(BF16)
    grad_b = jnp.dot(low_dz, head_full[model_width + hidden :], preferred_element_type=F32)
    low_db = (grad_b * gelu_slope(pre_b)).astype(BF16)
    grad_a = dot(low_db, head_full[model_width : model_width + hidden], ((1,), (1,)))
    low_da = (grad_a * gelu_slope(pre_a)).astype(BF16)
    grad_n = dot(low_da, head_full[:model_width], ((1,), (1,)))
    _, pull_norm = jax.vjp(layer_norm, cls, vectors[-2], vectors[-1])
    grad_cls, grad_gain, grad_shift = pull_norm(grad_n)

    packed = jnp.concatenate([low_n, low_a, low_dz, low_da, low_db, low_b], -1)
    packed = lax.all_gather(packed, ("fsdp", "dp"), axis=0, tiled=True)
    total_rows = model_width + hidden + width
    lefts, rights = packed[:, :total_rows], packed[:, total_rows:]
    start = lax.axis_index("fsdp") * own_rows
    left = lax.dynamic_slice_in_dim(lefts, start, own_rows, 1)
    row = start + lax.broadcasted_iota(jnp.int32, (1, own_rows), 1)
    kind = jnp.where(row < model_width, 0, jnp.where(row < model_width + hidden, 1, 2))
    left = jnp.concatenate([jnp.where(kind == index, left, 0) for index in range(3)], 0)
    right = jnp.concatenate(
        [rights[:, index * hidden : (index + 1) * hidden] for index in range(3)], 0
    )
    grad_head = dot(left, right, ((0,), (0,)))
    ends = jnp.stack([grad_gain, grad_shift])
    return grad_cls, ends, loss_total, teacher_total, grad_proto, grad_head


def per_device(
    patches,
    patch_mask,
    image_valid,
    centre,
    w_patch,
    first_patch,
    second_patch,
    teacher_patch,
    w_layer,
    first_layer,
    second_layer,
    teacher_layer,
    w_head,
    first_head,
    second_head,
    teacher_head,
    w_proto,
    first_proto,
    second_proto,
    teacher_proto,
    vectors,
    first_vectors,
    second_vectors,
    teacher_vectors,
):
    everyone = ("fsdp", "dp")
    local = patches.shape[0]
    place = lax.axis_index(everyone) * local
    fsdp_index = lax.axis_index("fsdp")
    counted = image_valid.astype(F32)
    counted_total = jnp.maximum(jnp.sum(counted), 1.0)
    covered = patch_mask.astype(F32)
    pixels = w_patch.shape[1]
    model_width, columns = w_layer.shape[1] * lax.axis_size("fsdp"), w_layer.shape[2]
    pad = packed_width_p(pixels) - pixels

    def low_blocks(patch, layers):
        patch = jnp.pad(patch, ((0, 0), (0, pad)))
        return [array.astype(BF16) for array in (patch, layers[0], layers[1])]

    head_s, head_t = w_head.astype(BF16), teacher_head.astype(BF16)
    blocks = low_blocks(teacher_patch, teacher_layer) + low_blocks(w_patch, w_layer)
    hidden = w_head.shape[1]
    fsdp_count = lax.axis_size("fsdp")
    own_rows, own_k = w_head.shape[0], w_proto.shape[0]
    total_rows = own_rows * fsdp_count
    own = own_kernels(local, own_rows, model_width, hidden, total_rows)
    if own:
        ranges = ((0, model_width), (model_width + hidden, total_rows))
        full = gather_rows(blocks, (head_s, head_t), ranges, fsdp_count, 1)
    else:
        full = [
            lax.all_gather(block, "fsdp", axis=0, tiled=True)
            for block in blocks + [head_s, head_t]
        ]
    teacher_patch_full, teacher_0, teacher_1, patch_full, layer_0, layer_1 = full[:6]

    teacher_rows = forward(
        patches, jnp.zeros_like(covered), teacher_patch_full, teacher_0, teacher_1,
        teacher_vectors, False,
    )[0]
    cls_rows, *saved = forward(patches, covered, patch_full, layer_0, layer_1, vectors, True)
    own_centre = lax.dynamic_slice_in_dim(centre, fsdp_index * own_k, own_k)
    if own:
        grad_cls, ends, loss_row, totals, grad_logits, unit_rows, grad_head = head_step(
            cls_rows, teacher_rows, vectors, teacher_vectors, full[6:], (head_s, head_t),
            own_centre, counted, (w_proto, teacher_proto), (fsdp_count, lax.axis_size("dp")), 3,
        )
        ends = ends[:2]
        loss_total = jnp.sum(loss_row)
        teacher_total = totals.reshape(-1)
        grad_proto = dot(grad_logits, unit_rows, ((0,), (0,)))
    else:
        grad_cls, ends, loss_total, teacher_total, grad_proto, grad_head = head_plain(
            cls_rows[:local], teacher_rows[:local], vectors, teacher_vectors, full[6], full[7],
            own_centre, counted, counted_total, w_proto, teacher_proto, own_rows,
        )
    grad_rows = jnp.pad(grad_cls, ((0, TAIL - grad_cls.shape[0]), (0, 0)))
    packed_grads = backward(
        patches, covered, patch_full, layer_0, layer_1, vectors, ends, grad_rows, saved
    )
    owned = reduce_all(packed_grads, own)
    base = packed_width_p(pixels)
    own_patch = owned[:, :pixels]
    own_layers = jnp.stack(
        [owned[:, base : base + columns], owned[:, base + columns : base + 2 * columns]]
    )
    own_rows_grad = owned[:, base + 2 * columns : base + 2 * columns + model_width]
    vector_grad = lax.all_gather(own_rows_grad, "fsdp", axis=0, tiled=True)[: vectors.shape[0]]
    owned_grads = (own_patch, own_layers, grad_head, grad_proto)
    owned_squares = sum((jnp.sum(gradient * gradient) for gradient in owned_grads))
    squares = lax.psum(owned_squares + jnp.sum(own_rows_grad * own_rows_grad), "fsdp")
    norm_value = jnp.sqrt(squares)
    factor = CLIP_NORM / jnp.maximum(norm_value, CLIP_NORM)
    updated_centre = CENTRE_KEEP * centre + (1.0 - CENTRE_KEEP) * teacher_total / counted_total
    weights_owned = (w_patch, w_layer, w_head, w_proto, vectors)
    moments = (first_patch, first_layer, first_head, first_proto, first_vectors)
    seconds = (second_patch, second_layer, second_head, second_proto, second_vectors)
    teachers = (teacher_patch, teacher_layer, teacher_head, teacher_proto, teacher_vectors)
    gradients = owned_grads + (vector_grad,)
    results = [loss_total, counted_total, norm_value, updated_centre]
    for group in range(5):
        updated, moment, second = adamw(
            weights_owned[group],
            moments[group],
            seconds[group],
            gradients[group],
            factor,
            RATES[group],
            DECAYS[group],
        )
        results.extend(
            [
                updated,
                moment,
                second,
                TEACHER_KEEP * teachers[group] + (1.0 - TEACHER_KEEP) * updated,
            ]
        )
    return tuple(results)


def solution(mesh):
    whole, rows, middle = P(), P("fsdp", None), P(None, "fsdp", None)
    in_specs = (
        (P(("fsdp", "dp"), None, None), P(("fsdp", "dp"), None), whole, whole)
        + (rows,) * 4
        + (middle,) * 4
        + (rows,) * 8
        + (whole,) * 4
    )
    out_specs = (whole,) * 4 + (rows,) * 4 + (middle,) * 4 + (rows,) * 8 + (whole,) * 4
    return jax.shard_map(
        per_device, mesh=mesh, in_specs=in_specs, out_specs=out_specs, check_vma=False
    )
```

```python
import functools

import jax
import jax.numpy as jnp
from jax import lax
from jax.experimental import pallas as pl
from jax.experimental.pallas import tpu as pltpu
from jax.sharding import PartitionSpec as P

HEADS = 6
STEP = 10
STUDENT_TEMP = 0.1
TEACHER_TEMP = 0.07
CENTRE_KEEP = 0.9
TEACHER_KEEP = 0.8
BETA_ONE = 0.9
BETA_TWO = 0.999
CLIP_NORM = 0.01
RATES = (0.1, 0.15, 0.07, 0.5, 0.5)
DECAYS = (0.04, 0.04, 0.04, 0.04, 0.0)
F32 = jnp.float32
BF16 = jnp.bfloat16
MESH = pl.DeviceIdType.MESH


def third_ranges(width, start):
    tiles = width // 128
    sizes = [(tiles + 2 - part) // 3 * 128 for part in range(3)]
    spans, at = [], start
    for size in sizes:
        spans.append((at, size))
        at += size
    return spans


def gather_kernel(items, early, lines, sources, heads, targets, between, send, recv, copied, send_e, recv_e):
    fsdp, dp = lax.axis_index("fsdp"), lax.axis_index("dp")
    z, x = fsdp // 2, fsdp % 2
    y, core = dp // 2, dp % 2
    across = z * 2 + 1 - x
    mate = y * 2 + 1 - core
    opposite = (1 - y) * 2 + core

    barrier = pltpu.get_barrier_semaphore()

    def greet(f, d):
        pl.semaphore_signal(barrier, 1, device_id=(f, d), device_id_type=pl.DeviceIdType.MESH)

    def when(condition, body):
        pl.when(condition)(body)

    for step in range(1, 2 * lines):
        greet(lax.rem(fsdp + step, 2 * lines), dp)
    greet(fsdp, mate)
    when(core == 0, lambda: greet(fsdp, opposite))
    pl.semaphore_wait(barrier, 2 * lines + 1 - core)

    hops = lines - 1
    UP, DOWN, ACROSS, OPPOSITE, MATE = 0, hops, 2 * hops, 4 * hops + 1, 4 * hops + 2

    def roles(body):
        when((core == 0) & (y == 0), lambda: body(0))
        when(core == 1, lambda: body(1))
        when((core == 0) & (y == 1), lambda: body(2))

    def region(index, part, f):
        number, rows, spans = items[index]
        at, size = spans[part]
        return targets[number].at[pl.ds(pl.multiple_of(f * rows, rows), rows), pl.ds(at, size)]

    def whole(index, part):
        number, rows, spans = items[index]
        at, size = spans[part]
        return targets[number].at[:, pl.ds(at, size)]

    def own(index, part):
        number, rows, spans = items[index]
        at, size = spans[part]
        return sources[number].at[:, pl.ds(at, size)]

    def move(index, slot, source, target, f, d):
        return pltpu.make_async_remote_copy(
            src_ref=source,
            dst_ref=target,
            send_sem=send.at[index, slot],
            recv_sem=recv.at[index, slot],
            device_id=(f, d),
            device_id_type=pl.DeviceIdType.MESH,
        )

    def piece(index, part, slot, f_source, f_target, mine=False):
        target = region(index, part, f_source)
        return move(index, slot, own(index, part) if mine else target, target, f_target, dp)

    def keep(index, part):
        return pltpu.make_async_copy(own(index, part), region(index, part, fsdp), copied.at[index])

    def z_steps(index, part, hop, act):
        mine = hop == 0
        if hop < hops:
            when(
                (z - hop >= 0) & (z + 1 < lines),
                lambda: act(piece(index, part, UP + hop, fsdp - 2 * hop, fsdp + 2, mine)),
            )
            when(
                (z + hop < lines) & (z > 0),
                lambda: act(piece(index, part, DOWN + hop, fsdp + 2 * hop, fsdp - 2, mine)),
            )

    def x_steps(index, part, hop, act):
        if hop == 0:
            act(piece(index, part, ACROSS, fsdp, across, True))
        else:
            when(
                z - hop >= 0,
                lambda: act(piece(index, part, ACROSS + hop, fsdp - 2 * hop, across)),
            )
            when(
                z + hop < lines,
                lambda: act(piece(index, part, ACROSS + hops + hop, fsdp + 2 * hop, across)),
            )

    def z_arrive(index, part, hop):
        when(
            z - hop >= 0,
            lambda: piece(index, part, UP + hop - 1, fsdp - 2 * hop, fsdp).wait_recv(),
        )
        when(
            z + hop < lines,
            lambda: piece(index, part, DOWN + hop - 1, fsdp + 2 * hop, fsdp).wait_recv(),
        )

    def x_arrive(index, part):
        piece(index, part, ACROSS, across, across).wait_recv()
        for hop in range(1, lines):
            when(
                z - hop >= 0,
                lambda hop=hop: piece(
                    index, part, ACROSS + hop, across - 2 * hop, across
                ).wait_recv(),
            )
            when(
                z + hop < lines,
                lambda hop=hop: piece(
                    index, part, ACROSS + hops + hop, across + 2 * hop, across
                ).wait_recv(),
            )

    def to_opposite(index, part):
        return move(index, OPPOSITE, whole(index, part), whole(index, part), fsdp, opposite)

    def to_mate(index, part, second=0):
        return move(index, MATE + second, whole(index, part), whole(index, part), fsdp, mate)

    def deal(part, act):
        for index, (number, places) in early.items():
            _, rows, spans = items[index]
            at, size = spans[part]
            target = sources[items[index][0]].at[:, pl.ds(at, size)]
            for f, (owner, start) in enumerate(places):
                source = heads[number].at[pl.ds(start, rows), pl.ds(at, size)]
                act(index, f, owner, source, target)

    def early_copy(index, f, source, target):
        return pltpu.make_async_remote_copy(
            src_ref=source,
            dst_ref=target,
            send_sem=send_e.at[index, f],
            recv_sem=recv_e.at[index],
            device_id=(f, dp),
            device_id_type=pl.DeviceIdType.MESH,
        )

    def deal_start(index, f, owner, source, target):
        if f == owner:
            when(
                fsdp == f,
                lambda: pltpu.make_async_copy(source, target, recv_e.at[index]).start(),
            )
        else:
            when(fsdp == owner, lambda: early_copy(index, f, source, target).start())

    def deal_end(index, f, owner, source, target):
        if f != owner:
            when(fsdp == owner, lambda: early_copy(index, f, source, target).wait_send())

    def dealt(index, part):
        _, rows, spans = items[index]
        at, size = spans[part]
        number, places = early[index]
        target = sources[items[index][0]].at[:, pl.ds(at, size)]
        for f, (owner, start) in enumerate(places):
            source = heads[number].at[pl.ds(start, rows), pl.ds(at, size)]
            if f == owner:
                when(
                    fsdp == f,
                    lambda source=source: pltpu.make_async_copy(
                        source, target, recv_e.at[index]
                    ).wait(),
                )
            else:
                when(
                    fsdp == f,
                    lambda f=f, source=source: early_copy(index, f, source, target).wait_recv(),
                )

    def stage(index, part, step):
        if step == 0:
            if index in early:
                dealt(index, part)
            keep(index, part).start()
            z_steps(index, part, 0, lambda copy: copy.start())
            x_steps(index, part, 0, lambda copy: copy.start())
        elif step < lines:
            z_arrive(index, part, step)
            z_steps(index, part, step, lambda copy: copy.start())
            x_steps(index, part, step, lambda copy: copy.start())
        elif step == lines:
            keep(index, part).wait()
            x_arrive(index, part)
            if part != 1:
                to_opposite(index, part).start()
            to_mate(index, part).start()
        elif step == lines + 1:
            if part != 1:
                to_opposite(index, 2 - part).wait_recv()
                to_mate(index, 2 - part, 1).start()
        else:
            if part != 1:
                to_mate(index, 1).wait_recv()
            else:
                when(y == 0, lambda: to_mate(index, 0).wait_recv())
                when(y == 0, lambda: to_mate(index, 2, 1).wait_recv())
                when(y == 1, lambda: to_mate(index, 2).wait_recv())
                when(y == 1, lambda: to_mate(index, 0, 1).wait_recv())

    steps = lines + 3

    def run(tick, part):
        for step in range(steps):
            if 0 <= tick - step < len(items):
                stage(tick - step, part, step)

    def close(part):
        for index in range(len(items)):
            for hop in range(lines):
                z_steps(index, part, hop, lambda copy: copy.wait_send())
                x_steps(index, part, hop, lambda copy: copy.wait_send())
            if part != 1:
                to_opposite(index, part).wait_send()
                to_mate(index, 2 - part, 1).wait_send()
            to_mate(index, part).wait_send()
        deal(part, deal_end)

    roles(lambda part: deal(part, deal_start))
    for tick in range(len(items) + steps - 1):
        roles(functools.partial(run, tick))
        between(tick - steps + 1)
    roles(close)


def gather_forward(
    arrays, heads, ranges, fsdp_count, patches, covered, vecs, teacher_vecs, collective_id
):
    lines = fsdp_count // 2
    head_rows, head_width = heads[0].shape
    shapes = [array.shape for array in arrays]
    items = [(number, shape[0], third_ranges(shape[1], 0)) for number, shape in enumerate(shapes)]
    early = {}
    count = len(arrays)
    for low, high in ranges:
        for number in range(len(heads)):
            rows = (high - low) // fsdp_count
            starts = [low + rows * f for f in range(fsdp_count)]
            early[len(items)] = (
                number,
                [(start // head_rows, start % head_rows) for start in starts],
            )
            shapes.append((rows, head_width))
            items.append((len(shapes) - 1, rows, third_ranges(head_width, 0)))
    slots = 4 * (lines - 1) + 4
    extra = len(shapes) - count
    full = [(fsdp_count * r, c) for r, c in shapes]
    images, pixel_rows, pixels = patches.shape
    model, columns = full[1]
    hidden = (columns - 4 * model) // 2
    tables = split_table(teacher_vecs, pixel_rows) + split_table(vecs, pixel_rows)
    per_image = saved_shapes(pixel_rows + TAIL, model)
    saved = len(per_image)

    def kernel(*refs):
        refs = list(refs)

        def take(number):
            taken = refs[:number]
            del refs[:number]
            return taken

        sources, head_refs = take(count), take(len(heads))
        patches_ref, covered_ref = take(2)
        table_refs = take(4)
        targets, dealt = take(len(shapes)), take(extra)
        cls_t, cls_s, x1c_out, o1_out = take(4)
        saved_out = take(saved)
        weights, kept = take(6), take(saved)
        cls_x, cls_o, load_sem, save_sem = take(4)

        def load(number):
            return pltpu.make_async_copy(targets[number], weights[number], load_sem.at[number])

        def save(number, image):
            return pltpu.make_async_copy(
                kept[number].at[image], saved_out[number].at[image], save_sem.at[number, image]
            )

        def run_image(net, image):
            places, rows = table_refs[2 * net : 2 * net + 2]
            values = image_forward(
                patches_ref[image],
                covered_ref[image] if net else None,
                weights[3 * net : 3 * net + 3],
                places,
                rows,
                hidden,
            )
            for number in range(saved if net else 0):
                kept[number][image] = values[number]
                save(number, image).start()
            x2, mixture = values[2], values[-1]
            cls_x[net, image : image + 1, :] = x2[pixel_rows : pixel_rows + 1, :]
            cls_o[net, image : image + 1, :] = mixture[:1, :].astype(F32)

        def run_class(net):
            out, x1c, mixed = class_forward(
                cls_x[net], cls_o[net], weights[3 * net + 2], table_refs[2 * net + 1], hidden
            )
            if net:
                cls_s[...] = out
                x1c_out[...] = x1c
                o1_out[...] = mixed
            else:
                cls_t[...] = out

        after = {item: [] for item in range(-lines - 3, len(items))}
        last = len(items) - 1
        for net in range(2):
            for image in range(images):
                at = min(3 * net + 2 + image + (net * max(0, images - 3)), last)
                after[at].append(functools.partial(run_image, net, image))
            after[at].append(functools.partial(run_class, net))

        def between(item):
            if item == -1:
                cls_x[...] = jnp.zeros_like(cls_x)
                cls_o[...] = jnp.zeros_like(cls_o)
            if 0 <= item < 6:
                load(item).start()
            if item in (2, 5):
                for number in range(item - 2, item + 1):
                    load(number).wait()
            for work in after[item]:
                work()

        gather_kernel(
            items, early, lines, sources + dealt, head_refs, targets, between, *refs
        )
        for number in range(saved):
            for image in range(images):
                save(number, image).wait()

    anywhere = pl.BlockSpec(memory_space=pl.ANY)
    vmem = pl.BlockSpec(memory_space=pltpu.VMEM)
    shape = jax.ShapeDtypeStruct
    sems = pltpu.SemaphoreType.DMA
    out = pl.pallas_call(
        kernel,
        out_shape=[shape(dims, BF16) for dims in full]
        + [shape(dims, BF16) for dims in shapes[count:]]
        + [shape((TAIL, model), kind) for kind in (F32, F32, F32, BF16)]
        + [shape((images,) + dims, kind) for dims, kind in per_image],
        in_specs=[anywhere] * (count + len(heads)) + [vmem] * 6,
        out_specs=[anywhere] * (len(shapes) + extra) + [vmem] * 4 + [anywhere] * saved,
        scratch_shapes=[pltpu.VMEM(dims, BF16) for dims in full[:6]]
        + [pltpu.VMEM((images,) + dims, kind) for dims, kind in per_image]
        + [pltpu.VMEM((2, TAIL, model), F32)] * 2
        + [
            sems((6,)),
            sems((saved, images)),
            sems((len(items), slots)),
            sems((len(items), slots)),
            sems((len(items),)),
            sems((len(items), fsdp_count)),
            sems((len(items),)),
        ],
        compiler_params=pltpu.CompilerParams(
            collective_id=collective_id, has_side_effects=True, vmem_limit_bytes=60 << 20
        ),
        name="gather_forward",
    )(*arrays, *heads, patches, covered[..., None], *tables)
    at = len(shapes) + extra
    cls_t, cls_s, x1c, o1 = out[at : at + 4]
    return out[: len(shapes)], cls_t, cls_s, list(out[at + 4 :]) + [x1c, o1]


def reduce_kernel(
    cuts, lines, places, grads, squares, patch_out, layers_out, vectors_out, norm_out, mate_a, mate_b, facing, side, sums, up_out, up_in, down_out, down_in,
    ending, ended, result, vectors, norms, send, recv, send_f, recv_f
):
    fsdp, dp = lax.axis_index("fsdp"), lax.axis_index("dp")
    z, x = fsdp // 2, fsdp % 2
    y, core = dp // 2, dp % 2
    across = z * 2 + 1 - x
    mate = y * 2 + 1 - core
    opposite = (1 - y) * 2 + core
    size = mate_a.shape[-1]
    lone = core == 1
    part = jnp.where(lone, 1, 2 * y)
    mate_part = jnp.where(lone, 2 * y, 1)

    barrier = pltpu.get_barrier_semaphore()

    def greet(f, d):
        pl.semaphore_signal(barrier, 1, device_id=(f, d), device_id_type=MESH)

    count = 2 * lines
    for step in range(1, count):
        greet(lax.rem(fsdp + step, count), dp)
    greet(fsdp, mate)
    greet(fsdp, opposite)
    pl.semaphore_wait(barrier, count + 1)

    MATE_A, MATE_B, FACING, ACROSS, UP, DOWN, ENDING, LAST_MATE, LAST_SECOND, LAST_FACING = range(10)

    def move(cut, slot, source, target, f, d):
        return pltpu.make_async_remote_copy(
            src_ref=source,
            dst_ref=target,
            send_sem=send.at[cut, slot],
            recv_sem=recv.at[cut, slot],
            device_id=(f, d),
            device_id_type=MESH,
        )

    def columns(cut, which):
        return pl.ds(pl.multiple_of((3 * cut + which) * size, 128), size)

    def mine(cut, which):
        return grads[:, :, :, columns(cut, which)].astype(F32)

    def to_mate_a(cut):
        return move(cut, MATE_A, grads.at[:, :, :, columns(cut, mate_part)], mate_a.at[cut], fsdp, mate)

    def to_mate_b(cut):
        return move(
            cut, MATE_B, grads.at[:, :, :, columns(cut, 2 - mate_part)], mate_b.at[cut], fsdp, mate
        )

    def to_facing(cut):
        return move(cut, FACING, mate_b.at[cut], facing.at[cut], fsdp, opposite)

    def to_across(cut):
        return move(cut, ACROSS, mate_a.at[cut, :, 1 - x], side.at[cut], across, dp)

    def going_up(cut, count):
        blocks = pl.ds(0, count)
        return move(cut, UP, up_out.at[cut, blocks], up_in.at[cut, blocks], fsdp + 2, dp)

    def going_down(cut, count):
        blocks = pl.ds(0, count)
        return move(cut, DOWN, down_out.at[cut, blocks], down_in.at[cut, blocks], fsdp - 2, dp)

    def to_ending(cut):
        return move(cut, ENDING, ending.at[cut], ended.at[cut], fsdp, opposite)

    def last(cut, slot, which, d):
        place = result.at[:, columns(cut, which)]
        return move(cut, slot, place, place, fsdp, d)

    def step_0(cut):
        to_mate_a(cut).start()
        pl.when(lone)(lambda: to_mate_b(cut).start())

    def step_1(cut):
        @pl.when(jnp.logical_not(lone))
        def _():
            to_mate_b(cut).wait_recv()
            mate_b[cut] = (mine(cut, 2 - part) + mate_b[cut].astype(F32)).astype(BF16)
            to_facing(cut).start()

    def step_2(cut):
        to_mate_a(cut).wait_recv()

        @pl.when(lone)
        def _():
            mate_a[cut] = (mine(cut, 1) + mate_a[cut].astype(F32)).astype(BF16)

        @pl.when(jnp.logical_not(lone))
        def _():
            to_facing(cut).wait_recv()
            both = mine(cut, part) + mate_a[cut].astype(F32) + facing[cut].astype(F32)
            mate_a[cut] = both.astype(BF16)

        to_across(cut).start()

    def step_3(cut):
        to_across(cut).wait_recv()
        sums[cut] = mate_a[cut, :, x].astype(F32) + side[cut].astype(F32)

    def lift(cut, hop):
        at = hop - 1

        @pl.when(z == at)
        def _():
            count = lines - hop
            if at > 0:
                going_up(cut, count + 1).wait_recv()
            for ahead in range(1, count + 1):
                value = sums[cut, at + ahead]
                if at > 0:
                    value = value + up_in[cut, ahead].astype(F32)
                up_out[cut, ahead - 1] = value.astype(BF16)
            going_up(cut, count).start()

        low = lines - hop

        @pl.when(z == low)
        def _():
            count = lines - hop
            if low < lines - 1:
                going_down(cut, count + 1).wait_recv()
            for ahead in range(1, count + 1):
                value = sums[cut, low - ahead]
                if low < lines - 1:
                    value = value + down_in[cut, ahead].astype(F32)
                down_out[cut, ahead - 1] = value.astype(BF16)
            going_down(cut, count).start()

    def finish(cut):
        for at in range(lines):

            @pl.when(z == at)
            def _(at=at):
                value = sums[cut, at]
                if at == lines - 1:
                    going_up(cut, 1).wait_recv()
                if at == 0:
                    going_down(cut, 1).wait_recv()
                if at > 0:
                    value = value + up_in[cut, 0].astype(F32)
                if at < lines - 1:
                    value = value + down_in[cut, 0].astype(F32)
                ending[cut] = value.astype(BF16)

        pl.when(lone)(lambda: to_ending(cut).start())

        @pl.when(jnp.logical_not(lone))
        def _():
            result[:, columns(cut, part)] = ending[cut]
            last(cut, LAST_FACING, part, opposite).start()
            last(cut, LAST_MATE, part, mate).start()

    def share(cut):
        @pl.when(lone)
        def _():
            to_ending(cut).wait_recv()
            both = ending[cut].astype(F32) + ended[cut].astype(F32)
            result[:, columns(cut, part)] = both.astype(BF16)
            last(cut, LAST_MATE, part, mate).start()

        @pl.when(jnp.logical_not(lone))
        def _():
            last(cut, LAST_FACING, 2 - part, opposite).wait_recv()
            last(cut, LAST_SECOND, 2 - part, mate).start()

    def close(cut):
        last(cut, LAST_MATE, mate_part, mate).wait_recv()
        pl.when(lone)(lambda: last(cut, LAST_SECOND, 2 - mate_part, mate).wait_recv())

    steps = [step_0, step_1, step_2, step_3]
    steps += [functools.partial(lambda hop, cut: lift(cut, hop), hop) for hop in range(1, lines)]
    steps += [finish, share, close]
    for tick in range(cuts + len(steps) - 1):
        for number, step in enumerate(steps):
            if 0 <= tick - number < cuts:
                step(tick - number)

    cut_0, cut_1, cut_2, width = places
    vectors[fsdp] = result[:, cut_2 : cut_2 + width]
    total = squares[...]
    for at in range(0, result.shape[1], 128):
        value = result[:, at : at + 128].astype(F32)
        value = value * value
        for row in range(0, value.shape[0], 8):
            total = total + value[row : row + 8, :]
    norms[fsdp] = total

    def tell(kind, ref, step):
        return pltpu.make_async_remote_copy(
            src_ref=ref.at[fsdp],
            dst_ref=ref.at[fsdp],
            send_sem=send_f.at[kind, step - 1],
            recv_sem=recv_f.at[kind, fsdp],
            device_id=(lax.rem(fsdp + step, count), dp),
            device_id_type=MESH,
        )

    def told(kind, ref, step):
        peer = lax.rem(fsdp + step, count)
        return pltpu.make_async_remote_copy(
            src_ref=ref.at[peer],
            dst_ref=ref.at[peer],
            send_sem=send_f.at[kind, step - 1],
            recv_sem=recv_f.at[kind, peer],
            device_id=(peer, dp),
            device_id_type=MESH,
        )

    for kind, ref in enumerate((norms, vectors)):
        for step in range(1, count):
            tell(kind, ref, step).start()
    patch_out[...] = result[:, :cut_0].astype(F32)
    layers_out[0] = result[:, cut_0:cut_1].astype(F32)
    layers_out[1] = result[:, cut_1:cut_2].astype(F32)
    for kind, ref in enumerate((norms, vectors)):
        for step in range(1, count):
            told(kind, ref, step).wait_recv()
    vectors_out[...] = vectors[...].astype(F32)
    total = norms[0]
    for f in range(1, count):
        total = total + norms[f]
    norm_out[...] = total
    for kind, ref in enumerate((norms, vectors)):
        for step in range(1, count):
            tell(kind, ref, step).wait_send()
    for cut in range(cuts):
        to_mate_a(cut).wait_send()
        to_across(cut).wait_send()
        for hop in range(1, lines):
            pl.when(z == hop - 1)(lambda hop=hop: going_up(cut, lines - hop).wait_send())
            pl.when(z == lines - hop)(lambda hop=hop: going_down(cut, lines - hop).wait_send())
        last(cut, LAST_MATE, part, mate).wait_send()

        @pl.when(lone)
        def _():
            to_mate_b(cut).wait_send()
            to_ending(cut).wait_send()

        @pl.when(jnp.logical_not(lone))
        def _():
            to_facing(cut).wait_send()
            last(cut, LAST_FACING, part, opposite).wait_send()
            last(cut, LAST_SECOND, 2 - part, mate).wait_send()


def reduce_rows(grads, squares, places, fsdp_count, cuts, collective_id):
    total, width = grads.shape
    lines, rows = fsdp_count // 2, total // fsdp_count
    size = width // (3 * cuts)
    blocks = (cuts, lines, 2, rows, size)
    cut_0, cut_1, cut_2, table = places
    shape = jax.ShapeDtypeStruct
    sems = pltpu.SemaphoreType.DMA
    return pl.pallas_call(
        functools.partial(reduce_kernel, cuts, lines, places),
        out_shape=[
            shape((rows, cut_0), F32),
            shape((2, rows, cut_1 - cut_0), F32),
            shape((fsdp_count, rows, table), F32),
            shape((8, 128), F32),
        ],
        in_specs=[pl.BlockSpec(memory_space=pltpu.VMEM)] * 2,
        out_specs=[pl.BlockSpec(memory_space=pltpu.VMEM)] * 4,
        scratch_shapes=[
            pltpu.VMEM(blocks, BF16),
            pltpu.VMEM(blocks, BF16),
            pltpu.VMEM(blocks, BF16),
            pltpu.VMEM((cuts, lines, rows, size), BF16),
            pltpu.VMEM((cuts, lines, rows, size), F32),
        ]
        + [pltpu.VMEM((cuts, lines - 1, rows, size), BF16)] * 4
        + [pltpu.VMEM((cuts, rows, size), BF16)] * 2
        + [
            pltpu.VMEM((rows, width), BF16),
            pltpu.VMEM((fsdp_count, rows, table), BF16),
            pltpu.VMEM((fsdp_count, 8, 128), F32),
            sems((cuts, 10)),
            sems((cuts, 10)),
            sems((2, fsdp_count - 1)),
            sems((2, fsdp_count)),
        ],
        compiler_params=pltpu.CompilerParams(
            collective_id=collective_id, has_side_effects=True, vmem_limit_bytes=32 << 20
        ),
        name="reduce_rows",
    )(grads.reshape(lines, 2, rows, width), squares)


GELU_A = 0.7978845608028654
GELU_B = 0.044715
TAIL = 16


def mm(left, right):
    return lax.dot_general(left, right, (((1,), (0,)), ((), ())), preferred_element_type=F32)


def mm_nt(left, right):
    return lax.dot_general(left, right, (((1,), (1,)), ((), ())), preferred_element_type=F32)


def mm_tn(left, right):
    return lax.dot_general(left, right, (((0,), (0,)), ((), ())), preferred_element_type=F32)


def norm_parts(x):
    centred = x - jnp.mean(x, -1, keepdims=True)
    lift = lax.rsqrt(jnp.mean(centred * centred, -1, keepdims=True) + 1e-06)
    return centred * lift, lift


def norm_back(grad, gain, unit_x, lift):
    inner = grad * gain
    return lift * (
        inner
        - jnp.mean(inner, -1, keepdims=True)
        - unit_x * jnp.mean(inner * unit_x, -1, keepdims=True)
    )


def gelu(x):
    return 0.5 * x * (1.0 + jnp.tanh(GELU_A * (x + GELU_B * (x * x * x))))


def gelu_both(x):
    square = x * x
    slope = jnp.tanh(GELU_A * x * (1.0 + GELU_B * square))
    half = 0.5 * (1.0 + slope)
    turn = half + 0.5 * x * (1.0 - slope * slope) * GELU_A * (1.0 + 3.0 * GELU_B * square)
    return x * half, turn


def half_masks(width):
    lane = lax.broadcasted_iota(jnp.int32, (1, 128), 1)
    first = (lane < width).astype(F32)
    return first, 1.0 - first


def column_sum(x):
    return jnp.sum(x, 0, keepdims=True)


def attend(q, keys, values, valid, scale, lse_store):
    rows, total = q.shape[0], keys.shape[0]
    masks = half_masks(64)
    column = lax.broadcasted_iota(jnp.int32, (rows, total), 1)
    lane = lax.broadcasted_iota(jnp.int32, (rows, 128), 1)
    mixed, lse = [], jnp.zeros((rows, 128), F32)
    for pair in range(HEADS // 2):
        span = slice(128 * pair, 128 * pair + 128)
        halves = []
        for side in range(2):
            asked = q[:, span] * (masks[side] * scale).astype(BF16)
            scores = mm_nt(asked, keys[:, span])
            scores = jnp.where(column < valid, scores, -1e30)
            top = jnp.max(scores, -1, keepdims=True)
            expo = jnp.exp(scores - top)
            total_e = jnp.sum(expo, -1, keepdims=True)
            halves.append(mm(expo.astype(BF16), values[:, span]) / total_e)
            if lse_store:
                lse = jnp.where(lane == 2 * pair + side, top + jnp.log(total_e), lse)
        mixed.append(jnp.where(lane < 64, halves[0], halves[1]))
    return jnp.concatenate(mixed, -1).astype(BF16), lse


def image_forward(pixel_rows, hide, weights, places, rows_table, hidden):
    weight_p, weight_0, weight_1 = weights
    model = weight_0.shape[0]
    count, pixels = pixel_rows.shape
    valid = count + 1
    scale = (model // HEADS) ** -0.5
    keep = hide is not None

    def vec(row):
        return rows_table[row : row + 1, :]

    def row(layer, index):
        return vec(2 + 6 * layer + index)

    tokens = mm_nt(pixel_rows, weight_p[:, :pixels]) + vec(1)
    if keep:
        tokens = tokens * (1.0 - hide) + vec(0) * hide
    x = jnp.concatenate([tokens + places[:count, :], places[count:, :]], 0)
    unit_x, _ = norm_parts(x)
    low = (unit_x * row(0, 0) + row(0, 1)).astype(BF16)
    qkv = mm(low, weight_0[:, : 3 * model]).astype(BF16)
    mixture, lse = attend(
        qkv[:, :model], qkv[:, model : 2 * model], qkv[:, 2 * model :], valid, scale, keep
    )
    x1 = x + row(0, 2) * mm(mixture, weight_0[:, 3 * model : 4 * model])
    unit_x, _ = norm_parts(x1)
    low = (unit_x * row(0, 3) + row(0, 4)).astype(BF16)
    wide = gelu(mm(low, weight_0[:, 4 * model : 4 * model + hidden])).astype(BF16)
    x2 = x1 + row(0, 5) * mm_nt(wide, weight_0[:, 4 * model + hidden :])

    unit_x, _ = norm_parts(x2)
    low = (unit_x * row(1, 0) + row(1, 1)).astype(BF16)
    kv = mm(low, weight_1[:, model : 3 * model]).astype(BF16)
    q1 = mm(low[count:, :], weight_1[:, :model]).astype(BF16)
    mixture1, lse1 = attend(q1, kv[:, :model], kv[:, model:], valid, scale, keep)
    return x, x1, x2, qkv, mixture, lse, kv, q1, lse1, mixture1


def class_forward(cls_x, cls_o, weight_1, rows_table, hidden):
    model = weight_1.shape[0]

    def row(index):
        return rows_table[8 + index : 9 + index, :]

    mixed = cls_o.astype(BF16)
    x1c = cls_x + row(2) * mm(mixed, weight_1[:, 3 * model : 4 * model])
    unit_c, _ = norm_parts(x1c)
    low_c = (unit_c * row(3) + row(4)).astype(BF16)
    wide_c = gelu(mm(low_c, weight_1[:, 4 * model : 4 * model + hidden])).astype(BF16)
    return x1c + row(5) * mm_nt(wide_c, weight_1[:, 4 * model + hidden :]), x1c, mixed


def saved_shapes(total, model):
    return [
        ((total, model), F32),
        ((total, model), F32),
        ((total, model), F32),
        ((total, 3 * model), BF16),
        ((total, model), BF16),
        ((total, 128), F32),
        ((total, 2 * model), BF16),
        ((TAIL, model), BF16),
        ((TAIL, 128), F32),
    ]


def forward_kernel(
    images, hidden, keep, patches, covered, weight_p, weight_0, weight_1, places, rows_table, *rest
):
    outs, (cls_x, cls_o) = rest[:-2], rest[-2:]
    image = pl.program_id(0)
    count = patches.shape[1]

    @pl.when(image == 0)
    def _():
        cls_x[...] = jnp.zeros_like(cls_x)
        cls_o[...] = jnp.zeros_like(cls_o)

    values = image_forward(
        patches[0],
        covered[0] if keep else None,
        (weight_p, weight_0, weight_1),
        places,
        rows_table,
        hidden,
    )
    cls_x[pl.ds(image, 1), :] = values[2][count : count + 1, :]
    cls_o[pl.ds(image, 1), :] = values[-1][:1, :].astype(F32)
    if keep:
        for number, value in enumerate(values[:-1]):
            outs[1 + number][0] = value

    @pl.when(image == images - 1)
    def _():
        out, x1c, mixed = class_forward(cls_x[...], cls_o[...], weight_1, rows_table, hidden)
        outs[0][...] = out
        if keep:
            outs[-2][...] = x1c
            outs[-1][...] = mixed


def fixed(shape):
    zeros = (0,) * len(shape)
    return pl.BlockSpec(shape, lambda i: zeros, pipeline_mode=pl.Buffered(1))


def each(shape):
    rest = (0,) * len(shape)
    return pl.BlockSpec((1,) + shape, lambda i: (i,) + rest)


def whole_out(shape):
    zeros = (0,) * len(shape)
    return pl.BlockSpec(shape, lambda i: zeros)


def split_table(vecs, count):
    places = jnp.concatenate(
        [
            vecs[1 : count + 1],
            vecs[:1] + vecs[count + 1 : count + 2],
            jnp.zeros((TAIL - 1, vecs.shape[1]), F32),
        ]
    )
    rows = vecs[count + 2 :]
    rows = jnp.concatenate([rows, jnp.zeros(((-rows.shape[0]) % 8, rows.shape[1]), F32)])
    return places, rows


def forward(patches, covered, weight_p, weight_0, weight_1, vecs, keep):
    images, count, pixels = patches.shape
    model, columns = weight_0.shape
    hidden = (columns - 4 * model) // 2
    total = count + TAIL
    places, rows = split_table(vecs, count)
    shape = jax.ShapeDtypeStruct
    outs = [shape((TAIL, model), F32)]
    out_specs = [whole_out((TAIL, model))]
    if keep:
        per_image = saved_shapes(total, model)
        outs += [shape((images,) + dims, kind) for dims, kind in per_image]
        out_specs += [each(dims) for dims, kind in per_image]
        outs += [shape((TAIL, model), F32), shape((TAIL, model), BF16)]
        out_specs += [whole_out((TAIL, model))] * 2
    return pl.pallas_call(
        functools.partial(forward_kernel, images, hidden, keep),
        grid=(images,),
        out_shape=outs,
        in_specs=[
            each((count, pixels)),
            each((count, 1)),
            fixed(weight_p.shape),
            fixed(weight_0.shape),
            fixed(weight_1.shape),
            fixed(places.shape),
            fixed(rows.shape),
        ],
        out_specs=out_specs,
        scratch_shapes=[pltpu.VMEM((TAIL, model), F32)] * 2,
        compiler_params=pltpu.CompilerParams(vmem_limit_bytes=56 << 20),
        name="backbone_forward",
    )(patches, covered[..., None], weight_p, weight_0, weight_1, places, rows)


def attend_back(grad_o, q, keys, values, lse, valid, scale):
    rows, total = q.shape[0], keys.shape[0]
    masks = half_masks(64)
    column = lax.broadcasted_iota(jnp.int32, (rows, total), 1)
    lane_row = lax.broadcasted_iota(jnp.int32, (rows, 128), 1)
    grad_q, grad_k, grad_v = [], [], []
    for pair in range(HEADS // 2):
        span = slice(128 * pair, 128 * pair + 128)
        out_q, out_k, out_v = [], None, None
        for side in range(2):
            mask = masks[side].astype(BF16)
            asked = q[:, span] * (masks[side] * scale).astype(BF16)
            given = grad_o[:, span] * mask
            head = 2 * pair + side
            scores = mm_nt(asked, keys[:, span])
            share = jnp.where(column < valid, jnp.exp(scores - lse[:, head : head + 1]), 0.0)
            grad_p = mm_nt(given, values[:, span])
            inner = jnp.sum(share * grad_p, -1, keepdims=True)
            grad_s = (share * (grad_p - inner)).astype(BF16)
            out_q.append(mm(grad_s, keys[:, span]))
            more_k = mm_tn(grad_s, asked)
            more_v = mm_tn(share.astype(BF16), given)
            out_k = more_k if out_k is None else out_k + more_k
            out_v = more_v if out_v is None else out_v + more_v
        grad_q.append(jnp.where(lane_row < 64, out_q[0], out_q[1]) * scale)
        grad_k.append(out_k)
        grad_v.append(out_v)
    return [jnp.concatenate(part, -1).astype(BF16) for part in (grad_q, grad_k, grad_v)]


def backward_kernel(
    images, hidden, count_, patches, covered, weight_p, weight_0, weight_1, rows_table, ends, grad_cls,
    x0_in, x1_in, x2_in, qkv_in, o0_in, lse0_in, kv_in, q1_in, lse1_in, x1c_in, o1_in,
    packed, acc_p, acc_0, acc_kv, acc_q, grad_c, grad_oc, places, rows
):
    image = pl.program_id(0)
    model = weight_0.shape[0]
    count, pixels = patches.shape[1], patches.shape[2]
    valid = count + 1
    scale = (model // HEADS) ** -0.5
    base_0 = packed_width_p(pixels)
    columns = weight_0.shape[1]
    base_1 = base_0 + columns
    base_v = base_1 + columns
    cut_o, cut_u, cut_d = 3 * model, 4 * model, 4 * model + hidden

    def row(layer, index):
        at = 2 + 6 * layer + index
        return rows_table[at : at + 1, :]

    def add_row(layer, index, value):
        at = 2 + 6 * layer + index
        rows[at : at + 1, :] += value

    @pl.when(image == 0)
    def _():
        for ref in (acc_p, acc_0, acc_kv, acc_q, places, rows):
            ref[...] = jnp.zeros_like(ref)
        grad_x = grad_cls[...]
        x1c = x1c_in[...]
        unit_x, lift = norm_parts(x1c)
        low = (unit_x * row(1, 3) + row(1, 4)).astype(BF16)
        wide, slope = gelu_both(mm(low, weight_1[:, cut_u:cut_d]))
        wide = wide.astype(BF16)
        down = mm_nt(wide, weight_1[:, cut_d:])
        add_row(1, 5, column_sum(grad_x * down))
        grad_d = (grad_x * row(1, 5)).astype(BF16)
        grad_u = (mm(grad_d, weight_1[:, cut_d:]) * slope).astype(BF16)
        packed[:, base_1 + cut_d : base_v] = mm_tn(grad_d, wide).astype(BF16)
        packed[:, base_1 + cut_u : base_1 + cut_d] = mm_tn(low, grad_u).astype(BF16)
        grad_n = mm_nt(grad_u, weight_1[:, cut_u:cut_d])
        add_row(1, 3, column_sum(grad_n * unit_x))
        add_row(1, 4, column_sum(grad_n))
        grad_x = grad_x + norm_back(grad_n, row(1, 3), unit_x, lift)
        mixed = o1_in[...]
        add_row(1, 2, column_sum(grad_x * mm(mixed, weight_1[:, cut_o:cut_u])))
        grad_a = (grad_x * row(1, 2)).astype(BF16)
        packed[:, base_1 + cut_o : base_1 + cut_u] = mm_tn(mixed, grad_a).astype(BF16)
        grad_c[...] = grad_x
        grad_oc[...] = mm_nt(grad_a, weight_1[:, cut_o:cut_u])

    first_row = lax.broadcasted_iota(jnp.int32, (TAIL, 1), 0) == 0

    grad_o1 = jnp.where(first_row, grad_oc[pl.ds(image, 1), :], 0.0).astype(BF16)
    kv = kv_in[0]
    grad_q, grad_k, grad_v = attend_back(
        grad_o1, q1_in[0], kv[:, :model], kv[:, model:], lse1_in[0], valid, scale
    )
    unit_x, lift = norm_parts(x2_in[0])
    low = (unit_x * row(1, 0) + row(1, 1)).astype(BF16)
    grad_kv = jnp.concatenate([grad_k, grad_v], -1)
    acc_kv[...] += mm_tn(low, grad_kv)
    acc_q[...] += mm_tn(low[count:, :], grad_q)
    grad_n = mm_nt(grad_kv, weight_1[:, model : 3 * model])
    tail = grad_n[count:, :] + mm_nt(grad_q, weight_1[:, :model])
    grad_n = jnp.concatenate([grad_n[:count, :], tail], 0)
    add_row(1, 0, column_sum(grad_n * unit_x))
    add_row(1, 1, column_sum(grad_n))
    grad_x = norm_back(grad_n, row(1, 0), unit_x, lift)
    tail = grad_x[count:, :] + jnp.where(first_row, grad_c[pl.ds(image, 1), :], 0.0)
    grad_x = jnp.concatenate([grad_x[:count, :], tail], 0)

    unit_x, lift = norm_parts(x1_in[0])
    low = (unit_x * row(0, 3) + row(0, 4)).astype(BF16)
    wide, slope = gelu_both(mm(low, weight_0[:, cut_u:cut_d]))
    wide = wide.astype(BF16)
    down = mm_nt(wide, weight_0[:, cut_d:])
    add_row(0, 5, column_sum(grad_x * down))
    grad_d = (grad_x * row(0, 5)).astype(BF16)
    grad_u = (mm(grad_d, weight_0[:, cut_d:]) * slope).astype(BF16)
    acc_0[:, cut_d:] += mm_tn(grad_d, wide)
    acc_0[:, cut_u:cut_d] += mm_tn(low, grad_u)
    grad_n = mm_nt(grad_u, weight_0[:, cut_u:cut_d])
    add_row(0, 3, column_sum(grad_n * unit_x))
    add_row(0, 4, column_sum(grad_n))
    grad_x = grad_x + norm_back(grad_n, row(0, 3), unit_x, lift)
    mixed = o0_in[0]
    add_row(0, 2, column_sum(grad_x * mm(mixed, weight_0[:, cut_o:cut_u])))
    grad_a = (grad_x * row(0, 2)).astype(BF16)
    acc_0[:, cut_o:cut_u] += mm_tn(mixed, grad_a)
    grad_o = mm_nt(grad_a, weight_0[:, cut_o:cut_u]).astype(BF16)
    qkv = qkv_in[0]
    grad_qkv = jnp.concatenate(
        attend_back(
            grad_o, qkv[:, :model], qkv[:, model : 2 * model], qkv[:, 2 * model :], lse0_in[0],
            valid, scale,
        ),
        -1,
    )
    unit_x, lift = norm_parts(x0_in[0])
    low = (unit_x * row(0, 0) + row(0, 1)).astype(BF16)
    acc_0[:, :cut_o] += mm_tn(low, grad_qkv)
    grad_n = mm_nt(grad_qkv, weight_0[:, :cut_o])
    add_row(0, 0, column_sum(grad_n * unit_x))
    add_row(0, 1, column_sum(grad_n))
    grad_x = grad_x + norm_back(grad_n, row(0, 0), unit_x, lift)

    places[...] += grad_x
    hide = covered[0]
    token = grad_x[:count, :]
    rows[0:1, :] += column_sum(token * hide)
    token = token * (1.0 - hide)
    rows[1:2, :] += column_sum(token)
    acc_p[...] += mm_tn(token.astype(BF16), patches[0])

    @pl.when(image == images - 1)
    def _():
        packed[:, :base_0] = jnp.concatenate(
            [acc_p[...], jnp.zeros((model, base_0 - pixels), F32)], -1
        ).astype(BF16)
        packed[:, base_0:base_1] = acc_0[...].astype(BF16)
        packed[:, base_1 : base_1 + model] = acc_q[...].astype(BF16)
        packed[:, base_1 + model : base_1 + cut_o] = acc_kv[...].astype(BF16)
        used = rows_table.shape[0]
        table = jnp.concatenate(
            [
                places[count : count + 1, :],
                places[:count, :],
                places[count : count + 1, :],
                rows[...] + ends[...],
            ],
            0,
        )
        table = jnp.concatenate(
            [table, jnp.zeros((model - table.shape[0], model), F32)], 0
        )
        packed[:, base_v : base_v + model] = table.astype(BF16)
        spare = packed.shape[1] - base_v - model
        if spare:
            packed[:, base_v + model :] = jnp.zeros((model, spare), BF16)


def packed_width_p(pixels):
    return (pixels + 127) // 128 * 128


def packed_width(pixels, columns, model):
    width = packed_width_p(pixels) + 2 * columns + model
    return (width + 3455) // 3456 * 3456


def backward(patches, covered, weight_p, weight_0, weight_1, vecs, ends, grad_cls, saved):
    images, count, pixels = patches.shape
    model, columns = weight_0.shape
    hidden = (columns - 4 * model) // 2
    total = count + TAIL
    _, rows = split_table(vecs, count)
    ends = jnp.concatenate(
        [jnp.zeros((14, model), F32), ends, jnp.zeros((rows.shape[0] - 16, model), F32)]
    )
    width = packed_width(pixels, columns, model)
    return pl.pallas_call(
        functools.partial(backward_kernel, images, hidden, count),
        grid=(images,),
        out_shape=jax.ShapeDtypeStruct((model, width), BF16),
        in_specs=[
            each((count, pixels)),
            each((count, 1)),
            fixed(weight_p.shape),
            fixed(weight_0.shape),
            fixed(weight_1.shape),
            fixed(rows.shape),
            fixed(ends.shape),
            fixed(grad_cls.shape),
        ]
        + [each(array.shape[1:]) for array in saved[:9]]
        + [fixed(array.shape) for array in saved[9:]],
        out_specs=whole_out((model, width)),
        scratch_shapes=[
            pltpu.VMEM((model, pixels), F32),
            pltpu.VMEM((model, columns), F32),
            pltpu.VMEM((model, 2 * model), F32),
            pltpu.VMEM((model, model), F32),
            pltpu.VMEM((TAIL, model), F32),
            pltpu.VMEM((TAIL, model), F32),
            pltpu.VMEM((total, model), F32),
            pltpu.VMEM(rows.shape, F32),
        ],
        compiler_params=pltpu.CompilerParams(vmem_limit_bytes=58 << 20),
        name="backbone_backward",
    )(patches, covered[..., None], weight_p, weight_0, weight_1, rows, ends, grad_cls, *saved)


def owners_of(low, high, rows, count):
    return [f for f in range(count) if f * rows < high and (f + 1) * rows > low]


def two_halves(value):
    half = value.shape[1] // 2
    return jnp.concatenate([value[:, :half], value[:, half:]], 0).astype(BF16)


def from_halves(slots):
    wide = slots.astype(F32)
    half = wide.shape[-1]
    first = wide[:, :8, :].reshape(-1, half)
    second = wide[:, 8:, :].reshape(-1, half)
    return jnp.concatenate([first, second], -1)


def student_rows(value, start=0):
    pieces = [value[at + start : at + start + 4, :] for at in range(0, value.shape[0], 8)]
    return jnp.concatenate(pieces, 0)


def sixteen(value):
    return jnp.concatenate([value, jnp.zeros_like(value)], 0).astype(BF16)


def head_kernel(
    sizes, cls, gains, first_s, first_t, third_s, third_t, shard_s, shard_t, centre, counted_row,
    counted_col, proto_s, proto_t,
    grad_cls, ends, loss_row, totals, grad_logits, unit_rows, grad_head, squares,
    table_s, table_t, loading, wide_s, wide_t, kept, left, acts, parts_out, parts_in, units,
    stats, pulls, pulled, backs, pieces, pieced, extra_1, extra_3, lefts, rights, tall,
    send, recv, send_z, recv_z, send_x, recv_x, send_d, recv_d,
):
    count, dp_count, rows, chunk = sizes
    fsdp, dp = lax.axis_index("fsdp"), lax.axis_index("dp")
    model, hidden = first_s.shape
    width = third_s.shape[0]
    top_2, top_3 = model, model + hidden
    top_4 = top_3 + width
    span = kept.shape[0] // 2
    base = fsdp * rows // 128 * 128
    offset = fsdp * rows - base
    slot_rows = 8 * count
    is_student = lax.broadcasted_iota(jnp.int32, (8, 1), 0) < 4
    owners_1 = owners_of(0, top_2, rows, count)
    owners_2 = owners_of(top_2, top_3, rows, count)
    owners_3 = owners_of(top_3, top_4, rows, count)

    load_s = pltpu.make_async_copy(proto_s, table_s, loading.at[0])
    load_t = pltpu.make_async_copy(proto_t, table_t, loading.at[1])
    load_s.start()
    load_t.start()

    barrier = pltpu.get_barrier_semaphore()
    for f_step in range(count):
        for d_step in range(dp_count):
            if f_step or d_step:
                peer_f = lax.rem(fsdp + f_step, count)
                peer_d = lax.rem(dp + d_step, dp_count)
                pl.semaphore_signal(barrier, 1, device_id=(peer_f, peer_d), device_id_type=MESH)
    pl.semaphore_wait(barrier, count * dp_count - 1)

    ACTS, PARTS, STATS, PULLS, BACKS, PIECES, TOTALS = range(7)

    def swap(kind, step, source_of, target):
        peer = lax.rem(fsdp + step, count)
        return pltpu.make_async_remote_copy(
            src_ref=source_of(peer),
            dst_ref=target.at[fsdp],
            send_sem=send.at[kind, step - 1],
            recv_sem=recv.at[kind, fsdp],
            device_id=(peer, dp),
            device_id_type=MESH,
        )

    def begin(kind, source_of, target):
        for step in range(1, count):
            swap(kind, step, source_of, target).start()

    def arrive(kind, target):
        for step in range(1, count):
            peer = lax.rem(fsdp + step, count)
            pltpu.make_async_remote_copy(
                src_ref=target.at[peer],
                dst_ref=target.at[peer],
                send_sem=send.at[kind, step - 1],
                recv_sem=recv.at[kind, peer],
                device_id=(peer, dp),
                device_id_type=MESH,
            ).wait_recv()

    def end(kind, source_of, target):
        for step in range(1, count):
            swap(kind, step, source_of, target).wait_send()

    def each_net(value, first, second, product):
        low = sixteen(value)
        return jnp.where(is_student, product(low, first)[:8, :], product(low, second)[:8, :])

    unit_c, lift_c = norm_parts(cls[...])
    normed = unit_c * gains[:8, :] + gains[8:, :]
    pre_a = each_net(normed, first_s[...], first_t[...], mm)
    act_a, slope_a = gelu_both(pre_a)
    acts[fsdp] = two_halves(act_a)
    begin(ACTS, lambda peer: acts.at[fsdp], acts)

    row = fsdp * rows + lax.broadcasted_iota(jnp.int32, (rows, 1), 0)
    inside = (row >= top_2) & (row < top_3)
    kept[...] = jnp.zeros_like(kept)
    place = pl.multiple_of(offset, 16)
    kept[pl.ds(place, rows), :] = jnp.where(inside, shard_s[...], 0.0).astype(BF16)
    kept[pl.ds(pl.multiple_of(span + offset, 16), rows), :] = jnp.where(
        inside, shard_t[...], 0.0
    ).astype(BF16)
    left[...] = jnp.zeros_like(left)
    columns = pl.ds(pl.multiple_of(base, 128), span)

    arrive(ACTS, acts)
    left[:, top_2:top_3] = from_halves(acts[...])
    asked = left[:, columns].astype(BF16)
    net = lax.broadcasted_iota(jnp.int32, (slot_rows, 1), 0) % 8 < 4
    product = jnp.where(net, mm(asked, kept[:span, :]), mm(asked, kept[span:, :]))
    for f in range(count):
        parts_out[f] = two_halves(product[8 * f : 8 * f + 8, :])
    parts_in[fsdp] = parts_out[fsdp]
    begin(PARTS, lambda peer: parts_out.at[peer], parts_in)
    arrive(PARTS, parts_in)
    summed = from_halves(parts_in[...])
    pre_b = summed[:8, :]
    for f in range(1, count):
        pre_b = pre_b + summed[8 * f : 8 * f + 8, :]
    act_b, slope_b = gelu_both(pre_b)
    raw = each_net(act_b, third_s[...], third_t[...], mm_nt)
    lift_z = lax.rsqrt(jnp.sum(raw * raw, -1, keepdims=True) + 1e-06)
    unit_z = raw * lift_z

    me = fsdp * dp_count + dp
    everyone = count * dp_count
    units[me] = two_halves(unit_z)

    def unit_copy(step):
        peer = lax.rem(me + step, everyone)
        return pltpu.make_async_remote_copy(
            src_ref=units.at[me],
            dst_ref=units.at[me],
            send_sem=send_z.at[step - 1],
            recv_sem=recv_z.at[me],
            device_id=(peer // dp_count, lax.rem(peer, dp_count)),
            device_id_type=MESH,
        )

    for step in range(1, everyone):
        unit_copy(step).start()

    def owner_copy(kind, owner, source, target):
        return pltpu.make_async_remote_copy(
            src_ref=source,
            dst_ref=target.at[fsdp],
            send_sem=send_x.at[kind, owner],
            recv_sem=recv_x.at[kind, fsdp],
            device_id=(owner, dp),
            device_id_type=MESH,
        )

    def owners_begin(kind, owners, target, value):
        target[fsdp] = value
        for owner in owners:
            pl.when(fsdp != owner)(
                lambda owner=owner: owner_copy(kind, owner, target.at[fsdp], target).start()
            )

    def owners_end(kind, owners, target):
        for owner in owners:
            pl.when(fsdp != owner)(
                lambda owner=owner: owner_copy(kind, owner, target.at[fsdp], target).wait_send()
            )

    def owners_arrive(kind, owners, target):
        for owner in owners:

            @pl.when(fsdp == owner)
            def _(owner=owner):
                for f in range(count):
                    if f != owner:
                        pltpu.make_async_remote_copy(
                            src_ref=target.at[f],
                            dst_ref=target.at[f],
                            send_sem=send_x.at[kind, owner],
                            recv_sem=recv_x.at[kind, f],
                            device_id=(f, dp),
                            device_id_type=MESH,
                        ).wait_recv()

    for step in range(1, everyone):
        peer = lax.rem(me + step, everyone)
        pltpu.make_async_remote_copy(
            src_ref=units.at[peer],
            dst_ref=units.at[peer],
            send_sem=send_z.at[step - 1],
            recv_sem=recv_z.at[peer],
            device_id=(peer // dp_count, lax.rem(peer, dp_count)),
            device_id_type=MESH,
        ).wait_recv()
    all_units = from_halves(units[...])
    all_units_s = student_rows(all_units)
    rows_s = all_units_s.astype(BF16)
    rows_t = student_rows(all_units, 4).astype(BF16)
    unit_rows[...] = rows_s

    load_s.wait()
    load_t.wait()
    images = rows_s.shape[0]
    chunks = table_s.shape[0] // chunk
    low_start = jnp.full((images, 128), -3.0e38, F32)

    def lanes(op, value):
        out = value[:, :128]
        for at in range(128, value.shape[1], 128):
            out = op(out, value[:, at : at + 128])
        return out

    def logits_pass(index, tops):
        top_t, top_s = tops
        at = pl.ds(pl.multiple_of(index * chunk, chunk), chunk)
        raw_t = mm_nt(rows_t, table_t[at, :].astype(BF16))
        totals[fsdp, pl.ds(index, 1), :] = column_sum(counted_col[...] * raw_t)
        scaled_t = (raw_t - centre[:, at]) * (1.0 / TEACHER_TEMP)
        scaled_s = mm_nt(rows_s, table_s[at, :].astype(BF16)) * (1.0 / STUDENT_TEMP)
        wide_t[:, at] = scaled_t
        wide_s[:, at] = scaled_s
        return (
            jnp.maximum(top_t, lanes(jnp.maximum, scaled_t)),
            jnp.maximum(top_s, lanes(jnp.maximum, scaled_s)),
        )

    top_t, top_s = lax.fori_loop(0, chunks, logits_pass, (low_start, low_start))
    top_t = jnp.max(top_t, -1, keepdims=True)
    top_s = jnp.max(top_s, -1, keepdims=True)
    begin(TOTALS, lambda peer: totals.at[fsdp], totals)

    def expo_pass(index, sums):
        sum_t, sum_s, cross = sums
        at = pl.ds(pl.multiple_of(index * chunk, chunk), chunk)
        shifted_s = wide_s[:, at] - top_s
        expo_t = jnp.exp(wide_t[:, at] - top_t)
        expo_s = jnp.exp(shifted_s)
        wide_t[:, at] = expo_t
        wide_s[:, at] = expo_s
        return (
            sum_t + lanes(jnp.add, expo_t),
            sum_s + lanes(jnp.add, expo_s),
            cross + lanes(jnp.add, expo_t * shifted_s),
        )

    zero = jnp.zeros((images, 128), F32)
    sum_t, sum_s, cross = lax.fori_loop(0, chunks, expo_pass, (zero, zero, zero))
    lane = lax.broadcasted_iota(jnp.int32, (images, 128), 1)
    columns_of = zero
    values = (top_t, jnp.sum(sum_t, -1, keepdims=True), top_s, jnp.sum(sum_s, -1, keepdims=True),
              jnp.sum(cross, -1, keepdims=True))
    for number, value in enumerate(values):
        columns_of = jnp.where(lane == number, value, columns_of)
    stats[fsdp] = columns_of.T[:8, :]
    begin(STATS, lambda peer: stats.at[fsdp], stats)
    arrive(STATS, stats)
    gathered = [stats[f] for f in range(count)]
    high_t, high_s = gathered[0][0:1, :], gathered[0][2:3, :]
    for part in gathered[1:]:
        high_t = jnp.maximum(high_t, part[0:1, :])
        high_s = jnp.maximum(high_s, part[2:3, :])
    total_t = total_s = crossed = jnp.zeros_like(high_t)
    for part in gathered:
        lift_t = jnp.exp(part[0:1, :] - high_t)
        total_t = total_t + part[1:2, :] * lift_t
        total_s = total_s + part[3:4, :] * jnp.exp(part[2:3, :] - high_s)
        crossed = crossed + lift_t * (part[4:5, :] + (part[2:3, :] - high_s) * part[1:2, :])
    counted = counted_row[...]
    loss_row[...] = counted * (jnp.log(total_s) - crossed / total_t)
    weighting = counted / jnp.maximum(jnp.sum(counted, -1, keepdims=True), 1.0) / STUDENT_TEMP
    mine = stats[fsdp]
    share_s = weighting * jnp.exp(mine[2:3, :] - high_s) / total_s
    share_t = weighting * jnp.exp(mine[0:1, :] - high_t) / total_t
    turned = jnp.concatenate([share_s, share_t, jnp.zeros((126, images), F32)], 0).T
    share_s, share_t = turned[:, 0:1], turned[:, 1:2]

    turned_rows = all_units_s.T.astype(BF16)
    squares[...] = jnp.zeros_like(squares)

    def add_squares(value):
        total = squares[...]
        for row in range(0, value.shape[0], 8):
            strip = value[row : row + 8, :]
            total = total + lanes(jnp.add, strip * strip)
        squares[...] = total

    def grad_pass(index, total):
        at = pl.ds(pl.multiple_of(index * chunk, chunk), chunk)
        low = (wide_s[:, at] * share_s - wide_t[:, at] * share_t).astype(BF16)
        grad_logits[:, at] = low
        add_squares(mm(turned_rows, low))
        return total + mm(low, table_s[at, :].astype(BF16))

    partial = lax.fori_loop(0, chunks, grad_pass, jnp.zeros((images, width), F32))
    for slot in range(0, everyone, 2):
        pair = partial[4 * slot : 4 * slot + 8, :]
        pulls[slot] = pair
        pulls[slot + 1] = jnp.concatenate([pair[4:, :], pair[:4, :]], 0)
    pulled[fsdp] = pulls[me]
    begin(PULLS, lambda peer: pulls.at[peer * dp_count + dp], pulled)
    arrive(PULLS, pulled)
    grad_z = pulled[0]
    for f in range(1, count):
        grad_z = grad_z + pulled[f]
    grad_z = jnp.where(is_student, grad_z, 0.0)
    grad_raw = lift_z * (grad_z - unit_z * jnp.sum(unit_z * grad_z, -1, keepdims=True))
    grad_b = mm(sixteen(grad_raw), third_s[...])[:8, :]
    pre_grad_b = jnp.where(is_student, grad_b * slope_b, 0.0)
    backs[fsdp] = two_halves(pre_grad_b)
    begin(BACKS, lambda peer: backs.at[fsdp], backs)
    arrive(BACKS, backs)
    grads_b = from_halves(backs[...])
    piece = mm_nt(grads_b.astype(BF16), kept[:span, :])
    for f in range(count):
        pieces[f] = piece[8 * f : 8 * f + 8, :]
    pieced[fsdp] = pieces[fsdp]
    begin(PIECES, lambda peer: pieces.at[peer], pieced)

    owned = [
        (fsdp >= owners[0]) & (fsdp <= owners[-1]) for owners in (owners_1, owners_2, owners_3)
    ]

    def group_copy(kind, step, place):
        peer = lax.rem(dp + step, dp_count)
        return pltpu.make_async_remote_copy(
            src_ref=place(dp),
            dst_ref=place(dp),
            send_sem=send_d.at[kind, step - 1],
            recv_sem=recv_d.at[kind, dp],
            device_id=(fsdp, peer),
            device_id_type=MESH,
        )

    def group_arrive(kind, place):
        for step in range(1, dp_count):
            peer = lax.rem(dp + step, dp_count)
            pltpu.make_async_remote_copy(
                src_ref=place(peer),
                dst_ref=place(peer),
                send_sem=send_d.at[kind, step - 1],
                recv_sem=recv_d.at[kind, peer],
                device_id=(fsdp, peer),
                device_id_type=MESH,
            ).wait_recv()

    def right_at(number):
        return lambda group: rights.at[group, number]

    def left_at(group):
        return lefts.at[group]

    def group_begin(kind, place):
        for step in range(1, dp_count):
            group_copy(kind, step, place).start()

    def group_end(kind, place):
        for step in range(1, dp_count):
            group_copy(kind, step, place).wait_send()

    @pl.when(owned[1])
    def _():
        rights[dp, 1] = student_rows(grads_b).astype(BF16)
        group_begin(2, right_at(1))

    owners_begin(1, owners_3, extra_3, two_halves(jnp.concatenate([act_b, grad_raw], -1)))
    arrive(PIECES, pieced)
    back_a = jnp.zeros((8, left.shape[1]), F32)
    for f in range(count):
        at = f * rows // 128 * 128
        value = [pieced[f]]
        if at:
            value = [jnp.zeros((8, at), F32)] + value
        if left.shape[1] - at - span:
            value = value + [jnp.zeros((8, left.shape[1] - at - span), F32)]
        back_a = back_a + jnp.concatenate(value, -1)
    pre_grad_a = jnp.where(is_student, back_a[:, top_2:top_3] * slope_a, 0.0)
    spare = jnp.zeros((8, 2 * extra_1.shape[2] - model - hidden), F32)
    owners_begin(
        0, owners_1, extra_1, two_halves(jnp.concatenate([normed, pre_grad_a, spare], -1))
    )
    grad_n = jnp.where(is_student, mm_nt(sixteen(pre_grad_a), first_s[...])[:8, :], 0.0)
    grad_cls[...] = norm_back(grad_n, gains[:8, :], unit_c, lift_c)
    ends[...] = jnp.concatenate(
        [column_sum(grad_n * unit_c), column_sum(grad_n), jnp.zeros((6, model), F32)], 0
    )

    owners_arrive(1, owners_3, extra_3)

    @pl.when(owned[2])
    def _():
        extra = from_halves(extra_3[...])
        left[:, top_3:top_4] = extra[:, hidden:]
        rights[dp, 2] = student_rows(extra[:, :hidden]).astype(BF16)
        group_begin(3, right_at(2))

    owners_arrive(0, owners_1, extra_1)

    @pl.when(owned[0])
    def _():
        extra = from_halves(extra_1[...])
        left[:, :top_2] = extra[:, :model]
        rights[dp, 0] = student_rows(extra[:, model : model + hidden]).astype(BF16)
        group_begin(1, right_at(0))

    lefts[dp] = student_rows(left[:, columns]).astype(BF16)
    group_begin(0, left_at)
    group_arrive(0, left_at)
    tall[...] = jnp.zeros_like(tall)
    column = base + lax.broadcasted_iota(jnp.int32, (1, span), 1)
    for number, (low, high) in enumerate(((0, top_2), (top_2, top_3), (top_3, top_4))):

        @pl.when(owned[number])
        def _(number=number, low=low, high=high):
            group_arrive(1 + number, right_at(number))
            own_side = jnp.concatenate([lefts[group] for group in range(dp_count)], 0)
            keep_columns = ((column >= low) & (column < high)).astype(F32)
            own_side = (own_side.astype(F32) * keep_columns).astype(BF16)
            other = jnp.concatenate([rights[group, number] for group in range(dp_count)], 0)
            tall[...] += mm_tn(own_side, other)
            group_end(1 + number, right_at(number))

    grad_head[...] = tall[pl.ds(place, rows), :]

    def square_pass(index, carry):
        add_squares(grad_head[pl.ds(pl.multiple_of(index * 16, 16), 16), :])
        return carry

    lax.fori_loop(0, rows // 16, square_pass, 0)
    group_end(0, left_at)
    arrive(TOTALS, totals)
    end(ACTS, lambda peer: acts.at[fsdp], acts)
    end(PARTS, lambda peer: parts_out.at[peer], parts_in)
    end(STATS, lambda peer: stats.at[fsdp], stats)
    end(PULLS, lambda peer: pulls.at[peer * dp_count + dp], pulled)
    end(BACKS, lambda peer: backs.at[fsdp], backs)
    end(PIECES, lambda peer: pieces.at[peer], pieced)
    end(TOTALS, lambda peer: totals.at[fsdp], totals)
    for step in range(1, everyone):
        unit_copy(step).wait_send()
    owners_end(0, owners_1, extra_1)
    owners_end(1, owners_3, extra_3)


def head_step(
    cls_s, cls_t, vecs_s, vecs_t, weights, shards, centre, counted, protos, counts, collective_id
):
    count, dp_count = counts
    model, hidden = weights[0].shape
    width = weights[2].shape[0]
    rows = shards[0].shape[0]
    owned_k = protos[0].shape[0]
    images = counted.shape[0]
    everyone = count * dp_count
    span = max(f * rows % 128 + rows for f in range(count))
    span = (span + 127) // 128 * 128
    extent = max(f * rows // 128 * 128 + span for f in range(count))
    chunk = 1024
    cls = jnp.concatenate([cls_s[:4], cls_t[:4]])
    gains = jnp.concatenate(
        [
            jnp.broadcast_to(vecs[vecs.shape[0] + row][None], (4, model))
            for row in (-2, -1)
            for vecs in (vecs_s, vecs_t)
        ]
    )
    shape = jax.ShapeDtypeStruct
    vmem = pl.BlockSpec(memory_space=pltpu.VMEM)
    anywhere = pl.BlockSpec(memory_space=pl.ANY)
    extra_width = (model + hidden + 255) // 256 * 128
    sems = pltpu.SemaphoreType.DMA
    return pl.pallas_call(
        functools.partial(head_kernel, (count, dp_count, rows, chunk)),
        out_shape=[
            shape((8, model), F32),
            shape((8, model), F32),
            shape((1, images), F32),
            shape((count, owned_k // chunk, chunk), F32),
            shape((images, owned_k), BF16),
            shape((images, width), BF16),
            shape((rows, hidden), F32),
            shape((8, 128), F32),
        ],
        in_specs=[vmem] * 11 + [anywhere] * 2,
        out_specs=[vmem] * 8,
        scratch_shapes=[
            pltpu.VMEM((owned_k, width), F32),
            pltpu.VMEM((owned_k, width), F32),
            sems((2,)),
            pltpu.VMEM((images, owned_k), F32),
            pltpu.VMEM((images, owned_k), F32),
            pltpu.VMEM((2 * span, hidden), BF16),
            pltpu.VMEM((8 * count, extent), F32),
            pltpu.VMEM((count, 16, hidden // 2), BF16),
            pltpu.VMEM((count, 16, hidden // 2), BF16),
            pltpu.VMEM((count, 16, hidden // 2), BF16),
            pltpu.VMEM((everyone, 16, width // 2), BF16),
            pltpu.VMEM((count, 8, 128), F32),
            pltpu.VMEM((everyone, 8, width), F32),
            pltpu.VMEM((count, 8, width), F32),
            pltpu.VMEM((count, 16, hidden // 2), BF16),
            pltpu.VMEM((count, 8, span), F32),
            pltpu.VMEM((count, 8, span), F32),
            pltpu.VMEM((count, 16, extra_width), BF16),
            pltpu.VMEM((count, 16, (hidden + width) // 2), BF16),
            pltpu.VMEM((dp_count, 4 * count, span), BF16),
            pltpu.VMEM((dp_count, 3, 4 * count, hidden), BF16),
            pltpu.VMEM((span, hidden), F32),
            sems((7, count - 1)),
            sems((7, count)),
            sems((everyone - 1,)),
            sems((everyone,)),
            sems((2, count)),
            sems((2, count)),
            sems((4, dp_count - 1)),
            sems((4, dp_count)),
        ],
        compiler_params=pltpu.CompilerParams(
            collective_id=collective_id, has_side_effects=True, vmem_limit_bytes=60 << 20
        ),
        name="head_step",
    )(
        cls, gains, *weights, *shards, centre[None], counted[None], counted[:, None], *protos
    )


def dot(left, right, dims):
    return lax.dot_general(left, right, (dims, ((), ())), preferred_element_type=F32)


def layer_norm(x, gain, shift):
    centred = x - jnp.mean(x, -1, keepdims=True)
    spread = jnp.mean(centred * centred, -1, keepdims=True)
    return centred * lax.rsqrt(spread + 1e-06) * gain + shift


def gelu_slope(x):
    _, pull = jax.vjp(jax.nn.gelu, x)
    return pull(jnp.ones_like(x))[0]


def head_forward(cls, weight, vecs):
    width, hidden = cls.shape[1], weight.shape[1]
    low_n = layer_norm(cls, vecs[-2], vecs[-1]).astype(BF16)
    pre_a = jnp.dot(low_n, weight[:width], preferred_element_type=F32)
    low_a = jax.nn.gelu(pre_a).astype(BF16)
    pre_b = jnp.dot(low_a, weight[width : width + hidden], preferred_element_type=F32)
    low_b = jax.nn.gelu(pre_b).astype(BF16)
    raw = dot(low_b, weight[width + hidden :], ((1,), (1,)))
    return low_n, pre_a, low_a, pre_b, low_b, raw


def unit(raw):
    return raw * lax.rsqrt(jnp.sum(raw * raw, -1, keepdims=True) + 1e-06)


def adamw(weight, moment, second, gradient, factor, step_rate, weight_decay):
    clipped = gradient * factor
    moment = BETA_ONE * moment + (1.0 - BETA_ONE) * clipped
    second = BETA_TWO * second + (1.0 - BETA_TWO) * clipped * clipped
    direction = (
        moment / (1.0 - BETA_ONE**STEP) / (jnp.sqrt(second / (1.0 - BETA_TWO**STEP)) + 1e-08)
    )
    return (weight - step_rate * (direction + weight_decay * weight), moment, second)


def own_kernels(local, head_rows, model, hidden, total):
    count = lax.axis_size("fsdp")
    if lax.axis_size("dp") != 4 or count not in (4, 8) or local != 4 or head_rows % 16:
        return False
    for low, high in ((0, model), (hidden + model, total)):
        rows = (high - low) // count
        if rows % 16 or any((low + rows * f) % head_rows + rows > head_rows for f in range(count)):
            return False
    return True


def head_plain(
    cls, teacher_cls, vectors, teacher_vectors, head_full, teacher_head_full, own_centre, counted,
    counted_total, w_proto, teacher_proto, own_rows,
):
    teacher_unit = unit(head_forward(teacher_cls, teacher_head_full, teacher_vectors)[-1])
    low_n, pre_a, low_a, pre_b, low_b, raw = head_forward(cls, head_full, vectors)
    bottleneck, pull_unit = jax.vjp(unit, raw)
    both = jnp.concatenate([teacher_unit.astype(BF16), bottleneck.astype(BF16)], -1)
    both = lax.all_gather(both, ("fsdp", "dp"), axis=0, tiled=True)
    width = raw.shape[1]
    teacher_rows, student_rows = both[:, :width], both[:, width:]

    low_proto = w_proto.astype(BF16)
    teacher_logits = dot(teacher_rows, teacher_proto.astype(BF16), ((1,), (1,)))
    logits = dot(student_rows, low_proto, ((1,), (1,)))
    scaled_t = (teacher_logits - own_centre) / TEACHER_TEMP
    scaled_s = logits / STUDENT_TEMP
    max_t = jnp.max(scaled_t, -1)
    max_s = jnp.max(scaled_s, -1)
    expo_t = jnp.exp(scaled_t - max_t[:, None])
    expo_s = jnp.exp(scaled_s - max_s[:, None])
    parts = jnp.stack(
        [
            max_t,
            jnp.sum(expo_t, -1),
            max_s,
            jnp.sum(expo_s, -1),
            jnp.sum(expo_t * (scaled_s - max_s[:, None]), -1),
        ]
    )
    parts = lax.all_gather(parts, "fsdp", axis=0)
    top_t = jnp.max(parts[:, 0], 0)
    lift_t = jnp.exp(parts[:, 0] - top_t)
    total_t = jnp.sum(parts[:, 1] * lift_t, 0)
    top_s = jnp.max(parts[:, 2], 0)
    total_s = jnp.sum(parts[:, 3] * jnp.exp(parts[:, 2] - top_s), 0)
    crossed = jnp.sum(lift_t * (parts[:, 4] + (parts[:, 2] - top_s) * parts[:, 1]), 0) / total_t
    losses = jnp.log(total_s) - crossed
    loss_total = jnp.sum(counted * losses)
    weighting = counted / counted_total / STUDENT_TEMP
    share_s = weighting * jnp.exp(max_s - top_s) / total_s
    share_t = weighting * jnp.exp(max_t - top_t) / total_t
    grad_logits = (expo_s * share_s[:, None] - expo_t * share_t[:, None]).astype(BF16)
    teacher_sum = jnp.sum(counted[:, None] * teacher_logits, 0)
    teacher_total = lax.all_gather(teacher_sum, "fsdp", axis=0, tiled=True)
    grad_proto = dot(grad_logits, student_rows, ((0,), (0,)))
    grad_rows = jnp.dot(grad_logits, low_proto, preferred_element_type=F32)
    dp_count = lax.axis_size("dp")
    grad_rows = grad_rows.reshape(-1, dp_count, cls.shape[0], width)
    grad_rows = lax.dynamic_index_in_dim(grad_rows, lax.axis_index("dp"), 1, keepdims=False)
    grad_bottleneck = lax.psum_scatter(grad_rows, "fsdp", scatter_dimension=0, tiled=False)

    model_width, hidden = cls.shape[1], head_full.shape[1]
    local = cls.shape[0]
    low_dz = pull_unit(grad_bottleneck)[0].astype(BF16)
    grad_b = jnp.dot(low_dz, head_full[model_width + hidden :], preferred_element_type=F32)
    low_db = (grad_b * gelu_slope(pre_b)).astype(BF16)
    grad_a = dot(low_db, head_full[model_width : model_width + hidden], ((1,), (1,)))
    low_da = (grad_a * gelu_slope(pre_a)).astype(BF16)
    grad_n = dot(low_da, head_full[:model_width], ((1,), (1,)))
    _, pull_norm = jax.vjp(layer_norm, cls, vectors[-2], vectors[-1])
    grad_cls, grad_gain, grad_shift = pull_norm(grad_n)

    packed = jnp.concatenate([low_n, low_a, low_dz, low_da, low_db, low_b], -1)
    packed = lax.all_gather(packed, ("fsdp", "dp"), axis=0, tiled=True)
    total_rows = model_width + hidden + width
    lefts, rights = packed[:, :total_rows], packed[:, total_rows:]
    start = lax.axis_index("fsdp") * own_rows
    left = lax.dynamic_slice_in_dim(lefts, start, own_rows, 1)
    row = start + lax.broadcasted_iota(jnp.int32, (1, own_rows), 1)
    kind = jnp.where(row < model_width, 0, jnp.where(row < model_width + hidden, 1, 2))
    left = jnp.concatenate([jnp.where(kind == index, left, 0) for index in range(3)], 0)
    right = jnp.concatenate(
        [rights[:, index * hidden : (index + 1) * hidden] for index in range(3)], 0
    )
    grad_head = dot(left, right, ((0,), (0,)))
    ends = jnp.stack([grad_gain, grad_shift])
    return grad_cls, ends, loss_total, teacher_total, grad_proto, grad_head


def per_device(
    patches,
    patch_mask,
    image_valid,
    centre,
    w_patch,
    first_patch,
    second_patch,
    teacher_patch,
    w_layer,
    first_layer,
    second_layer,
    teacher_layer,
    w_head,
    first_head,
    second_head,
    teacher_head,
    w_proto,
    first_proto,
    second_proto,
    teacher_proto,
    vectors,
    first_vectors,
    second_vectors,
    teacher_vectors,
):
    everyone = ("fsdp", "dp")
    local = patches.shape[0]
    place = lax.axis_index(everyone) * local
    fsdp_index = lax.axis_index("fsdp")
    counted = image_valid.astype(F32)
    counted_total = jnp.maximum(jnp.sum(counted), 1.0)
    covered = patch_mask.astype(F32)
    pixels = w_patch.shape[1]
    model_width, columns = w_layer.shape[1] * lax.axis_size("fsdp"), w_layer.shape[2]
    pad = packed_width_p(pixels) - pixels

    def low_blocks(patch, layers):
        patch = jnp.pad(patch, ((0, 0), (0, pad)))
        return [array.astype(BF16) for array in (patch, layers[0], layers[1])]

    head_s, head_t = w_head.astype(BF16), teacher_head.astype(BF16)
    blocks = low_blocks(teacher_patch, teacher_layer) + low_blocks(w_patch, w_layer)
    hidden = w_head.shape[1]
    fsdp_count = lax.axis_size("fsdp")
    own_rows, own_k = w_head.shape[0], w_proto.shape[0]
    total_rows = own_rows * fsdp_count
    own = own_kernels(local, own_rows, model_width, hidden, total_rows)
    if own:
        ranges = ((0, model_width), (model_width + hidden, total_rows))
        full, teacher_rows, cls_rows, saved = gather_forward(
            blocks, (head_s, head_t), ranges, fsdp_count, patches, covered, vectors,
            teacher_vectors, 1,
        )
    else:
        full = [
            lax.all_gather(block, "fsdp", axis=0, tiled=True)
            for block in blocks + [head_s, head_t]
        ]
        teacher_rows = forward(
            patches, jnp.zeros_like(covered), *full[:3], teacher_vectors, False
        )[0]
        cls_rows, *saved = forward(patches, covered, *full[3:6], vectors, True)
    patch_full, layer_0, layer_1 = full[3:6]
    own_centre = lax.dynamic_slice_in_dim(centre, fsdp_index * own_k, own_k)
    if own:
        grad_cls, ends, loss_row, totals, grad_logits, unit_rows, grad_head, part = head_step(
            cls_rows, teacher_rows, vectors, teacher_vectors, full[6:], (head_s, head_t),
            own_centre, counted, (w_proto, teacher_proto), (fsdp_count, lax.axis_size("dp")), 3,
        )
        ends = ends[:2]
        loss_total = jnp.sum(loss_row)
        teacher_total = totals.reshape(-1)
        grad_proto = dot(grad_logits, unit_rows, ((0,), (0,)))
    else:
        grad_cls, ends, loss_total, teacher_total, grad_proto, grad_head = head_plain(
            cls_rows[:local], teacher_rows[:local], vectors, teacher_vectors, full[6], full[7],
            own_centre, counted, counted_total, w_proto, teacher_proto, own_rows,
        )
    grad_rows = jnp.pad(grad_cls, ((0, TAIL - grad_cls.shape[0]), (0, 0)))
    packed_grads = backward(
        patches, covered, patch_full, layer_0, layer_1, vectors, ends, grad_rows, saved
    )
    cut_0 = packed_width_p(pixels)
    cut_1, cut_2 = cut_0 + columns, cut_0 + 2 * columns
    if own:
        places = (cut_0, cut_1, cut_2, model_width)
        own_patch, own_layers, table, sums = reduce_rows(
            packed_grads, part, places, fsdp_count, 9, 2
        )
        vector_grad = table.reshape(model_width, model_width)[: vectors.shape[0]]
        own_patch = own_patch[:, :pixels]
        squares = jnp.sum(sums)
    else:
        owned = lax.psum_scatter(packed_grads, "fsdp", scatter_dimension=0, tiled=True)
        owned = lax.psum(owned, "dp").astype(F32)
        own_patch = owned[:, :pixels]
        own_layers = jnp.stack([owned[:, cut_0:cut_1], owned[:, cut_1:cut_2]])
        own_table = owned[:, cut_2 : cut_2 + model_width]
        table = lax.all_gather(own_table, "fsdp", axis=0, tiled=True)
        vector_grad = table[: vectors.shape[0]]
        parts = (own_patch, own_layers, grad_head, grad_proto, own_table)
        squares = lax.psum(sum(jnp.sum(value * value) for value in parts), "fsdp")
    owned_grads = (own_patch, own_layers, grad_head, grad_proto)
    norm_value = jnp.sqrt(squares)
    factor = CLIP_NORM / jnp.maximum(norm_value, CLIP_NORM)
    updated_centre = CENTRE_KEEP * centre + (1.0 - CENTRE_KEEP) * teacher_total / counted_total
    weights_owned = (w_patch, w_layer, w_head, w_proto, vectors)
    moments = (first_patch, first_layer, first_head, first_proto, first_vectors)
    seconds = (second_patch, second_layer, second_head, second_proto, second_vectors)
    teachers = (teacher_patch, teacher_layer, teacher_head, teacher_proto, teacher_vectors)
    gradients = owned_grads + (vector_grad,)
    results = [loss_total, counted_total, norm_value, updated_centre]
    for group in range(5):
        updated, moment, second = adamw(
            weights_owned[group],
            moments[group],
            seconds[group],
            gradients[group],
            factor,
            RATES[group],
            DECAYS[group],
        )
        results.extend(
            [
                updated,
                moment,
                second,
                TEACHER_KEEP * teachers[group] + (1.0 - TEACHER_KEEP) * updated,
            ]
        )
    return tuple(results)


def solution(mesh):
    whole, rows, middle = P(), P("fsdp", None), P(None, "fsdp", None)
    in_specs = (
        (P(("fsdp", "dp"), None, None), P(("fsdp", "dp"), None), whole, whole)
        + (rows,) * 4
        + (middle,) * 4
        + (rows,) * 8
        + (whole,) * 4
    )
    out_specs = (whole,) * 4 + (rows,) * 4 + (middle,) * 4 + (rows,) * 8 + (whole,) * 4
    return jax.shard_map(
        per_device, mesh=mesh, in_specs=in_specs, out_specs=out_specs, check_vma=False
    )
```

```python
import functools

import jax
import jax.numpy as jnp
from jax import lax
from jax.experimental import pallas as pl
from jax.experimental.pallas import tpu as pltpu
from jax.sharding import PartitionSpec as P

HEADS = 6
STEP = 10
STUDENT_TEMP = 0.1
TEACHER_TEMP = 0.07
CENTRE_KEEP = 0.9
TEACHER_KEEP = 0.8
BETA_ONE = 0.9
BETA_TWO = 0.999
CLIP_NORM = 0.01
RATES = (0.1, 0.15, 0.07, 0.5, 0.5)
DECAYS = (0.04, 0.04, 0.04, 0.04, 0.0)
F32 = jnp.float32
BF16 = jnp.bfloat16
MESH = pl.DeviceIdType.MESH


def third_ranges(width, start):
    tiles = width // 128
    sizes = [(tiles + 2 - part) // 3 * 128 for part in range(3)]
    spans, at = [], start
    for size in sizes:
        spans.append((at, size))
        at += size
    return spans


def gather_kernel(items, early, lines, sources, heads, targets, between, send, recv, copied, send_e, recv_e):
    fsdp, dp = lax.axis_index("fsdp"), lax.axis_index("dp")
    z, x = fsdp // 2, fsdp % 2
    y, core = dp // 2, dp % 2
    across = z * 2 + 1 - x
    mate = y * 2 + 1 - core
    opposite = (1 - y) * 2 + core

    barrier = pltpu.get_barrier_semaphore()

    def greet(f, d):
        pl.semaphore_signal(barrier, 1, device_id=(f, d), device_id_type=pl.DeviceIdType.MESH)

    def when(condition, body):
        pl.when(condition)(body)

    for step in range(1, 2 * lines):
        greet(lax.rem(fsdp + step, 2 * lines), dp)
    greet(fsdp, mate)
    when(core == 0, lambda: greet(fsdp, opposite))
    pl.semaphore_wait(barrier, 2 * lines + 1 - core)

    hops = lines - 1
    UP, DOWN, ACROSS, OPPOSITE, MATE = 0, hops, 2 * hops, 4 * hops + 1, 4 * hops + 2

    def roles(body):
        when((core == 0) & (y == 0), lambda: body(0))
        when(core == 1, lambda: body(1))
        when((core == 0) & (y == 1), lambda: body(2))

    def region(index, part, f):
        number, rows, spans = items[index]
        at, size = spans[part]
        return targets[number].at[pl.ds(pl.multiple_of(f * rows, rows), rows), pl.ds(at, size)]

    def whole(index, part):
        number, rows, spans = items[index]
        at, size = spans[part]
        return targets[number].at[:, pl.ds(at, size)]

    def own(index, part):
        number, rows, spans = items[index]
        at, size = spans[part]
        return sources[number].at[:, pl.ds(at, size)]

    def move(index, slot, source, target, f, d):
        return pltpu.make_async_remote_copy(
            src_ref=source,
            dst_ref=target,
            send_sem=send.at[index, slot],
            recv_sem=recv.at[index, slot],
            device_id=(f, d),
            device_id_type=pl.DeviceIdType.MESH,
        )

    def piece(index, part, slot, f_source, f_target, mine=False):
        target = region(index, part, f_source)
        return move(index, slot, own(index, part) if mine else target, target, f_target, dp)

    def keep(index, part):
        return pltpu.make_async_copy(own(index, part), region(index, part, fsdp), copied.at[index])

    def z_steps(index, part, hop, act):
        mine = hop == 0
        if hop < hops:
            when(
                (z - hop >= 0) & (z + 1 < lines),
                lambda: act(piece(index, part, UP + hop, fsdp - 2 * hop, fsdp + 2, mine)),
            )
            when(
                (z + hop < lines) & (z > 0),
                lambda: act(piece(index, part, DOWN + hop, fsdp + 2 * hop, fsdp - 2, mine)),
            )

    def x_steps(index, part, hop, act):
        if hop == 0:
            act(piece(index, part, ACROSS, fsdp, across, True))
        else:
            when(
                z - hop >= 0,
                lambda: act(piece(index, part, ACROSS + hop, fsdp - 2 * hop, across)),
            )
            when(
                z + hop < lines,
                lambda: act(piece(index, part, ACROSS + hops + hop, fsdp + 2 * hop, across)),
            )

    def z_arrive(index, part, hop):
        when(
            z - hop >= 0,
            lambda: piece(index, part, UP + hop - 1, fsdp - 2 * hop, fsdp).wait_recv(),
        )
        when(
            z + hop < lines,
            lambda: piece(index, part, DOWN + hop - 1, fsdp + 2 * hop, fsdp).wait_recv(),
        )

    def x_arrive(index, part):
        piece(index, part, ACROSS, across, across).wait_recv()
        for hop in range(1, lines):
            when(
                z - hop >= 0,
                lambda hop=hop: piece(
                    index, part, ACROSS + hop, across - 2 * hop, across
                ).wait_recv(),
            )
            when(
                z + hop < lines,
                lambda hop=hop: piece(
                    index, part, ACROSS + hops + hop, across + 2 * hop, across
                ).wait_recv(),
            )

    def to_opposite(index, part):
        return move(index, OPPOSITE, whole(index, part), whole(index, part), fsdp, opposite)

    def to_mate(index, part, second=0):
        return move(index, MATE + second, whole(index, part), whole(index, part), fsdp, mate)

    def deal(part, act):
        for index, (number, places) in early.items():
            _, rows, spans = items[index]
            at, size = spans[part]
            target = sources[items[index][0]].at[:, pl.ds(at, size)]
            for f, (owner, start) in enumerate(places):
                source = heads[number].at[pl.ds(start, rows), pl.ds(at, size)]
                act(index, f, owner, source, target)

    def early_copy(index, f, source, target):
        return pltpu.make_async_remote_copy(
            src_ref=source,
            dst_ref=target,
            send_sem=send_e.at[index, f],
            recv_sem=recv_e.at[index],
            device_id=(f, dp),
            device_id_type=pl.DeviceIdType.MESH,
        )

    def deal_start(index, f, owner, source, target):
        if f == owner:
            when(
                fsdp == f,
                lambda: pltpu.make_async_copy(source, target, recv_e.at[index]).start(),
            )
        else:
            when(fsdp == owner, lambda: early_copy(index, f, source, target).start())

    def deal_end(index, f, owner, source, target):
        if f != owner:
            when(fsdp == owner, lambda: early_copy(index, f, source, target).wait_send())

    def dealt(index, part):
        _, rows, spans = items[index]
        at, size = spans[part]
        number, places = early[index]
        target = sources[items[index][0]].at[:, pl.ds(at, size)]
        for f, (owner, start) in enumerate(places):
            source = heads[number].at[pl.ds(start, rows), pl.ds(at, size)]
            if f == owner:
                when(
                    fsdp == f,
                    lambda source=source: pltpu.make_async_copy(
                        source, target, recv_e.at[index]
                    ).wait(),
                )
            else:
                when(
                    fsdp == f,
                    lambda f=f, source=source: early_copy(index, f, source, target).wait_recv(),
                )

    def stage(index, part, step):
        if step == 0:
            if index in early:
                dealt(index, part)
            keep(index, part).start()
            z_steps(index, part, 0, lambda copy: copy.start())
            x_steps(index, part, 0, lambda copy: copy.start())
        elif step < lines:
            z_arrive(index, part, step)
            z_steps(index, part, step, lambda copy: copy.start())
            x_steps(index, part, step, lambda copy: copy.start())
        elif step == lines:
            keep(index, part).wait()
            x_arrive(index, part)
            if part != 1:
                to_opposite(index, part).start()
            to_mate(index, part).start()
        elif step == lines + 1:
            if part != 1:
                to_opposite(index, 2 - part).wait_recv()
                to_mate(index, 2 - part, 1).start()
        else:
            if part != 1:
                to_mate(index, 1).wait_recv()
            else:
                when(y == 0, lambda: to_mate(index, 0).wait_recv())
                when(y == 0, lambda: to_mate(index, 2, 1).wait_recv())
                when(y == 1, lambda: to_mate(index, 2).wait_recv())
                when(y == 1, lambda: to_mate(index, 0, 1).wait_recv())

    steps = lines + 3

    def run(tick, part):
        for step in range(steps):
            if 0 <= tick - step < len(items):
                stage(tick - step, part, step)

    def close(part):
        for index in range(len(items)):
            for hop in range(lines):
                z_steps(index, part, hop, lambda copy: copy.wait_send())
                x_steps(index, part, hop, lambda copy: copy.wait_send())
            if part != 1:
                to_opposite(index, part).wait_send()
                to_mate(index, 2 - part, 1).wait_send()
            to_mate(index, part).wait_send()
        deal(part, deal_end)

    roles(lambda part: deal(part, deal_start))
    for tick in range(len(items) + steps - 1):
        roles(functools.partial(run, tick))
        between(tick - steps + 1)
    roles(close)


def gather_forward(
    arrays, heads, ranges, fsdp_count, patches, covered, vecs, teacher_vecs, collective_id
):
    lines = fsdp_count // 2
    head_rows, head_width = heads[0].shape
    shapes = [array.shape for array in arrays]
    count = len(arrays)
    items, whole_at = [], {}
    for number in (0, 1, 3, 4, 2, 5):
        rows, width = shapes[number]
        cuts = 2 if width % 256 == 0 and width > 1024 else 1
        for cut in range(cuts):
            items.append((number, rows, third_ranges(width // cuts, cut * (width // cuts))))
        whole_at[number] = len(items) - 1
    early = {}
    for low, high in ranges:
        for number in range(len(heads)):
            rows = (high - low) // fsdp_count
            starts = [low + rows * f for f in range(fsdp_count)]
            early[len(items)] = (
                number,
                [(start // head_rows, start % head_rows) for start in starts],
            )
            shapes.append((rows, head_width))
            items.append((len(shapes) - 1, rows, third_ranges(head_width, 0)))
    slots = 4 * (lines - 1) + 4
    extra = len(shapes) - count
    full = [(fsdp_count * r, c) for r, c in shapes]
    images, pixel_rows, pixels = patches.shape
    model, columns = full[1]
    hidden = (columns - 4 * model) // 2
    tables = split_table(teacher_vecs, pixel_rows) + split_table(vecs, pixel_rows)
    per_image = saved_shapes(pixel_rows + TAIL, model)
    saved = len(per_image)

    def kernel(*refs):
        refs = list(refs)

        def take(number):
            taken = refs[:number]
            del refs[:number]
            return taken

        sources, head_refs = take(count), take(len(heads))
        patches_ref, covered_ref = take(2)
        table_refs = take(4)
        targets, dealt = take(len(shapes)), take(extra)
        cls_t, cls_s, x1c_out, o1_out = take(4)
        saved_out = take(saved)
        weights, kept = take(6), take(saved)
        cls_x, cls_o, teacher_x, load_sem, save_sem = take(5)

        def load(number):
            return pltpu.make_async_copy(targets[number], weights[number], load_sem.at[number])

        def save(number, image):
            return pltpu.make_async_copy(
                kept[number].at[image], saved_out[number].at[image], save_sem.at[number, image]
            )

        def keep_values(first, image, values):
            for number, value in enumerate(values):
                kept[first + number][image] = value
                save(first + number, image).start()

        def run_first(net, image):
            if image == 0:
                load(3 * net).wait()
                load(3 * net + 1).wait()
            values = image_first(
                patches_ref[image],
                covered_ref[image] if net else None,
                weights[3 * net],
                weights[3 * net + 1],
                table_refs[2 * net],
                table_refs[2 * net + 1],
                hidden,
            )
            x2 = values[2]
            if net:
                keep_values(0, image, values)
            else:
                teacher_x[image] = x2
            cls_x[net, image : image + 1, :] = x2[pixel_rows : pixel_rows + 1, :]

        def run_second(net):
            load(3 * net + 2).wait()
            for image in range(images):
                values = image_second(
                    kept[2][image] if net else teacher_x[image],
                    weights[3 * net + 2],
                    table_refs[2 * net + 1],
                    pixel_rows,
                    net == 1,
                )
                if net:
                    keep_values(6, image, values[:-1])
                cls_o[net, image : image + 1, :] = values[-1][:1, :].astype(F32)
            out, x1c, mixed = class_forward(
                cls_x[net], cls_o[net], weights[3 * net + 2], table_refs[2 * net + 1], hidden
            )
            if net:
                cls_s[...] = out
                x1c_out[...] = x1c
                o1_out[...] = mixed
            else:
                cls_t[...] = out

        waiting = [
            (whole_at[3 * net + 1] + 1, functools.partial(run_first, net, image))
            for net in range(2)
            for image in range(images)
        ]
        waiting += [
            (whole_at[3 * net + 2] + 1, functools.partial(run_second, net)) for net in range(2)
        ]

        def between(item):
            if item == -1:
                cls_x[...] = jnp.zeros_like(cls_x)
                cls_o[...] = jnp.zeros_like(cls_o)
            if waiting and waiting[0][0] <= item:
                waiting.pop(0)[1]()
            for number in range(6):
                if whole_at[number] == item:
                    load(number).start()
            if item == len(items) - 1:
                while waiting:
                    waiting.pop(0)[1]()

        gather_kernel(
            items, early, lines, sources + dealt, head_refs, targets, between, *refs
        )
        for number in range(saved):
            for image in range(images):
                save(number, image).wait()

    anywhere = pl.BlockSpec(memory_space=pl.ANY)
    vmem = pl.BlockSpec(memory_space=pltpu.VMEM)
    shape = jax.ShapeDtypeStruct
    sems = pltpu.SemaphoreType.DMA
    out = pl.pallas_call(
        kernel,
        out_shape=[shape(dims, BF16) for dims in full]
        + [shape(dims, BF16) for dims in shapes[count:]]
        + [shape((TAIL, model), kind) for kind in (F32, F32, F32, BF16)]
        + [shape((images,) + dims, kind) for dims, kind in per_image],
        in_specs=[anywhere] * (count + len(heads)) + [vmem] * 6,
        out_specs=[anywhere] * (len(shapes) + extra) + [vmem] * 4 + [anywhere] * saved,
        scratch_shapes=[pltpu.VMEM(dims, BF16) for dims in full[:6]]
        + [pltpu.VMEM((images,) + dims, kind) for dims, kind in per_image]
        + [pltpu.VMEM((2, TAIL, model), F32)] * 2
        + [
            pltpu.VMEM((images, pixel_rows + TAIL, model), F32),
            sems((6,)),
            sems((saved, images)),
            sems((len(items), slots)),
            sems((len(items), slots)),
            sems((len(items),)),
            sems((len(items), fsdp_count)),
            sems((len(items),)),
        ],
        compiler_params=pltpu.CompilerParams(
            collective_id=collective_id, has_side_effects=True, vmem_limit_bytes=60 << 20
        ),
        name="gather_forward",
    )(*arrays, *heads, patches, covered[..., None], *tables)
    at = len(shapes) + extra
    cls_t, cls_s, x1c, o1 = out[at : at + 4]
    return out[: len(shapes)], cls_t, cls_s, list(out[at + 4 :]) + [x1c, o1]


def reduce_kernel(
    cuts, lines, places, part_of, squares, outs, work, mate_a, mate_b, facing, side,
    spread, landed, halves, result, vectors, norms, send, recv, send_z, recv_z, send_l, recv_l,
    send_f, recv_f
):
    patch_out, layers_out, vectors_out, norm_out = outs
    fsdp, dp = lax.axis_index("fsdp"), lax.axis_index("dp")
    z, x = fsdp // 2, fsdp % 2
    y, core = dp // 2, dp % 2
    across = z * 2 + 1 - x
    mate = y * 2 + 1 - core
    opposite = (1 - y) * 2 + core
    size = mate_a.shape[-1]
    lone = core == 1
    part = jnp.where(lone, 1, 2 * y)
    mate_part = jnp.where(lone, 2 * y, 1)

    barrier = pltpu.get_barrier_semaphore()

    def greet(f, d):
        pl.semaphore_signal(barrier, 1, device_id=(f, d), device_id_type=MESH)

    count = 2 * lines
    for step in range(1, count):
        greet(lax.rem(fsdp + step, count), dp)
    for step in range(1, 4):
        greet(fsdp, lax.rem(dp + step, 4))
    pl.semaphore_wait(barrier, count + 2)

    MATE_A, MATE_B, FACING, ACROSS = range(4)

    def move(cut, slot, source, target, f, d):
        return pltpu.make_async_remote_copy(
            src_ref=source,
            dst_ref=target,
            send_sem=send.at[cut, slot],
            recv_sem=recv.at[cut, slot],
            device_id=(f, d),
            device_id_type=MESH,
        )

    def columns(cut, which):
        return pl.ds(pl.multiple_of((3 * cut + which) * size, 128), size)

    def mine(cut, which):
        return part_of(cut, which, size)[...].astype(F32)

    def to_mate_a(cut):
        return move(cut, MATE_A, part_of(cut, mate_part, size), mate_a.at[cut], fsdp, mate)

    def to_mate_b(cut):
        return move(
            cut, MATE_B, part_of(cut, 2 - mate_part, size), mate_b.at[cut], fsdp, mate
        )

    def to_facing(cut):
        return move(cut, FACING, mate_b.at[cut], facing.at[cut], fsdp, opposite)

    def to_across(cut):
        return move(cut, ACROSS, mate_a.at[cut, :, 1 - x], side.at[cut], across, dp)

    def along(cut, to, source):
        return pltpu.make_async_remote_copy(
            src_ref=spread.at[cut, to],
            dst_ref=landed.at[cut, source],
            send_sem=send_z.at[cut, to],
            recv_sem=recv_z.at[cut, source],
            device_id=(2 * to + x, dp),
            device_id_type=MESH,
        )

    def share_of(cut, group):
        if group % 2:
            return halves.at[cut, group // 2]
        return result.at[:, columns(cut, group)]

    def hand(cut, group, to):
        place = share_of(cut, group)
        return pltpu.make_async_remote_copy(
            src_ref=place,
            dst_ref=place,
            send_sem=send_l.at[cut, to],
            recv_sem=recv_l.at[cut, group],
            device_id=(fsdp, to),
            device_id_type=MESH,
        )

    def step_0(cut):
        to_mate_a(cut).start()
        pl.when(lone)(lambda: to_mate_b(cut).start())

    def step_1(cut):
        @pl.when(jnp.logical_not(lone))
        def _():
            to_mate_b(cut).wait_recv()
            mate_b[cut] = (mine(cut, 2 - part) + mate_b[cut].astype(F32)).astype(BF16)
            to_facing(cut).start()

    def step_2(cut):
        to_mate_a(cut).wait_recv()

        @pl.when(lone)
        def _():
            mate_a[cut] = (mine(cut, 1) + mate_a[cut].astype(F32)).astype(BF16)

        @pl.when(jnp.logical_not(lone))
        def _():
            to_facing(cut).wait_recv()
            both = mine(cut, part) + mate_a[cut].astype(F32) + facing[cut].astype(F32)
            mate_a[cut] = both.astype(BF16)

        to_across(cut).start()

    def step_3(cut):
        to_across(cut).wait_recv()
        total = mate_a[cut, :, x].astype(F32) + side[cut].astype(F32)
        spread[cut] = total.astype(BF16)
        landed[cut, z] = spread[cut, z]
        for to in range(lines):
            pl.when(z != to)(lambda to=to: along(cut, to, z).start())

    def step_4(cut):
        for source in range(lines):
            pl.when(z != source)(lambda source=source: along(cut, source, source).wait_recv())
        total = landed[cut, 0].astype(F32)
        for source in range(1, lines):
            total = total + landed[cut, source].astype(F32)
        total = total.astype(BF16)
        for group in range(4):

            @pl.when(dp == group)
            def _(group=group):
                share_of(cut, group)[...] = total
                for to in range(4):
                    if to != group:
                        hand(cut, group, to).start()

    def step_5(cut):
        for group in range(4):
            pl.when(dp != group)(lambda group=group: hand(cut, group, group).wait_recv())
        both = halves[cut, 0].astype(F32) + halves[cut, 1].astype(F32)
        result[:, columns(cut, 1)] = both.astype(BF16)

    steps = [step_0, step_1, step_2, step_3, step_4, step_5]
    due, done, tick = [], [], 0
    while len(due) < cuts or min(done) < len(steps):
        ready, pause = work(tick)
        if len(due) < ready:
            due.append(tick)
            done.append(0)
        for cut in reversed(range(len(due))):
            if done[cut] < len(steps) and due[cut] <= tick:
                steps[done[cut]](cut)
                done[cut] += 1
                due[cut] = tick + pause
        tick += 1

    patch_at, patch_width, table_at, width, layer_spans = places
    vectors[fsdp] = result[:, table_at : table_at + width]
    total = squares[...]
    for at in range(0, result.shape[1], 128):
        value = result[:, at : at + 128].astype(F32)
        value = value * value
        for row in range(0, value.shape[0], 8):
            total = total + value[row : row + 8, :]
    norms[fsdp] = total

    def tell(kind, ref, step):
        return pltpu.make_async_remote_copy(
            src_ref=ref.at[fsdp],
            dst_ref=ref.at[fsdp],
            send_sem=send_f.at[kind, step - 1],
            recv_sem=recv_f.at[kind, fsdp],
            device_id=(lax.rem(fsdp + step, count), dp),
            device_id_type=MESH,
        )

    def told(kind, ref, step):
        peer = lax.rem(fsdp + step, count)
        return pltpu.make_async_remote_copy(
            src_ref=ref.at[peer],
            dst_ref=ref.at[peer],
            send_sem=send_f.at[kind, step - 1],
            recv_sem=recv_f.at[kind, peer],
            device_id=(peer, dp),
            device_id_type=MESH,
        )

    for kind, ref in enumerate((norms, vectors)):
        for step in range(1, count):
            tell(kind, ref, step).start()
    patch_out[...] = result[:, patch_at : patch_at + patch_width].astype(F32)
    for layer, to, start, span in layer_spans:
        layers_out[layer, :, to : to + span] = result[:, start : start + span].astype(F32)
    for kind, ref in enumerate((norms, vectors)):
        for step in range(1, count):
            told(kind, ref, step).wait_recv()
    vectors_out[...] = vectors[...].astype(F32)
    total = norms[0]
    for f in range(1, count):
        total = total + norms[f]
    norm_out[...] = total
    for kind, ref in enumerate((norms, vectors)):
        for step in range(1, count):
            tell(kind, ref, step).wait_send()
    for cut in range(cuts):
        to_mate_a(cut).wait_send()
        to_across(cut).wait_send()
        for to in range(lines):
            pl.when(z != to)(lambda to=to: along(cut, to, z).wait_send())
        for group in range(4):

            @pl.when(dp == group)
            def _(group=group):
                for to in range(4):
                    if to != group:
                        hand(cut, group, to).wait_send()

        pl.when(lone)(lambda: to_mate_b(cut).wait_send())
        pl.when(jnp.logical_not(lone))(lambda: to_facing(cut).wait_send())


GELU_A = 0.7978845608028654
GELU_B = 0.044715
TAIL = 16


def mm(left, right):
    return lax.dot_general(left, right, (((1,), (0,)), ((), ())), preferred_element_type=F32)


def mm_nt(left, right):
    return lax.dot_general(left, right, (((1,), (1,)), ((), ())), preferred_element_type=F32)


def mm_tn(left, right):
    return lax.dot_general(left, right, (((0,), (0,)), ((), ())), preferred_element_type=F32)


def norm_parts(x):
    centred = x - jnp.mean(x, -1, keepdims=True)
    lift = lax.rsqrt(jnp.mean(centred * centred, -1, keepdims=True) + 1e-06)
    return centred * lift, lift


def norm_back(grad, gain, unit_x, lift):
    inner = grad * gain
    return lift * (
        inner
        - jnp.mean(inner, -1, keepdims=True)
        - unit_x * jnp.mean(inner * unit_x, -1, keepdims=True)
    )


def gelu(x):
    return 0.5 * x * (1.0 + jnp.tanh(GELU_A * (x + GELU_B * (x * x * x))))


def gelu_both(x):
    square = x * x
    slope = jnp.tanh(GELU_A * x * (1.0 + GELU_B * square))
    half = 0.5 * (1.0 + slope)
    turn = half + 0.5 * x * (1.0 - slope * slope) * GELU_A * (1.0 + 3.0 * GELU_B * square)
    return x * half, turn


def half_masks(width):
    lane = lax.broadcasted_iota(jnp.int32, (1, 128), 1)
    first = (lane < width).astype(F32)
    return first, 1.0 - first


def column_sum(x):
    return jnp.sum(x, 0, keepdims=True)


def attend(q, keys, values, valid, scale, lse_store):
    rows, total = q.shape[0], keys.shape[0]
    masks = half_masks(64)
    column = lax.broadcasted_iota(jnp.int32, (rows, total), 1)
    lane = lax.broadcasted_iota(jnp.int32, (rows, 128), 1)
    mixed, lse = [], jnp.zeros((rows, 128), F32)
    for pair in range(HEADS // 2):
        span = slice(128 * pair, 128 * pair + 128)
        halves = []
        for side in range(2):
            asked = q[:, span] * (masks[side] * scale).astype(BF16)
            scores = mm_nt(asked, keys[:, span])
            scores = jnp.where(column < valid, scores, -1e30)
            top = jnp.max(scores, -1, keepdims=True)
            expo = jnp.exp(scores - top)
            total_e = jnp.sum(expo, -1, keepdims=True)
            halves.append(mm(expo.astype(BF16), values[:, span]) / total_e)
            if lse_store:
                lse = jnp.where(lane == 2 * pair + side, top + jnp.log(total_e), lse)
        mixed.append(jnp.where(lane < 64, halves[0], halves[1]))
    return jnp.concatenate(mixed, -1).astype(BF16), lse


def image_first(pixel_rows, hide, weight_p, weight_0, places, rows_table, hidden):
    model = weight_0.shape[0]
    count, pixels = pixel_rows.shape
    scale = (model // HEADS) ** -0.5
    keep = hide is not None

    def vec(row):
        return rows_table[row : row + 1, :]

    tokens = mm_nt(pixel_rows, weight_p[:, :pixels]) + vec(1)
    if keep:
        tokens = tokens * (1.0 - hide) + vec(0) * hide
    x = jnp.concatenate([tokens + places[:count, :], places[count:, :]], 0)
    unit_x, _ = norm_parts(x)
    low = (unit_x * vec(2) + vec(3)).astype(BF16)
    qkv = mm(low, weight_0[:, : 3 * model]).astype(BF16)
    mixture, lse = attend(
        qkv[:, :model], qkv[:, model : 2 * model], qkv[:, 2 * model :], count + 1, scale, keep
    )
    x1 = x + vec(4) * mm(mixture, weight_0[:, 3 * model : 4 * model])
    unit_x, _ = norm_parts(x1)
    low = (unit_x * vec(5) + vec(6)).astype(BF16)
    wide = gelu(mm(low, weight_0[:, 4 * model : 4 * model + hidden])).astype(BF16)
    x2 = x1 + vec(7) * mm_nt(wide, weight_0[:, 4 * model + hidden :])
    return x, x1, x2, qkv, mixture, lse


def image_second(x2, weight_1, rows_table, count, keep):
    model = weight_1.shape[0]
    scale = (model // HEADS) ** -0.5
    unit_x, _ = norm_parts(x2)
    low = (unit_x * rows_table[8:9, :] + rows_table[9:10, :]).astype(BF16)
    kv = mm(low, weight_1[:, model : 3 * model]).astype(BF16)
    q1 = mm(low[count:, :], weight_1[:, :model]).astype(BF16)
    mixture1, lse1 = attend(q1, kv[:, :model], kv[:, model:], count + 1, scale, keep)
    return kv, q1, lse1, mixture1


def class_forward(cls_x, cls_o, weight_1, rows_table, hidden):
    model = weight_1.shape[0]

    def row(index):
        return rows_table[8 + index : 9 + index, :]

    mixed = cls_o.astype(BF16)
    x1c = cls_x + row(2) * mm(mixed, weight_1[:, 3 * model : 4 * model])
    unit_c, _ = norm_parts(x1c)
    low_c = (unit_c * row(3) + row(4)).astype(BF16)
    wide_c = gelu(mm(low_c, weight_1[:, 4 * model : 4 * model + hidden])).astype(BF16)
    return x1c + row(5) * mm_nt(wide_c, weight_1[:, 4 * model + hidden :]), x1c, mixed


def saved_shapes(total, model):
    return [
        ((total, model), F32),
        ((total, model), F32),
        ((total, model), F32),
        ((total, 3 * model), BF16),
        ((total, model), BF16),
        ((total, 128), F32),
        ((total, 2 * model), BF16),
        ((TAIL, model), BF16),
        ((TAIL, 128), F32),
    ]


def forward_kernel(
    images, hidden, keep, patches, covered, weight_p, weight_0, weight_1, places, rows_table, *rest
):
    outs, (cls_x, cls_o) = rest[:-2], rest[-2:]
    image = pl.program_id(0)
    count = patches.shape[1]

    @pl.when(image == 0)
    def _():
        cls_x[...] = jnp.zeros_like(cls_x)
        cls_o[...] = jnp.zeros_like(cls_o)

    hide = covered[0] if keep else None
    values = image_first(patches[0], hide, weight_p, weight_0, places, rows_table, hidden)
    values += image_second(values[2], weight_1, rows_table, count, keep)
    cls_x[pl.ds(image, 1), :] = values[2][count : count + 1, :]
    cls_o[pl.ds(image, 1), :] = values[-1][:1, :].astype(F32)
    if keep:
        for number, value in enumerate(values[:-1]):
            outs[1 + number][0] = value

    @pl.when(image == images - 1)
    def _():
        out, x1c, mixed = class_forward(cls_x[...], cls_o[...], weight_1, rows_table, hidden)
        outs[0][...] = out
        if keep:
            outs[-2][...] = x1c
            outs[-1][...] = mixed


def fixed(shape):
    zeros = (0,) * len(shape)
    return pl.BlockSpec(shape, lambda i: zeros, pipeline_mode=pl.Buffered(1))


def each(shape):
    rest = (0,) * len(shape)
    return pl.BlockSpec((1,) + shape, lambda i: (i,) + rest)


def whole_out(shape):
    zeros = (0,) * len(shape)
    return pl.BlockSpec(shape, lambda i: zeros)


def split_table(vecs, count):
    places = jnp.concatenate(
        [
            vecs[1 : count + 1],
            vecs[:1] + vecs[count + 1 : count + 2],
            jnp.zeros((TAIL - 1, vecs.shape[1]), F32),
        ]
    )
    rows = vecs[count + 2 :]
    rows = jnp.concatenate([rows, jnp.zeros(((-rows.shape[0]) % 8, rows.shape[1]), F32)])
    return places, rows


def forward(patches, covered, weight_p, weight_0, weight_1, vecs, keep):
    images, count, pixels = patches.shape
    model, columns = weight_0.shape
    hidden = (columns - 4 * model) // 2
    total = count + TAIL
    places, rows = split_table(vecs, count)
    shape = jax.ShapeDtypeStruct
    outs = [shape((TAIL, model), F32)]
    out_specs = [whole_out((TAIL, model))]
    if keep:
        per_image = saved_shapes(total, model)
        outs += [shape((images,) + dims, kind) for dims, kind in per_image]
        out_specs += [each(dims) for dims, kind in per_image]
        outs += [shape((TAIL, model), F32), shape((TAIL, model), BF16)]
        out_specs += [whole_out((TAIL, model))] * 2
    return pl.pallas_call(
        functools.partial(forward_kernel, images, hidden, keep),
        grid=(images,),
        out_shape=outs,
        in_specs=[
            each((count, pixels)),
            each((count, 1)),
            fixed(weight_p.shape),
            fixed(weight_0.shape),
            fixed(weight_1.shape),
            fixed(places.shape),
            fixed(rows.shape),
        ],
        out_specs=out_specs,
        scratch_shapes=[pltpu.VMEM((TAIL, model), F32)] * 2,
        compiler_params=pltpu.CompilerParams(vmem_limit_bytes=56 << 20),
        name="backbone_forward",
    )(patches, covered[..., None], weight_p, weight_0, weight_1, places, rows)


def attend_back(grad_o, q, keys, values, lse, valid, scale):
    rows, total = q.shape[0], keys.shape[0]
    masks = half_masks(64)
    column = lax.broadcasted_iota(jnp.int32, (rows, total), 1)
    lane_row = lax.broadcasted_iota(jnp.int32, (rows, 128), 1)
    grad_q, grad_k, grad_v = [], [], []
    for pair in range(HEADS // 2):
        span = slice(128 * pair, 128 * pair + 128)
        out_q, out_k, out_v = [], None, None
        for side in range(2):
            mask = masks[side].astype(BF16)
            asked = q[:, span] * (masks[side] * scale).astype(BF16)
            given = grad_o[:, span] * mask
            head = 2 * pair + side
            scores = mm_nt(asked, keys[:, span])
            share = jnp.where(column < valid, jnp.exp(scores - lse[:, head : head + 1]), 0.0)
            grad_p = mm_nt(given, values[:, span])
            inner = jnp.sum(share * grad_p, -1, keepdims=True)
            grad_s = (share * (grad_p - inner)).astype(BF16)
            out_q.append(mm(grad_s, keys[:, span]))
            more_k = mm_tn(grad_s, asked)
            more_v = mm_tn(share.astype(BF16), given)
            out_k = more_k if out_k is None else out_k + more_k
            out_v = more_v if out_v is None else out_v + more_v
        grad_q.append(jnp.where(lane_row < 64, out_q[0], out_q[1]) * scale)
        grad_k.append(out_k)
        grad_v.append(out_v)
    return [jnp.concatenate(part, -1).astype(BF16) for part in (grad_q, grad_k, grad_v)]


def last_back_kernel(
    images, hidden, weight_1, rows_table, grad_cls, x2_in, kv_in, q1_in, lse1_in, x1c_in, o1_in,
    packed, grad_out, rows, acc_kv, acc_q, grad_c, grad_oc
):
    image = pl.program_id(0)
    model = weight_1.shape[0]
    count = x2_in.shape[1] - TAIL
    valid = count + 1
    scale = (model // HEADS) ** -0.5
    cut_o, cut_u, cut_d = 3 * model, 4 * model, 4 * model + hidden

    def row(index):
        return rows_table[8 + index : 9 + index, :]

    def add_row(index, value):
        rows[8 + index : 9 + index, :] += value

    @pl.when(image == 0)
    def _():
        for ref in (acc_kv, acc_q, rows):
            ref[...] = jnp.zeros_like(ref)
        grad_x = grad_cls[...]
        x1c = x1c_in[...]
        unit_x, lift = norm_parts(x1c)
        low = (unit_x * row(3) + row(4)).astype(BF16)
        wide, slope = gelu_both(mm(low, weight_1[:, cut_u:cut_d]))
        wide = wide.astype(BF16)
        down = mm_nt(wide, weight_1[:, cut_d:])
        add_row(5, column_sum(grad_x * down))
        grad_d = (grad_x * row(5)).astype(BF16)
        grad_u = (mm(grad_d, weight_1[:, cut_d:]) * slope).astype(BF16)
        packed[:, cut_d:] = mm_tn(grad_d, wide).astype(BF16)
        packed[:, cut_u:cut_d] = mm_tn(low, grad_u).astype(BF16)
        grad_n = mm_nt(grad_u, weight_1[:, cut_u:cut_d])
        add_row(3, column_sum(grad_n * unit_x))
        add_row(4, column_sum(grad_n))
        grad_x = grad_x + norm_back(grad_n, row(3), unit_x, lift)
        mixed = o1_in[...]
        add_row(2, column_sum(grad_x * mm(mixed, weight_1[:, cut_o:cut_u])))
        grad_a = (grad_x * row(2)).astype(BF16)
        packed[:, cut_o:cut_u] = mm_tn(mixed, grad_a).astype(BF16)
        grad_c[...] = grad_x
        grad_oc[...] = mm_nt(grad_a, weight_1[:, cut_o:cut_u])

    first_row = lax.broadcasted_iota(jnp.int32, (TAIL, 1), 0) == 0
    grad_o1 = jnp.where(first_row, grad_oc[pl.ds(image, 1), :], 0.0).astype(BF16)
    kv = kv_in[0]
    grad_q, grad_k, grad_v = attend_back(
        grad_o1, q1_in[0], kv[:, :model], kv[:, model:], lse1_in[0], valid, scale
    )
    unit_x, lift = norm_parts(x2_in[0])
    low = (unit_x * row(0) + row(1)).astype(BF16)
    grad_kv = jnp.concatenate([grad_k, grad_v], -1)
    acc_kv[...] += mm_tn(low, grad_kv)
    acc_q[...] += mm_tn(low[count:, :], grad_q)
    grad_n = mm_nt(grad_kv, weight_1[:, model : 3 * model])
    tail = grad_n[count:, :] + mm_nt(grad_q, weight_1[:, :model])
    grad_n = jnp.concatenate([grad_n[:count, :], tail], 0)
    add_row(0, column_sum(grad_n * unit_x))
    add_row(1, column_sum(grad_n))
    grad_x = norm_back(grad_n, row(0), unit_x, lift)
    tail = grad_x[count:, :] + jnp.where(first_row, grad_c[pl.ds(image, 1), :], 0.0)
    grad_out[0] = jnp.concatenate([grad_x[:count, :], tail], 0)

    @pl.when(image == images - 1)
    def _():
        packed[:, :model] = acc_q[...].astype(BF16)
        packed[:, model:cut_o] = acc_kv[...].astype(BF16)


def last_back(weight_1, rows, grad_cls, saved):
    x2, kv, q1, lse1, x1c, o1 = [saved[index] for index in (2, 6, 7, 8, 9, 10)]
    images = x2.shape[0]
    model, columns = weight_1.shape
    hidden = (columns - 4 * model) // 2
    shape = jax.ShapeDtypeStruct
    return pl.pallas_call(
        functools.partial(last_back_kernel, images, hidden),
        grid=(images,),
        out_shape=[shape(weight_1.shape, BF16), shape(x2.shape, F32), shape(rows.shape, F32)],
        in_specs=[fixed(weight_1.shape), fixed(rows.shape), fixed(grad_cls.shape)]
        + [each(array.shape[1:]) for array in (x2, kv, q1, lse1)]
        + [fixed(x1c.shape), fixed(o1.shape)],
        out_specs=[whole_out(weight_1.shape), each(x2.shape[1:]), whole_out(rows.shape)],
        scratch_shapes=[
            pltpu.VMEM((model, 2 * model), F32),
            pltpu.VMEM((model, model), F32),
            pltpu.VMEM((TAIL, model), F32),
            pltpu.VMEM((TAIL, model), F32),
        ],
        compiler_params=pltpu.CompilerParams(vmem_limit_bytes=48 << 20),
        name="last_layer_backward",
    )(weight_1, rows, grad_cls, x2, kv, q1, lse1, x1c, o1)


def first_back(refs, image, hidden, work, rows, store_mlp, store_mix, store_rest):
    patches, covered, weight_0, rows_table, grad_in, x0_in, x1_in, qkv_in, o0_in, lse0_in = refs
    model = weight_0.shape[0]
    images, count, pixels = patches.shape
    valid = count + 1
    scale = (model // HEADS) ** -0.5
    cut_o, cut_u, cut_d = 3 * model, 4 * model, 4 * model + hidden
    acc, acc_p, grad_s, grad_t, places = work

    def row(index):
        return rows_table[2 + index : 3 + index, :]

    def add_row(index, value):
        rows[2 + index : 3 + index, :] += value

    def add(ref, at, value):
        span = slice(at, at + value.shape[1])
        if image == 0:
            ref[:, span] = value
        else:
            ref[:, span] += value

    def mlp():
        grad_x = grad_in[image]
        unit_x, lift = norm_parts(x1_in[image])
        low = (unit_x * row(3) + row(4)).astype(BF16)
        wide, slope = gelu_both(mm(low, weight_0[:, cut_u:cut_d]))
        wide = wide.astype(BF16)
        down = mm_nt(wide, weight_0[:, cut_d:])
        add_row(5, column_sum(grad_x * down))
        grad_d = (grad_x * row(5)).astype(BF16)
        grad_u = (mm(grad_d, weight_0[:, cut_d:]) * slope).astype(BF16)
        add(acc, 0, mm_tn(low, grad_u))
        add(acc, hidden, mm_tn(grad_d, wide))
        grad_n = mm_nt(grad_u, weight_0[:, cut_u:cut_d])
        add_row(3, column_sum(grad_n * unit_x))
        add_row(4, column_sum(grad_n))
        grad_s[image] = grad_x + norm_back(grad_n, row(3), unit_x, lift)
        if image == images - 1:
            store_mlp()

    def attention():
        grad_x = grad_s[image]
        mixed = o0_in[image]
        add_row(2, column_sum(grad_x * mm(mixed, weight_0[:, cut_o:cut_u])))
        grad_a = (grad_x * row(2)).astype(BF16)
        add(acc, cut_o, mm_tn(mixed, grad_a))
        grad_o = mm_nt(grad_a, weight_0[:, cut_o:cut_u]).astype(BF16)
        qkv = qkv_in[image]
        grad_qkv = attend_back(
            grad_o, qkv[:, :model], qkv[:, model : 2 * model], qkv[:, 2 * model :],
            lse0_in[image], valid, scale,
        )
        grad_qkv = jnp.concatenate(grad_qkv, -1)
        grad_t[image] = grad_qkv
        unit_x, _ = norm_parts(x0_in[image])
        low = (unit_x * row(0) + row(1)).astype(BF16)
        add(acc, 0, mm_tn(low, grad_qkv))
        if image == images - 1:
            store_mix()

    def rest():
        grad_qkv = grad_t[image]
        unit_x, lift = norm_parts(x0_in[image])
        grad_n = mm_nt(grad_qkv, weight_0[:, :cut_o])
        add_row(0, column_sum(grad_n * unit_x))
        add_row(1, column_sum(grad_n))
        grad_x = grad_s[image] + norm_back(grad_n, row(0), unit_x, lift)
        places[...] += grad_x
        hide = covered[image]
        token = grad_x[:count, :]
        rows[0:1, :] += column_sum(token * hide)
        token = token * (1.0 - hide)
        rows[1:2, :] += column_sum(token)
        add(acc_p, 0, mm_tn(token.astype(BF16), patches[image]))
        if image == images - 1:
            store_rest()

    return mlp, attention, rest


def table_of(places, rows, count, total):
    table = jnp.concatenate(
        [places[count : count + 1, :], places[:count, :], places[count : count + 1, :], rows[...]],
        0,
    )
    return jnp.concatenate(
        [table, jnp.zeros((total - table.shape[0], table.shape[1]), F32)], 0
    )


def plan_of(pixels, columns, model, size):
    hidden = (columns - 4 * model) // 2
    patch_width = packed_width_p(pixels)
    patch_at = 2 * columns
    table_at = patch_at + patch_width
    width = (table_at + model + 3 * size - 1) // (3 * size) * 3 * size
    spans = (
        (1, 0, 0, columns),
        (0, 0, columns + 2 * hidden, 4 * model),
        (0, 4 * model, columns, 2 * hidden),
    )
    return (patch_at, patch_width, table_at, model, spans), width


def first_back_kernel(images, hidden, *refs):
    ins, (rows_in, tail, *work, rows) = refs[:10], refs[10:]
    start_sums(work[-1], rows, rows_in)
    run = back_pieces(ins, images, hidden, work, rows, tail, lambda value: value.astype(BF16))
    for piece, _ in run:
        piece()


def back_pieces(ins, images, hidden, work, rows, tail, shaped):
    acc, acc_p, _, _, places = work
    model = acc.shape[0]
    _, count, pixels = ins[0].shape
    mix = 2 * hidden
    patch_at = mix + 4 * model
    table_at = patch_at + packed_width_p(pixels)

    def store_mlp():
        tail[..., :mix] = shaped(acc[:, :mix])

    def store_mix():
        tail[..., mix:patch_at] = shaped(acc[:, : 4 * model])

    def store_rest():
        spare = tail.shape[-1] - table_at - model
        ends = [acc_p[...], jnp.zeros((model, packed_width_p(pixels) - pixels), F32)]
        ends.append(table_of(places, rows, count, model))
        if spare:
            ends.append(jnp.zeros((model, spare), F32))
        tail[..., patch_at:] = shaped(jnp.concatenate(ends, -1))

    blocks = [
        first_back(ins, image, hidden, work, rows, store_mlp, store_mix, store_rest)
        for image in range(images)
    ]
    return [
        (blocks[image][phase], phase + (image == images - 1))
        for phase in range(3)
        for image in range(images)
    ]


def start_sums(places, rows, rows_in):
    places[...] = jnp.zeros_like(places)
    rows[...] = rows_in[...]


def back_scratch(images, total, model, hidden, pixels, rows_shape):
    return [
        pltpu.VMEM((model, max(2 * hidden, 4 * model)), F32),
        pltpu.VMEM((model, pixels), F32),
        pltpu.VMEM((images, total, model), F32),
        pltpu.VMEM((images, total, 3 * model), BF16),
        pltpu.VMEM((total, model), F32),
        pltpu.VMEM(rows_shape, F32),
    ]


def first_back_plain(patches, covered, weight_0, rows, grad_in, saved, rows_in, width):
    images, count, pixels = patches.shape
    model, columns = weight_0.shape
    hidden = (columns - 4 * model) // 2
    ins = [patches, covered[..., None], weight_0, rows, grad_in]
    ins += [saved[index] for index in (0, 1, 3, 4, 5)] + [rows_in]
    vmem = pl.BlockSpec(memory_space=pltpu.VMEM)
    return pl.pallas_call(
        functools.partial(first_back_kernel, images, hidden),
        out_shape=jax.ShapeDtypeStruct((model, width), BF16),
        in_specs=[vmem] * len(ins),
        out_specs=vmem,
        scratch_shapes=back_scratch(images, count + TAIL, model, hidden, pixels, rows.shape),
        compiler_params=pltpu.CompilerParams(vmem_limit_bytes=58 << 20),
        name="first_layer_backward",
    )(*ins)


def back_reduce(
    patches, covered, weight_0, rows, grad_in, saved, rows_in, grads_1, squares, fsdp_count,
    collective_id
):
    images, count, pixels = patches.shape
    model, columns = weight_0.shape
    hidden = (columns - 4 * model) // 2
    size = model
    places, width = plan_of(pixels, columns, model, size)
    lines, own = fsdp_count // 2, model // fsdp_count
    cuts = width // (3 * size)
    last_cuts = columns // (3 * size)
    mlp_cuts = last_cuts + 2 * hidden // (3 * size)
    mix_cuts = 2 * last_cuts
    split = (lines, 2, own)
    ins = [patches, covered[..., None], weight_0, rows, grad_in]
    ins += [saved[index] for index in (0, 1, 3, 4, 5)]
    ins += [rows_in, grads_1.reshape(split + (columns,)), squares]
    blocks = (cuts,) + split + (size,)

    def kernel(*refs):
        parts, (rows_ref, grads_ref, squares_ref) = refs[:10], refs[10:13]
        outs, tail = refs[13:17], refs[17]
        work, rows_s, rest = refs[18:23], refs[23], refs[24:]
        whole = [last_cuts, mlp_cuts, mix_cuts, cuts]
        ready = [last_cuts]

        def shaped(value):
            return value.reshape(split + (value.shape[1],)).astype(BF16)

        start_sums(work[-1], rows_s, rows_ref)
        queue = back_pieces(parts, images, hidden, work, rows_s, tail, shaped)

        def part_of(cut, which, size):
            ref = grads_ref if cut < last_cuts else tail
            at = cut if cut < last_cuts else cut - last_cuts
            return ref.at[:, :, :, pl.ds(pl.multiple_of((3 * at + which) * size, 128), size)]

        def between(tick):
            if tick and queue:
                piece, done = queue.pop(0)
                piece()
                ready[0] = whole[done]
            return ready[0], 2 if queue else 1

        reduce_kernel(cuts, lines, places, part_of, squares_ref, outs, between, *rest)

    shape = jax.ShapeDtypeStruct
    sems = pltpu.SemaphoreType.DMA
    vmem = pl.BlockSpec(memory_space=pltpu.VMEM)
    return pl.pallas_call(
        kernel,
        out_shape=[
            shape((own, places[1]), F32),
            shape((2, own, columns), F32),
            shape((fsdp_count, own, model), F32),
            shape((8, 128), F32),
        ],
        in_specs=[vmem] * len(ins),
        out_specs=[vmem] * 4,
        scratch_shapes=[pltpu.VMEM(split + (width - columns,), BF16)]
        + back_scratch(images, count + TAIL, model, hidden, pixels, rows.shape)
        + [pltpu.VMEM(blocks, BF16)] * 3
        + [pltpu.VMEM((cuts, lines, own, size), BF16)] * 3
        + [
            pltpu.VMEM((cuts, 2, own, size), BF16),
            pltpu.VMEM((own, width), BF16),
            pltpu.VMEM((fsdp_count, own, model), BF16),
            pltpu.VMEM((fsdp_count, 8, 128), F32),
            sems((cuts, 4)),
            sems((cuts, 4)),
            sems((cuts, lines)),
            sems((cuts, lines)),
            sems((cuts, 4)),
            sems((cuts, 4)),
            sems((2, fsdp_count - 1)),
            sems((2, fsdp_count)),
        ],
        compiler_params=pltpu.CompilerParams(
            collective_id=collective_id, has_side_effects=True, vmem_limit_bytes=60 << 20
        ),
        name="back_reduce",
    )(*ins)


def packed_width_p(pixels):
    return (pixels + 127) // 128 * 128


def owners_of(low, high, rows, count):
    return [f for f in range(count) if f * rows < high and (f + 1) * rows > low]


def two_halves(value):
    half = value.shape[1] // 2
    return jnp.concatenate([value[:, :half], value[:, half:]], 0).astype(BF16)


def from_halves(slots):
    wide = slots.astype(F32)
    half = wide.shape[-1]
    first = wide[:, :8, :].reshape(-1, half)
    second = wide[:, 8:, :].reshape(-1, half)
    return jnp.concatenate([first, second], -1)


def student_rows(value, start=0):
    pieces = [value[at + start : at + start + 4, :] for at in range(0, value.shape[0], 8)]
    return jnp.concatenate(pieces, 0)


def sixteen(value):
    return jnp.concatenate([value, jnp.zeros_like(value)], 0).astype(BF16)


def head_kernel(
    sizes, cls, gains, first_s, first_t, third_s, third_t, shard_s, shard_t, centre, counted_row,
    counted_col, proto_s, proto_t,
    grad_cls, ends, loss_row, totals, grad_logits, unit_rows, grad_head, squares,
    table_s, table_t, loading, wide_s, wide_t, kept, left, acts, parts_out, parts_in, units,
    stats, pulls, pulled, backs, pieces, pieced, extra_1, extra_3, lefts, rights, tall,
    send, recv, send_z, recv_z, send_x, recv_x, send_d, recv_d,
):
    count, dp_count, rows, chunk = sizes
    fsdp, dp = lax.axis_index("fsdp"), lax.axis_index("dp")
    model, hidden = first_s.shape
    width = third_s.shape[0]
    top_2, top_3 = model, model + hidden
    top_4 = top_3 + width
    span = kept.shape[0] // 2
    base = fsdp * rows // 128 * 128
    offset = fsdp * rows - base
    slot_rows = 8 * count
    is_student = lax.broadcasted_iota(jnp.int32, (8, 1), 0) < 4
    owners_1 = owners_of(0, top_2, rows, count)
    owners_2 = owners_of(top_2, top_3, rows, count)
    owners_3 = owners_of(top_3, top_4, rows, count)

    load_s = pltpu.make_async_copy(proto_s, table_s, loading.at[0])
    load_t = pltpu.make_async_copy(proto_t, table_t, loading.at[1])
    load_s.start()
    load_t.start()

    barrier = pltpu.get_barrier_semaphore()
    for f_step in range(count):
        for d_step in range(dp_count):
            if f_step or d_step:
                peer_f = lax.rem(fsdp + f_step, count)
                peer_d = lax.rem(dp + d_step, dp_count)
                pl.semaphore_signal(barrier, 1, device_id=(peer_f, peer_d), device_id_type=MESH)
    pl.semaphore_wait(barrier, count * dp_count - 1)

    ACTS, PARTS, STATS, PULLS, BACKS, PIECES, TOTALS = range(7)

    def swap(kind, step, source_of, target):
        peer = lax.rem(fsdp + step, count)
        return pltpu.make_async_remote_copy(
            src_ref=source_of(peer),
            dst_ref=target.at[fsdp],
            send_sem=send.at[kind, step - 1],
            recv_sem=recv.at[kind, fsdp],
            device_id=(peer, dp),
            device_id_type=MESH,
        )

    def begin(kind, source_of, target):
        for step in range(1, count):
            swap(kind, step, source_of, target).start()

    def arrive(kind, target):
        for step in range(1, count):
            peer = lax.rem(fsdp + step, count)
            pltpu.make_async_remote_copy(
                src_ref=target.at[peer],
                dst_ref=target.at[peer],
                send_sem=send.at[kind, step - 1],
                recv_sem=recv.at[kind, peer],
                device_id=(peer, dp),
                device_id_type=MESH,
            ).wait_recv()

    def end(kind, source_of, target):
        for step in range(1, count):
            swap(kind, step, source_of, target).wait_send()

    def each_net(value, first, second, product):
        low = sixteen(value)
        return jnp.where(is_student, product(low, first)[:8, :], product(low, second)[:8, :])

    unit_c, lift_c = norm_parts(cls[...])
    normed = unit_c * gains[:8, :] + gains[8:, :]
    pre_a = each_net(normed, first_s[...], first_t[...], mm)
    act_a, slope_a = gelu_both(pre_a)
    acts[fsdp] = two_halves(act_a)
    begin(ACTS, lambda peer: acts.at[fsdp], acts)

    row = fsdp * rows + lax.broadcasted_iota(jnp.int32, (rows, 1), 0)
    inside = (row >= top_2) & (row < top_3)
    kept[...] = jnp.zeros_like(kept)
    place = pl.multiple_of(offset, 16)
    kept[pl.ds(place, rows), :] = jnp.where(inside, shard_s[...], 0.0).astype(BF16)
    kept[pl.ds(pl.multiple_of(span + offset, 16), rows), :] = jnp.where(
        inside, shard_t[...], 0.0
    ).astype(BF16)
    left[...] = jnp.zeros_like(left)
    columns = pl.ds(pl.multiple_of(base, 128), span)

    arrive(ACTS, acts)
    left[:, top_2:top_3] = from_halves(acts[...])
    asked = left[:, columns].astype(BF16)
    net = lax.broadcasted_iota(jnp.int32, (slot_rows, 1), 0) % 8 < 4
    product = jnp.where(net, mm(asked, kept[:span, :]), mm(asked, kept[span:, :]))
    for f in range(count):
        parts_out[f] = two_halves(product[8 * f : 8 * f + 8, :])
    parts_in[fsdp] = parts_out[fsdp]
    begin(PARTS, lambda peer: parts_out.at[peer], parts_in)
    arrive(PARTS, parts_in)
    summed = from_halves(parts_in[...])
    pre_b = summed[:8, :]
    for f in range(1, count):
        pre_b = pre_b + summed[8 * f : 8 * f + 8, :]
    act_b, slope_b = gelu_both(pre_b)
    raw = each_net(act_b, third_s[...], third_t[...], mm_nt)
    lift_z = lax.rsqrt(jnp.sum(raw * raw, -1, keepdims=True) + 1e-06)
    unit_z = raw * lift_z

    me = fsdp * dp_count + dp
    everyone = count * dp_count
    units[me] = two_halves(unit_z)

    def unit_copy(step):
        peer = lax.rem(me + step, everyone)
        return pltpu.make_async_remote_copy(
            src_ref=units.at[me],
            dst_ref=units.at[me],
            send_sem=send_z.at[step - 1],
            recv_sem=recv_z.at[me],
            device_id=(peer // dp_count, lax.rem(peer, dp_count)),
            device_id_type=MESH,
        )

    for step in range(1, everyone):
        unit_copy(step).start()

    def owner_copy(kind, owner, source, target):
        return pltpu.make_async_remote_copy(
            src_ref=source,
            dst_ref=target.at[fsdp],
            send_sem=send_x.at[kind, owner],
            recv_sem=recv_x.at[kind, fsdp],
            device_id=(owner, dp),
            device_id_type=MESH,
        )

    def owners_begin(kind, owners, target, value):
        target[fsdp] = value
        for owner in owners:
            pl.when(fsdp != owner)(
                lambda owner=owner: owner_copy(kind, owner, target.at[fsdp], target).start()
            )

    def owners_end(kind, owners, target):
        for owner in owners:
            pl.when(fsdp != owner)(
                lambda owner=owner: owner_copy(kind, owner, target.at[fsdp], target).wait_send()
            )

    def owners_arrive(kind, owners, target):
        for owner in owners:

            @pl.when(fsdp == owner)
            def _(owner=owner):
                for f in range(count):
                    if f != owner:
                        pltpu.make_async_remote_copy(
                            src_ref=target.at[f],
                            dst_ref=target.at[f],
                            send_sem=send_x.at[kind, owner],
                            recv_sem=recv_x.at[kind, f],
                            device_id=(f, dp),
                            device_id_type=MESH,
                        ).wait_recv()

    for step in range(1, everyone):
        peer = lax.rem(me + step, everyone)
        pltpu.make_async_remote_copy(
            src_ref=units.at[peer],
            dst_ref=units.at[peer],
            send_sem=send_z.at[step - 1],
            recv_sem=recv_z.at[peer],
            device_id=(peer // dp_count, lax.rem(peer, dp_count)),
            device_id_type=MESH,
        ).wait_recv()
    all_units = from_halves(units[...])
    all_units_s = student_rows(all_units)
    rows_s = all_units_s.astype(BF16)
    rows_t = student_rows(all_units, 4).astype(BF16)
    unit_rows[...] = rows_s

    load_s.wait()
    load_t.wait()
    images = rows_s.shape[0]
    chunks = table_s.shape[0] // chunk
    low_start = jnp.full((images, 128), -3.0e38, F32)

    def lanes(op, value):
        out = value[:, :128]
        for at in range(128, value.shape[1], 128):
            out = op(out, value[:, at : at + 128])
        return out

    def logits_pass(index, tops):
        top_t, top_s = tops
        at = pl.ds(pl.multiple_of(index * chunk, chunk), chunk)
        raw_t = mm_nt(rows_t, table_t[at, :].astype(BF16))
        totals[fsdp, pl.ds(index, 1), :] = column_sum(counted_col[...] * raw_t)
        scaled_t = (raw_t - centre[:, at]) * (1.0 / TEACHER_TEMP)
        scaled_s = mm_nt(rows_s, table_s[at, :].astype(BF16)) * (1.0 / STUDENT_TEMP)
        wide_t[:, at] = scaled_t
        wide_s[:, at] = scaled_s
        return (
            jnp.maximum(top_t, lanes(jnp.maximum, scaled_t)),
            jnp.maximum(top_s, lanes(jnp.maximum, scaled_s)),
        )

    top_t, top_s = lax.fori_loop(0, chunks, logits_pass, (low_start, low_start))
    top_t = jnp.max(top_t, -1, keepdims=True)
    top_s = jnp.max(top_s, -1, keepdims=True)
    begin(TOTALS, lambda peer: totals.at[fsdp], totals)

    def expo_pass(index, sums):
        sum_t, sum_s, cross = sums
        at = pl.ds(pl.multiple_of(index * chunk, chunk), chunk)
        shifted_s = wide_s[:, at] - top_s
        expo_t = jnp.exp(wide_t[:, at] - top_t)
        expo_s = jnp.exp(shifted_s)
        wide_t[:, at] = expo_t
        wide_s[:, at] = expo_s
        return (
            sum_t + lanes(jnp.add, expo_t),
            sum_s + lanes(jnp.add, expo_s),
            cross + lanes(jnp.add, expo_t * shifted_s),
        )

    zero = jnp.zeros((images, 128), F32)
    sum_t, sum_s, cross = lax.fori_loop(0, chunks, expo_pass, (zero, zero, zero))
    lane = lax.broadcasted_iota(jnp.int32, (images, 128), 1)
    columns_of = zero
    values = (top_t, jnp.sum(sum_t, -1, keepdims=True), top_s, jnp.sum(sum_s, -1, keepdims=True),
              jnp.sum(cross, -1, keepdims=True))
    for number, value in enumerate(values):
        columns_of = jnp.where(lane == number, value, columns_of)
    stats[fsdp] = columns_of.T[:8, :]
    begin(STATS, lambda peer: stats.at[fsdp], stats)
    arrive(STATS, stats)
    gathered = [stats[f] for f in range(count)]
    high_t, high_s = gathered[0][0:1, :], gathered[0][2:3, :]
    for part in gathered[1:]:
        high_t = jnp.maximum(high_t, part[0:1, :])
        high_s = jnp.maximum(high_s, part[2:3, :])
    total_t = total_s = crossed = jnp.zeros_like(high_t)
    for part in gathered:
        lift_t = jnp.exp(part[0:1, :] - high_t)
        total_t = total_t + part[1:2, :] * lift_t
        total_s = total_s + part[3:4, :] * jnp.exp(part[2:3, :] - high_s)
        crossed = crossed + lift_t * (part[4:5, :] + (part[2:3, :] - high_s) * part[1:2, :])
    counted = counted_row[...]
    loss_row[...] = counted * (jnp.log(total_s) - crossed / total_t)
    weighting = counted / jnp.maximum(jnp.sum(counted, -1, keepdims=True), 1.0) / STUDENT_TEMP
    mine = stats[fsdp]
    share_s = weighting * jnp.exp(mine[2:3, :] - high_s) / total_s
    share_t = weighting * jnp.exp(mine[0:1, :] - high_t) / total_t
    turned = jnp.concatenate([share_s, share_t, jnp.zeros((126, images), F32)], 0).T
    share_s, share_t = turned[:, 0:1], turned[:, 1:2]

    turned_rows = all_units_s.T.astype(BF16)
    squares[...] = jnp.zeros_like(squares)

    def add_squares(value):
        total = squares[...]
        for row in range(0, value.shape[0], 8):
            strip = value[row : row + 8, :]
            total = total + lanes(jnp.add, strip * strip)
        squares[...] = total

    def grad_pass(index, total):
        at = pl.ds(pl.multiple_of(index * chunk, chunk), chunk)
        low = (wide_s[:, at] * share_s - wide_t[:, at] * share_t).astype(BF16)
        grad_logits[:, at] = low
        add_squares(mm(turned_rows, low))
        return total + mm(low, table_s[at, :].astype(BF16))

    partial = lax.fori_loop(0, chunks, grad_pass, jnp.zeros((images, width), F32))
    for slot in range(0, everyone, 2):
        pair = partial[4 * slot : 4 * slot + 8, :]
        pulls[slot] = pair
        pulls[slot + 1] = jnp.concatenate([pair[4:, :], pair[:4, :]], 0)
    pulled[fsdp] = pulls[me]
    begin(PULLS, lambda peer: pulls.at[peer * dp_count + dp], pulled)
    arrive(PULLS, pulled)
    grad_z = pulled[0]
    for f in range(1, count):
        grad_z = grad_z + pulled[f]
    grad_z = jnp.where(is_student, grad_z, 0.0)
    grad_raw = lift_z * (grad_z - unit_z * jnp.sum(unit_z * grad_z, -1, keepdims=True))
    grad_b = mm(sixteen(grad_raw), third_s[...])[:8, :]
    pre_grad_b = jnp.where(is_student, grad_b * slope_b, 0.0)
    backs[fsdp] = two_halves(pre_grad_b)
    begin(BACKS, lambda peer: backs.at[fsdp], backs)
    arrive(BACKS, backs)
    grads_b = from_halves(backs[...])
    piece = mm_nt(grads_b.astype(BF16), kept[:span, :])
    for f in range(count):
        pieces[f] = piece[8 * f : 8 * f + 8, :]
    pieced[fsdp] = pieces[fsdp]
    begin(PIECES, lambda peer: pieces.at[peer], pieced)

    owned = [
        (fsdp >= owners[0]) & (fsdp <= owners[-1]) for owners in (owners_1, owners_2, owners_3)
    ]

    def group_copy(kind, step, place):
        peer = lax.rem(dp + step, dp_count)
        return pltpu.make_async_remote_copy(
            src_ref=place(dp),
            dst_ref=place(dp),
            send_sem=send_d.at[kind, step - 1],
            recv_sem=recv_d.at[kind, dp],
            device_id=(fsdp, peer),
            device_id_type=MESH,
        )

    def group_arrive(kind, place):
        for step in range(1, dp_count):
            peer = lax.rem(dp + step, dp_count)
            pltpu.make_async_remote_copy(
                src_ref=place(peer),
                dst_ref=place(peer),
                send_sem=send_d.at[kind, step - 1],
                recv_sem=recv_d.at[kind, peer],
                device_id=(fsdp, peer),
                device_id_type=MESH,
            ).wait_recv()

    def right_at(number):
        return lambda group: rights.at[group, number]

    def left_at(group):
        return lefts.at[group]

    def group_begin(kind, place):
        for step in range(1, dp_count):
            group_copy(kind, step, place).start()

    def group_end(kind, place):
        for step in range(1, dp_count):
            group_copy(kind, step, place).wait_send()

    @pl.when(owned[1])
    def _():
        rights[dp, 1] = student_rows(grads_b).astype(BF16)
        group_begin(2, right_at(1))

    owners_begin(1, owners_3, extra_3, two_halves(jnp.concatenate([act_b, grad_raw], -1)))
    arrive(PIECES, pieced)
    back_a = jnp.zeros((8, left.shape[1]), F32)
    for f in range(count):
        at = f * rows // 128 * 128
        value = [pieced[f]]
        if at:
            value = [jnp.zeros((8, at), F32)] + value
        if left.shape[1] - at - span:
            value = value + [jnp.zeros((8, left.shape[1] - at - span), F32)]
        back_a = back_a + jnp.concatenate(value, -1)
    pre_grad_a = jnp.where(is_student, back_a[:, top_2:top_3] * slope_a, 0.0)
    spare = jnp.zeros((8, 2 * extra_1.shape[2] - model - hidden), F32)
    owners_begin(
        0, owners_1, extra_1, two_halves(jnp.concatenate([normed, pre_grad_a, spare], -1))
    )
    grad_n = jnp.where(is_student, mm_nt(sixteen(pre_grad_a), first_s[...])[:8, :], 0.0)
    grad_cls[...] = norm_back(grad_n, gains[:8, :], unit_c, lift_c)
    ends[...] = jnp.concatenate(
        [column_sum(grad_n * unit_c), column_sum(grad_n), jnp.zeros((6, model), F32)], 0
    )

    owners_arrive(1, owners_3, extra_3)

    @pl.when(owned[2])
    def _():
        extra = from_halves(extra_3[...])
        left[:, top_3:top_4] = extra[:, hidden:]
        rights[dp, 2] = student_rows(extra[:, :hidden]).astype(BF16)
        group_begin(3, right_at(2))

    owners_arrive(0, owners_1, extra_1)

    @pl.when(owned[0])
    def _():
        extra = from_halves(extra_1[...])
        left[:, :top_2] = extra[:, :model]
        rights[dp, 0] = student_rows(extra[:, model : model + hidden]).astype(BF16)
        group_begin(1, right_at(0))

    lefts[dp] = student_rows(left[:, columns]).astype(BF16)
    group_begin(0, left_at)
    group_arrive(0, left_at)
    tall[...] = jnp.zeros_like(tall)
    column = base + lax.broadcasted_iota(jnp.int32, (1, span), 1)
    for number, (low, high) in enumerate(((0, top_2), (top_2, top_3), (top_3, top_4))):

        @pl.when(owned[number])
        def _(number=number, low=low, high=high):
            group_arrive(1 + number, right_at(number))
            own_side = jnp.concatenate([lefts[group] for group in range(dp_count)], 0)
            keep_columns = ((column >= low) & (column < high)).astype(F32)
            own_side = (own_side.astype(F32) * keep_columns).astype(BF16)
            other = jnp.concatenate([rights[group, number] for group in range(dp_count)], 0)
            tall[...] += mm_tn(own_side, other)
            group_end(1 + number, right_at(number))

    grad_head[...] = tall[pl.ds(place, rows), :]

    def square_pass(index, carry):
        add_squares(grad_head[pl.ds(pl.multiple_of(index * 16, 16), 16), :])
        return carry

    lax.fori_loop(0, rows // 16, square_pass, 0)
    group_end(0, left_at)
    arrive(TOTALS, totals)
    end(ACTS, lambda peer: acts.at[fsdp], acts)
    end(PARTS, lambda peer: parts_out.at[peer], parts_in)
    end(STATS, lambda peer: stats.at[fsdp], stats)
    end(PULLS, lambda peer: pulls.at[peer * dp_count + dp], pulled)
    end(BACKS, lambda peer: backs.at[fsdp], backs)
    end(PIECES, lambda peer: pieces.at[peer], pieced)
    end(TOTALS, lambda peer: totals.at[fsdp], totals)
    for step in range(1, everyone):
        unit_copy(step).wait_send()
    owners_end(0, owners_1, extra_1)
    owners_end(1, owners_3, extra_3)


def head_step(
    cls_s, cls_t, vecs_s, vecs_t, weights, shards, centre, counted, protos, counts, collective_id
):
    count, dp_count = counts
    model, hidden = weights[0].shape
    width = weights[2].shape[0]
    rows = shards[0].shape[0]
    owned_k = protos[0].shape[0]
    images = counted.shape[0]
    everyone = count * dp_count
    span = max(f * rows % 128 + rows for f in range(count))
    span = (span + 127) // 128 * 128
    extent = max(f * rows // 128 * 128 + span for f in range(count))
    chunk = 1024
    cls = jnp.concatenate([cls_s[:4], cls_t[:4]])
    gains = jnp.concatenate(
        [
            jnp.broadcast_to(vecs[vecs.shape[0] + row][None], (4, model))
            for row in (-2, -1)
            for vecs in (vecs_s, vecs_t)
        ]
    )
    shape = jax.ShapeDtypeStruct
    vmem = pl.BlockSpec(memory_space=pltpu.VMEM)
    anywhere = pl.BlockSpec(memory_space=pl.ANY)
    extra_width = (model + hidden + 255) // 256 * 128
    sems = pltpu.SemaphoreType.DMA
    return pl.pallas_call(
        functools.partial(head_kernel, (count, dp_count, rows, chunk)),
        out_shape=[
            shape((8, model), F32),
            shape((8, model), F32),
            shape((1, images), F32),
            shape((count, owned_k // chunk, chunk), F32),
            shape((images, owned_k), BF16),
            shape((images, width), BF16),
            shape((rows, hidden), F32),
            shape((8, 128), F32),
        ],
        in_specs=[vmem] * 11 + [anywhere] * 2,
        out_specs=[vmem] * 8,
        scratch_shapes=[
            pltpu.VMEM((owned_k, width), F32),
            pltpu.VMEM((owned_k, width), F32),
            sems((2,)),
            pltpu.VMEM((images, owned_k), F32),
            pltpu.VMEM((images, owned_k), F32),
            pltpu.VMEM((2 * span, hidden), BF16),
            pltpu.VMEM((8 * count, extent), F32),
            pltpu.VMEM((count, 16, hidden // 2), BF16),
            pltpu.VMEM((count, 16, hidden // 2), BF16),
            pltpu.VMEM((count, 16, hidden // 2), BF16),
            pltpu.VMEM((everyone, 16, width // 2), BF16),
            pltpu.VMEM((count, 8, 128), F32),
            pltpu.VMEM((everyone, 8, width), F32),
            pltpu.VMEM((count, 8, width), F32),
            pltpu.VMEM((count, 16, hidden // 2), BF16),
            pltpu.VMEM((count, 8, span), F32),
            pltpu.VMEM((count, 8, span), F32),
            pltpu.VMEM((count, 16, extra_width), BF16),
            pltpu.VMEM((count, 16, (hidden + width) // 2), BF16),
            pltpu.VMEM((dp_count, 4 * count, span), BF16),
            pltpu.VMEM((dp_count, 3, 4 * count, hidden), BF16),
            pltpu.VMEM((span, hidden), F32),
            sems((7, count - 1)),
            sems((7, count)),
            sems((everyone - 1,)),
            sems((everyone,)),
            sems((2, count)),
            sems((2, count)),
            sems((4, dp_count - 1)),
            sems((4, dp_count)),
        ],
        compiler_params=pltpu.CompilerParams(
            collective_id=collective_id, has_side_effects=True, vmem_limit_bytes=60 << 20
        ),
        name="head_step",
    )(
        cls, gains, *weights, *shards, centre[None], counted[None], counted[:, None], *protos
    )


def dot(left, right, dims):
    return lax.dot_general(left, right, (dims, ((), ())), preferred_element_type=F32)


def layer_norm(x, gain, shift):
    centred = x - jnp.mean(x, -1, keepdims=True)
    spread = jnp.mean(centred * centred, -1, keepdims=True)
    return centred * lax.rsqrt(spread + 1e-06) * gain + shift


def gelu_slope(x):
    _, pull = jax.vjp(jax.nn.gelu, x)
    return pull(jnp.ones_like(x))[0]


def head_forward(cls, weight, vecs):
    width, hidden = cls.shape[1], weight.shape[1]
    low_n = layer_norm(cls, vecs[-2], vecs[-1]).astype(BF16)
    pre_a = jnp.dot(low_n, weight[:width], preferred_element_type=F32)
    low_a = jax.nn.gelu(pre_a).astype(BF16)
    pre_b = jnp.dot(low_a, weight[width : width + hidden], preferred_element_type=F32)
    low_b = jax.nn.gelu(pre_b).astype(BF16)
    raw = dot(low_b, weight[width + hidden :], ((1,), (1,)))
    return low_n, pre_a, low_a, pre_b, low_b, raw


def unit(raw):
    return raw * lax.rsqrt(jnp.sum(raw * raw, -1, keepdims=True) + 1e-06)


def adamw(weight, moment, second, gradient, factor, step_rate, weight_decay):
    clipped = gradient * factor
    moment = BETA_ONE * moment + (1.0 - BETA_ONE) * clipped
    second = BETA_TWO * second + (1.0 - BETA_TWO) * clipped * clipped
    direction = (
        moment / (1.0 - BETA_ONE**STEP) / (jnp.sqrt(second / (1.0 - BETA_TWO**STEP)) + 1e-08)
    )
    return (weight - step_rate * (direction + weight_decay * weight), moment, second)


def own_kernels(local, head_rows, model, hidden, total, layer_columns):
    count = lax.axis_size("fsdp")
    if lax.axis_size("dp") != 4 or count not in (4, 8) or local != 4 or head_rows % 16:
        return False
    if model % (16 * count) or hidden % 256 or layer_columns % (3 * model):
        return False
    for low, high in ((0, model), (hidden + model, total)):
        rows = (high - low) // count
        if rows % 16 or any((low + rows * f) % head_rows + rows > head_rows for f in range(count)):
            return False
    return True


def head_plain(
    cls, teacher_cls, vectors, teacher_vectors, head_full, teacher_head_full, own_centre, counted,
    counted_total, w_proto, teacher_proto, own_rows,
):
    teacher_unit = unit(head_forward(teacher_cls, teacher_head_full, teacher_vectors)[-1])
    low_n, pre_a, low_a, pre_b, low_b, raw = head_forward(cls, head_full, vectors)
    bottleneck, pull_unit = jax.vjp(unit, raw)
    both = jnp.concatenate([teacher_unit.astype(BF16), bottleneck.astype(BF16)], -1)
    both = lax.all_gather(both, ("fsdp", "dp"), axis=0, tiled=True)
    width = raw.shape[1]
    teacher_rows, student_rows = both[:, :width], both[:, width:]

    low_proto = w_proto.astype(BF16)
    teacher_logits = dot(teacher_rows, teacher_proto.astype(BF16), ((1,), (1,)))
    logits = dot(student_rows, low_proto, ((1,), (1,)))
    scaled_t = (teacher_logits - own_centre) / TEACHER_TEMP
    scaled_s = logits / STUDENT_TEMP
    max_t = jnp.max(scaled_t, -1)
    max_s = jnp.max(scaled_s, -1)
    expo_t = jnp.exp(scaled_t - max_t[:, None])
    expo_s = jnp.exp(scaled_s - max_s[:, None])
    parts = jnp.stack(
        [
            max_t,
            jnp.sum(expo_t, -1),
            max_s,
            jnp.sum(expo_s, -1),
            jnp.sum(expo_t * (scaled_s - max_s[:, None]), -1),
        ]
    )
    parts = lax.all_gather(parts, "fsdp", axis=0)
    top_t = jnp.max(parts[:, 0], 0)
    lift_t = jnp.exp(parts[:, 0] - top_t)
    total_t = jnp.sum(parts[:, 1] * lift_t, 0)
    top_s = jnp.max(parts[:, 2], 0)
    total_s = jnp.sum(parts[:, 3] * jnp.exp(parts[:, 2] - top_s), 0)
    crossed = jnp.sum(lift_t * (parts[:, 4] + (parts[:, 2] - top_s) * parts[:, 1]), 0) / total_t
    losses = jnp.log(total_s) - crossed
    loss_total = jnp.sum(counted * losses)
    weighting = counted / counted_total / STUDENT_TEMP
    share_s = weighting * jnp.exp(max_s - top_s) / total_s
    share_t = weighting * jnp.exp(max_t - top_t) / total_t
    grad_logits = (expo_s * share_s[:, None] - expo_t * share_t[:, None]).astype(BF16)
    teacher_sum = jnp.sum(counted[:, None] * teacher_logits, 0)
    teacher_total = lax.all_gather(teacher_sum, "fsdp", axis=0, tiled=True)
    grad_proto = dot(grad_logits, student_rows, ((0,), (0,)))
    grad_rows = jnp.dot(grad_logits, low_proto, preferred_element_type=F32)
    dp_count = lax.axis_size("dp")
    grad_rows = grad_rows.reshape(-1, dp_count, cls.shape[0], width)
    grad_rows = lax.dynamic_index_in_dim(grad_rows, lax.axis_index("dp"), 1, keepdims=False)
    grad_bottleneck = lax.psum_scatter(grad_rows, "fsdp", scatter_dimension=0, tiled=False)

    model_width, hidden = cls.shape[1], head_full.shape[1]
    local = cls.shape[0]
    low_dz = pull_unit(grad_bottleneck)[0].astype(BF16)
    grad_b = jnp.dot(low_dz, head_full[model_width + hidden :], preferred_element_type=F32)
    low_db = (grad_b * gelu_slope(pre_b)).astype(BF16)
    grad_a = dot(low_db, head_full[model_width : model_width + hidden], ((1,), (1,)))
    low_da = (grad_a * gelu_slope(pre_a)).astype(BF16)
    grad_n = dot(low_da, head_full[:model_width], ((1,), (1,)))
    _, pull_norm = jax.vjp(layer_norm, cls, vectors[-2], vectors[-1])
    grad_cls, grad_gain, grad_shift = pull_norm(grad_n)

    packed = jnp.concatenate([low_n, low_a, low_dz, low_da, low_db, low_b], -1)
    packed = lax.all_gather(packed, ("fsdp", "dp"), axis=0, tiled=True)
    total_rows = model_width + hidden + width
    lefts, rights = packed[:, :total_rows], packed[:, total_rows:]
    start = lax.axis_index("fsdp") * own_rows
    left = lax.dynamic_slice_in_dim(lefts, start, own_rows, 1)
    row = start + lax.broadcasted_iota(jnp.int32, (1, own_rows), 1)
    kind = jnp.where(row < model_width, 0, jnp.where(row < model_width + hidden, 1, 2))
    left = jnp.concatenate([jnp.where(kind == index, left, 0) for index in range(3)], 0)
    right = jnp.concatenate(
        [rights[:, index * hidden : (index + 1) * hidden] for index in range(3)], 0
    )
    grad_head = dot(left, right, ((0,), (0,)))
    ends = jnp.stack([grad_gain, grad_shift])
    return grad_cls, ends, loss_total, teacher_total, grad_proto, grad_head


def per_device(
    patches,
    patch_mask,
    image_valid,
    centre,
    w_patch,
    first_patch,
    second_patch,
    teacher_patch,
    w_layer,
    first_layer,
    second_layer,
    teacher_layer,
    w_head,
    first_head,
    second_head,
    teacher_head,
    w_proto,
    first_proto,
    second_proto,
    teacher_proto,
    vectors,
    first_vectors,
    second_vectors,
    teacher_vectors,
):
    everyone = ("fsdp", "dp")
    local = patches.shape[0]
    place = lax.axis_index(everyone) * local
    fsdp_index = lax.axis_index("fsdp")
    counted = image_valid.astype(F32)
    counted_total = jnp.maximum(jnp.sum(counted), 1.0)
    covered = patch_mask.astype(F32)
    pixels = w_patch.shape[1]
    model_width, columns = w_layer.shape[1] * lax.axis_size("fsdp"), w_layer.shape[2]
    pad = packed_width_p(pixels) - pixels

    def low_blocks(patch, layers):
        patch = jnp.pad(patch, ((0, 0), (0, pad)))
        return [array.astype(BF16) for array in (patch, layers[0], layers[1])]

    head_s, head_t = w_head.astype(BF16), teacher_head.astype(BF16)
    blocks = low_blocks(teacher_patch, teacher_layer) + low_blocks(w_patch, w_layer)
    hidden = w_head.shape[1]
    fsdp_count = lax.axis_size("fsdp")
    own_rows, own_k = w_head.shape[0], w_proto.shape[0]
    total_rows = own_rows * fsdp_count
    own = own_kernels(local, own_rows, model_width, hidden, total_rows, columns)
    if own:
        ranges = ((0, model_width), (model_width + hidden, total_rows))
        full, teacher_rows, cls_rows, saved = gather_forward(
            blocks, (head_s, head_t), ranges, fsdp_count, patches, covered, vectors,
            teacher_vectors, 1,
        )
    else:
        full = [
            lax.all_gather(block, "fsdp", axis=0, tiled=True)
            for block in blocks + [head_s, head_t]
        ]
        teacher_rows = forward(
            patches, jnp.zeros_like(covered), *full[:3], teacher_vectors, False
        )[0]
        cls_rows, *saved = forward(patches, covered, *full[3:6], vectors, True)
    patch_full, layer_0, layer_1 = full[3:6]
    own_centre = lax.dynamic_slice_in_dim(centre, fsdp_index * own_k, own_k)
    if own:
        grad_cls, ends, loss_row, totals, grad_logits, unit_rows, grad_head, part = head_step(
            cls_rows, teacher_rows, vectors, teacher_vectors, full[6:], (head_s, head_t),
            own_centre, counted, (w_proto, teacher_proto), (fsdp_count, lax.axis_size("dp")), 3,
        )
        ends = ends[:2]
        loss_total = jnp.sum(loss_row)
        teacher_total = totals.reshape(-1)
        grad_proto = dot(grad_logits, unit_rows, ((0,), (0,)))
    else:
        grad_cls, ends, loss_total, teacher_total, grad_proto, grad_head = head_plain(
            cls_rows[:local], teacher_rows[:local], vectors, teacher_vectors, full[6], full[7],
            own_centre, counted, counted_total, w_proto, teacher_proto, own_rows,
        )
    grad_rows = jnp.pad(grad_cls, ((0, TAIL - grad_cls.shape[0]), (0, 0)))
    _, rows_table = split_table(vectors, patches.shape[1])
    grads_1, grad_x, rows_grad = last_back(layer_1, rows_table, grad_rows, saved)
    rows_grad = rows_grad.at[14:16].add(ends)
    if own:
        own_patch, own_layers, table, sums = back_reduce(
            patches, covered, layer_0, rows_table, grad_x, saved, rows_grad, grads_1, part,
            fsdp_count, 2,
        )
        vector_grad = table.reshape(model_width, model_width)[: vectors.shape[0]]
        own_patch = own_patch[:, :pixels]
        squares = jnp.sum(sums)
    else:
        places, width = plan_of(pixels, columns, model_width, model_width)
        tail = first_back_plain(
            patches, covered, layer_0, rows_table, grad_x, saved, rows_grad, width - columns
        )
        packed_grads = jnp.concatenate([grads_1, tail], 1)
        owned = lax.psum_scatter(packed_grads, "fsdp", scatter_dimension=0, tiled=True)
        owned = lax.psum(owned, "dp").astype(F32)
        patch_at, _, table_at, _, spans = places
        own_patch = owned[:, patch_at : patch_at + pixels]
        first_layer_parts = [
            owned[:, start : start + span] for layer, _, start, span in spans if layer == 0
        ]
        own_layers = jnp.stack([jnp.concatenate(first_layer_parts, 1), owned[:, :columns]])
        own_table = owned[:, table_at : table_at + model_width]
        table = lax.all_gather(own_table, "fsdp", axis=0, tiled=True)
        vector_grad = table[: vectors.shape[0]]
        parts = (own_patch, own_layers, grad_head, grad_proto, own_table)
        squares = lax.psum(sum(jnp.sum(value * value) for value in parts), "fsdp")
    owned_grads = (own_patch, own_layers, grad_head, grad_proto)
    norm_value = jnp.sqrt(squares)
    factor = CLIP_NORM / jnp.maximum(norm_value, CLIP_NORM)
    updated_centre = CENTRE_KEEP * centre + (1.0 - CENTRE_KEEP) * teacher_total / counted_total
    weights_owned = (w_patch, w_layer, w_head, w_proto, vectors)
    moments = (first_patch, first_layer, first_head, first_proto, first_vectors)
    seconds = (second_patch, second_layer, second_head, second_proto, second_vectors)
    teachers = (teacher_patch, teacher_layer, teacher_head, teacher_proto, teacher_vectors)
    gradients = owned_grads + (vector_grad,)
    results = [loss_total, counted_total, norm_value, updated_centre]
    for group in range(5):
        updated, moment, second = adamw(
            weights_owned[group],
            moments[group],
            seconds[group],
            gradients[group],
            factor,
            RATES[group],
            DECAYS[group],
        )
        results.extend(
            [
                updated,
                moment,
                second,
                TEACHER_KEEP * teachers[group] + (1.0 - TEACHER_KEEP) * updated,
            ]
        )
    return tuple(results)


def solution(mesh):
    whole, rows, middle = P(), P("fsdp", None), P(None, "fsdp", None)
    in_specs = (
        (P(("fsdp", "dp"), None, None), P(("fsdp", "dp"), None), whole, whole)
        + (rows,) * 4
        + (middle,) * 4
        + (rows,) * 8
        + (whole,) * 4
    )
    out_specs = (whole,) * 4 + (rows,) * 4 + (middle,) * 4 + (rows,) * 8 + (whole,) * 4
    return jax.shard_map(
        per_device, mesh=mesh, in_specs=in_specs, out_specs=out_specs, check_vma=False
    )
```

```python
import functools

import jax
import jax.numpy as jnp
from jax import lax
from jax.experimental import pallas as pl
from jax.experimental.pallas import tpu as pltpu
from jax.sharding import PartitionSpec as P

HEADS = 6
STEP = 10
STUDENT_TEMP = 0.1
TEACHER_TEMP = 0.07
CENTRE_KEEP = 0.9
TEACHER_KEEP = 0.8
BETA_ONE = 0.9
BETA_TWO = 0.999
CLIP_NORM = 0.01
RATES = (0.1, 0.15, 0.07, 0.5, 0.5)
DECAYS = (0.04, 0.04, 0.04, 0.04, 0.0)
F32 = jnp.float32
BF16 = jnp.bfloat16
MESH = pl.DeviceIdType.MESH


def third_ranges(width, start):
    tiles = width // 128
    sizes = [(tiles + 2 - part) // 3 * 128 for part in range(3)]
    spans, at = [], start
    for size in sizes:
        spans.append((at, size))
        at += size
    return spans


def gather_kernel(items, early, lines, sources, heads, targets, between, send, recv, copied, send_e, recv_e):
    fsdp, dp = lax.axis_index("fsdp"), lax.axis_index("dp")
    z, x = fsdp // 2, fsdp % 2
    y, core = dp // 2, dp % 2
    across = z * 2 + 1 - x
    mate = y * 2 + 1 - core
    opposite = (1 - y) * 2 + core

    barrier = pltpu.get_barrier_semaphore()

    def greet(f, d):
        pl.semaphore_signal(barrier, 1, device_id=(f, d), device_id_type=pl.DeviceIdType.MESH)

    def when(condition, body):
        pl.when(condition)(body)

    for step in range(1, 2 * lines):
        greet(lax.rem(fsdp + step, 2 * lines), dp)
    greet(fsdp, mate)
    when(core == 0, lambda: greet(fsdp, opposite))
    pl.semaphore_wait(barrier, 2 * lines + 1 - core)

    hops = lines - 1
    UP, DOWN, ACROSS, OPPOSITE, MATE = 0, hops, 2 * hops, 4 * hops + 1, 4 * hops + 2

    def roles(body):
        when((core == 0) & (y == 0), lambda: body(0))
        when(core == 1, lambda: body(1))
        when((core == 0) & (y == 1), lambda: body(2))

    def region(index, part, f):
        number, rows, spans = items[index]
        at, size = spans[part]
        return targets[number].at[pl.ds(pl.multiple_of(f * rows, rows), rows), pl.ds(at, size)]

    def whole(index, part):
        number, rows, spans = items[index]
        at, size = spans[part]
        return targets[number].at[:, pl.ds(at, size)]

    def own(index, part):
        number, rows, spans = items[index]
        at, size = spans[part]
        return sources[number].at[:, pl.ds(at, size)]

    def move(index, slot, source, target, f, d):
        return pltpu.make_async_remote_copy(
            src_ref=source,
            dst_ref=target,
            send_sem=send.at[index, slot],
            recv_sem=recv.at[index, slot],
            device_id=(f, d),
            device_id_type=pl.DeviceIdType.MESH,
        )

    def piece(index, part, slot, f_source, f_target, mine=False):
        target = region(index, part, f_source)
        return move(index, slot, own(index, part) if mine else target, target, f_target, dp)

    def keep(index, part):
        return pltpu.make_async_copy(own(index, part), region(index, part, fsdp), copied.at[index])

    def z_steps(index, part, hop, act):
        mine = hop == 0
        if hop < hops:
            when(
                (z - hop >= 0) & (z + 1 < lines),
                lambda: act(piece(index, part, UP + hop, fsdp - 2 * hop, fsdp + 2, mine)),
            )
            when(
                (z + hop < lines) & (z > 0),
                lambda: act(piece(index, part, DOWN + hop, fsdp + 2 * hop, fsdp - 2, mine)),
            )

    def x_steps(index, part, hop, act):
        if hop == 0:
            act(piece(index, part, ACROSS, fsdp, across, True))
        else:
            when(
                z - hop >= 0,
                lambda: act(piece(index, part, ACROSS + hop, fsdp - 2 * hop, across)),
            )
            when(
                z + hop < lines,
                lambda: act(piece(index, part, ACROSS + hops + hop, fsdp + 2 * hop, across)),
            )

    def z_arrive(index, part, hop):
        when(
            z - hop >= 0,
            lambda: piece(index, part, UP + hop - 1, fsdp - 2 * hop, fsdp).wait_recv(),
        )
        when(
            z + hop < lines,
            lambda: piece(index, part, DOWN + hop - 1, fsdp + 2 * hop, fsdp).wait_recv(),
        )

    def x_arrive(index, part):
        piece(index, part, ACROSS, across, across).wait_recv()
        for hop in range(1, lines):
            when(
                z - hop >= 0,
                lambda hop=hop: piece(
                    index, part, ACROSS + hop, across - 2 * hop, across
                ).wait_recv(),
            )
            when(
                z + hop < lines,
                lambda hop=hop: piece(
                    index, part, ACROSS + hops + hop, across + 2 * hop, across
                ).wait_recv(),
            )

    def to_opposite(index, part):
        return move(index, OPPOSITE, whole(index, part), whole(index, part), fsdp, opposite)

    def to_mate(index, part, second=0):
        return move(index, MATE + second, whole(index, part), whole(index, part), fsdp, mate)

    def deal(part, act):
        for index, (number, places) in early.items():
            _, rows, spans = items[index]
            at, size = spans[part]
            target = sources[items[index][0]].at[:, pl.ds(at, size)]
            for f, (owner, start) in enumerate(places):
                source = heads[number].at[pl.ds(start, rows), pl.ds(at, size)]
                act(index, f, owner, source, target)

    def early_copy(index, f, source, target):
        return pltpu.make_async_remote_copy(
            src_ref=source,
            dst_ref=target,
            send_sem=send_e.at[index, f],
            recv_sem=recv_e.at[index],
            device_id=(f, dp),
            device_id_type=pl.DeviceIdType.MESH,
        )

    def deal_start(index, f, owner, source, target):
        if f == owner:
            when(
                fsdp == f,
                lambda: pltpu.make_async_copy(source, target, recv_e.at[index]).start(),
            )
        else:
            when(fsdp == owner, lambda: early_copy(index, f, source, target).start())

    def deal_end(index, f, owner, source, target):
        if f != owner:
            when(fsdp == owner, lambda: early_copy(index, f, source, target).wait_send())

    def dealt(index, part):
        _, rows, spans = items[index]
        at, size = spans[part]
        number, places = early[index]
        target = sources[items[index][0]].at[:, pl.ds(at, size)]
        for f, (owner, start) in enumerate(places):
            source = heads[number].at[pl.ds(start, rows), pl.ds(at, size)]
            if f == owner:
                when(
                    fsdp == f,
                    lambda source=source: pltpu.make_async_copy(
                        source, target, recv_e.at[index]
                    ).wait(),
                )
            else:
                when(
                    fsdp == f,
                    lambda f=f, source=source: early_copy(index, f, source, target).wait_recv(),
                )

    def stage(index, part, step):
        if step == 0:
            if index in early:
                dealt(index, part)
            keep(index, part).start()
            z_steps(index, part, 0, lambda copy: copy.start())
            x_steps(index, part, 0, lambda copy: copy.start())
        elif step < lines:
            z_arrive(index, part, step)
            z_steps(index, part, step, lambda copy: copy.start())
            x_steps(index, part, step, lambda copy: copy.start())
        elif step == lines:
            keep(index, part).wait()
            x_arrive(index, part)
            if part != 1:
                to_opposite(index, part).start()
            to_mate(index, part).start()
        elif step == lines + 1:
            if part != 1:
                to_opposite(index, 2 - part).wait_recv()
                to_mate(index, 2 - part, 1).start()
        else:
            if part != 1:
                to_mate(index, 1).wait_recv()
            else:
                when(y == 0, lambda: to_mate(index, 0).wait_recv())
                when(y == 0, lambda: to_mate(index, 2, 1).wait_recv())
                when(y == 1, lambda: to_mate(index, 2).wait_recv())
                when(y == 1, lambda: to_mate(index, 0, 1).wait_recv())

    steps = lines + 3

    def run(tick, part):
        for step in range(steps):
            if 0 <= tick - step < len(items):
                stage(tick - step, part, step)

    def close(part):
        for index in range(len(items)):
            for hop in range(lines):
                z_steps(index, part, hop, lambda copy: copy.wait_send())
                x_steps(index, part, hop, lambda copy: copy.wait_send())
            if part != 1:
                to_opposite(index, part).wait_send()
                to_mate(index, 2 - part, 1).wait_send()
            to_mate(index, part).wait_send()
        deal(part, deal_end)

    roles(lambda part: deal(part, deal_start))
    for tick in range(len(items) + steps - 1):
        roles(functools.partial(run, tick))
        between(tick - steps + 1)
    roles(close)


def gather_forward(
    arrays, heads, ranges, fsdp_count, patches, covered, vecs, teacher_vecs, collective_id
):
    lines = fsdp_count // 2
    head_rows, head_width = heads[0].shape
    shapes = [array.shape for array in arrays]
    count = len(arrays)
    items, whole_at = [], {}
    for number in (0, 1, 3, 4, 2, 5):
        rows, width = shapes[number]
        cuts = 2 if width % 256 == 0 and width > 1024 else 1
        for cut in range(cuts):
            items.append((number, rows, third_ranges(width // cuts, cut * (width // cuts))))
        whole_at[number] = len(items) - 1
    early = {}
    for low, high in ranges:
        for number in range(len(heads)):
            rows = (high - low) // fsdp_count
            starts = [low + rows * f for f in range(fsdp_count)]
            early[len(items)] = (
                number,
                [(start // head_rows, start % head_rows) for start in starts],
            )
            shapes.append((rows, head_width))
            items.append((len(shapes) - 1, rows, third_ranges(head_width, 0)))
    slots = 4 * (lines - 1) + 4
    extra = len(shapes) - count
    full = [(fsdp_count * r, c) for r, c in shapes]
    images, pixel_rows, pixels = patches.shape
    model, columns = full[1]
    hidden = (columns - 4 * model) // 2
    tables = split_table(teacher_vecs, pixel_rows) + split_table(vecs, pixel_rows)
    per_image = saved_shapes(pixel_rows + TAIL, model)
    saved = len(per_image)

    def kernel(*refs):
        refs = list(refs)

        def take(number):
            taken = refs[:number]
            del refs[:number]
            return taken

        sources, head_refs = take(count), take(len(heads))
        patches_ref, covered_ref = take(2)
        table_refs = take(4)
        targets, dealt = take(len(shapes)), take(extra)
        cls_t, cls_s, x1c_out, o1_out = take(4)
        saved_out = take(saved)
        weights, kept = take(6), take(saved)
        cls_x, cls_o, teacher_x, load_sem, save_sem = take(5)

        def load(number):
            return pltpu.make_async_copy(targets[number], weights[number], load_sem.at[number])

        def save(number, image):
            return pltpu.make_async_copy(
                kept[number].at[image], saved_out[number].at[image], save_sem.at[number, image]
            )

        def keep_values(first, image, values):
            for number, value in enumerate(values):
                kept[first + number][image] = value
                save(first + number, image).start()

        def run_first(net, image):
            if image == 0:
                load(3 * net).wait()
                load(3 * net + 1).wait()
            values = image_first(
                patches_ref[image],
                covered_ref[image] if net else None,
                weights[3 * net],
                weights[3 * net + 1],
                table_refs[2 * net],
                table_refs[2 * net + 1],
                hidden,
            )
            x2 = values[2]
            if net:
                keep_values(0, image, values)
            else:
                teacher_x[image] = x2
            cls_x[net, image : image + 1, :] = x2[pixel_rows : pixel_rows + 1, :]

        def run_second(net):
            load(3 * net + 2).wait()
            for image in range(images):
                values = image_second(
                    kept[2][image] if net else teacher_x[image],
                    weights[3 * net + 2],
                    table_refs[2 * net + 1],
                    pixel_rows,
                    net == 1,
                )
                if net:
                    keep_values(6, image, values[:-1])
                cls_o[net, image : image + 1, :] = values[-1][:1, :].astype(F32)
            out, x1c, mixed = class_forward(
                cls_x[net], cls_o[net], weights[3 * net + 2], table_refs[2 * net + 1], hidden
            )
            if net:
                cls_s[...] = out
                x1c_out[...] = x1c
                o1_out[...] = mixed
            else:
                cls_t[...] = out

        waiting = [
            (whole_at[3 * net + 1] + 1, functools.partial(run_first, net, image))
            for net in range(2)
            for image in range(images)
        ]
        waiting += [
            (whole_at[3 * net + 2] + 1, functools.partial(run_second, net)) for net in range(2)
        ]

        def between(item):
            if item == -1:
                cls_x[...] = jnp.zeros_like(cls_x)
                cls_o[...] = jnp.zeros_like(cls_o)
            if waiting and waiting[0][0] <= item:
                waiting.pop(0)[1]()
            for number in range(6):
                if whole_at[number] == item:
                    load(number).start()
            if item == len(items) - 1:
                while waiting:
                    waiting.pop(0)[1]()

        gather_kernel(
            items, early, lines, sources + dealt, head_refs, targets, between, *refs
        )
        for number in range(saved):
            for image in range(images):
                save(number, image).wait()

    anywhere = pl.BlockSpec(memory_space=pl.ANY)
    vmem = pl.BlockSpec(memory_space=pltpu.VMEM)
    shape = jax.ShapeDtypeStruct
    sems = pltpu.SemaphoreType.DMA
    out = pl.pallas_call(
        kernel,
        out_shape=[shape(dims, BF16) for dims in full]
        + [shape(dims, BF16) for dims in shapes[count:]]
        + [shape((TAIL, model), kind) for kind in (F32, F32, F32, BF16)]
        + [shape((images,) + dims, kind) for dims, kind in per_image],
        in_specs=[anywhere] * (count + len(heads)) + [vmem] * 6,
        out_specs=[anywhere] * (len(shapes) + extra) + [vmem] * 4 + [anywhere] * saved,
        scratch_shapes=[pltpu.VMEM(dims, BF16) for dims in full[:6]]
        + [pltpu.VMEM((images,) + dims, kind) for dims, kind in per_image]
        + [pltpu.VMEM((2, TAIL, model), F32)] * 2
        + [
            pltpu.VMEM((images, pixel_rows + TAIL, model), F32),
            sems((6,)),
            sems((saved, images)),
            sems((len(items), slots)),
            sems((len(items), slots)),
            sems((len(items),)),
            sems((len(items), fsdp_count)),
            sems((len(items),)),
        ],
        compiler_params=pltpu.CompilerParams(
            collective_id=collective_id, has_side_effects=True, vmem_limit_bytes=60 << 20
        ),
        name="gather_forward",
    )(*arrays, *heads, patches, covered[..., None], *tables)
    at = len(shapes) + extra
    cls_t, cls_s, x1c, o1 = out[at : at + 4]
    return out[: len(shapes)], cls_t, cls_s, list(out[at + 4 :]) + [x1c, o1]


def reduce_kernel(
    cuts, lines, places, part_of, squares, outs, work, mate_a, mate_b, facing, side,
    spread, landed, halves, result, vectors, norms, send, recv, send_z, recv_z, send_l, recv_l,
    send_f, recv_f
):
    patch_out, layers_out, vectors_out, norm_out = outs
    fsdp, dp = lax.axis_index("fsdp"), lax.axis_index("dp")
    z, x = fsdp // 2, fsdp % 2
    y, core = dp // 2, dp % 2
    across = z * 2 + 1 - x
    mate = y * 2 + 1 - core
    opposite = (1 - y) * 2 + core
    size = mate_a.shape[-1]
    lone = core == 1
    part = jnp.where(lone, 1, 2 * y)
    mate_part = jnp.where(lone, 2 * y, 1)

    barrier = pltpu.get_barrier_semaphore()

    def greet(f, d):
        pl.semaphore_signal(barrier, 1, device_id=(f, d), device_id_type=MESH)

    count = 2 * lines
    for step in range(1, count):
        greet(lax.rem(fsdp + step, count), dp)
    for step in range(1, 4):
        greet(fsdp, lax.rem(dp + step, 4))
    pl.semaphore_wait(barrier, count + 2)

    MATE_A, MATE_B, FACING, ACROSS = range(4)

    def move(cut, slot, source, target, f, d):
        return pltpu.make_async_remote_copy(
            src_ref=source,
            dst_ref=target,
            send_sem=send.at[cut, slot],
            recv_sem=recv.at[cut, slot],
            device_id=(f, d),
            device_id_type=MESH,
        )

    def columns(cut, which):
        return pl.ds(pl.multiple_of((3 * cut + which) * size, 128), size)

    def mine(cut, which):
        return part_of(cut, which, size)[...].astype(F32)

    def to_mate_a(cut):
        return move(cut, MATE_A, part_of(cut, mate_part, size), mate_a.at[cut], fsdp, mate)

    def to_mate_b(cut):
        return move(
            cut, MATE_B, part_of(cut, 2 - mate_part, size), mate_b.at[cut], fsdp, mate
        )

    def to_facing(cut):
        return move(cut, FACING, mate_b.at[cut], facing.at[cut], fsdp, opposite)

    def to_across(cut):
        return move(cut, ACROSS, mate_a.at[cut, :, 1 - x], side.at[cut], across, dp)

    def along(cut, to, source):
        return pltpu.make_async_remote_copy(
            src_ref=spread.at[cut, to],
            dst_ref=landed.at[cut, source],
            send_sem=send_z.at[cut, to],
            recv_sem=recv_z.at[cut, source],
            device_id=(2 * to + x, dp),
            device_id_type=MESH,
        )

    def share_of(cut, group):
        if group % 2:
            return halves.at[cut, group // 2]
        return result.at[:, columns(cut, group)]

    def hand(cut, group, to):
        place = share_of(cut, group)
        return pltpu.make_async_remote_copy(
            src_ref=place,
            dst_ref=place,
            send_sem=send_l.at[cut, to],
            recv_sem=recv_l.at[cut, group],
            device_id=(fsdp, to),
            device_id_type=MESH,
        )

    def step_0(cut):
        to_mate_a(cut).start()
        pl.when(lone)(lambda: to_mate_b(cut).start())

    def step_1(cut):
        @pl.when(jnp.logical_not(lone))
        def _():
            to_mate_b(cut).wait_recv()
            mate_b[cut] = (mine(cut, 2 - part) + mate_b[cut].astype(F32)).astype(BF16)
            to_facing(cut).start()

    def step_2(cut):
        to_mate_a(cut).wait_recv()

        @pl.when(lone)
        def _():
            mate_a[cut] = (mine(cut, 1) + mate_a[cut].astype(F32)).astype(BF16)

        @pl.when(jnp.logical_not(lone))
        def _():
            to_facing(cut).wait_recv()
            both = mine(cut, part) + mate_a[cut].astype(F32) + facing[cut].astype(F32)
            mate_a[cut] = both.astype(BF16)

        to_across(cut).start()

    def step_3(cut):
        to_across(cut).wait_recv()
        total = mate_a[cut, :, x].astype(F32) + side[cut].astype(F32)
        spread[cut] = total.astype(BF16)
        landed[cut, z] = spread[cut, z]
        for to in range(lines):
            pl.when(z != to)(lambda to=to: along(cut, to, z).start())

    def step_4(cut):
        for source in range(lines):
            pl.when(z != source)(lambda source=source: along(cut, source, source).wait_recv())
        total = landed[cut, 0].astype(F32)
        for source in range(1, lines):
            total = total + landed[cut, source].astype(F32)
        total = total.astype(BF16)
        for group in range(4):

            @pl.when(dp == group)
            def _(group=group):
                share_of(cut, group)[...] = total
                for to in range(4):
                    if to != group:
                        hand(cut, group, to).start()

    def step_5(cut):
        for group in range(4):
            pl.when(dp != group)(lambda group=group: hand(cut, group, group).wait_recv())
        both = halves[cut, 0].astype(F32) + halves[cut, 1].astype(F32)
        result[:, columns(cut, 1)] = both.astype(BF16)

    steps = [step_0, step_1, step_2, step_3, step_4, step_5]
    due, done, tick = [], [], 0
    while len(due) < cuts or min(done) < len(steps):
        ready, pause = work(tick)
        if len(due) < ready:
            due.append(tick)
            done.append(0)
        for cut in reversed(range(len(due))):
            if done[cut] < len(steps) and due[cut] <= tick:
                steps[done[cut]](cut)
                done[cut] += 1
                due[cut] = tick + pause
        tick += 1

    patch_at, patch_width, table_at, width, layer_spans = places
    vectors[fsdp] = result[:, table_at : table_at + width]
    total = squares[...]
    for at in range(0, result.shape[1], 128):
        value = result[:, at : at + 128].astype(F32)
        value = value * value
        for row in range(0, value.shape[0], 8):
            total = total + value[row : row + 8, :]
    norms[fsdp] = total

    def tell(kind, ref, step):
        return pltpu.make_async_remote_copy(
            src_ref=ref.at[fsdp],
            dst_ref=ref.at[fsdp],
            send_sem=send_f.at[kind, step - 1],
            recv_sem=recv_f.at[kind, fsdp],
            device_id=(lax.rem(fsdp + step, count), dp),
            device_id_type=MESH,
        )

    def told(kind, ref, step):
        peer = lax.rem(fsdp + step, count)
        return pltpu.make_async_remote_copy(
            src_ref=ref.at[peer],
            dst_ref=ref.at[peer],
            send_sem=send_f.at[kind, step - 1],
            recv_sem=recv_f.at[kind, peer],
            device_id=(peer, dp),
            device_id_type=MESH,
        )

    for kind, ref in enumerate((norms, vectors)):
        for step in range(1, count):
            tell(kind, ref, step).start()
    patch_out[...] = result[:, patch_at : patch_at + patch_width].astype(F32)
    for layer, to, start, span in layer_spans:
        layers_out[layer, :, to : to + span] = result[:, start : start + span].astype(F32)
    for kind, ref in enumerate((norms, vectors)):
        for step in range(1, count):
            told(kind, ref, step).wait_recv()
    vectors_out[...] = vectors[...].astype(F32)
    total = norms[0]
    for f in range(1, count):
        total = total + norms[f]
    total = jnp.sum(jnp.sum(total, 0, keepdims=True), -1, keepdims=True)
    norm_out[...] = jnp.broadcast_to(total, norm_out.shape)
    for kind, ref in enumerate((norms, vectors)):
        for step in range(1, count):
            tell(kind, ref, step).wait_send()
    for cut in range(cuts):
        to_mate_a(cut).wait_send()
        to_across(cut).wait_send()
        for to in range(lines):
            pl.when(z != to)(lambda to=to: along(cut, to, z).wait_send())
        for group in range(4):

            @pl.when(dp == group)
            def _(group=group):
                for to in range(4):
                    if to != group:
                        hand(cut, group, to).wait_send()

        pl.when(lone)(lambda: to_mate_b(cut).wait_send())
        pl.when(jnp.logical_not(lone))(lambda: to_facing(cut).wait_send())


GELU_A = 0.7978845608028654
GELU_B = 0.044715
TAIL = 16


def mm(left, right):
    return lax.dot_general(left, right, (((1,), (0,)), ((), ())), preferred_element_type=F32)


def mm_nt(left, right):
    return lax.dot_general(left, right, (((1,), (1,)), ((), ())), preferred_element_type=F32)


def mm_tn(left, right):
    return lax.dot_general(left, right, (((0,), (0,)), ((), ())), preferred_element_type=F32)


def norm_parts(x):
    centred = x - jnp.mean(x, -1, keepdims=True)
    lift = lax.rsqrt(jnp.mean(centred * centred, -1, keepdims=True) + 1e-06)
    return centred * lift, lift


def norm_back(grad, gain, unit_x, lift):
    inner = grad * gain
    return lift * (
        inner
        - jnp.mean(inner, -1, keepdims=True)
        - unit_x * jnp.mean(inner * unit_x, -1, keepdims=True)
    )


def gelu(x):
    return 0.5 * x * (1.0 + jnp.tanh(GELU_A * (x + GELU_B * (x * x * x))))


def gelu_both(x):
    square = x * x
    slope = jnp.tanh(GELU_A * x * (1.0 + GELU_B * square))
    half = 0.5 * (1.0 + slope)
    turn = half + 0.5 * x * (1.0 - slope * slope) * GELU_A * (1.0 + 3.0 * GELU_B * square)
    return x * half, turn


def half_masks(width):
    lane = lax.broadcasted_iota(jnp.int32, (1, 128), 1)
    first = (lane < width).astype(F32)
    return first, 1.0 - first


def column_sum(x):
    return jnp.sum(x, 0, keepdims=True)


def attend(q, keys, values, valid, scale, lse_store):
    rows, total = q.shape[0], keys.shape[0]
    masks = half_masks(64)
    column = lax.broadcasted_iota(jnp.int32, (rows, total), 1)
    lane = lax.broadcasted_iota(jnp.int32, (rows, 128), 1)
    mixed, lse = [], jnp.zeros((rows, 128), F32)
    for pair in range(HEADS // 2):
        span = slice(128 * pair, 128 * pair + 128)
        halves = []
        for side in range(2):
            asked = q[:, span] * (masks[side] * scale).astype(BF16)
            scores = mm_nt(asked, keys[:, span])
            scores = jnp.where(column < valid, scores, -1e30)
            top = jnp.max(scores, -1, keepdims=True)
            expo = jnp.exp(scores - top)
            total_e = jnp.sum(expo, -1, keepdims=True)
            halves.append(mm(expo.astype(BF16), values[:, span]) / total_e)
            if lse_store:
                lse = jnp.where(lane == 2 * pair + side, top + jnp.log(total_e), lse)
        mixed.append(jnp.where(lane < 64, halves[0], halves[1]))
    return jnp.concatenate(mixed, -1).astype(BF16), lse


def image_first(pixel_rows, hide, weight_p, weight_0, places, rows_table, hidden):
    model = weight_0.shape[0]
    count, pixels = pixel_rows.shape
    scale = (model // HEADS) ** -0.5
    keep = hide is not None

    def vec(row):
        return rows_table[row : row + 1, :]

    tokens = mm_nt(pixel_rows, weight_p[:, :pixels]) + vec(1)
    if keep:
        tokens = tokens * (1.0 - hide) + vec(0) * hide
    x = jnp.concatenate([tokens + places[:count, :], places[count:, :]], 0)
    unit_x, _ = norm_parts(x)
    low = (unit_x * vec(2) + vec(3)).astype(BF16)
    qkv = mm(low, weight_0[:, : 3 * model]).astype(BF16)
    mixture, lse = attend(
        qkv[:, :model], qkv[:, model : 2 * model], qkv[:, 2 * model :], count + 1, scale, keep
    )
    x1 = x + vec(4) * mm(mixture, weight_0[:, 3 * model : 4 * model])
    unit_x, _ = norm_parts(x1)
    low = (unit_x * vec(5) + vec(6)).astype(BF16)
    wide = gelu(mm(low, weight_0[:, 4 * model : 4 * model + hidden])).astype(BF16)
    x2 = x1 + vec(7) * mm_nt(wide, weight_0[:, 4 * model + hidden :])
    return x, x1, x2, qkv, mixture, lse


def image_second(x2, weight_1, rows_table, count, keep):
    model = weight_1.shape[0]
    scale = (model // HEADS) ** -0.5
    unit_x, _ = norm_parts(x2)
    low = (unit_x * rows_table[8:9, :] + rows_table[9:10, :]).astype(BF16)
    kv = mm(low, weight_1[:, model : 3 * model]).astype(BF16)
    q1 = mm(low[count:, :], weight_1[:, :model]).astype(BF16)
    mixture1, lse1 = attend(q1, kv[:, :model], kv[:, model:], count + 1, scale, keep)
    return kv, q1, lse1, mixture1


def class_forward(cls_x, cls_o, weight_1, rows_table, hidden):
    model = weight_1.shape[0]

    def row(index):
        return rows_table[8 + index : 9 + index, :]

    mixed = cls_o.astype(BF16)
    x1c = cls_x + row(2) * mm(mixed, weight_1[:, 3 * model : 4 * model])
    unit_c, _ = norm_parts(x1c)
    low_c = (unit_c * row(3) + row(4)).astype(BF16)
    wide_c = gelu(mm(low_c, weight_1[:, 4 * model : 4 * model + hidden])).astype(BF16)
    return x1c + row(5) * mm_nt(wide_c, weight_1[:, 4 * model + hidden :]), x1c, mixed


def saved_shapes(total, model):
    return [
        ((total, model), F32),
        ((total, model), F32),
        ((total, model), F32),
        ((total, 3 * model), BF16),
        ((total, model), BF16),
        ((total, 128), F32),
        ((total, 2 * model), BF16),
        ((TAIL, model), BF16),
        ((TAIL, 128), F32),
    ]


def forward_kernel(
    images, hidden, keep, patches, covered, weight_p, weight_0, weight_1, places, rows_table, *rest
):
    outs, (cls_x, cls_o) = rest[:-2], rest[-2:]
    image = pl.program_id(0)
    count = patches.shape[1]

    @pl.when(image == 0)
    def _():
        cls_x[...] = jnp.zeros_like(cls_x)
        cls_o[...] = jnp.zeros_like(cls_o)

    hide = covered[0] if keep else None
    values = image_first(patches[0], hide, weight_p, weight_0, places, rows_table, hidden)
    values += image_second(values[2], weight_1, rows_table, count, keep)
    cls_x[pl.ds(image, 1), :] = values[2][count : count + 1, :]
    cls_o[pl.ds(image, 1), :] = values[-1][:1, :].astype(F32)
    if keep:
        for number, value in enumerate(values[:-1]):
            outs[1 + number][0] = value

    @pl.when(image == images - 1)
    def _():
        out, x1c, mixed = class_forward(cls_x[...], cls_o[...], weight_1, rows_table, hidden)
        outs[0][...] = out
        if keep:
            outs[-2][...] = x1c
            outs[-1][...] = mixed


def fixed(shape):
    zeros = (0,) * len(shape)
    return pl.BlockSpec(shape, lambda i: zeros, pipeline_mode=pl.Buffered(1))


def each(shape):
    rest = (0,) * len(shape)
    return pl.BlockSpec((1,) + shape, lambda i: (i,) + rest)


def whole_out(shape):
    zeros = (0,) * len(shape)
    return pl.BlockSpec(shape, lambda i: zeros)


def split_table(vecs, count):
    places = jnp.concatenate(
        [
            vecs[1 : count + 1],
            vecs[:1] + vecs[count + 1 : count + 2],
            jnp.zeros((TAIL - 1, vecs.shape[1]), F32),
        ]
    )
    rows = vecs[count + 2 :]
    rows = jnp.concatenate([rows, jnp.zeros(((-rows.shape[0]) % 8, rows.shape[1]), F32)])
    return places, rows


def forward(patches, covered, weight_p, weight_0, weight_1, vecs, keep):
    images, count, pixels = patches.shape
    model, columns = weight_0.shape
    hidden = (columns - 4 * model) // 2
    total = count + TAIL
    places, rows = split_table(vecs, count)
    shape = jax.ShapeDtypeStruct
    outs = [shape((TAIL, model), F32)]
    out_specs = [whole_out((TAIL, model))]
    if keep:
        per_image = saved_shapes(total, model)
        outs += [shape((images,) + dims, kind) for dims, kind in per_image]
        out_specs += [each(dims) for dims, kind in per_image]
        outs += [shape((TAIL, model), F32), shape((TAIL, model), BF16)]
        out_specs += [whole_out((TAIL, model))] * 2
    return pl.pallas_call(
        functools.partial(forward_kernel, images, hidden, keep),
        grid=(images,),
        out_shape=outs,
        in_specs=[
            each((count, pixels)),
            each((count, 1)),
            fixed(weight_p.shape),
            fixed(weight_0.shape),
            fixed(weight_1.shape),
            fixed(places.shape),
            fixed(rows.shape),
        ],
        out_specs=out_specs,
        scratch_shapes=[pltpu.VMEM((TAIL, model), F32)] * 2,
        compiler_params=pltpu.CompilerParams(vmem_limit_bytes=56 << 20),
        name="backbone_forward",
    )(patches, covered[..., None], weight_p, weight_0, weight_1, places, rows)


def attend_back(grad_o, q, keys, values, lse, valid, scale):
    rows, total = q.shape[0], keys.shape[0]
    masks = half_masks(64)
    column = lax.broadcasted_iota(jnp.int32, (rows, total), 1)
    lane_row = lax.broadcasted_iota(jnp.int32, (rows, 128), 1)
    grad_q, grad_k, grad_v = [], [], []
    for pair in range(HEADS // 2):
        span = slice(128 * pair, 128 * pair + 128)
        out_q, out_k, out_v = [], None, None
        for side in range(2):
            mask = masks[side].astype(BF16)
            asked = q[:, span] * (masks[side] * scale).astype(BF16)
            given = grad_o[:, span] * mask
            head = 2 * pair + side
            scores = mm_nt(asked, keys[:, span])
            share = jnp.where(column < valid, jnp.exp(scores - lse[:, head : head + 1]), 0.0)
            grad_p = mm_nt(given, values[:, span])
            inner = jnp.sum(share * grad_p, -1, keepdims=True)
            grad_s = (share * (grad_p - inner)).astype(BF16)
            out_q.append(mm(grad_s, keys[:, span]))
            more_k = mm_tn(grad_s, asked)
            more_v = mm_tn(share.astype(BF16), given)
            out_k = more_k if out_k is None else out_k + more_k
            out_v = more_v if out_v is None else out_v + more_v
        grad_q.append(jnp.where(lane_row < 64, out_q[0], out_q[1]) * scale)
        grad_k.append(out_k)
        grad_v.append(out_v)
    return [jnp.concatenate(part, -1).astype(BF16) for part in (grad_q, grad_k, grad_v)]


def last_back_kernel(
    images, hidden, weight_1, rows_table, ends, grad_cls, x2_in, kv_in, q1_in, lse1_in, x1c_in, o1_in,
    packed, grad_out, rows, acc_kv, acc_q, grad_c, grad_oc
):
    image = pl.program_id(0)
    model = weight_1.shape[0]
    count = x2_in.shape[1] - TAIL
    valid = count + 1
    scale = (model // HEADS) ** -0.5
    cut_o, cut_u, cut_d = 3 * model, 4 * model, 4 * model + hidden

    def row(index):
        return rows_table[8 + index : 9 + index, :]

    def add_row(index, value):
        rows[8 + index : 9 + index, :] += value

    @pl.when(image == 0)
    def _():
        for ref in (acc_kv, acc_q, rows):
            ref[...] = jnp.zeros_like(ref)
        rows[14:16, :] = ends[:2, :]
        grad_x = grad_cls[...]
        x1c = x1c_in[...]
        unit_x, lift = norm_parts(x1c)
        low = (unit_x * row(3) + row(4)).astype(BF16)
        wide, slope = gelu_both(mm(low, weight_1[:, cut_u:cut_d]))
        wide = wide.astype(BF16)
        down = mm_nt(wide, weight_1[:, cut_d:])
        add_row(5, column_sum(grad_x * down))
        grad_d = (grad_x * row(5)).astype(BF16)
        grad_u = (mm(grad_d, weight_1[:, cut_d:]) * slope).astype(BF16)
        packed[:, cut_d:] = mm_tn(grad_d, wide).astype(BF16)
        packed[:, cut_u:cut_d] = mm_tn(low, grad_u).astype(BF16)
        grad_n = mm_nt(grad_u, weight_1[:, cut_u:cut_d])
        add_row(3, column_sum(grad_n * unit_x))
        add_row(4, column_sum(grad_n))
        grad_x = grad_x + norm_back(grad_n, row(3), unit_x, lift)
        mixed = o1_in[...]
        add_row(2, column_sum(grad_x * mm(mixed, weight_1[:, cut_o:cut_u])))
        grad_a = (grad_x * row(2)).astype(BF16)
        packed[:, cut_o:cut_u] = mm_tn(mixed, grad_a).astype(BF16)
        grad_c[...] = grad_x
        grad_oc[...] = mm_nt(grad_a, weight_1[:, cut_o:cut_u])

    first_row = lax.broadcasted_iota(jnp.int32, (TAIL, 1), 0) == 0
    grad_o1 = jnp.where(first_row, grad_oc[pl.ds(image, 1), :], 0.0).astype(BF16)
    kv = kv_in[0]
    grad_q, grad_k, grad_v = attend_back(
        grad_o1, q1_in[0], kv[:, :model], kv[:, model:], lse1_in[0], valid, scale
    )
    unit_x, lift = norm_parts(x2_in[0])
    low = (unit_x * row(0) + row(1)).astype(BF16)
    grad_kv = jnp.concatenate([grad_k, grad_v], -1)
    acc_kv[...] += mm_tn(low, grad_kv)
    acc_q[...] += mm_tn(low[count:, :], grad_q)
    grad_n = mm_nt(grad_kv, weight_1[:, model : 3 * model])
    tail = grad_n[count:, :] + mm_nt(grad_q, weight_1[:, :model])
    grad_n = jnp.concatenate([grad_n[:count, :], tail], 0)
    add_row(0, column_sum(grad_n * unit_x))
    add_row(1, column_sum(grad_n))
    grad_x = norm_back(grad_n, row(0), unit_x, lift)
    tail = grad_x[count:, :] + jnp.where(first_row, grad_c[pl.ds(image, 1), :], 0.0)
    grad_out[0] = jnp.concatenate([grad_x[:count, :], tail], 0)

    @pl.when(image == images - 1)
    def _():
        packed[:, :model] = acc_q[...].astype(BF16)
        packed[:, model:cut_o] = acc_kv[...].astype(BF16)


def last_back(weight_1, rows, ends, grad_cls, saved):
    x2, kv, q1, lse1, x1c, o1 = [saved[index] for index in (2, 6, 7, 8, 9, 10)]
    images = x2.shape[0]
    model, columns = weight_1.shape
    hidden = (columns - 4 * model) // 2
    shape = jax.ShapeDtypeStruct
    return pl.pallas_call(
        functools.partial(last_back_kernel, images, hidden),
        grid=(images,),
        out_shape=[shape(weight_1.shape, BF16), shape(x2.shape, F32), shape(rows.shape, F32)],
        in_specs=[fixed(array.shape) for array in (weight_1, rows, ends, grad_cls)]
        + [each(array.shape[1:]) for array in (x2, kv, q1, lse1)]
        + [fixed(x1c.shape), fixed(o1.shape)],
        out_specs=[whole_out(weight_1.shape), each(x2.shape[1:]), whole_out(rows.shape)],
        scratch_shapes=[
            pltpu.VMEM((model, 2 * model), F32),
            pltpu.VMEM((model, model), F32),
            pltpu.VMEM((TAIL, model), F32),
            pltpu.VMEM((TAIL, model), F32),
        ],
        compiler_params=pltpu.CompilerParams(vmem_limit_bytes=48 << 20),
        name="last_layer_backward",
    )(weight_1, rows, ends, grad_cls, x2, kv, q1, lse1, x1c, o1)


def first_back(refs, image, hidden, work, rows, store_mlp, store_mix, store_rest):
    patches, covered, weight_0, rows_table, grad_in, x0_in, x1_in, qkv_in, o0_in, lse0_in = refs
    model = weight_0.shape[0]
    images, count, pixels = patches.shape
    valid = count + 1
    scale = (model // HEADS) ** -0.5
    cut_o, cut_u, cut_d = 3 * model, 4 * model, 4 * model + hidden
    acc, acc_p, grad_s, grad_t, places = work

    def row(index):
        return rows_table[2 + index : 3 + index, :]

    def add_row(index, value):
        rows[2 + index : 3 + index, :] += value

    def add(ref, at, value):
        span = slice(at, at + value.shape[1])
        if image == 0:
            ref[:, span] = value
        else:
            ref[:, span] += value

    def mlp():
        grad_x = grad_in[image]
        unit_x, lift = norm_parts(x1_in[image])
        low = (unit_x * row(3) + row(4)).astype(BF16)
        wide, slope = gelu_both(mm(low, weight_0[:, cut_u:cut_d]))
        wide = wide.astype(BF16)
        down = mm_nt(wide, weight_0[:, cut_d:])
        add_row(5, column_sum(grad_x * down))
        grad_d = (grad_x * row(5)).astype(BF16)
        grad_u = (mm(grad_d, weight_0[:, cut_d:]) * slope).astype(BF16)
        add(acc, 0, mm_tn(low, grad_u))
        add(acc, hidden, mm_tn(grad_d, wide))
        grad_n = mm_nt(grad_u, weight_0[:, cut_u:cut_d])
        add_row(3, column_sum(grad_n * unit_x))
        add_row(4, column_sum(grad_n))
        grad_s[image] = grad_x + norm_back(grad_n, row(3), unit_x, lift)
        if image == images - 1:
            store_mlp()

    def attention():
        grad_x = grad_s[image]
        mixed = o0_in[image]
        add_row(2, column_sum(grad_x * mm(mixed, weight_0[:, cut_o:cut_u])))
        grad_a = (grad_x * row(2)).astype(BF16)
        add(acc, cut_o, mm_tn(mixed, grad_a))
        grad_o = mm_nt(grad_a, weight_0[:, cut_o:cut_u]).astype(BF16)
        qkv = qkv_in[image]
        grad_qkv = attend_back(
            grad_o, qkv[:, :model], qkv[:, model : 2 * model], qkv[:, 2 * model :],
            lse0_in[image], valid, scale,
        )
        grad_qkv = jnp.concatenate(grad_qkv, -1)
        grad_t[image] = grad_qkv
        unit_x, _ = norm_parts(x0_in[image])
        low = (unit_x * row(0) + row(1)).astype(BF16)
        add(acc, 0, mm_tn(low, grad_qkv))
        if image == images - 1:
            store_mix()

    def rest():
        grad_qkv = grad_t[image]
        unit_x, lift = norm_parts(x0_in[image])
        grad_n = mm_nt(grad_qkv, weight_0[:, :cut_o])
        add_row(0, column_sum(grad_n * unit_x))
        add_row(1, column_sum(grad_n))
        grad_x = grad_s[image] + norm_back(grad_n, row(0), unit_x, lift)
        places[...] += grad_x
        hide = covered[image]
        token = grad_x[:count, :]
        rows[0:1, :] += column_sum(token * hide)
        token = token * (1.0 - hide)
        rows[1:2, :] += column_sum(token)
        add(acc_p, 0, mm_tn(token.astype(BF16), patches[image]))
        if image == images - 1:
            store_rest()

    return mlp, attention, rest


def table_of(places, rows, count, total):
    table = jnp.concatenate(
        [places[count : count + 1, :], places[:count, :], places[count : count + 1, :], rows[...]],
        0,
    )
    return jnp.concatenate(
        [table, jnp.zeros((total - table.shape[0], table.shape[1]), F32)], 0
    )


def plan_of(pixels, columns, model, size):
    hidden = (columns - 4 * model) // 2
    patch_width = packed_width_p(pixels)
    patch_at = 2 * columns
    table_at = patch_at + patch_width
    width = (table_at + model + 3 * size - 1) // (3 * size) * 3 * size
    spans = (
        (1, 0, 0, columns),
        (0, 0, columns + 2 * hidden, 4 * model),
        (0, 4 * model, columns, 2 * hidden),
    )
    return (patch_at, patch_width, table_at, model, spans), width


def first_back_kernel(images, hidden, *refs):
    ins, (rows_in, tail, *work, rows) = refs[:10], refs[10:]
    start_sums(work[-1], rows, rows_in)
    run = back_pieces(ins, images, hidden, work, rows, tail, lambda value: value.astype(BF16))
    for piece, _ in run:
        piece()


def back_pieces(ins, images, hidden, work, rows, tail, shaped):
    acc, acc_p, _, _, places = work
    model = acc.shape[0]
    _, count, pixels = ins[0].shape
    mix = 2 * hidden
    patch_at = mix + 4 * model
    table_at = patch_at + packed_width_p(pixels)

    def store_mlp():
        tail[..., :mix] = shaped(acc[:, :mix])

    def store_mix():
        tail[..., mix:patch_at] = shaped(acc[:, : 4 * model])

    def store_rest():
        spare = tail.shape[-1] - table_at - model
        ends = [acc_p[...], jnp.zeros((model, packed_width_p(pixels) - pixels), F32)]
        ends.append(table_of(places, rows, count, model))
        if spare:
            ends.append(jnp.zeros((model, spare), F32))
        tail[..., patch_at:] = shaped(jnp.concatenate(ends, -1))

    blocks = [
        first_back(ins, image, hidden, work, rows, store_mlp, store_mix, store_rest)
        for image in range(images)
    ]
    return [
        (blocks[image][phase], phase + (image == images - 1))
        for phase in range(3)
        for image in range(images)
    ]


def start_sums(places, rows, rows_in):
    places[...] = jnp.zeros_like(places)
    rows[...] = rows_in[...]


def back_scratch(images, total, model, hidden, pixels, rows_shape):
    return [
        pltpu.VMEM((model, max(2 * hidden, 4 * model)), F32),
        pltpu.VMEM((model, pixels), F32),
        pltpu.VMEM((images, total, model), F32),
        pltpu.VMEM((images, total, 3 * model), BF16),
        pltpu.VMEM((total, model), F32),
        pltpu.VMEM(rows_shape, F32),
    ]


def first_back_plain(patches, covered, weight_0, rows, grad_in, saved, rows_in, width):
    images, count, pixels = patches.shape
    model, columns = weight_0.shape
    hidden = (columns - 4 * model) // 2
    ins = [patches, covered[..., None], weight_0, rows, grad_in]
    ins += [saved[index] for index in (0, 1, 3, 4, 5)] + [rows_in]
    vmem = pl.BlockSpec(memory_space=pltpu.VMEM)
    return pl.pallas_call(
        functools.partial(first_back_kernel, images, hidden),
        out_shape=jax.ShapeDtypeStruct((model, width), BF16),
        in_specs=[vmem] * len(ins),
        out_specs=vmem,
        scratch_shapes=back_scratch(images, count + TAIL, model, hidden, pixels, rows.shape),
        compiler_params=pltpu.CompilerParams(vmem_limit_bytes=58 << 20),
        name="first_layer_backward",
    )(*ins)


def back_reduce(
    patches, covered, weight_0, rows, grad_in, saved, rows_in, grads_1, squares, fsdp_count,
    collective_id
):
    images, count, pixels = patches.shape
    model, columns = weight_0.shape
    hidden = (columns - 4 * model) // 2
    size = model
    places, width = plan_of(pixels, columns, model, size)
    lines, own = fsdp_count // 2, model // fsdp_count
    cuts = width // (3 * size)
    last_cuts = columns // (3 * size)
    mlp_cuts = last_cuts + 2 * hidden // (3 * size)
    mix_cuts = 2 * last_cuts
    split = (lines, 2, own)
    ins = [patches, covered[..., None], weight_0, rows, grad_in]
    ins += [saved[index] for index in (0, 1, 3, 4, 5)]
    ins += [rows_in, grads_1.reshape(split + (columns,)), squares]
    blocks = (cuts,) + split + (size,)

    def kernel(*refs):
        parts, (rows_ref, grads_ref, squares_ref) = refs[:10], refs[10:13]
        outs, tail = refs[13:17], refs[17]
        work, rows_s, rest = refs[18:23], refs[23], refs[24:]
        whole = [last_cuts, mlp_cuts, mix_cuts, cuts]
        ready = [last_cuts]

        def shaped(value):
            return value.reshape(split + (value.shape[1],)).astype(BF16)

        start_sums(work[-1], rows_s, rows_ref)
        queue = back_pieces(parts, images, hidden, work, rows_s, tail, shaped)

        def part_of(cut, which, size):
            ref = grads_ref if cut < last_cuts else tail
            at = cut if cut < last_cuts else cut - last_cuts
            return ref.at[:, :, :, pl.ds(pl.multiple_of((3 * at + which) * size, 128), size)]

        def between(tick):
            if tick and queue:
                piece, done = queue.pop(0)
                piece()
                ready[0] = whole[done]
            return ready[0], 2 if queue else 1

        reduce_kernel(cuts, lines, places, part_of, squares_ref, outs, between, *rest)

    shape = jax.ShapeDtypeStruct
    sems = pltpu.SemaphoreType.DMA
    vmem = pl.BlockSpec(memory_space=pltpu.VMEM)
    return pl.pallas_call(
        kernel,
        out_shape=[
            shape((own, places[1]), F32),
            shape((2, own, columns), F32),
            shape((fsdp_count, own, model), F32),
            shape((8, 128), F32),
        ],
        in_specs=[vmem] * len(ins),
        out_specs=[vmem] * 4,
        scratch_shapes=[pltpu.VMEM(split + (width - columns,), BF16)]
        + back_scratch(images, count + TAIL, model, hidden, pixels, rows.shape)
        + [pltpu.VMEM(blocks, BF16)] * 3
        + [pltpu.VMEM((cuts, lines, own, size), BF16)] * 3
        + [
            pltpu.VMEM((cuts, 2, own, size), BF16),
            pltpu.VMEM((own, width), BF16),
            pltpu.VMEM((fsdp_count, own, model), BF16),
            pltpu.VMEM((fsdp_count, 8, 128), F32),
            sems((cuts, 4)),
            sems((cuts, 4)),
            sems((cuts, lines)),
            sems((cuts, lines)),
            sems((cuts, 4)),
            sems((cuts, 4)),
            sems((2, fsdp_count - 1)),
            sems((2, fsdp_count)),
        ],
        compiler_params=pltpu.CompilerParams(
            collective_id=collective_id, has_side_effects=True, vmem_limit_bytes=60 << 20
        ),
        name="back_reduce",
    )(*ins)


def packed_width_p(pixels):
    return (pixels + 127) // 128 * 128


def owners_of(low, high, rows, count):
    return [f for f in range(count) if f * rows < high and (f + 1) * rows > low]


def two_halves(value):
    half = value.shape[1] // 2
    return jnp.concatenate([value[:, :half], value[:, half:]], 0).astype(BF16)


def from_halves(slots):
    wide = slots.astype(F32)
    half = wide.shape[-1]
    first = wide[:, :8, :].reshape(-1, half)
    second = wide[:, 8:, :].reshape(-1, half)
    return jnp.concatenate([first, second], -1)


def student_rows(value, start=0):
    pieces = [value[at + start : at + start + 4, :] for at in range(0, value.shape[0], 8)]
    return jnp.concatenate(pieces, 0)


def sixteen(value):
    return jnp.concatenate([value, jnp.zeros_like(value)], 0).astype(BF16)


def head_kernel(
    sizes, cls_s, cls_t, gains, counted_row, counted_col, first_s_far, first_t_far, third_s_far,
    third_t_far, shard_s_far, shard_t_far, centre_far, proto_s, proto_t,
    grad_cls, ends, loss_row, totals, grad_logits, unit_rows, grad_head, squares,
    first_s, first_t, third_s, third_t, shard_s, shard_t, centre, table_s, table_t, loading, wide_s, wide_t, kept, left, acts, parts_out, parts_in, units,
    stats, pulls, pulled, backs, pieces, pieced, extra_1, extra_3, lefts, rights, tall,
    send, recv, send_z, recv_z, send_x, recv_x, send_d, recv_d,
):
    count, dp_count, rows, chunk = sizes
    fsdp, dp = lax.axis_index("fsdp"), lax.axis_index("dp")
    model, hidden = first_s.shape
    width = third_s.shape[0]
    top_2, top_3 = model, model + hidden
    top_4 = top_3 + width
    span = kept.shape[0] // 2
    base = fsdp * rows // 128 * 128
    offset = fsdp * rows - base
    slot_rows = 8 * count
    is_student = lax.broadcasted_iota(jnp.int32, (8, 1), 0) < 4
    owners_1 = owners_of(0, top_2, rows, count)
    owners_2 = owners_of(top_2, top_3, rows, count)
    owners_3 = owners_of(top_3, top_4, rows, count)

    own_k = table_s.shape[0]
    centre_part = centre_far.at[:, pl.ds(pl.multiple_of(fsdp * own_k, 128), own_k)]
    loads = [
        pltpu.make_async_copy(source, target, loading.at[number])
        for number, (source, target) in enumerate(
            (
                (first_s_far, first_s),
                (first_t_far, first_t),
                (shard_s_far, shard_s),
                (shard_t_far, shard_t),
                (third_s_far, third_s),
                (third_t_far, third_t),
                (centre_part, centre),
                (proto_s, table_s),
                (proto_t, table_t),
            )
        )
    ]
    for load in loads:
        load.start()

    barrier = pltpu.get_barrier_semaphore()
    for f_step in range(count):
        for d_step in range(dp_count):
            if f_step or d_step:
                peer_f = lax.rem(fsdp + f_step, count)
                peer_d = lax.rem(dp + d_step, dp_count)
                pl.semaphore_signal(barrier, 1, device_id=(peer_f, peer_d), device_id_type=MESH)
    pl.semaphore_wait(barrier, count * dp_count - 1)

    ACTS, PARTS, STATS, PULLS, BACKS, PIECES, TOTALS = range(7)

    def swap(kind, step, source_of, target):
        peer = lax.rem(fsdp + step, count)
        return pltpu.make_async_remote_copy(
            src_ref=source_of(peer),
            dst_ref=target.at[fsdp],
            send_sem=send.at[kind, step - 1],
            recv_sem=recv.at[kind, fsdp],
            device_id=(peer, dp),
            device_id_type=MESH,
        )

    def begin(kind, source_of, target):
        for step in range(1, count):
            swap(kind, step, source_of, target).start()

    def arrive(kind, target):
        for step in range(1, count):
            peer = lax.rem(fsdp + step, count)
            pltpu.make_async_remote_copy(
                src_ref=target.at[peer],
                dst_ref=target.at[peer],
                send_sem=send.at[kind, step - 1],
                recv_sem=recv.at[kind, peer],
                device_id=(peer, dp),
                device_id_type=MESH,
            ).wait_recv()

    def end(kind, source_of, target):
        for step in range(1, count):
            swap(kind, step, source_of, target).wait_send()

    def each_net(value, first, second, product):
        low = sixteen(value)
        return jnp.where(is_student, product(low, first)[:8, :], product(low, second)[:8, :])

    unit_c, lift_c = norm_parts(jnp.concatenate([cls_s[:4, :], cls_t[:4, :]], 0))
    loads[0].wait()
    loads[1].wait()
    normed = unit_c * gains[:8, :] + gains[8:, :]
    pre_a = each_net(normed, first_s[...], first_t[...], mm)
    act_a, slope_a = gelu_both(pre_a)
    acts[fsdp] = two_halves(act_a)
    begin(ACTS, lambda peer: acts.at[fsdp], acts)

    row = fsdp * rows + lax.broadcasted_iota(jnp.int32, (rows, 1), 0)
    inside = (row >= top_2) & (row < top_3)
    kept[...] = jnp.zeros_like(kept)
    loads[2].wait()
    loads[3].wait()
    place = pl.multiple_of(offset, 16)
    kept[pl.ds(place, rows), :] = jnp.where(inside, shard_s[...], 0.0).astype(BF16)
    kept[pl.ds(pl.multiple_of(span + offset, 16), rows), :] = jnp.where(
        inside, shard_t[...], 0.0
    ).astype(BF16)
    left[...] = jnp.zeros_like(left)
    columns = pl.ds(pl.multiple_of(base, 128), span)

    arrive(ACTS, acts)
    left[:, top_2:top_3] = from_halves(acts[...])
    asked = left[:, columns].astype(BF16)
    net = lax.broadcasted_iota(jnp.int32, (slot_rows, 1), 0) % 8 < 4
    product = jnp.where(net, mm(asked, kept[:span, :]), mm(asked, kept[span:, :]))
    for f in range(count):
        parts_out[f] = two_halves(product[8 * f : 8 * f + 8, :])
    parts_in[fsdp] = parts_out[fsdp]
    begin(PARTS, lambda peer: parts_out.at[peer], parts_in)
    arrive(PARTS, parts_in)
    summed = from_halves(parts_in[...])
    pre_b = summed[:8, :]
    for f in range(1, count):
        pre_b = pre_b + summed[8 * f : 8 * f + 8, :]
    act_b, slope_b = gelu_both(pre_b)
    loads[4].wait()
    loads[5].wait()
    raw = each_net(act_b, third_s[...], third_t[...], mm_nt)
    lift_z = lax.rsqrt(jnp.sum(raw * raw, -1, keepdims=True) + 1e-06)
    unit_z = raw * lift_z

    me = fsdp * dp_count + dp
    everyone = count * dp_count
    units[me] = two_halves(unit_z)

    def unit_copy(step):
        peer = lax.rem(me + step, everyone)
        return pltpu.make_async_remote_copy(
            src_ref=units.at[me],
            dst_ref=units.at[me],
            send_sem=send_z.at[step - 1],
            recv_sem=recv_z.at[me],
            device_id=(peer // dp_count, lax.rem(peer, dp_count)),
            device_id_type=MESH,
        )

    for step in range(1, everyone):
        unit_copy(step).start()

    def owner_copy(kind, owner, source, target):
        return pltpu.make_async_remote_copy(
            src_ref=source,
            dst_ref=target.at[fsdp],
            send_sem=send_x.at[kind, owner],
            recv_sem=recv_x.at[kind, fsdp],
            device_id=(owner, dp),
            device_id_type=MESH,
        )

    def owners_begin(kind, owners, target, value):
        target[fsdp] = value
        for owner in owners:
            pl.when(fsdp != owner)(
                lambda owner=owner: owner_copy(kind, owner, target.at[fsdp], target).start()
            )

    def owners_end(kind, owners, target):
        for owner in owners:
            pl.when(fsdp != owner)(
                lambda owner=owner: owner_copy(kind, owner, target.at[fsdp], target).wait_send()
            )

    def owners_arrive(kind, owners, target):
        for owner in owners:

            @pl.when(fsdp == owner)
            def _(owner=owner):
                for f in range(count):
                    if f != owner:
                        pltpu.make_async_remote_copy(
                            src_ref=target.at[f],
                            dst_ref=target.at[f],
                            send_sem=send_x.at[kind, owner],
                            recv_sem=recv_x.at[kind, f],
                            device_id=(f, dp),
                            device_id_type=MESH,
                        ).wait_recv()

    for step in range(1, everyone):
        peer = lax.rem(me + step, everyone)
        pltpu.make_async_remote_copy(
            src_ref=units.at[peer],
            dst_ref=units.at[peer],
            send_sem=send_z.at[step - 1],
            recv_sem=recv_z.at[peer],
            device_id=(peer // dp_count, lax.rem(peer, dp_count)),
            device_id_type=MESH,
        ).wait_recv()
    all_units = from_halves(units[...])
    all_units_s = student_rows(all_units)
    rows_s = all_units_s.astype(BF16)
    rows_t = student_rows(all_units, 4).astype(BF16)
    unit_rows[...] = rows_s

    for load in loads[6:]:
        load.wait()
    images = rows_s.shape[0]
    chunks = table_s.shape[0] // chunk
    low_start = jnp.full((images, 128), -3.0e38, F32)

    def lanes(op, value):
        out = value[:, :128]
        for at in range(128, value.shape[1], 128):
            out = op(out, value[:, at : at + 128])
        return out

    def logits_pass(index, tops):
        top_t, top_s = tops
        at = pl.ds(pl.multiple_of(index * chunk, chunk), chunk)
        raw_t = mm_nt(rows_t, table_t[at, :].astype(BF16))
        totals[fsdp, pl.ds(index, 1), :] = column_sum(counted_col[...] * raw_t)
        scaled_t = (raw_t - centre[:, at]) * (1.0 / TEACHER_TEMP)
        scaled_s = mm_nt(rows_s, table_s[at, :].astype(BF16)) * (1.0 / STUDENT_TEMP)
        wide_t[:, at] = scaled_t
        wide_s[:, at] = scaled_s
        return (
            jnp.maximum(top_t, lanes(jnp.maximum, scaled_t)),
            jnp.maximum(top_s, lanes(jnp.maximum, scaled_s)),
        )

    top_t, top_s = lax.fori_loop(0, chunks, logits_pass, (low_start, low_start))
    top_t = jnp.max(top_t, -1, keepdims=True)
    top_s = jnp.max(top_s, -1, keepdims=True)
    begin(TOTALS, lambda peer: totals.at[fsdp], totals)

    def expo_pass(index, sums):
        sum_t, sum_s, cross = sums
        at = pl.ds(pl.multiple_of(index * chunk, chunk), chunk)
        shifted_s = wide_s[:, at] - top_s
        expo_t = jnp.exp(wide_t[:, at] - top_t)
        expo_s = jnp.exp(shifted_s)
        wide_t[:, at] = expo_t
        wide_s[:, at] = expo_s
        return (
            sum_t + lanes(jnp.add, expo_t),
            sum_s + lanes(jnp.add, expo_s),
            cross + lanes(jnp.add, expo_t * shifted_s),
        )

    zero = jnp.zeros((images, 128), F32)
    sum_t, sum_s, cross = lax.fori_loop(0, chunks, expo_pass, (zero, zero, zero))
    lane = lax.broadcasted_iota(jnp.int32, (images, 128), 1)
    columns_of = zero
    values = (top_t, jnp.sum(sum_t, -1, keepdims=True), top_s, jnp.sum(sum_s, -1, keepdims=True),
              jnp.sum(cross, -1, keepdims=True))
    for number, value in enumerate(values):
        columns_of = jnp.where(lane == number, value, columns_of)
    stats[fsdp] = columns_of.T[:8, :]
    begin(STATS, lambda peer: stats.at[fsdp], stats)
    arrive(STATS, stats)
    gathered = [stats[f] for f in range(count)]
    high_t, high_s = gathered[0][0:1, :], gathered[0][2:3, :]
    for part in gathered[1:]:
        high_t = jnp.maximum(high_t, part[0:1, :])
        high_s = jnp.maximum(high_s, part[2:3, :])
    total_t = total_s = crossed = jnp.zeros_like(high_t)
    for part in gathered:
        lift_t = jnp.exp(part[0:1, :] - high_t)
        total_t = total_t + part[1:2, :] * lift_t
        total_s = total_s + part[3:4, :] * jnp.exp(part[2:3, :] - high_s)
        crossed = crossed + lift_t * (part[4:5, :] + (part[2:3, :] - high_s) * part[1:2, :])
    counted = counted_row[...]
    losses = counted * (jnp.log(total_s) - crossed / total_t)
    loss_row[...] = jnp.broadcast_to(jnp.sum(losses, -1, keepdims=True), losses.shape)
    weighting = counted / jnp.maximum(jnp.sum(counted, -1, keepdims=True), 1.0) / STUDENT_TEMP
    mine = stats[fsdp]
    share_s = weighting * jnp.exp(mine[2:3, :] - high_s) / total_s
    share_t = weighting * jnp.exp(mine[0:1, :] - high_t) / total_t
    turned = jnp.concatenate([share_s, share_t, jnp.zeros((126, images), F32)], 0).T
    share_s, share_t = turned[:, 0:1], turned[:, 1:2]

    turned_rows = all_units_s.T.astype(BF16)
    squares[...] = jnp.zeros_like(squares)

    def add_squares(value):
        total = squares[...]
        for row in range(0, value.shape[0], 8):
            strip = value[row : row + 8, :]
            total = total + lanes(jnp.add, strip * strip)
        squares[...] = total

    def grad_pass(index, total):
        at = pl.ds(pl.multiple_of(index * chunk, chunk), chunk)
        low = (wide_s[:, at] * share_s - wide_t[:, at] * share_t).astype(BF16)
        grad_logits[:, at] = low
        add_squares(mm(turned_rows, low))
        return total + mm(low, table_s[at, :].astype(BF16))

    partial = lax.fori_loop(0, chunks, grad_pass, jnp.zeros((images, width), F32))
    for slot in range(0, everyone, 2):
        pair = partial[4 * slot : 4 * slot + 8, :]
        pulls[slot] = pair
        pulls[slot + 1] = jnp.concatenate([pair[4:, :], pair[:4, :]], 0)
    pulled[fsdp] = pulls[me]
    begin(PULLS, lambda peer: pulls.at[peer * dp_count + dp], pulled)
    arrive(PULLS, pulled)
    grad_z = pulled[0]
    for f in range(1, count):
        grad_z = grad_z + pulled[f]
    grad_z = jnp.where(is_student, grad_z, 0.0)
    grad_raw = lift_z * (grad_z - unit_z * jnp.sum(unit_z * grad_z, -1, keepdims=True))
    grad_b = mm(sixteen(grad_raw), third_s[...])[:8, :]
    pre_grad_b = jnp.where(is_student, grad_b * slope_b, 0.0)
    backs[fsdp] = two_halves(pre_grad_b)
    begin(BACKS, lambda peer: backs.at[fsdp], backs)
    arrive(BACKS, backs)
    grads_b = from_halves(backs[...])
    piece = mm_nt(grads_b.astype(BF16), kept[:span, :])
    for f in range(count):
        pieces[f] = piece[8 * f : 8 * f + 8, :]
    pieced[fsdp] = pieces[fsdp]
    begin(PIECES, lambda peer: pieces.at[peer], pieced)

    owned = [
        (fsdp >= owners[0]) & (fsdp <= owners[-1]) for owners in (owners_1, owners_2, owners_3)
    ]

    def group_copy(kind, step, place):
        peer = lax.rem(dp + step, dp_count)
        return pltpu.make_async_remote_copy(
            src_ref=place(dp),
            dst_ref=place(dp),
            send_sem=send_d.at[kind, step - 1],
            recv_sem=recv_d.at[kind, dp],
            device_id=(fsdp, peer),
            device_id_type=MESH,
        )

    def group_arrive(kind, place):
        for step in range(1, dp_count):
            peer = lax.rem(dp + step, dp_count)
            pltpu.make_async_remote_copy(
                src_ref=place(peer),
                dst_ref=place(peer),
                send_sem=send_d.at[kind, step - 1],
                recv_sem=recv_d.at[kind, peer],
                device_id=(fsdp, peer),
                device_id_type=MESH,
            ).wait_recv()

    def right_at(number):
        return lambda group: rights.at[group, number]

    def left_at(group):
        return lefts.at[group]

    def group_begin(kind, place):
        for step in range(1, dp_count):
            group_copy(kind, step, place).start()

    def group_end(kind, place):
        for step in range(1, dp_count):
            group_copy(kind, step, place).wait_send()

    @pl.when(owned[1])
    def _():
        rights[dp, 1] = student_rows(grads_b).astype(BF16)
        group_begin(2, right_at(1))

    owners_begin(1, owners_3, extra_3, two_halves(jnp.concatenate([act_b, grad_raw], -1)))
    arrive(PIECES, pieced)
    back_a = jnp.zeros((8, left.shape[1]), F32)
    for f in range(count):
        at = f * rows // 128 * 128
        value = [pieced[f]]
        if at:
            value = [jnp.zeros((8, at), F32)] + value
        if left.shape[1] - at - span:
            value = value + [jnp.zeros((8, left.shape[1] - at - span), F32)]
        back_a = back_a + jnp.concatenate(value, -1)
    pre_grad_a = jnp.where(is_student, back_a[:, top_2:top_3] * slope_a, 0.0)
    spare = jnp.zeros((8, 2 * extra_1.shape[2] - model - hidden), F32)
    owners_begin(
        0, owners_1, extra_1, two_halves(jnp.concatenate([normed, pre_grad_a, spare], -1))
    )
    grad_n = jnp.where(is_student, mm_nt(sixteen(pre_grad_a), first_s[...])[:8, :], 0.0)
    grad_c = norm_back(grad_n, gains[:8, :], unit_c, lift_c)
    grad_cls[...] = jnp.concatenate([grad_c, jnp.zeros_like(grad_c)], 0)
    ends[...] = jnp.concatenate(
        [column_sum(grad_n * unit_c), column_sum(grad_n), jnp.zeros((6, model), F32)], 0
    )

    owners_arrive(1, owners_3, extra_3)

    @pl.when(owned[2])
    def _():
        extra = from_halves(extra_3[...])
        left[:, top_3:top_4] = extra[:, hidden:]
        rights[dp, 2] = student_rows(extra[:, :hidden]).astype(BF16)
        group_begin(3, right_at(2))

    owners_arrive(0, owners_1, extra_1)

    @pl.when(owned[0])
    def _():
        extra = from_halves(extra_1[...])
        left[:, :top_2] = extra[:, :model]
        rights[dp, 0] = student_rows(extra[:, model : model + hidden]).astype(BF16)
        group_begin(1, right_at(0))

    lefts[dp] = student_rows(left[:, columns]).astype(BF16)
    group_begin(0, left_at)
    group_arrive(0, left_at)
    tall[...] = jnp.zeros_like(tall)
    column = base + lax.broadcasted_iota(jnp.int32, (1, span), 1)
    for number, (low, high) in enumerate(((0, top_2), (top_2, top_3), (top_3, top_4))):

        @pl.when(owned[number])
        def _(number=number, low=low, high=high):
            group_arrive(1 + number, right_at(number))
            own_side = jnp.concatenate([lefts[group] for group in range(dp_count)], 0)
            keep_columns = ((column >= low) & (column < high)).astype(F32)
            own_side = (own_side.astype(F32) * keep_columns).astype(BF16)
            other = jnp.concatenate([rights[group, number] for group in range(dp_count)], 0)
            tall[...] += mm_tn(own_side, other)
            group_end(1 + number, right_at(number))

    grad_head[...] = tall[pl.ds(place, rows), :]

    def square_pass(index, carry):
        add_squares(grad_head[pl.ds(pl.multiple_of(index * 16, 16), 16), :])
        return carry

    lax.fori_loop(0, rows // 16, square_pass, 0)
    group_end(0, left_at)
    arrive(TOTALS, totals)
    end(ACTS, lambda peer: acts.at[fsdp], acts)
    end(PARTS, lambda peer: parts_out.at[peer], parts_in)
    end(STATS, lambda peer: stats.at[fsdp], stats)
    end(PULLS, lambda peer: pulls.at[peer * dp_count + dp], pulled)
    end(BACKS, lambda peer: backs.at[fsdp], backs)
    end(PIECES, lambda peer: pieces.at[peer], pieced)
    end(TOTALS, lambda peer: totals.at[fsdp], totals)
    for step in range(1, everyone):
        unit_copy(step).wait_send()
    owners_end(0, owners_1, extra_1)
    owners_end(1, owners_3, extra_3)


def head_step(
    cls_s, cls_t, vecs_s, vecs_t, weights, shards, centre, counted, protos, counts, collective_id
):
    count, dp_count = counts
    model, hidden = weights[0].shape
    width = weights[2].shape[0]
    rows = shards[0].shape[0]
    owned_k = protos[0].shape[0]
    images = counted.shape[0]
    everyone = count * dp_count
    span = max(f * rows % 128 + rows for f in range(count))
    span = (span + 127) // 128 * 128
    extent = max(f * rows // 128 * 128 + span for f in range(count))
    chunk = 1024
    gains = jnp.concatenate(
        [
            jnp.broadcast_to(vecs[vecs.shape[0] + row][None], (4, model))
            for row in (-2, -1)
            for vecs in (vecs_s, vecs_t)
        ]
    )
    shape = jax.ShapeDtypeStruct
    vmem = pl.BlockSpec(memory_space=pltpu.VMEM)
    anywhere = pl.BlockSpec(memory_space=pl.ANY)
    extra_width = (model + hidden + 255) // 256 * 128
    sems = pltpu.SemaphoreType.DMA
    return pl.pallas_call(
        functools.partial(head_kernel, (count, dp_count, rows, chunk)),
        out_shape=[
            shape((16, model), F32),
            shape((8, model), F32),
            shape((1, images), F32),
            shape((count, owned_k // chunk, chunk), F32),
            shape((images, owned_k), BF16),
            shape((images, width), BF16),
            shape((rows, hidden), F32),
            shape((8, 128), F32),
        ],
        in_specs=[vmem] * 5 + [anywhere] * 9,
        out_specs=[vmem] * 8,
        scratch_shapes=[pltpu.VMEM(array.shape, BF16) for array in (*weights, *shards)]
        + [
            pltpu.VMEM((1, owned_k), F32),
            pltpu.VMEM((owned_k, width), F32),
            pltpu.VMEM((owned_k, width), F32),
            sems((9,)),
            pltpu.VMEM((images, owned_k), F32),
            pltpu.VMEM((images, owned_k), F32),
            pltpu.VMEM((2 * span, hidden), BF16),
            pltpu.VMEM((8 * count, extent), F32),
            pltpu.VMEM((count, 16, hidden // 2), BF16),
            pltpu.VMEM((count, 16, hidden // 2), BF16),
            pltpu.VMEM((count, 16, hidden // 2), BF16),
            pltpu.VMEM((everyone, 16, width // 2), BF16),
            pltpu.VMEM((count, 8, 128), F32),
            pltpu.VMEM((everyone, 8, width), F32),
            pltpu.VMEM((count, 8, width), F32),
            pltpu.VMEM((count, 16, hidden // 2), BF16),
            pltpu.VMEM((count, 8, span), F32),
            pltpu.VMEM((count, 8, span), F32),
            pltpu.VMEM((count, 16, extra_width), BF16),
            pltpu.VMEM((count, 16, (hidden + width) // 2), BF16),
            pltpu.VMEM((dp_count, 4 * count, span), BF16),
            pltpu.VMEM((dp_count, 3, 4 * count, hidden), BF16),
            pltpu.VMEM((span, hidden), F32),
            sems((7, count - 1)),
            sems((7, count)),
            sems((everyone - 1,)),
            sems((everyone,)),
            sems((2, count)),
            sems((2, count)),
            sems((4, dp_count - 1)),
            sems((4, dp_count)),
        ],
        compiler_params=pltpu.CompilerParams(
            collective_id=collective_id, has_side_effects=True, vmem_limit_bytes=60 << 20
        ),
        name="head_step",
    )(
        cls_s, cls_t, gains, counted[None], counted[:, None], *weights, *shards, centre[None], *protos
    )


def dot(left, right, dims):
    return lax.dot_general(left, right, (dims, ((), ())), preferred_element_type=F32)


def layer_norm(x, gain, shift):
    centred = x - jnp.mean(x, -1, keepdims=True)
    spread = jnp.mean(centred * centred, -1, keepdims=True)
    return centred * lax.rsqrt(spread + 1e-06) * gain + shift


def gelu_slope(x):
    _, pull = jax.vjp(jax.nn.gelu, x)
    return pull(jnp.ones_like(x))[0]


def head_forward(cls, weight, vecs):
    width, hidden = cls.shape[1], weight.shape[1]
    low_n = layer_norm(cls, vecs[-2], vecs[-1]).astype(BF16)
    pre_a = jnp.dot(low_n, weight[:width], preferred_element_type=F32)
    low_a = jax.nn.gelu(pre_a).astype(BF16)
    pre_b = jnp.dot(low_a, weight[width : width + hidden], preferred_element_type=F32)
    low_b = jax.nn.gelu(pre_b).astype(BF16)
    raw = dot(low_b, weight[width + hidden :], ((1,), (1,)))
    return low_n, pre_a, low_a, pre_b, low_b, raw


def unit(raw):
    return raw * lax.rsqrt(jnp.sum(raw * raw, -1, keepdims=True) + 1e-06)


def adamw(weight, moment, second, gradient, factor, step_rate, weight_decay):
    clipped = gradient * factor
    moment = BETA_ONE * moment + (1.0 - BETA_ONE) * clipped
    second = BETA_TWO * second + (1.0 - BETA_TWO) * clipped * clipped
    direction = (
        moment / (1.0 - BETA_ONE**STEP) / (jnp.sqrt(second / (1.0 - BETA_TWO**STEP)) + 1e-08)
    )
    return (weight - step_rate * (direction + weight_decay * weight), moment, second)


def own_kernels(local, head_rows, model, hidden, total, layer_columns):
    count = lax.axis_size("fsdp")
    if lax.axis_size("dp") != 4 or count not in (4, 8) or local != 4 or head_rows % 16:
        return False
    if model % (16 * count) or hidden % 256 or layer_columns % (3 * model):
        return False
    for low, high in ((0, model), (hidden + model, total)):
        rows = (high - low) // count
        if rows % 16 or any((low + rows * f) % head_rows + rows > head_rows for f in range(count)):
            return False
    return True


def head_plain(
    cls, teacher_cls, vectors, teacher_vectors, head_full, teacher_head_full, own_centre, counted,
    counted_total, w_proto, teacher_proto, own_rows,
):
    teacher_unit = unit(head_forward(teacher_cls, teacher_head_full, teacher_vectors)[-1])
    low_n, pre_a, low_a, pre_b, low_b, raw = head_forward(cls, head_full, vectors)
    bottleneck, pull_unit = jax.vjp(unit, raw)
    both = jnp.concatenate([teacher_unit.astype(BF16), bottleneck.astype(BF16)], -1)
    both = lax.all_gather(both, ("fsdp", "dp"), axis=0, tiled=True)
    width = raw.shape[1]
    teacher_rows, student_rows = both[:, :width], both[:, width:]

    low_proto = w_proto.astype(BF16)
    teacher_logits = dot(teacher_rows, teacher_proto.astype(BF16), ((1,), (1,)))
    logits = dot(student_rows, low_proto, ((1,), (1,)))
    scaled_t = (teacher_logits - own_centre) / TEACHER_TEMP
    scaled_s = logits / STUDENT_TEMP
    max_t = jnp.max(scaled_t, -1)
    max_s = jnp.max(scaled_s, -1)
    expo_t = jnp.exp(scaled_t - max_t[:, None])
    expo_s = jnp.exp(scaled_s - max_s[:, None])
    parts = jnp.stack(
        [
            max_t,
            jnp.sum(expo_t, -1),
            max_s,
            jnp.sum(expo_s, -1),
            jnp.sum(expo_t * (scaled_s - max_s[:, None]), -1),
        ]
    )
    parts = lax.all_gather(parts, "fsdp", axis=0)
    top_t = jnp.max(parts[:, 0], 0)
    lift_t = jnp.exp(parts[:, 0] - top_t)
    total_t = jnp.sum(parts[:, 1] * lift_t, 0)
    top_s = jnp.max(parts[:, 2], 0)
    total_s = jnp.sum(parts[:, 3] * jnp.exp(parts[:, 2] - top_s), 0)
    crossed = jnp.sum(lift_t * (parts[:, 4] + (parts[:, 2] - top_s) * parts[:, 1]), 0) / total_t
    losses = jnp.log(total_s) - crossed
    loss_total = jnp.sum(counted * losses)
    weighting = counted / counted_total / STUDENT_TEMP
    share_s = weighting * jnp.exp(max_s - top_s) / total_s
    share_t = weighting * jnp.exp(max_t - top_t) / total_t
    grad_logits = (expo_s * share_s[:, None] - expo_t * share_t[:, None]).astype(BF16)
    teacher_sum = jnp.sum(counted[:, None] * teacher_logits, 0)
    teacher_total = lax.all_gather(teacher_sum, "fsdp", axis=0, tiled=True)
    grad_proto = dot(grad_logits, student_rows, ((0,), (0,)))
    grad_rows = jnp.dot(grad_logits, low_proto, preferred_element_type=F32)
    dp_count = lax.axis_size("dp")
    grad_rows = grad_rows.reshape(-1, dp_count, cls.shape[0], width)
    grad_rows = lax.dynamic_index_in_dim(grad_rows, lax.axis_index("dp"), 1, keepdims=False)
    grad_bottleneck = lax.psum_scatter(grad_rows, "fsdp", scatter_dimension=0, tiled=False)

    model_width, hidden = cls.shape[1], head_full.shape[1]
    local = cls.shape[0]
    low_dz = pull_unit(grad_bottleneck)[0].astype(BF16)
    grad_b = jnp.dot(low_dz, head_full[model_width + hidden :], preferred_element_type=F32)
    low_db = (grad_b * gelu_slope(pre_b)).astype(BF16)
    grad_a = dot(low_db, head_full[model_width : model_width + hidden], ((1,), (1,)))
    low_da = (grad_a * gelu_slope(pre_a)).astype(BF16)
    grad_n = dot(low_da, head_full[:model_width], ((1,), (1,)))
    _, pull_norm = jax.vjp(layer_norm, cls, vectors[-2], vectors[-1])
    grad_cls, grad_gain, grad_shift = pull_norm(grad_n)

    packed = jnp.concatenate([low_n, low_a, low_dz, low_da, low_db, low_b], -1)
    packed = lax.all_gather(packed, ("fsdp", "dp"), axis=0, tiled=True)
    total_rows = model_width + hidden + width
    lefts, rights = packed[:, :total_rows], packed[:, total_rows:]
    start = lax.axis_index("fsdp") * own_rows
    left = lax.dynamic_slice_in_dim(lefts, start, own_rows, 1)
    row = start + lax.broadcasted_iota(jnp.int32, (1, own_rows), 1)
    kind = jnp.where(row < model_width, 0, jnp.where(row < model_width + hidden, 1, 2))
    left = jnp.concatenate([jnp.where(kind == index, left, 0) for index in range(3)], 0)
    right = jnp.concatenate(
        [rights[:, index * hidden : (index + 1) * hidden] for index in range(3)], 0
    )
    grad_head = dot(left, right, ((0,), (0,)))
    ends = jnp.stack([grad_gain, grad_shift])
    return grad_cls, ends, loss_total, teacher_total, grad_proto, grad_head


def per_device(
    patches,
    patch_mask,
    image_valid,
    centre,
    w_patch,
    first_patch,
    second_patch,
    teacher_patch,
    w_layer,
    first_layer,
    second_layer,
    teacher_layer,
    w_head,
    first_head,
    second_head,
    teacher_head,
    w_proto,
    first_proto,
    second_proto,
    teacher_proto,
    vectors,
    first_vectors,
    second_vectors,
    teacher_vectors,
):
    everyone = ("fsdp", "dp")
    local = patches.shape[0]
    place = lax.axis_index(everyone) * local
    fsdp_index = lax.axis_index("fsdp")
    counted = image_valid.astype(F32)
    counted_total = jnp.maximum(jnp.sum(counted), 1.0)
    covered = patch_mask.astype(F32)
    pixels = w_patch.shape[1]
    model_width, columns = w_layer.shape[1] * lax.axis_size("fsdp"), w_layer.shape[2]
    pad = packed_width_p(pixels) - pixels

    def low_blocks(patch, layers):
        patch = jnp.pad(patch, ((0, 0), (0, pad)))
        return [array.astype(BF16) for array in (patch, layers[0], layers[1])]

    head_s, head_t = w_head.astype(BF16), teacher_head.astype(BF16)
    blocks = low_blocks(teacher_patch, teacher_layer) + low_blocks(w_patch, w_layer)
    hidden = w_head.shape[1]
    fsdp_count = lax.axis_size("fsdp")
    own_rows, own_k = w_head.shape[0], w_proto.shape[0]
    total_rows = own_rows * fsdp_count
    own = own_kernels(local, own_rows, model_width, hidden, total_rows, columns)
    if own:
        ranges = ((0, model_width), (model_width + hidden, total_rows))
        full, teacher_rows, cls_rows, saved = gather_forward(
            blocks, (head_s, head_t), ranges, fsdp_count, patches, covered, vectors,
            teacher_vectors, 1,
        )
    else:
        full = [
            lax.all_gather(block, "fsdp", axis=0, tiled=True)
            for block in blocks + [head_s, head_t]
        ]
        teacher_rows = forward(
            patches, jnp.zeros_like(covered), *full[:3], teacher_vectors, False
        )[0]
        cls_rows, *saved = forward(patches, covered, *full[3:6], vectors, True)
    patch_full, layer_0, layer_1 = full[3:6]
    if own:
        grad_cls, ends, loss_row, totals, grad_logits, unit_rows, grad_head, part = head_step(
            cls_rows, teacher_rows, vectors, teacher_vectors, full[6:], (head_s, head_t),
            centre, counted, (w_proto, teacher_proto), (fsdp_count, lax.axis_size("dp")), 3,
        )
        loss_total = loss_row[0, 0]
        teacher_total = totals.reshape(-1)
        grad_proto = dot(grad_logits, unit_rows, ((0,), (0,)))
    else:
        grad_cls, ends, loss_total, teacher_total, grad_proto, grad_head = head_plain(
            cls_rows[:local], teacher_rows[:local], vectors, teacher_vectors, full[6], full[7],
            lax.dynamic_slice_in_dim(centre, fsdp_index * own_k, own_k), counted, counted_total,
            w_proto, teacher_proto, own_rows,
        )
        ends = jnp.pad(ends, ((0, 6), (0, 0)))
        grad_cls = jnp.pad(grad_cls, ((0, TAIL - local), (0, 0)))
    _, rows_table = split_table(vectors, patches.shape[1])
    grads_1, grad_x, rows_grad = last_back(layer_1, rows_table, ends, grad_cls, saved)
    if own:
        own_patch, own_layers, table, sums = back_reduce(
            patches, covered, layer_0, rows_table, grad_x, saved, rows_grad, grads_1, part,
            fsdp_count, 2,
        )
        vector_grad = table.reshape(model_width, model_width)[: vectors.shape[0]]
        own_patch = own_patch[:, :pixels]
        squares = sums[0, 0]
    else:
        places, width = plan_of(pixels, columns, model_width, model_width)
        tail = first_back_plain(
            patches, covered, layer_0, rows_table, grad_x, saved, rows_grad, width - columns
        )
        packed_grads = jnp.concatenate([grads_1, tail], 1)
        owned = lax.psum_scatter(packed_grads, "fsdp", scatter_dimension=0, tiled=True)
        owned = lax.psum(owned, "dp").astype(F32)
        patch_at, _, table_at, _, spans = places
        own_patch = owned[:, patch_at : patch_at + pixels]
        first_layer_parts = [
            owned[:, start : start + span] for layer, _, start, span in spans if layer == 0
        ]
        own_layers = jnp.stack([jnp.concatenate(first_layer_parts, 1), owned[:, :columns]])
        own_table = owned[:, table_at : table_at + model_width]
        table = lax.all_gather(own_table, "fsdp", axis=0, tiled=True)
        vector_grad = table[: vectors.shape[0]]
        parts = (own_patch, own_layers, grad_head, grad_proto, own_table)
        squares = lax.psum(sum(jnp.sum(value * value) for value in parts), "fsdp")
    owned_grads = (own_patch, own_layers, grad_head, grad_proto)
    norm_value = jnp.sqrt(squares)
    factor = CLIP_NORM / jnp.maximum(norm_value, CLIP_NORM)
    updated_centre = CENTRE_KEEP * centre + (1.0 - CENTRE_KEEP) * teacher_total / counted_total
    weights_owned = (w_patch, w_layer, w_head, w_proto, vectors)
    moments = (first_patch, first_layer, first_head, first_proto, first_vectors)
    seconds = (second_patch, second_layer, second_head, second_proto, second_vectors)
    teachers = (teacher_patch, teacher_layer, teacher_head, teacher_proto, teacher_vectors)
    gradients = owned_grads + (vector_grad,)
    results = [loss_total, counted_total, norm_value, updated_centre]
    for group in range(5):
        updated, moment, second = adamw(
            weights_owned[group],
            moments[group],
            seconds[group],
            gradients[group],
            factor,
            RATES[group],
            DECAYS[group],
        )
        results.extend(
            [
                updated,
                moment,
                second,
                TEACHER_KEEP * teachers[group] + (1.0 - TEACHER_KEEP) * updated,
            ]
        )
    return tuple(results)


def solution(mesh):
    whole, rows, middle = P(), P("fsdp", None), P(None, "fsdp", None)
    in_specs = (
        (P(("fsdp", "dp"), None, None), P(("fsdp", "dp"), None), whole, whole)
        + (rows,) * 4
        + (middle,) * 4
        + (rows,) * 8
        + (whole,) * 4
    )
    out_specs = (whole,) * 4 + (rows,) * 4 + (middle,) * 4 + (rows,) * 8 + (whole,) * 4
    return jax.shard_map(
        per_device, mesh=mesh, in_specs=in_specs, out_specs=out_specs, check_vma=False
    )
```
